32 devices in a mesh: section: 2 (over core), dp: 16 (over z, y, x).
Axes of the slice: x: 2, y: 2, z: 4, core: 2. Of those that a mesh axis runs over, the one named last changes fastest.
Arguments:
- patches: bfloat16 [32, 512, 768], P('dp'), may hold values from -6 to 6
- segment_ids: int32 [32, 512], P('dp'), may hold values from 0 to 3, never falling along the last dimension, each value on 1 to 257 neighbouring positions
- pad_counts: int32 [32], P('dp'), may hold values from 0 to 64
- norm1_gain: float32 [2, 768], P('section'), may hold values from 0.25 to 1.75
- norm1_bias: float32 [2, 768], P('section'), may hold values from -1.75 to 1.75
- qkv_weight: bfloat16 [2, 768, 2304], P('section'), may hold values from -0.21875 to 0.21875
- query_bias: float32 [2, 768], P('section'), may hold values from -3 to 3
- value_bias: float32 [2, 768], P('section'), may hold values from -3 to 3
- rel_table: float32 [2, 12, 513], P('section'), may hold values from -6 to 6
- proj_weight: bfloat16 [2, 768, 768], P('section'), may hold values from -1.75 to 1.75
- proj_bias: float32 [2, 768], P('section'), may hold values from -1.75 to 1.75
- scale_attn: float32 [2, 768], P('section'), may hold values from 0.5 to 1.5
- norm2_gain: float32 [2, 768], P('section'), may hold values from 0.25 to 1.75
- norm2_bias: float32 [2, 768], P('section'), may hold values from -1.75 to 1.75
- fc1_weight: bfloat16 [2, 768, 3072], P('section'), may hold values from -0.21875 to 0.21875
- fc1_bias: float32 [2, 3072], P('section'), may hold values from -1.75 to 1.75
- fc2_weight: bfloat16 [2, 3072, 768], P('section'), may hold values from -0.109375 to 0.109375
- fc2_bias: float32 [2, 768], P('section'), may hold values from -1.75 to 1.75
- scale_mlp: float32 [2, 768], P('section'), may hold values from 0.5 to 1.5
- cotangent: bfloat16 [32, 512, 768], P('dp'), may hold values from -8 to 8
Outputs:
- layer_outputs: bfloat16 [2, 32, 512, 768], P('section', 'dp')
- input_grads: bfloat16 [2, 32, 512, 768], P('section', 'dp')
- grad_norm1_gain: float32 [2, 768], P('section')
- grad_norm1_bias: float32 [2, 768], P('section')
- grad_qkv_weight: float32 [2, 768, 2304], P('section')
- grad_query_bias: float32 [2, 768], P('section')
- grad_value_bias: float32 [2, 768], P('section')
- grad_rel_table: float32 [2, 12, 513], P('section')
- grad_proj_weight: float32 [2, 768, 768], P('section')
- grad_proj_bias: float32 [2, 768], P('section')
- grad_scale_attn: float32 [2, 768], P('section')
- grad_norm2_gain: float32 [2, 768], P('section')
- grad_norm2_bias: float32 [2, 768], P('section')
- grad_fc1_weight: float32 [2, 768, 3072], P('section')
- grad_fc1_bias: float32 [2, 3072], P('section')
- grad_fc2_weight: float32 [2, 3072, 768], P('section')
- grad_fc2_bias: float32 [2, 768], P('section')
- grad_scale_mlp: float32 [2, 768], P('section')
The draws below stay inside these ranges and needn't reach their ends.
Inputs may be any that keep to these rules, and one draw needn't show every extreme that they name: `segment_ids`: each row numbers its images from 0 upward, never falling; each image takes 1 to 257 positions, and one image in each row takes exactly 257. The last pad_counts positions of a row are padding.
All inputs are finite; a program needn't handle non-finite values.
Results may differ from the reference program's by a relative error of at most 0.015.
Values may be sent and summed in bfloat16 or wider, within the bound.
A program may use at most 384 MiB of HBM per device.

```python
import math
import jax
import jax.numpy as jnp
import numpy as np
from jax import lax

D = 768
FF = 3072
H = 12
HD = 64
MB_TOK = 512
LMAX = 257
SEGS = 4
NREL = 513
ROWS = 32


def draw_cotangent(key, part):
    key = jax.random.fold_in(key, 7)
    rising = jnp.arange(ROWS, dtype=jnp.float32) / max(ROWS - 1, 1)
    base = jax.random.normal(key, (ROWS, MB_TOK, D), jnp.float32)
    factor = 3.0 ** rising / 1.7
    return jnp.clip(base * factor[:, None, None], -8.0, 8.0).astype(jnp.bfloat16)


def set_ends(values, own_key, low, largest):
    longest = values.shape.index(max(values.shape))
    spots = []
    for shift in (0, 1):
        where = [jax.random.randint(jax.random.fold_in(own_key, axis), (), 0, length) for axis, length in enumerate(values.shape)]
        where[longest] = (where[longest] + shift) % values.shape[longest]
        spots.append(tuple(where))
    return values.at[spots[0]].set(low).at[spots[1]].set(largest)


def levels(own_key, dims, shards, low, largest):
    loudness, own = 1.0, jax.random.fold_in(own_key, 6)
    for position, parts in shards:
        heights = jnp.exp(jax.random.uniform(jax.random.fold_in(own, position), (parts,), jnp.float32, low / len(shards), largest / len(shards)))
        loudness = loudness * jnp.repeat(heights, dims[position] // parts).reshape([-1 if axis == position else 1 for axis in range(len(dims))])
    return loudness


def profile(amount, total, bound, slope):
    loads = [(1 << 20) // math.isqrt(grade ** slope) + 1 for grade in range(2, amount + 1)]
    rest, given = total - bound - (amount - 1), [1] * (amount - 1)
    while rest > 0:
        movable = [i for i in range(amount - 1) if given[i] < bound]
        pool, budget = sum([loads[i] for i in movable]), rest
        for i in movable:
            addition = min(bound - given[i], max(1, budget * loads[i] // pool), rest)
            given[i] = given[i] + addition
            rest = rest - addition
    return np.array([bound] + given)


def uneven_parts(rng, count, total, most, slope):
    if count == 2:
        one = jax.random.randint(rng, (), max(1, total - most), min(most, total - 1) + 1)
        return jnp.stack([one, total - one])
    tallies = jnp.asarray(profile(count, total, most, slope), jnp.int32)
    twos = (count - 1) // 2
    donor, receiver = tallies[1:1 + 2 * twos:2], tallies[2:2 + 2 * twos:2]
    margin = jnp.minimum(donor - 1, most - receiver)
    shifted = jax.random.randint(jax.random.fold_in(rng, 1), (twos,), 0, 1 << 20) % (margin + 1)
    tallies = tallies.at[1:1 + 2 * twos:2].set(donor - shifted).at[2:2 + 2 * twos:2].set(receiver + shifted)
    return tallies[jax.random.permutation(jax.random.fold_in(rng, 2), count)]


def noise(stream_key, dims, deviation, bound, pieces=(), kind=jnp.bfloat16):
    array = jax.random.normal(stream_key, dims, jnp.float32) * deviation
    if len(pieces) > 0:
        array = levels(stream_key, dims, pieces, -0.22, 0.18) * array
    return jnp.clip(array, min=-bound, max=bound).astype(kind)


def setup_inputs(seed: int = 0) -> dict:
    key_list = jax.random.split(jax.random.key(seed), 21)
    return {
        "patches": noise(key_list[0], (ROWS, MB_TOK, D), 1.0, 6.0, ((0, 16),)),
        "segment_ids": jax.vmap(lambda own: jnp.searchsorted(jnp.cumsum(uneven_parts(own, SEGS, MB_TOK, LMAX, 1)), jnp.arange(MB_TOK), side="right"))(jax.random.split(key_list[1], ROWS)).reshape((ROWS, MB_TOK)).astype(jnp.int32),
        "pad_counts": set_ends(jax.random.randint(key_list[2], (ROWS,), 0, MB_TOK // 8 + 1), jax.random.fold_in(key_list[2], 1), 0, (MB_TOK // 8 + 1) - 1).astype(jnp.int32),
        "norm1_gain": jnp.clip(1.0 + 0.15 * jax.random.normal(key_list[3], (2, D), jnp.float32), 0.25, 1.75),
        "norm1_bias": noise(key_list[4], (2, D), 0.3, 1.75, ((0, 2),), jnp.float32),
        "qkv_weight": noise(key_list[5], (2, D, 3 * D), D ** -0.5, 0.21875, ((0, 2),)),
        "query_bias": noise(key_list[6], (2, D), 0.5, 3.0, ((0, 2),), jnp.float32),
        "value_bias": noise(key_list[7], (2, D), 0.5, 3.0, ((0, 2),), jnp.float32),
        "rel_table": noise(key_list[8], (2, H, NREL), 1.0, 6.0, ((0, 2),), jnp.float32),
        "proj_weight": noise(key_list[9], (2, D, D), (D // 64) ** -0.5, 1.75, ((0, 2),)),
        "proj_bias": noise(key_list[10], (2, D), 0.3, 1.75, ((0, 2),), jnp.float32),
        "scale_attn": jnp.clip(0.5 + 1.0 * jax.random.uniform(key_list[11], (2, D), jnp.float32) ** levels(key_list[11], (2, D), ((0, 2),), -0.2, 0.2), 0.5, 1.5),
        "norm2_gain": jnp.clip(1.0 + 0.15 * jax.random.normal(key_list[12], (2, D), jnp.float32), 0.25, 1.75),
        "norm2_bias": noise(key_list[13], (2, D), 0.3, 1.75, ((0, 2),), jnp.float32),
        "fc1_weight": noise(key_list[14], (2, D, FF), D ** -0.5, 0.21875, ((0, 2),)),
        "fc1_bias": noise(key_list[15], (2, FF), 0.3, 1.75, ((0, 2),), jnp.float32),
        "fc2_weight": noise(key_list[16], (2, FF, D), FF ** -0.5, 0.109375, ((0, 2),)),
        "fc2_bias": noise(key_list[17], (2, D), 0.3, 1.75, ((0, 2),), jnp.float32),
        "scale_mlp": jnp.clip(0.5 + 1.0 * jax.random.uniform(key_list[18], (2, D), jnp.float32) ** levels(key_list[18], (2, D), ((0, 2),), -0.2, 0.2), 0.5, 1.5),
        "cotangent": draw_cotangent(jax.random.fold_in(key_list[20], 71), 0),
    }


@jax.custom_vjp
def low(v):
    return lax.optimization_barrier(v.astype(jnp.bfloat16)).astype(jnp.float32)

@jax.custom_vjp
def low_back(v):
    return v

def low_keep(v):
    return (low(v), None)

def low_pass(kept, grad):
    return (grad,)

def back_keep(v):
    return (v, None)

def back_low(kept, grad):
    return (low(grad),)
low.defvjp(low_keep, low_pass)
low_back.defvjp(back_keep, back_low)

def round_both(values):
    return low_back(low(values))

def matmul(left, right):
    return jnp.dot(left, right, precision=lax.Precision.HIGHEST, preferred_element_type=jnp.float32)

def geometry(segments, padding, longest):
    length = segments.shape[0]
    positions = jnp.arange(length, dtype=jnp.int32)
    boundary = jnp.concatenate([jnp.ones((1,), bool), segments[1:] != segments[:-1]])
    starts = lax.cummax(jnp.where(boundary, positions, 0).astype(jnp.int32), axis=0)
    places = positions - starts
    living = positions < length - padding
    allowed = (segments[:, None] == segments[None, :]) & living[None, :] | (positions[:, None] == positions[None, :])
    rel_index = jnp.clip(places[None, :] - places[:, None] + longest - 1, 0, 2 * longest - 2).astype(jnp.int32)
    return (allowed, rel_index)

def normalize(values):
    centered = values - lax.optimization_barrier(jnp.mean(values, -1, keepdims=True))
    return centered * lax.rsqrt(lax.optimization_barrier(jnp.mean(centered * centered, -1, keepdims=True)) + 1e-06)

def layer(stream, params, allowed, rel_index):
    gain_one, shift_one, qkv_weight, query_bias, value_bias, rel_table, proj_weight, proj_bias, scale_attn, gain_two, shift_two, fc1_weight, fc1_bias, fc2_weight, fc2_bias, scale_mlp = params
    length = stream.shape[0]
    factor = HD ** (-0.5)
    normed_one = low(normalize(stream) * gain_one + shift_one)
    projected = matmul(normed_one, qkv_weight)
    queries = round_both((projected[:, :D] + query_bias) * factor).reshape(length, H, HD)
    keys_part = round_both(projected[:, D:2 * D]).reshape(length, H, HD)
    values_part = round_both(projected[:, 2 * D:] + value_bias).reshape(length, H, HD)
    raw = low_back(jnp.einsum('qhd,khd->hqk', queries, keys_part, precision=lax.Precision.HIGHEST))
    scores = jnp.where(allowed[None], raw + rel_table[:, rel_index], -1000000000.0)
    probs = low(jax.nn.softmax(scores, axis=-1))
    mixed = round_both(jnp.einsum('hqk,khd->qhd', probs, values_part, precision=lax.Precision.HIGHEST).reshape(length, D))
    proj_out = low_back(matmul(mixed, proj_weight) + proj_bias)
    resid = stream + scale_attn * proj_out
    normed_two = low(normalize(resid) * gain_two + shift_two)
    pre_act = low_back(matmul(normed_two, fc1_weight) + fc1_bias)
    activated = low(jax.nn.gelu(pre_act, approximate=False))
    mlp_out = low_back(matmul(activated, fc2_weight) + fc2_bias)
    return resid + scale_mlp * mlp_out

def reference(patches, segment_ids, pad_counts, norm1_gain, norm1_bias, qkv_weight, query_bias, value_bias, rel_table, proj_weight, proj_bias, scale_attn, norm2_gain, norm2_bias, fc1_weight, fc1_bias, fc2_weight, fc2_bias, scale_mlp, cotangent):
    params = tuple((p.astype(jnp.float32) for p in (norm1_gain, norm1_bias, qkv_weight, query_bias, value_bias, rel_table, proj_weight, proj_bias, scale_attn, norm2_gain, norm2_bias, fc1_weight, fc1_bias, fc2_weight, fc2_bias, scale_mlp)))
    zeros = jax.tree.map(jnp.zeros_like, params)

    def step(carry, row):
        tokens_row, segments, padding, cot_row = row
        allowed, rel_index = geometry(segments, padding, LMAX)

        def model(weights, offset, stream):
            first = tuple((t[0] for t in weights))
            second = tuple((t[1] for t in weights))
            lower = round_both(layer(stream, first, allowed, rel_index))
            upper = low(layer(lower + offset, second, allowed, rel_index))
            return (upper, lower)
        stream = tokens_row.astype(jnp.float32)
        offset = jnp.zeros_like(stream)
        upper, back, lower = jax.vjp(model, params, offset, stream, has_aux=True)
        grad_params, grad_offset, grad_stream = back(cot_row.astype(jnp.float32))
        return (jax.tree.map(jnp.add, carry, grad_params), (lower, upper, grad_stream, grad_offset))
    totals, (lowers, uppers, grad_in, grad_mid) = lax.scan(step, zeros, (patches, segment_ids, pad_counts, cotangent))
    outputs = jnp.stack([lowers, uppers]).astype(jnp.bfloat16)
    grads_in = jnp.stack([grad_in, grad_mid]).astype(jnp.bfloat16)
    return (outputs, grads_in, totals[0], totals[1], totals[2], totals[3], totals[4], totals[5], totals[6], totals[7], totals[8], totals[9], totals[10], totals[11], totals[12], totals[13], totals[14], totals[15])
```

```python
import functools
import math

import jax
import jax.numpy as jnp
from jax import lax
from jax.experimental import pallas as pl
from jax.experimental.pallas import tpu as pltpu
from jax.sharding import PartitionSpec as P


MESH = pl.DeviceIdType.MESH
BLOCK = 256


def reduce_kernel(
    bits, chunks, blocks, lag, *refs
):
    (a_ref, dm_ref, h2_ref, dz_ref, h1_ref, dp_ref, o_ref, dproj_ref, small_ref, out_ref, small_out_ref) = refs[:11]
    (lhs, rhs, grads, total, small_total, *received) = refs[11 : 16 + 2 * bits]
    (load_sem, send_sem, recv_sem, small_send, small_recv, store_sem) = refs[16 + 2 * bits :]
    small_received = received[bits:]
    me = lax.axis_index("dp")
    rows = BLOCK * blocks
    width = grads.shape[1]
    per_side = width // BLOCK
    last = 2 * bits

    barrier = pltpu.get_barrier_semaphore()
    for place in range(bits):
        stride = 1 << place
        other = me + stride * (1 - 2 * ((me // stride) % 2))
        pl.semaphore_signal(barrier, inc=1, device_id={"dp": other}, device_id_type=MESH)
    pl.semaphore_wait(barrier, bits)

    families = (
        (a_ref, dm_ref, 4 * per_side, True),
        (h2_ref, dz_ref, 4 * per_side, False),
        (h1_ref, dp_ref, 3 * per_side, False),
        (o_ref, dproj_ref, per_side, False),
    )
    n_blocks = 12 * per_side

    def load(block):
        slot = block % 2
        first = 0
        for left, right, count, walks in families:
            @pl.when((block >= first) & (block < first + count))
            def _():
                local = block - first
                if walks:
                    left_column = local * BLOCK
                    right_column = 0
                else:
                    left_column = (local % per_side) * BLOCK
                    right_column = (local // per_side) * width
                pltpu.make_async_copy(
                    left.at[:, pl.ds(pl.multiple_of(left_column, BLOCK), BLOCK)],
                    lhs.at[slot],
                    load_sem.at[0, slot],
                ).start()
                pltpu.make_async_copy(
                    right.at[:, pl.ds(pl.multiple_of(right_column, BLOCK), width)],
                    rhs.at[slot],
                    load_sem.at[1, slot],
                ).start()
            first += count

    def produce(block):
        slot = block % 2
        pltpu.make_async_copy(lhs.at[slot], lhs.at[slot], load_sem.at[0, slot]).wait()
        pltpu.make_async_copy(rhs.at[slot], rhs.at[slot], load_sem.at[1, slot]).wait()

        @pl.when(block + 1 < n_blocks)
        def _():
            load(block + 1)

        grads[pl.ds(pl.multiple_of(block * BLOCK, BLOCK), BLOCK), :] = lax.dot_general(
            lhs[slot], rhs[slot], (((0,), (0,)), ((), ())), preferred_element_type=jnp.float32
        ).astype(jnp.bfloat16)

    def turn(chunk):
        place = chunk % 9
        return place % 2 + place // 5 - place // 6

    def partner(rotation, stage):
        stride = lax.shift_left(jnp.int32(1), (stage + rotation) % bits)
        mine = (me // stride) % 2
        return mine, me + stride * (1 - 2 * mine)

    def offset(base, height, rotation, stage):
        for earlier in range(stage):
            mine, _ = partner(rotation, earlier)
            base = base + mine * (height >> (earlier + 1))
        return base

    def piece(ref, start, size):
        return ref.at[pl.ds(pl.multiple_of(start, size), size)]

    def send(position, base, height, rotation, source, landing, result, slot, sems):
        send_at, recv_at = sems
        if position < bits:
            stage = position
            half = height >> (stage + 1)
            mine, other = partner(rotation, stage)
            start = offset(base, height, rotation, stage) + (1 - mine) * half
            src, dst = piece(source, start, half), landing[stage].at[slot]
        else:
            stage = last - 1 - position
            half = height >> (stage + 1)
            mine, other = partner(rotation, stage)
            start = offset(base, height, rotation, stage + 1)
            src = dst = piece(result, start, half)
        return pltpu.make_async_remote_copy(
            src_ref=src,
            dst_ref=dst,
            send_sem=send_at.at[position],
            recv_sem=recv_at.at[position, slot],
            device_id={"dp": other},
            device_id_type=MESH,
        )

    def take(position, base, height, rotation, source, landing, result, slot, sems):
        send(position - 1, base, height, rotation, source, landing, result, slot, sems).wait_recv()
        stage = position - 1
        if stage < bits:
            half = height >> (stage + 1)
            start = pl.multiple_of(offset(base, height, rotation, stage + 1), half)
            keep = pl.ds(start, half)
            value = source[keep, :].astype(jnp.float32) + landing[stage][slot].astype(jnp.float32)
            target = result if stage == bits - 1 else source
            target[keep, :] = value.astype(target.dtype)

    def step(position, *way):
        if position > 0:
            take(position, *way)
        if position < last:
            send(position, *way).start()

    main = (grads, received[:bits], total)
    main_sems = (send_sem, recv_sem)

    def walk(position, chunk):
        if position == 0:
            for sub in range(blocks):
                block = chunk * blocks + sub

                @pl.when(block < n_blocks)
                def _():
                    produce(block)

        base = chunk * rows
        step(position, base, rows, turn(chunk), *main, chunk, main_sems)
        if position == last:
            there = pl.ds(pl.multiple_of(base, rows), rows)
            pltpu.make_async_copy(total.at[there], out_ref.at[there], store_sem.at[0]).start()

    def walk_small(position):
        height = small_ref.shape[0]
        way = (0, height, 0, small_ref, small_received, small_total, 0, (small_send, small_recv))
        step(position, *way)

    load(jnp.int32(0))

    @pl.loop(0, chunks + lag * last)
    def _(tick):
        for position in range(last + 1):
            chunk = tick - lag * position

            @pl.when((chunk >= 0) & (chunk < chunks))
            def _():
                walk(position, chunk)

            @pl.when(tick == lag * position)
            def _():
                walk_small(position)

    small_out_ref[...] = small_total[...]
    for position in range(last):
        stage = position if position < bits else last - 1 - position
        size = received[stage]
        pltpu.make_async_copy(size, size, send_sem.at[position]).wait()
        size = small_received[stage]
        pltpu.make_async_copy(size, size, small_send.at[position]).wait()
    pltpu.make_async_copy(total, out_ref, store_sem.at[0]).wait()


def reduce_gradients(a, dm, h2, dz, h1, packed, o, dproj, small):
    parts = lax.axis_size("dp")
    bits = parts.bit_length() - 1
    blocks = max(1, 16 * parts // BLOCK)
    tokens, width = h1.shape
    n_blocks = 12 * width // BLOCK
    chunks = -(-n_blocks // blocks)
    rows = BLOCK * blocks
    height = small.shape[0]
    bf16 = jnp.bfloat16
    return pl.pallas_call(
        functools.partial(reduce_kernel, bits, chunks, blocks, 2),
        out_shape=(
            jax.ShapeDtypeStruct((chunks * rows, width), bf16),
            jax.ShapeDtypeStruct(small.shape, jnp.float32),
        ),
        in_specs=[pl.BlockSpec(memory_space=pl.ANY)] * 8 + [pl.BlockSpec(memory_space=pltpu.VMEM)],
        out_specs=(pl.BlockSpec(memory_space=pl.ANY), pl.BlockSpec(memory_space=pltpu.VMEM)),
        scratch_shapes=[
            pltpu.VMEM((2, tokens, BLOCK), bf16),
            pltpu.VMEM((2, tokens, width), bf16),
            pltpu.VMEM((chunks * rows, width), bf16),
            pltpu.VMEM((chunks * rows, width), bf16),
            pltpu.VMEM(small.shape, jnp.float32),
            *[pltpu.VMEM((chunks, rows >> (s + 1), width), bf16) for s in range(bits)],
            *[pltpu.VMEM((1, height >> (s + 1), 128), jnp.float32) for s in range(bits)],
            pltpu.SemaphoreType.DMA((2, 2)),
            pltpu.SemaphoreType.DMA((2 * bits,)),
            pltpu.SemaphoreType.DMA((2 * bits, chunks)),
            pltpu.SemaphoreType.DMA((2 * bits,)),
            pltpu.SemaphoreType.DMA((2 * bits, 1)),
            pltpu.SemaphoreType.DMA((1,)),
        ],
        compiler_params=pltpu.CompilerParams(
            collective_id=0, has_side_effects=True, vmem_limit_bytes=60 * 1024 * 1024
        ),
        name="reduce_gradients",
    )(a, dm, h2, dz, h1, packed, o, dproj, small)


def shifted(block, axis, distance):
    devices = range(lax.axis_size(axis))
    route = [(i - distance, i) for i in devices if i - distance in devices]
    return lax.ppermute(block, axis, route)


def geometry(segments, padding):
    length = segments.shape[0]
    positions = jnp.arange(length, dtype=jnp.int32)
    living = positions < length - padding
    return (segments[:, None] == segments[None, :]) & living[None, :] | (
        positions[:, None] == positions[None, :]
    )


def bias_block(rel_table, length):
    heads, entries = rel_table.shape
    margin = (2 * length - 1 - entries) // 2
    extended = jnp.pad(rel_table, ((0, 0), (margin, margin + 1)))
    tiled = jnp.tile(extended, (1, length))[:, : length * (2 * length - 1)]
    return tiled.reshape(heads, length, 2 * length - 1)[:, :, length - 1 :]


def bias_grad(score_grad, entries):
    heads, length, ignored = score_grad.shape
    widened = jnp.pad(score_grad, ((0, 0), (0, 0), (length - 1, 0))).reshape(heads, -1)
    widened = jnp.pad(widened, ((0, 0), (0, length))).reshape(heads, length, 2 * length)
    column_sums = jnp.sum(widened, 1)
    margin = (2 * length - 1 - entries) // 2
    return column_sums[:, margin : margin + entries]


def normalize(values):
    centered = values - jnp.mean(values, -1, keepdims=True)
    inverse = lax.rsqrt(jnp.mean(centered * centered, -1, keepdims=True) + 1e-06)
    return (centered * inverse, inverse)


def norm_back(upper, scaled, inverse):
    return inverse * (
        upper
        - jnp.mean(upper, -1, keepdims=True)
        - scaled * jnp.mean(upper * scaled, -1, keepdims=True)
    )


def gelu_value(inputs):
    return 0.5 * inputs * (1.0 + lax.erf(inputs / math.sqrt(2.0)))


def gelu_slope(inputs):
    return 0.5 * (1.0 + lax.erf(inputs / math.sqrt(2.0))) + inputs * jnp.exp(
        -0.5 * inputs * inputs
    ) / math.sqrt(2.0 * math.pi)


def outer_product(left, right):
    return lax.dot_general(
        left, right, (((0,), (0,)), ((), ())), preferred_element_type=jnp.float32
    )


def attention_scores(queries, keys_part, rel_table, allowed):
    length, width = queries.shape
    heads = rel_table.shape[0]
    raw = jnp.einsum(
        "qhd,khd->hqk",
        queries.reshape(length, heads, -1),
        keys_part.reshape(length, heads, -1),
        preferred_element_type=jnp.float32,
    )
    return jnp.where(allowed[None], raw + bias_block(rel_table, length), -1000000000.0)


def forward(layer_in, params, allowed):
    (
        gain_one,
        shift_one,
        qkv_weight,
        query_bias,
        value_bias,
        rel_table,
        proj_weight,
        proj_bias,
        scale_attn,
        gain_two,
        shift_two,
        fc1_weight,
        fc1_bias,
        fc2_weight,
        fc2_bias,
        scale_mlp,
    ) = params
    length, width = layer_in.shape
    heads = rel_table.shape[0]
    factor = (width // heads) ** (-0.5)
    stream = layer_in.astype(jnp.float32)
    scaled_one, inverse_one = normalize(stream)
    normed_one = (scaled_one * gain_one + shift_one).astype(jnp.bfloat16)
    projected = jnp.dot(normed_one, qkv_weight, preferred_element_type=jnp.float32)
    queries = ((projected[:, :width] + query_bias) * factor).astype(jnp.bfloat16)
    keys_part = projected[:, width : 2 * width].astype(jnp.bfloat16)
    values_part = (projected[:, 2 * width :] + value_bias).astype(jnp.bfloat16)
    scores = attention_scores(queries, keys_part, rel_table, allowed)
    highest = jnp.max(scores, -1, keepdims=True)
    expo = jnp.exp(scores - highest)
    totals = jnp.sum(expo, -1, keepdims=True)
    log_total = highest + jnp.log(totals)
    probs_low = (expo / totals).astype(jnp.bfloat16)
    mixed = (
        jnp.einsum(
            "hqk,khd->qhd",
            probs_low,
            values_part.reshape(length, heads, -1),
            preferred_element_type=jnp.float32,
        )
        .reshape(length, width)
        .astype(jnp.bfloat16)
    )
    proj_out = jnp.dot(mixed, proj_weight, preferred_element_type=jnp.float32) + proj_bias
    resid = stream + scale_attn * proj_out
    scaled_two, inverse_two = normalize(resid)
    normed_two = (scaled_two * gain_two + shift_two).astype(jnp.bfloat16)
    pre_act = jnp.dot(normed_two, fc1_weight, preferred_element_type=jnp.float32) + fc1_bias
    activated = gelu_value(pre_act).astype(jnp.bfloat16)
    mlp_out = jnp.dot(activated, fc2_weight, preferred_element_type=jnp.float32) + fc2_bias
    result = (resid + scale_mlp * mlp_out).astype(jnp.bfloat16)
    saved = (
        scaled_one,
        inverse_one,
        normed_one,
        queries,
        keys_part,
        values_part,
        log_total,
        mixed,
        proj_out,
        scaled_two,
        inverse_two,
        normed_two,
        pre_act,
        activated,
        mlp_out,
    )
    return (result, saved)


def backward(upstream, saved, params, allowed):
    (
        gain_one,
        shift_one,
        qkv_weight,
        query_bias,
        value_bias,
        rel_table,
        proj_weight,
        proj_bias,
        scale_attn,
        gain_two,
        shift_two,
        fc1_weight,
        fc1_bias,
        fc2_weight,
        fc2_bias,
        scale_mlp,
    ) = params
    (
        scaled_one,
        inverse_one,
        normed_one,
        queries,
        keys_part,
        values_part,
        log_total,
        mixed,
        proj_out,
        scaled_two,
        inverse_two,
        normed_two,
        pre_act,
        activated,
        mlp_out,
    ) = saved
    length, width = queries.shape
    heads = rel_table.shape[0]
    factor = (width // heads) ** (-0.5)
    out_grad = (upstream * scale_mlp).astype(jnp.bfloat16)
    scale_mlp_grad = jnp.sum(upstream * mlp_out, 0)
    fc2_bias_grad = jnp.sum(out_grad.astype(jnp.float32), 0)
    act_grad = jnp.dot(out_grad, fc2_weight.T, preferred_element_type=jnp.float32)
    pre_grad = (act_grad * gelu_slope(pre_act)).astype(jnp.bfloat16)
    fc1_bias_grad = jnp.sum(pre_grad.astype(jnp.float32), 0)
    normed_two_grad = jnp.dot(pre_grad, fc1_weight.T, preferred_element_type=jnp.float32)
    gain_two_grad = jnp.sum(normed_two_grad * scaled_two, 0)
    shift_two_grad = jnp.sum(normed_two_grad, 0)
    resid_grad = upstream + norm_back(normed_two_grad * gain_two, scaled_two, inverse_two)
    proj_grad = (resid_grad * scale_attn).astype(jnp.bfloat16)
    scale_attn_grad = jnp.sum(resid_grad * proj_out, 0)
    proj_bias_grad = jnp.sum(proj_grad.astype(jnp.float32), 0)
    mixed_grad = jnp.dot(proj_grad, proj_weight.T, preferred_element_type=jnp.float32).astype(
        jnp.bfloat16
    )
    mixed_grad = mixed_grad.reshape(length, heads, -1)
    query_heads = queries.reshape(length, heads, -1)
    key_heads = keys_part.reshape(length, heads, -1)
    value_heads = values_part.reshape(length, heads, -1)
    scores = attention_scores(queries, keys_part, rel_table, allowed)
    probs = jnp.exp(scores - log_total)
    prob_grad = jnp.einsum(
        "qhd,khd->hqk", mixed_grad, value_heads, preferred_element_type=jnp.float32
    )
    score_grad = probs * (prob_grad - jnp.sum(probs * prob_grad, -1, keepdims=True))
    table_grad = bias_grad(score_grad, rel_table.shape[1])
    score_low = score_grad.astype(jnp.bfloat16)
    query_grad = jnp.einsum(
        "hqk,khd->qhd", score_low, key_heads, preferred_element_type=jnp.float32
    )
    query_grad = query_grad.reshape(length, width).astype(jnp.bfloat16)
    key_grad = jnp.einsum(
        "hqk,qhd->khd", score_low, query_heads, preferred_element_type=jnp.float32
    )
    key_grad = key_grad.reshape(length, width).astype(jnp.bfloat16)
    value_grad = jnp.einsum(
        "hqk,qhd->khd", probs.astype(jnp.bfloat16), mixed_grad, preferred_element_type=jnp.float32
    )
    value_grad = value_grad.reshape(length, width).astype(jnp.bfloat16)
    query_scaled = query_grad.astype(jnp.float32) * factor
    query_bias_grad = jnp.sum(query_scaled, 0)
    value_bias_grad = jnp.sum(value_grad.astype(jnp.float32), 0)
    packed_grad = jnp.concatenate([query_scaled.astype(jnp.bfloat16), key_grad, value_grad], 1)
    normed_one_grad = jnp.dot(packed_grad, qkv_weight.T, preferred_element_type=jnp.float32)
    gain_one_grad = jnp.sum(normed_one_grad * scaled_one, 0)
    shift_one_grad = jnp.sum(normed_one_grad, 0)
    input_grad = resid_grad + norm_back(normed_one_grad * gain_one, scaled_one, inverse_one)
    smalls = (
        gain_one_grad,
        shift_one_grad,
        query_bias_grad,
        value_bias_grad,
        table_grad,
        proj_bias_grad,
        scale_attn_grad,
        gain_two_grad,
        shift_two_grad,
        fc1_bias_grad,
        fc2_bias_grad,
        scale_mlp_grad,
    )
    pieces = (packed_grad, proj_grad, pre_grad, out_grad)
    return (input_grad, smalls, pieces)


def pick_slot(stack, slot_id):
    return lax.dynamic_index_in_dim(stack, slot_id, 0, keepdims=False)


def place_slot(store, value, slot_id, is_valid):
    return jnp.where(is_valid, lax.dynamic_update_index_in_dim(store, value, slot_id, 0), store)


def unpack_flat(flat, shapes):
    pieces_out = []
    offset = 0
    for shape in shapes:
        count = math.prod(shape)
        pieces_out.append(flat[offset : offset + count].reshape(shape))
        offset = offset + count
    return pieces_out


def per_device(
    patches,
    segment_ids,
    pad_counts,
    norm1_gain,
    norm1_bias,
    qkv_weight,
    query_bias,
    value_bias,
    rel_table,
    proj_weight,
    proj_bias,
    scale_attn,
    norm2_gain,
    norm2_bias,
    fc1_weight,
    fc1_bias,
    fc2_weight,
    fc2_bias,
    scale_mlp,
    cotangent,
):
    params = tuple(
        (
            p[0]
            for p in (
                norm1_gain,
                norm1_bias,
                qkv_weight,
                query_bias,
                value_bias,
                rel_table,
                proj_weight,
                proj_bias,
                scale_attn,
                norm2_gain,
                norm2_bias,
                fc1_weight,
                fc1_bias,
                fc2_weight,
                fc2_bias,
                scale_mlp,
            )
        )
    )
    section_id = lax.axis_index("section")
    micro = patches.shape[0]
    allowed_all = jnp.stack(
        [geometry(segment_ids[number], pad_counts[number]) for number in range(micro)]
    )
    received = jnp.zeros(patches.shape[1:], jnp.bfloat16)
    outputs = jnp.zeros_like(patches)
    inputs_kept = jnp.zeros_like(patches)
    for tick_id in range(micro + 1):
        slot_id = tick_id - section_id
        is_valid = (slot_id >= 0) & (slot_id < micro)
        safe_slot = jnp.clip(slot_id, 0, micro - 1)
        layer_in = jnp.where(section_id == 0, patches[min(tick_id, micro - 1)], received)
        result, saved = forward(layer_in, params, pick_slot(allowed_all, safe_slot))
        outputs = place_slot(outputs, result, safe_slot, is_valid)
        inputs_kept = place_slot(inputs_kept, layer_in, safe_slot, is_valid)
        if tick_id < micro:
            received = shifted(result, "section", 1)
    returned = jnp.zeros(patches.shape[1:], jnp.bfloat16)
    in_grads = jnp.zeros_like(patches)
    small_sum = None
    kept = []
    for tick_id in range(micro + 1):
        slot_id = tick_id - 1 + section_id
        is_valid = (slot_id >= 0) & (slot_id < micro)
        safe_slot = jnp.clip(slot_id, 0, micro - 1)
        arrived = jnp.where(section_id == 1, cotangent[min(tick_id, micro - 1)], returned)
        arrived, kept, small_sum, inputs_kept = lax.optimization_barrier((arrived, kept, small_sum, inputs_kept))
        upstream = arrived.astype(jnp.float32) * is_valid.astype(jnp.float32)
        allowed = pick_slot(allowed_all, safe_slot)
        ignored, saved = forward(pick_slot(inputs_kept, safe_slot), params, allowed)
        input_grad, smalls, pieces = backward(upstream, saved, params, allowed)
        grad_low = input_grad.astype(jnp.bfloat16)
        in_grads = place_slot(in_grads, grad_low, safe_slot, is_valid)
        if tick_id < micro:
            returned = shifted(grad_low, "section", -1)
        small_sum = smalls if small_sum is None else jax.tree.map(jnp.add, small_sum, smalls)
        kept.append((saved[13], pieces[3], saved[11], pieces[2], saved[2], pieces[0], saved[7], pieces[1]))

    def of_rows(*ticks):
        rows = [jnp.where(section_id == 1, ticks[number], ticks[number + 1]) for number in range(micro)]
        return jnp.concatenate(rows, 0)

    small_shapes = [item.shape for item in small_sum]
    parts = lax.axis_size("dp")
    count = sum(math.prod(shape) for shape in small_shapes)
    height = -(-count // (128 * 8 * parts)) * 8 * parts
    small_flat = jnp.concatenate([item.reshape(-1) for item in small_sum])
    small_flat = jnp.pad(small_flat, (0, height * 128 - count)).reshape(height, 128)
    summed, small_full = reduce_gradients(*[of_rows(*ticks) for ticks in zip(*kept)], small_flat)
    small_full = small_full.reshape(-1)
    small_parts = unpack_flat(small_full, small_shapes)
    width = patches.shape[2]

    def side_by_side(first, amount):
        piece = summed[first * width : (first + amount) * width].reshape(amount, width, width)
        return piece.transpose(1, 0, 2).reshape(width, amount * width).astype(jnp.float32)

    fc2_grad = summed[: 4 * width].astype(jnp.float32)
    fc1_grad = side_by_side(4, 4)
    qkv_grad = side_by_side(8, 3)
    proj_grad_all = side_by_side(11, 1)
    return (
        outputs[None],
        in_grads[None],
        small_parts[0][None],
        small_parts[1][None],
        qkv_grad[None],
        small_parts[2][None],
        small_parts[3][None],
        small_parts[4][None],
        proj_grad_all[None],
        small_parts[5][None],
        small_parts[6][None],
        small_parts[7][None],
        small_parts[8][None],
        fc1_grad[None],
        small_parts[9][None],
        fc2_grad[None],
        small_parts[10][None],
        small_parts[11][None],
    )


def solution(mesh):
    placed = (
        P("dp", None, None),
        P("dp", None),
        P("dp"),
        P("section", None),
        P("section", None),
        P("section", None, None),
        P("section", None),
        P("section", None),
        P("section", None, None),
        P("section", None, None),
        P("section", None),
        P("section", None),
        P("section", None),
        P("section", None),
        P("section", None, None),
        P("section", None),
        P("section", None, None),
        P("section", None),
        P("section", None),
        P("dp", None, None),
    )
    return jax.shard_map(
        per_device,
        mesh=mesh,
        in_specs=placed,
        out_specs=(
            P("section", "dp", None, None),
            P("section", "dp", None, None),
            P("section", None),
            P("section", None),
            P("section", None, None),
            P("section", None),
            P("section", None),
            P("section", None, None),
            P("section", None, None),
            P("section", None),
            P("section", None),
            P("section", None),
            P("section", None),
            P("section", None, None),
            P("section", None),
            P("section", None, None),
            P("section", None),
            P("section", None),
        ),
        check_vma=False,
    )
```

```python
import functools
import math

import jax
import jax.numpy as jnp
from jax import lax
from jax.experimental import pallas as pl
from jax.experimental.pallas import tpu as pltpu
from jax.sharding import PartitionSpec as P

MESH = pl.DeviceIdType.MESH
BF16, F32 = jnp.bfloat16, jnp.float32
VMEM_BYTES = 60 * 1024 * 1024
LANES = 128
HALF = 64
REACH = 2 * LANES
GAIN1, SHIFT1, QBIAS, VBIAS, PBIAS, SCALE_A, GAIN2, SHIFT2, B2, SCALE_M, B1 = range(11)


def dot(left, right, left_dim, right_dim):
    return lax.dot_general(
        left, right, (((left_dim,), (right_dim,)), ((), ())), preferred_element_type=F32
    )


def nn(left, right):
    return dot(left, right, 1, 0)


def nt(left, right):
    return dot(left, right, 1, 1)


def normalize(values):
    centered = values - jnp.mean(values, -1, keepdims=True)
    inverse = lax.rsqrt(jnp.mean(centered * centered, -1, keepdims=True) + 1e-06)
    return centered * inverse, inverse


def norm_back(upper, scaled, inverse):
    return inverse * (
        upper
        - jnp.mean(upper, -1, keepdims=True)
        - scaled * jnp.mean(upper * scaled, -1, keepdims=True)
    )


def fold(values):
    return jnp.sum(values.reshape(values.shape[0] // 8, 8, values.shape[1]), 0)


def half_mask(shape, which):
    return lax.broadcasted_iota(jnp.int32, shape, 1) // HALF == which


def chunk(index, size):
    return pl.ds(pl.multiple_of(index * size, size), size)


def bias_kernel(ext_ref, out_ref):
    width = ext_ref.shape[2]
    rows = jnp.broadcast_to(ext_ref[0], (LANES, width))
    skewed = pltpu.roll(rows, 0, 1, stride=1, stride_axis=0)
    out_ref[0] = skewed[:, : out_ref.shape[1]].T


def bias_columns(rel_table, length):
    heads, entries = rel_table.shape
    span = 2 * length - LANES
    margin = LANES + (length - LANES) - entries // 2 - LANES
    total = span + LANES
    ext = jnp.pad(rel_table, ((0, 0), (margin, total - margin - entries)), mode="edge")
    return pl.pallas_call(
        bias_kernel,
        grid=(heads,),
        out_shape=jax.ShapeDtypeStruct((heads, span, LANES), F32),
        in_specs=[pl.BlockSpec((1, 1, total), lambda h: (h, 0, 0))],
        out_specs=pl.BlockSpec((1, span, LANES), lambda h: (h, 0, 0)),
        name="bias_columns",
    )(ext[:, None, :])


def table_kernel(diag_ref, out_ref):
    span = diag_ref.shape[2]
    total = span + LANES
    columns = (diag_ref[0, 0] + diag_ref[1, 0]).T
    columns = jnp.concatenate([columns, jnp.zeros((LANES, LANES), F32)], 1)
    gathered = columns[:8]
    for group in range(1, LANES // 8):
        gathered = gathered + pltpu.roll(columns[8 * group : 8 * group + 8], total - 8 * group, 1)
    row = lax.broadcasted_iota(jnp.int32, gathered.shape, 0)
    for place in range(3):
        moved = pltpu.roll(gathered, total - (1 << place), 1)
        gathered = jnp.where((row // (1 << place)) % 2 == 1, moved, gathered)
    out_ref[0] = jnp.sum(gathered, 0, keepdims=True)[:, LANES : LANES + out_ref.shape[2]]


def table_gradient(diagonals):
    rows, heads, span, lanes = diagonals.shape
    width = 5 * LANES
    return pl.pallas_call(
        table_kernel,
        grid=(heads,),
        out_shape=jax.ShapeDtypeStruct((heads, 1, width), F32),
        in_specs=[pl.BlockSpec((rows, 1, span, lanes), lambda h: (0, h, 0, 0))],
        out_specs=pl.BlockSpec((1, 1, width), lambda h: (h, 0, 0)),
        name="table_gradient",
    )(diagonals)[:, 0]


def key_rows(query_block, blocks):
    reach = REACH // LANES
    return max(0, query_block - reach) * LANES, min(blocks, query_block + reach + 1) * LANES


def forward_kernel(aliased, info, x_ref, segc_ref, segr_ref, vec_ref, *refs):
    bias_hbm, wqkv_hbm, wp_hbm, w1_hbm, w2_hbm = refs[:5]
    refs = refs[5 + (13 if aliased else 0) :]
    y_ref, *stores = refs[:14]
    (bias, wqkv, wp, w1, w2, mask, h1, qkv, probs, mixed, proj, x1, h2, act, slope, mlp, wide_mixed, total, xin, load_sem, store_sem, prob_sem) = refs[14:]
    h1_o, qkv_o, prob_o, mixed_o, proj_o, x1_o, h2_o, act_o, slope_o, mlp_o, y_o, xin_o, wide_o = stores
    length, width = x_ref.shape
    hidden = w1.shape[1]
    blocks = length // LANES
    slot = info[1]
    factor = HALF ** (-0.5)
    loads = [(wqkv_hbm, wqkv), (bias_hbm, bias), (wp_hbm, wp), (w1_hbm, w1), (w2_hbm, w2)]

    def load(number):
        return pltpu.make_async_copy(*loads[number], load_sem.at[number])

    def store(number, source, there):
        return pltpu.make_async_copy(source, there.at[slot], store_sem.at[number])

    def vector(row):
        return vec_ref[row : row + 1, :]

    @pl.when(info[0] == 1)
    def _():
        for number in range(len(loads)):
            load(number).start()

        @pl.loop(0, length // 64)
        def _(step):
            rows = chunk(step, 64)
            xin[rows, :] = x_ref[rows, :]
            scaled, _ = normalize(x_ref[rows, :].astype(F32))
            h1[rows, :] = (scaled * vector(GAIN1) + vector(SHIFT1)).astype(BF16)
            shape = (64, length)
            key = lax.broadcasted_iota(jnp.int32, shape, 0) + step * 64
            query = lax.broadcasted_iota(jnp.int32, shape, 1)
            same = segc_ref[slot, rows, :] == segr_ref[slot]
            allowed = (same & (key < length - info[2])) | (key == query)
            mask[rows, :] = jnp.where(allowed, 0.0, -1000000000.0)

        store(0, h1, h1_o).start()
        store(11, xin, xin_o).start()
        load(0).wait()
        for part in range(3):
            columns = pl.ds(part * width, width)
            result = nn(h1[...], wqkv[:, columns])
            if part == 0:
                result = (result + vector(QBIAS)) * factor
            if part == 2:
                result = result + vector(VBIAS)
            qkv[:, columns] = result.astype(BF16)
        store(1, qkv, qkv_o).start()
        load(1).wait()

        def prob_store(pair):
            return pltpu.make_async_copy(
                probs.at[pair % 2], prob_o.at[slot, pl.ds(2 * pair, 2)], prob_sem.at[pair % 2]
            )

        @pl.loop(0, width // LANES)
        def _(pair):
            @pl.when(pair >= 2)
            def _():
                prob_store(pair - 2).wait()

            side = pair % 2
            columns = chunk(pair, LANES)
            queries = qkv[:, columns]
            keys = qkv[:, pl.ds(pl.multiple_of(width + pair * LANES, LANES), LANES)]
            values = qkv[:, pl.ds(pl.multiple_of(2 * width + pair * LANES, LANES), LANES)].T
            outs = []
            for which in range(2):
                own_keys = jnp.where(half_mask(keys.shape, which), keys, jnp.zeros_like(keys))
                for wide in range(blocks // 2):
                    scores = nt(own_keys, queries[2 * LANES * wide : 2 * LANES * (wide + 1)])
                    for part in range(2):
                        place = 2 * wide + part
                        low, high = key_rows(place, blocks)
                        lanes = pl.ds(place * LANES, LANES)
                        first = (blocks - 1 - place) * LANES
                        here = (
                            scores[low:high, part * LANES : (part + 1) * LANES]
                            + bias[2 * pair + which, pl.ds(first + low, high - low), :]
                            + mask[low:high, lanes]
                        )
                        expo = jnp.exp(here - jnp.max(here, 0, keepdims=True))
                        scale = 1.0 / jnp.sum(expo, 0, keepdims=True)
                        probs[side, which, low:high, lanes] = (expo * scale).astype(BF16)
                        if low > 0:
                            probs[side, which, :low, lanes] = jnp.zeros((low, LANES), BF16)
                        if high < length:
                            probs[side, which, high:, lanes] = jnp.zeros((length - high, LANES), BF16)
                outs.append(nn(values[which * HALF : (which + 1) * HALF], probs[side, which]))
            out = jnp.concatenate(outs, 0).T
            wide_mixed[:, columns] = out
            mixed[:, columns] = out.astype(BF16)
            prob_store(pair).start()

        store(3, mixed, mixed_o).start()
        store(12, wide_mixed, wide_o).start()
        load(2).wait()

        @pl.loop(0, length // LANES)
        def _(step):
            rows = chunk(step, LANES)
            out = nn(mixed[rows, :], wp[...]) + vector(PBIAS)
            proj[rows, :] = out.astype(BF16)
            resid = x_ref[rows, :].astype(F32) + vector(SCALE_A) * out
            x1[rows, :] = resid
            scaled, _ = normalize(resid)
            h2[rows, :] = (scaled * vector(GAIN2) + vector(SHIFT2)).astype(BF16)

        store(4, proj, proj_o).start()
        store(5, x1, x1_o).start()
        store(6, h2, h2_o).start()
        load(3).wait()
        load(4).wait()
        for part in range(hidden // width):
            columns = pl.ds(part * width, width)
            for high in range(2):
                rows = pl.ds(high * (length // 2), length // 2)
                pre = nn(h2[rows, :], w1[:, columns]) + vector(B1 + part)
                normal = 0.5 * (1.0 + lax.erf(pre * math.sqrt(0.5)))
                density = jnp.exp(-0.5 * pre * pre) * (1.0 / math.sqrt(2.0 * math.pi))
                act[rows, columns] = (pre * normal).astype(BF16)
                slope[rows, columns] = (normal + pre * density).astype(BF16)
                more = nn(act[rows, columns], w2[columns, :])
                total[rows, :] = more if part == 0 else total[rows, :] + more
        store(7, act, act_o).start()
        store(8, slope, slope_o).start()

        @pl.loop(0, length // 64)
        def _(step):
            rows = chunk(step, 64)
            out = total[rows, :] + vector(B2)
            mlp[rows, :] = out.astype(BF16)
            y_ref[rows, :] = (x1[rows, :] + vector(SCALE_M) * out).astype(BF16)

        store(9, mlp, mlp_o).start()
        store(10, y_ref, y_o).start()
        for pair in (width // LANES - 2, width // LANES - 1):
            prob_store(pair).wait()
        ends = {0: (h1, h1_o), 1: (qkv, qkv_o), 3: (mixed, mixed_o), 4: (proj, proj_o), 5: (x1, x1_o), 6: (h2, h2_o),
                7: (act, act_o), 8: (slope, slope_o), 9: (mlp, mlp_o), 10: (y_ref, y_o), 11: (xin, xin_o), 12: (wide_mixed, wide_o)}
        for number, (source, there) in ends.items():
            store(number, source, there).wait()


def hbm_specs(count):
    return [pl.BlockSpec(memory_space=pl.ANY)] * count


def vmem_specs(count):
    return [pl.BlockSpec(memory_space=pltpu.VMEM)] * count


def forward(info, layer_in, segments, vectors, bias, weights, kept):
    length, width = layer_in.shape
    micro = segments.shape[0]
    wqkv, wp, w1, w2 = weights
    hidden = w1.shape[1]
    heads = bias.shape[0]
    stored = [
        ((length, width), BF16),
        ((length, 3 * width), BF16),
        ((heads, length, length), BF16),
        ((length, width), BF16),
        ((length, width), BF16),
        ((length, width), F32),
        ((length, width), BF16),
        ((length, hidden), BF16),
        ((length, hidden), BF16),
        ((length, width), BF16),
        ((length, width), BF16),
        ((length, width), BF16),
        ((length, width), F32),
    ]
    scratch = [pltpu.VMEM(x.shape, x.dtype) for x in (bias, wqkv, wp, w1, w2)]
    scratch.append(pltpu.VMEM((length, length), F32))
    scratch += [pltpu.VMEM((2, 2, length, length) if n == 2 else shape, kind) for n, (shape, kind) in enumerate(stored[:10])]
    scratch += [pltpu.VMEM((length, width), F32), pltpu.VMEM((length, width), F32), pltpu.VMEM((length, width), BF16)]
    scratch += [pltpu.SemaphoreType.DMA((5,)), pltpu.SemaphoreType.DMA((13,)), pltpu.SemaphoreType.DMA((2,))]
    aliased = kept is not None
    operands = [info, layer_in, segments[:, :, None], segments[:, None, :], vectors, bias, *weights]
    first = len(operands)
    out = pl.pallas_call(
        functools.partial(forward_kernel, aliased),
        out_shape=[jax.ShapeDtypeStruct((length, width), BF16)]
        + [jax.ShapeDtypeStruct((micro, *shape), kind) for shape, kind in stored],
        in_specs=[pl.BlockSpec(memory_space=pltpu.SMEM)] + vmem_specs(4) + hbm_specs(5 + (13 if aliased else 0)),
        out_specs=vmem_specs(1) + hbm_specs(13),
        scratch_shapes=scratch,
        input_output_aliases={first + n: 1 + n for n in range(13)} if aliased else {},
        compiler_params=pltpu.CompilerParams(vmem_limit_bytes=VMEM_BYTES),
        name="forward_layer",
    )(*operands, *(kept if aliased else ()))
    return out[0], out[1:]


def backward_kernel(aliased, info, g_ref, vec_ref, *refs):
    (wqkv_hbm, wp_hbm, w1_hbm, w2_hbm, qkv_i, prob_i, mixed_i, proj_i, x1_i, slope_i, mlp_i, xin_i) = refs[:12]
    refs = refs[12 + (7 if aliased else 0) :]
    dx_ref, *stores = refs[:8]
    (wqkv, wp, w1, w2, qkv, probs, mixed, proj, x1, slope, mlp, xin, dm, dz, dproj, packed, dx1, total, dmixed, dscore, diag, sums, load_sem, store_sem, prob_sem, diag_sem) = refs[8:]
    dm_o, dz_o, dproj_o, packed_o, dx_o, diag_o, sums_o = stores
    length, width = g_ref.shape
    hidden = w1.shape[1]
    blocks = length // LANES
    pairs = width // LANES
    slot = info[1]
    factor = HALF ** (-0.5)
    loads = [
        (mlp_i.at[slot], mlp), (w2_hbm, w2), (slope_i.at[slot], slope), (w1_hbm, w1), (x1_i.at[slot], x1),
        (proj_i.at[slot], proj), (wp_hbm, wp), (qkv_i.at[slot], qkv), (mixed_i.at[slot], mixed), (wqkv_hbm, wqkv),
        (xin_i.at[slot], xin),
    ]
    step_rows = 64
    steps = length // step_rows

    def load(number):
        return pltpu.make_async_copy(*loads[number], load_sem.at[number])

    def store(number, source, there):
        return pltpu.make_async_copy(source, there.at[slot], store_sem.at[number])

    def prob_load(pair):
        return pltpu.make_async_copy(
            prob_i.at[slot, pl.ds(2 * pair, 2)], probs.at[pair % 2], prob_sem.at[pair % 2]
        )

    def diag_store(pair):
        return pltpu.make_async_copy(
            diag.at[pair % 2], diag_o.at[slot, pl.ds(2 * pair, 2)], diag_sem.at[pair % 2]
        )

    def vector(row):
        return vec_ref[row : row + 1, :]

    def put(row, partial):
        sums[row : row + 1, :] = jnp.sum(partial, 0, keepdims=True)

    nothing = jnp.zeros((8, width), F32)

    @pl.when(info[0] == 1)
    def _():
        for number in range(len(loads)):
            load(number).start()
        prob_load(0).start()
        load(0).wait()

        def first(step, carry):
            rows = chunk(step, step_rows)
            upstream = g_ref[rows, :].astype(F32)
            low = (upstream * vector(SCALE_M)).astype(BF16)
            dm[rows, :] = low
            return carry[0] + fold(upstream * mlp[rows, :].astype(F32)), carry[1] + fold(low.astype(F32))

        scale_sum, bias_sum = lax.fori_loop(0, steps, first, (nothing, nothing))
        put(SCALE_M, scale_sum)
        put(B2, bias_sum)
        store(0, dm, dm_o).start()
        load(1).wait()
        load(2).wait()
        load(3).wait()
        for part in range(hidden // width):
            columns = pl.ds(part * width, width)
            act_sum = nothing
            for high in range(2):
                rows = pl.ds(high * (length // 2), length // 2)
                low = (nt(dm[rows, :], w2[columns, :]) * slope[rows, columns].astype(F32)).astype(BF16)
                dz[rows, columns] = low
                act_sum = act_sum + fold(low.astype(F32))
                more = nt(dz[rows, columns], w1[:, columns])
                total[rows, :] = more if part == 0 else total[rows, :] + more
            put(B1 + part, act_sum)
        store(1, dz, dz_o).start()
        load(4).wait()
        load(5).wait()

        def second(step, carry):
            rows = chunk(step, step_rows)
            upper = total[rows, :]
            scaled, inverse = normalize(x1[rows, :])
            resid = g_ref[rows, :].astype(F32) + norm_back(upper * vector(GAIN2), scaled, inverse)
            dx1[rows, :] = resid
            low = (resid * vector(SCALE_A)).astype(BF16)
            dproj[rows, :] = low
            terms = (upper * scaled, upper, resid * proj[rows, :].astype(F32), low.astype(F32))
            return tuple(old + fold(term) for old, term in zip(carry, terms))

        for row, partial in zip((GAIN2, SHIFT2, SCALE_A, PBIAS), lax.fori_loop(0, steps, second, (nothing,) * 4)):
            put(row, partial)
        store(2, dproj, dproj_o).start()
        load(6).wait()
        dmixed[...] = nt(dproj[...], wp[...]).astype(BF16)
        load(7).wait()
        load(8).wait()

        @pl.loop(0, pairs)
        def _(pair):
            prob_load(pair).wait()

            @pl.when(pair + 1 < pairs)
            def _():
                prob_load(pair + 1).start()

            @pl.when(pair >= 2)
            def _():
                diag_store(pair - 2).wait()

            side = pair % 2
            columns = chunk(pair, LANES)
            key_columns = pl.ds(pl.multiple_of(width + pair * LANES, LANES), LANES)
            value_columns = pl.ds(pl.multiple_of(2 * width + pair * LANES, LANES), LANES)
            values = qkv[:, value_columns]
            above = dmixed[:, columns]
            queries_t = qkv[:, columns].T
            keys_t = qkv[:, key_columns].T
            above_t = above.T
            products = (above.astype(F32) * mixed[:, columns]).T
            grads = [], [], []
            for which in range(2):
                half = slice(which * HALF, (which + 1) * HALF)
                delta = jnp.sum(products[half], 0, keepdims=True)
                own_values = jnp.where(half_mask(values.shape, which), values, jnp.zeros_like(values))
                edge = (blocks - 1) * LANES
                diag[side, which, :edge, :] = jnp.zeros((edge, LANES), F32)
                for wide in range(blocks // 2):
                    prob_grad = nt(own_values, above[2 * LANES * wide : 2 * LANES * (wide + 1)])
                    for part in range(2):
                        place = 2 * wide + part
                        low, high = key_rows(place, blocks)
                        lanes = pl.ds(place * LANES, LANES)
                        first_row = (blocks - 1 - place) * LANES
                        here = probs[side, which, low:high, lanes].astype(F32) * (
                            prob_grad[low:high, part * LANES : (part + 1) * LANES]
                            - delta[:, place * LANES : (place + 1) * LANES]
                        )
                        dscore[which, low:high, lanes] = here.astype(BF16)
                        if low > 0:
                            dscore[which, :low, lanes] = jnp.zeros((low, LANES), BF16)
                        if high < length:
                            dscore[which, high:, lanes] = jnp.zeros((length - high, LANES), BF16)
                        there = pl.ds(first_row + low, high - low)
                        if place == 0:
                            diag[side, which, there, :] = here
                            diag[side, which, edge + high :, :] = jnp.zeros((length - high, LANES), F32)
                        else:
                            diag[side, which, there, :] = diag[side, which, there, :] + here
                grads[0].append(nn(keys_t[half], dscore[which]))
                grads[1].append(nt(queries_t[half], dscore[which]))
                grads[2].append(nt(above_t[half], probs[side, which]))
            diag_store(pair).start()
            for found, where, scale in zip(grads, (columns, key_columns, value_columns), (factor, None, None)):
                low = jnp.concatenate(found, 0).astype(BF16)
                if scale is not None:
                    low = (low.astype(F32) * scale).astype(BF16)
                packed[:, where] = low.T

        store(3, packed, packed_o).start()
        load(9).wait()
        total[...] = nt(packed[...], wqkv[...])
        load(10).wait()

        def third(step, carry):
            rows = chunk(step, step_rows)
            upper = total[rows, :]
            scaled, inverse = normalize(xin[rows, :].astype(F32))
            dx_ref[rows, :] = (dx1[rows, :] + norm_back(upper * vector(GAIN1), scaled, inverse)).astype(BF16)
            terms = (
                upper * scaled,
                upper,
                packed[rows, :width].astype(F32),
                packed[rows, 2 * width :].astype(F32),
            )
            return tuple(old + fold(term) for old, term in zip(carry, terms))

        for row, partial in zip((GAIN1, SHIFT1, QBIAS, VBIAS), lax.fori_loop(0, steps, third, (nothing,) * 4)):
            put(row, partial)
        store(4, dx_ref, dx_o).start()
        store(6, sums, sums_o).start()
        for pair in (pairs - 2, pairs - 1):
            diag_store(pair).wait()
        ends = {0: (dm, dm_o), 1: (dz, dz_o), 2: (dproj, dproj_o), 3: (packed, packed_o), 4: (dx_ref, dx_o), 6: (sums, sums_o)}
        for number, (source, there) in ends.items():
            store(number, source, there).wait()


def backward(info, upstream, vectors, weights, saved, kept):
    length, width = upstream.shape
    wqkv, wp, w1, w2 = weights
    hidden = w1.shape[1]
    h1, qkv, probs, mixed, proj, x1, h2, act, slope, mlp, y, xin, wide = saved
    micro, heads = probs.shape[:2]
    span = 2 * length - LANES
    summed = (16, width)
    stored = [
        ((length, width), BF16),
        ((length, hidden), BF16),
        ((length, width), BF16),
        ((length, 3 * width), BF16),
        ((length, width), BF16),
        ((heads, span, LANES), F32),
        (summed, F32),
    ]
    reads = [qkv, probs, wide, proj, x1, slope, mlp, xin]
    scratch = [pltpu.VMEM(x.shape, x.dtype) for x in weights]
    scratch += [pltpu.VMEM((2, 2, length, length) if x is probs else x.shape[1:], x.dtype) for x in reads]
    scratch += [pltpu.VMEM(shape, kind) for shape, kind in stored[:4]]
    scratch += [
        pltpu.VMEM((length, width), F32),
        pltpu.VMEM((length, width), F32),
        pltpu.VMEM((length, width), BF16),
        pltpu.VMEM((2, length, length), BF16),
        pltpu.VMEM((2, 2, span, LANES), F32),
        pltpu.VMEM(summed, F32),
        pltpu.SemaphoreType.DMA((11,)),
        pltpu.SemaphoreType.DMA((7,)),
        pltpu.SemaphoreType.DMA((2,)),
        pltpu.SemaphoreType.DMA((2,)),
    ]
    aliased = kept is not None
    operands = [info, upstream, vectors, *weights, *reads]
    first = len(operands)
    out = pl.pallas_call(
        functools.partial(backward_kernel, aliased),
        out_shape=[jax.ShapeDtypeStruct((length, width), BF16)]
        + [jax.ShapeDtypeStruct((micro, *shape), kind) for shape, kind in stored],
        in_specs=[pl.BlockSpec(memory_space=pltpu.SMEM)] + vmem_specs(2) + hbm_specs(12 + (7 if aliased else 0)),
        out_specs=vmem_specs(1) + hbm_specs(7),
        scratch_shapes=scratch,
        input_output_aliases={first + n: 1 + n for n in range(7)} if aliased else {},
        compiler_params=pltpu.CompilerParams(vmem_limit_bytes=VMEM_BYTES),
        name="backward_layer",
    )(*operands, *(kept if aliased else ()))
    return out[0], out[1:]


def widen_kernel(sum_ref, fc2_ref, fc1_ref, qkv_ref, proj_ref):
    block = pl.program_id(0)
    for target, low, high in ((fc2_ref, 0, 4), (fc1_ref, 4, 8), (qkv_ref, 8, 11), (proj_ref, 11, 12)):

        @pl.when((block >= low) & (block < high))
        def _():
            target[...] = sum_ref[...].astype(F32)


def widen(summed, width):
    square = (width, width)
    return pl.pallas_call(
        widen_kernel,
        grid=(12,),
        out_shape=[
            jax.ShapeDtypeStruct((4 * width, width), F32),
            jax.ShapeDtypeStruct((width, 4 * width), F32),
            jax.ShapeDtypeStruct((width, 3 * width), F32),
            jax.ShapeDtypeStruct((width, width), F32),
        ],
        in_specs=[pl.BlockSpec(square, lambda b: (b, 0))],
        out_specs=[
            pl.BlockSpec(square, lambda b: (jnp.minimum(b, 3), 0)),
            pl.BlockSpec(square, lambda b: (0, jnp.clip(b - 4, 0, 3))),
            pl.BlockSpec(square, lambda b: (0, jnp.clip(b - 8, 0, 2))),
            pl.BlockSpec(square, lambda b: (0, 0)),
        ],
        compiler_params=pltpu.CompilerParams(vmem_limit_bytes=VMEM_BYTES),
        name="widen",
    )(summed)


BLOCK = 256


def reduce_kernel(
    bits, chunks, blocks, lag, *refs
):
    (a_ref, dm_ref, h2_ref, dz_ref, h1_ref, dp_ref, o_ref, dproj_ref, small_ref, out_ref, small_out_ref) = refs[:11]
    (lhs, rhs, grads, total, small_total, *received) = refs[11 : 16 + 2 * bits]
    (load_sem, send_sem, recv_sem, small_send, small_recv, store_sem) = refs[16 + 2 * bits :]
    small_received = received[bits:]
    me = lax.axis_index("dp")
    rows = BLOCK * blocks
    width = grads.shape[1]
    per_side = width // BLOCK
    last = 2 * bits

    barrier = pltpu.get_barrier_semaphore()
    for place in range(bits):
        stride = 1 << place
        other = me + stride * (1 - 2 * ((me // stride) % 2))
        pl.semaphore_signal(barrier, inc=1, device_id={"dp": other}, device_id_type=MESH)
    pl.semaphore_wait(barrier, bits)

    families = (
        (a_ref, dm_ref, 4 * per_side, True),
        (h2_ref, dz_ref, 4 * per_side, False),
        (h1_ref, dp_ref, 3 * per_side, False),
        (o_ref, dproj_ref, per_side, False),
    )
    n_blocks = 12 * per_side

    def load(block):
        slot = block % 2
        first = 0
        for left, right, count, walks in families:
            @pl.when((block >= first) & (block < first + count))
            def _():
                local = block - first
                if walks:
                    left_column = local * BLOCK
                    right_column = 0
                else:
                    left_column = (local % per_side) * BLOCK
                    right_column = (local // per_side) * width
                pltpu.make_async_copy(
                    left.at[:, pl.ds(pl.multiple_of(left_column, BLOCK), BLOCK)],
                    lhs.at[slot],
                    load_sem.at[0, slot],
                ).start()
                pltpu.make_async_copy(
                    right.at[:, pl.ds(pl.multiple_of(right_column, BLOCK), width)],
                    rhs.at[slot],
                    load_sem.at[1, slot],
                ).start()
            first += count

    def produce(block):
        slot = block % 2
        pltpu.make_async_copy(lhs.at[slot], lhs.at[slot], load_sem.at[0, slot]).wait()
        pltpu.make_async_copy(rhs.at[slot], rhs.at[slot], load_sem.at[1, slot]).wait()

        @pl.when(block + 1 < n_blocks)
        def _():
            load(block + 1)

        grads[pl.ds(pl.multiple_of(block * BLOCK, BLOCK), BLOCK), :] = lax.dot_general(
            lhs[slot], rhs[slot], (((0,), (0,)), ((), ())), preferred_element_type=jnp.float32
        ).astype(jnp.bfloat16)

    def turn(chunk):
        place = chunk % 9
        return place % 2 + place // 5 - place // 6

    def partner(rotation, stage):
        stride = lax.shift_left(jnp.int32(1), (stage + rotation) % bits)
        mine = (me // stride) % 2
        return mine, me + stride * (1 - 2 * mine)

    def offset(base, height, rotation, stage):
        for earlier in range(stage):
            mine, _ = partner(rotation, earlier)
            base = base + mine * (height >> (earlier + 1))
        return base

    def piece(ref, start, size):
        return ref.at[pl.ds(pl.multiple_of(start, size), size)]

    def send(position, base, height, rotation, source, landing, result, slot, sems):
        send_at, recv_at = sems
        if position < bits:
            stage = position
            half = height >> (stage + 1)
            mine, other = partner(rotation, stage)
            start = offset(base, height, rotation, stage) + (1 - mine) * half
            src, dst = piece(source, start, half), landing[stage].at[slot]
        else:
            stage = last - 1 - position
            half = height >> (stage + 1)
            mine, other = partner(rotation, stage)
            start = offset(base, height, rotation, stage + 1)
            src = dst = piece(result, start, half)
        return pltpu.make_async_remote_copy(
            src_ref=src,
            dst_ref=dst,
            send_sem=send_at.at[position],
            recv_sem=recv_at.at[position, slot],
            device_id={"dp": other},
            device_id_type=MESH,
        )

    def take(position, base, height, rotation, source, landing, result, slot, sems):
        send(position - 1, base, height, rotation, source, landing, result, slot, sems).wait_recv()
        stage = position - 1
        if stage < bits:
            half = height >> (stage + 1)
            start = pl.multiple_of(offset(base, height, rotation, stage + 1), half)
            keep = pl.ds(start, half)
            value = source[keep, :].astype(jnp.float32) + landing[stage][slot].astype(jnp.float32)
            target = result if stage == bits - 1 else source
            target[keep, :] = value.astype(target.dtype)

    def step(position, *way):
        if position > 0:
            take(position, *way)
        if position < last:
            send(position, *way).start()

    main = (grads, received[:bits], total)
    main_sems = (send_sem, recv_sem)

    def walk(position, chunk):
        if position == 0:
            for sub in range(blocks):
                block = chunk * blocks + sub

                @pl.when(block < n_blocks)
                def _():
                    produce(block)

        base = chunk * rows
        step(position, base, rows, turn(chunk), *main, chunk, main_sems)
        if position == last:
            there = pl.ds(pl.multiple_of(base, rows), rows)
            pltpu.make_async_copy(total.at[there], out_ref.at[there], store_sem.at[0]).start()

    def walk_small(position):
        height = small_ref.shape[0]
        way = (0, height, 0, small_ref, small_received, small_total, 0, (small_send, small_recv))
        step(position, *way)

    load(jnp.int32(0))

    @pl.loop(0, chunks + lag * last)
    def _(tick):
        for position in range(last + 1):
            chunk = tick - lag * position

            @pl.when((chunk >= 0) & (chunk < chunks))
            def _():
                walk(position, chunk)

            @pl.when(tick == lag * position)
            def _():
                walk_small(position)

    small_out_ref[...] = small_total[...]
    for position in range(last):
        stage = position if position < bits else last - 1 - position
        size = received[stage]
        pltpu.make_async_copy(size, size, send_sem.at[position]).wait()
        size = small_received[stage]
        pltpu.make_async_copy(size, size, small_send.at[position]).wait()
    pltpu.make_async_copy(total, out_ref, store_sem.at[0]).wait()


def reduce_gradients(a, dm, h2, dz, h1, packed, o, dproj, small):
    parts = lax.axis_size("dp")
    bits = parts.bit_length() - 1
    blocks = max(1, 16 * parts // BLOCK)
    tokens, width = h1.shape
    n_blocks = 12 * width // BLOCK
    chunks = -(-n_blocks // blocks)
    rows = BLOCK * blocks
    height = small.shape[0]
    bf16 = jnp.bfloat16
    return pl.pallas_call(
        functools.partial(reduce_kernel, bits, chunks, blocks, 2),
        out_shape=(
            jax.ShapeDtypeStruct((chunks * rows, width), bf16),
            jax.ShapeDtypeStruct(small.shape, jnp.float32),
        ),
        in_specs=[pl.BlockSpec(memory_space=pl.ANY)] * 8 + [pl.BlockSpec(memory_space=pltpu.VMEM)],
        out_specs=(pl.BlockSpec(memory_space=pl.ANY), pl.BlockSpec(memory_space=pltpu.VMEM)),
        scratch_shapes=[
            pltpu.VMEM((2, tokens, BLOCK), bf16),
            pltpu.VMEM((2, tokens, width), bf16),
            pltpu.VMEM((chunks * rows, width), bf16),
            pltpu.VMEM((chunks * rows, width), bf16),
            pltpu.VMEM(small.shape, jnp.float32),
            *[pltpu.VMEM((chunks, rows >> (s + 1), width), bf16) for s in range(bits)],
            *[pltpu.VMEM((1, height >> (s + 1), 128), jnp.float32) for s in range(bits)],
            pltpu.SemaphoreType.DMA((2, 2)),
            pltpu.SemaphoreType.DMA((2 * bits,)),
            pltpu.SemaphoreType.DMA((2 * bits, chunks)),
            pltpu.SemaphoreType.DMA((2 * bits,)),
            pltpu.SemaphoreType.DMA((2 * bits, 1)),
            pltpu.SemaphoreType.DMA((1,)),
        ],
        compiler_params=pltpu.CompilerParams(
            collective_id=0, has_side_effects=True, vmem_limit_bytes=60 * 1024 * 1024
        ),
        name="reduce_gradients",
    )(a, dm, h2, dz, h1, packed, o, dproj, small)


def shifted(block, axis, distance):
    devices = range(lax.axis_size(axis))
    route = [(i - distance, i) for i in devices if i - distance in devices]
    return lax.ppermute(block, axis, route)


def per_device(
    patches,
    segment_ids,
    pad_counts,
    norm1_gain,
    norm1_bias,
    qkv_weight,
    query_bias,
    value_bias,
    rel_table,
    proj_weight,
    proj_bias,
    scale_attn,
    norm2_gain,
    norm2_bias,
    fc1_weight,
    fc1_bias,
    fc2_weight,
    fc2_bias,
    scale_mlp,
    cotangent,
):
    section_id = lax.axis_index("section")
    micro, length, width = patches.shape
    vectors = jnp.concatenate(
        [
            norm1_gain,
            norm1_bias,
            query_bias,
            value_bias,
            proj_bias,
            scale_attn,
            norm2_gain,
            norm2_bias,
            fc2_bias,
            scale_mlp,
            fc1_bias.reshape(-1, width),
        ],
        0,
    )
    weights = (qkv_weight[0], proj_weight[0], fc1_weight[0], fc2_weight[0])
    bias = bias_columns(rel_table[0], length)

    def info_of(slot_id):
        is_valid = (slot_id >= 0) & (slot_id < micro)
        safe_slot = jnp.clip(slot_id, 0, micro - 1)
        padding = lax.dynamic_index_in_dim(pad_counts, safe_slot, 0, keepdims=False)
        return jnp.stack([is_valid.astype(jnp.int32), safe_slot, padding])

    received = jnp.zeros(patches.shape[1:], BF16)
    saved = None
    for tick_id in range(micro + 1):
        layer_in = jnp.where(section_id == 0, patches[min(tick_id, micro - 1)], received)
        result, saved = forward(
            info_of(tick_id - section_id), layer_in, segment_ids, vectors, bias, weights, saved
        )
        if tick_id < micro:
            received = shifted(result, "section", 1)
    returned = jnp.zeros(patches.shape[1:], BF16)
    kept = None
    for tick_id in range(micro + 1):
        upstream = jnp.where(section_id == 1, cotangent[min(tick_id, micro - 1)], returned)
        input_grad, kept = backward(
            info_of(tick_id - 1 + section_id), upstream, vectors, weights, saved, kept
        )
        if tick_id < micro:
            returned = shifted(input_grad, "section", -1)
    dm, dz, dproj, packed, in_grads, diagonals, sums = kept
    h1, mixed, h2, act, outputs = saved[0], saved[3], saved[6], saved[7], saved[10]
    table = table_gradient(diagonals)
    sums = jnp.sum(sums, 0)[:14]
    flat = jnp.concatenate([sums.reshape(-1, LANES), table.reshape(-1, LANES)], 0)
    parts = lax.axis_size("dp")
    height = -(-flat.shape[0] // (8 * parts)) * 8 * parts
    flat = jnp.pad(flat, ((0, height - flat.shape[0]), (0, 0)))
    left = [x.reshape(micro * length, -1) for x in (act, dm, h2, dz, h1, packed, mixed, dproj)]
    summed, small = reduce_gradients(*left, flat)
    fc2_grad, fc1_grad, qkv_grad, proj_grad = widen(summed, width)
    lines = width // LANES
    small_sums = small[: 14 * lines].reshape(14, width)
    table_grad = small[14 * lines : 14 * lines + table.size // LANES].reshape(table.shape)[:, : rel_table.shape[2]]

    def line(row):
        return small_sums[row : row + 1]

    return (
        outputs[None],
        in_grads[None],
        line(GAIN1),
        line(SHIFT1),
        qkv_grad[None],
        line(QBIAS),
        line(VBIAS),
        table_grad[None],
        proj_grad[None],
        line(PBIAS),
        line(SCALE_A),
        line(GAIN2),
        line(SHIFT2),
        fc1_grad[None],
        small_sums[B1 : B1 + 4].reshape(1, 4 * width),
        fc2_grad[None],
        line(B2),
        line(SCALE_M),
    )


def solution(mesh):
    placed = (
        P("dp", None, None),
        P("dp", None),
        P("dp"),
        P("section", None),
        P("section", None),
        P("section", None, None),
        P("section", None),
        P("section", None),
        P("section", None, None),
        P("section", None, None),
        P("section", None),
        P("section", None),
        P("section", None),
        P("section", None),
        P("section", None, None),
        P("section", None),
        P("section", None, None),
        P("section", None),
        P("section", None),
        P("dp", None, None),
    )
    return jax.shard_map(
        per_device,
        mesh=mesh,
        in_specs=placed,
        out_specs=(
            P("section", "dp", None, None),
            P("section", "dp", None, None),
            P("section", None),
            P("section", None),
            P("section", None, None),
            P("section", None),
            P("section", None),
            P("section", None, None),
            P("section", None, None),
            P("section", None),
            P("section", None),
            P("section", None),
            P("section", None),
            P("section", None, None),
            P("section", None),
            P("section", None, None),
            P("section", None),
            P("section", None),
        ),
        check_vma=False,
    )
```

```python
import functools
import math

import jax
import jax.numpy as jnp
from jax import lax
from jax.experimental import pallas as pl
from jax.experimental.pallas import tpu as pltpu
from jax.sharding import PartitionSpec as P

MESH = pl.DeviceIdType.MESH
BF16, F32 = jnp.bfloat16, jnp.float32
VMEM_BYTES = 60 * 1024 * 1024
LANES = 128
TAIL = (
    0.11652249842882156,
    0.06748615205287933,
    0.2689361274242401,
    -0.23702505230903625,
    0.3898930847644806,
    -0.10581281781196594,
)
HALF = 64
REACH = 2 * LANES
GAIN1, SHIFT1, QBIAS, VBIAS, PBIAS, SCALE_A, GAIN2, SHIFT2, B2, SCALE_M, B1 = range(11)
VECTORS = 11
STORED = 13


def dot(left, right, left_dim, right_dim):
    return lax.dot_general(
        left, right, (((left_dim,), (right_dim,)), ((), ())), preferred_element_type=F32
    )


def nn(left, right):
    return dot(left, right, 1, 0)


def nt(left, right):
    return dot(left, right, 1, 1)


def normalize(values):
    centered = values - jnp.mean(values, -1, keepdims=True)
    inverse = lax.rsqrt(jnp.mean(centered * centered, -1, keepdims=True) + 1e-06)
    return centered * inverse, inverse


def norm_back(upper, scaled, inverse):
    return inverse * (
        upper
        - jnp.mean(upper, -1, keepdims=True)
        - scaled * jnp.mean(upper * scaled, -1, keepdims=True)
    )


def fold(values):
    return jnp.sum(values.reshape(values.shape[0] // 8, 8, values.shape[1]), 0)


def half_mask(shape, which):
    return lax.broadcasted_iota(jnp.int32, shape, 1) // HALF == which


def chunk(index, size):
    return pl.ds(pl.multiple_of(index * size, size), size)


def skew_bias(reversed_row, target):
    span, lanes = target.shape
    rows = pltpu.roll(jnp.broadcast_to(reversed_row, (8, reversed_row.shape[1])), 0, 1, stride=1, stride_axis=0)
    tiles = span // lanes
    for fine in range(lanes // 8):
        moved = rows if fine == 0 else pltpu.roll(rows, 8 * fine, 1)
        for coarse in range(tiles):
            place = 8 * (fine + lanes // 8 * coarse)
            target[place : place + 8, :] = moved[:, lanes * (tiles - coarse) : lanes * (tiles - coarse + 1)]


def gather_diagonals(source):
    span, lanes = source.shape
    tiles = span // lanes
    width = span + lanes
    blank = jnp.zeros((8, lanes), F32)
    found = None
    for fine in range(lanes // 8):
        places = [8 * (fine + lanes // 8 * coarse) for coarse in reversed(range(tiles))]
        line = jnp.concatenate([blank] + [source[place : place + 8, :] for place in places], 1)
        if fine > 0:
            line = pltpu.roll(line, width - 8 * fine, 1)
        found = line if found is None else found + line
    row = lax.broadcasted_iota(jnp.int32, found.shape, 0)
    for place in range(3):
        moved = pltpu.roll(found, width - (1 << place), 1)
        found = jnp.where((row // (1 << place)) % 2 == 1, moved, found)
    return jnp.sum(found, 0, keepdims=True)


def normal_tail(size, expo):
    ratio = 1.0 / (1.0 + 0.28 * size)
    value = TAIL[-1]
    for coefficient in TAIL[-2::-1]:
        value = value * ratio + coefficient
    return value * ratio * expo


def key_rows(query_block, blocks):
    reach = REACH // LANES
    return max(0, query_block - reach) * LANES, min(blocks, query_block + reach + 1) * LANES


def forward_kernel(tick, pads, patches_hbm, received_hbm, seg_ref, ext_ref, *refs):
    vectors, refs = refs[:VECTORS], refs[VECTORS:]
    wqkv_hbm, wp_hbm, w1_hbm, w2_hbm = refs[:4]
    refs = refs[4 + (STORED + 1 if tick > 0 else 0) :]
    y_ref, bias_o, *stores = refs[: STORED + 2]
    (bias, wqkv, wp, w1, w2, mask, h1, qkv, probs, mixed, proj, x1, h2, act, slope, mlp, wide_mixed, total, xin, pre, load_sem, store_sem, prob_sem, bias_sem) = refs[STORED + 2 :]
    h1_o, qkv_o, prob_o, mixed_o, proj_o, x1_o, h2_o, act_o, slope_o, mlp_o, y_o, xin_o, wide_o = stores
    length, width = xin.shape
    hidden = w1.shape[1]
    heads = bias.shape[0]
    blocks = length // LANES
    section = lax.axis_index("section")
    slot = tick - section
    active = (slot >= 0) & (slot < seg_ref.shape[0])
    factor = HALF ** (-0.5)
    loads = [(wqkv_hbm, wqkv), (wp_hbm, wp), (w1_hbm, w1), (w2_hbm, w2)]

    def load(number):
        return pltpu.make_async_copy(*loads[number], load_sem.at[number])

    def store(number, source, there):
        return pltpu.make_async_copy(source, there.at[slot], store_sem.at[number])

    def vector(row):
        return vectors[row][...]

    def bias_load():
        return pltpu.make_async_copy(bias_o, bias, bias_sem.at[0])

    def bias_store():
        return pltpu.make_async_copy(bias, bias_o, bias_sem.at[0])

    @pl.when(active)
    def _():
        @pl.when(section == 0)
        def _():
            pltpu.make_async_copy(patches_hbm.at[slot], xin, load_sem.at[4]).start()

        @pl.when(section == 1)
        def _():
            pltpu.make_async_copy(received_hbm, xin, load_sem.at[4]).start()

        for number in range(len(loads)):
            load(number).start()
        if tick > 0:
            bias_load().start()

    if tick == 0:

        @pl.loop(0, heads)
        def _(head):
            skew_bias(ext_ref[pl.ds(head, 1), :], bias.at[head])

        bias_store().start()

    @pl.when(active)
    def _():
        pltpu.make_async_copy(received_hbm, xin, load_sem.at[4]).wait()
        segment = seg_ref[pl.ds(slot, 1), :].astype(F32)
        key_segment = jnp.broadcast_to(segment, (LANES, length)).T

        @pl.loop(0, length // 64)
        def _(step):
            rows = chunk(step, 64)
            scaled, _ = normalize(xin[rows, :].astype(F32))
            h1[rows, :] = (scaled * vector(GAIN1) + vector(SHIFT1)).astype(BF16)

        key = lax.broadcasted_iota(jnp.int32, (length, LANES), 0)
        living = key < length - pads[slot]
        for place in range(blocks):
            lanes = slice(place * LANES, (place + 1) * LANES)
            query = lax.broadcasted_iota(jnp.int32, (length, LANES), 1) + place * LANES
            allowed = ((key_segment == segment[:, lanes]) & living) | (key == query)
            mask[:, lanes] = jnp.where(allowed, 0.0, -1000000000.0)

        store(0, h1, h1_o).start()
        store(11, xin, xin_o).start()
        load(0).wait()
        for part in range(3):
            columns = pl.ds(part * width, width)
            result = nn(h1[...], wqkv[:, columns])
            if part == 0:
                result = (result + vector(QBIAS)) * factor
            if part == 2:
                result = result + vector(VBIAS)
            qkv[:, columns] = result.astype(BF16)
        store(1, qkv, qkv_o).start()
        if tick > 0:
            bias_load().wait()

        def prob_store(pair):
            return pltpu.make_async_copy(
                probs.at[pair % 2], prob_o.at[slot, pl.ds(2 * pair, 2)], prob_sem.at[pair % 2]
            )

        @pl.loop(0, width // LANES)
        def _(pair):
            @pl.when(pair >= 2)
            def _():
                prob_store(pair - 2).wait()

            side = pair % 2
            columns = chunk(pair, LANES)
            queries = qkv[:, columns]
            keys = qkv[:, pl.ds(pl.multiple_of(width + pair * LANES, LANES), LANES)]
            values = qkv[:, pl.ds(pl.multiple_of(2 * width + pair * LANES, LANES), LANES)].T
            outs = []
            for which in range(2):
                own_keys = jnp.where(half_mask(keys.shape, which), keys, jnp.zeros_like(keys))
                for wide in range(blocks // 2):
                    scores = nt(own_keys, queries[2 * LANES * wide : 2 * LANES * (wide + 1)])
                    for part in range(2):
                        place = 2 * wide + part
                        low, high = key_rows(place, blocks)
                        lanes = pl.ds(place * LANES, LANES)
                        first = (blocks - 1 - place) * LANES
                        here = (
                            scores[low:high, part * LANES : (part + 1) * LANES]
                            + bias[2 * pair + which, pl.ds(first + low, high - low), :]
                            + mask[low:high, lanes]
                        )
                        expo = jnp.exp(here - jnp.max(here, 0, keepdims=True))
                        scale = 1.0 / jnp.sum(expo, 0, keepdims=True)
                        probs[side, which, low:high, lanes] = (expo * scale).astype(BF16)
                        if low > 0:
                            probs[side, which, :low, lanes] = jnp.zeros((low, LANES), BF16)
                        if high < length:
                            probs[side, which, high:, lanes] = jnp.zeros((length - high, LANES), BF16)
                outs.append(nn(values[which * HALF : (which + 1) * HALF], probs[side, which]))
            out = jnp.concatenate(outs, 0).T
            wide_mixed[:, columns] = out
            mixed[:, columns] = out.astype(BF16)
            prob_store(pair).start()

        store(3, mixed, mixed_o).start()
        store(12, wide_mixed, wide_o).start()
        load(1).wait()

        @pl.loop(0, length // LANES)
        def _(step):
            rows = chunk(step, LANES)
            out = nn(mixed[rows, :], wp[...]) + vector(PBIAS)
            proj[rows, :] = out.astype(BF16)
            resid = xin[rows, :].astype(F32) + vector(SCALE_A) * out
            x1[rows, :] = resid
            scaled, _ = normalize(resid)
            h2[rows, :] = (scaled * vector(GAIN2) + vector(SHIFT2)).astype(BF16)

        store(4, proj, proj_o).start()
        store(5, x1, x1_o).start()
        store(6, h2, h2_o).start()
        load(2).wait()
        load(3).wait()
        pieces = [
            (pl.ds(high * (length // 2), length // 2), pl.ds(part * width, width))
            for part in range(hidden // width)
            for high in range(2)
        ]

        def expand(number):
            rows, columns = pieces[number]
            pre[number % 2] = nn(h2[rows, :], w1[:, columns]) + vectors[B1][:, columns]

        expand(0)
        for number, (rows, columns) in enumerate(pieces):
            if number + 1 < len(pieces):
                expand(number + 1)
            here = pre[number % 2]
            expo = jnp.exp(-0.5 * here * here)
            tail = normal_tail(jnp.abs(here), expo)
            normal = jnp.where(here < 0.0, tail, 1.0 - tail)
            act[rows, columns] = (here * normal).astype(BF16)
            slope[rows, columns] = (normal + here * (expo * (1.0 / math.sqrt(2.0 * math.pi)))).astype(BF16)
            more = nn(act[rows, columns], w2[columns, :])
            total[rows, :] = more if number < 2 else total[rows, :] + more
        store(7, act, act_o).start()
        store(8, slope, slope_o).start()

        @pl.loop(0, length // 64)
        def _(step):
            rows = chunk(step, 64)
            out = total[rows, :] + vector(B2)
            mlp[rows, :] = out.astype(BF16)
            y_ref[rows, :] = (x1[rows, :] + vector(SCALE_M) * out).astype(BF16)

        store(9, mlp, mlp_o).start()
        store(10, y_ref, y_o).start()
        for pair in (width // LANES - 2, width // LANES - 1):
            prob_store(pair).wait()
        ends = {0: (h1, h1_o), 1: (qkv, qkv_o), 3: (mixed, mixed_o), 4: (proj, proj_o), 5: (x1, x1_o), 6: (h2, h2_o),
                7: (act, act_o), 8: (slope, slope_o), 9: (mlp, mlp_o), 10: (y_ref, y_o), 11: (xin, xin_o), 12: (wide_mixed, wide_o)}
        for number, (source, there) in ends.items():
            store(number, source, there).wait()

    if tick == 0:
        bias_store().wait()


def hbm_specs(count):
    return [pl.BlockSpec(memory_space=pl.ANY)] * count


def vmem_specs(count):
    return [pl.BlockSpec(memory_space=pltpu.VMEM)] * count


def forward(tick, pads, patches, received, segments, ext, vectors, weights, kept):
    micro, length, width = patches.shape
    wqkv, wp, w1, w2 = weights
    hidden = w1.shape[1]
    heads = ext.shape[0]
    stored = [
        ((length, width), BF16),
        ((length, 3 * width), BF16),
        ((heads, length, length), BF16),
        ((length, width), BF16),
        ((length, width), BF16),
        ((length, width), F32),
        ((length, width), BF16),
        ((length, hidden), BF16),
        ((length, hidden), BF16),
        ((length, width), BF16),
        ((length, width), BF16),
        ((length, width), BF16),
        ((length, width), F32),
    ]
    bias = jax.ShapeDtypeStruct((heads, 2 * length - LANES, LANES), F32)
    scratch = [pltpu.VMEM(x.shape, x.dtype) for x in (bias, wqkv, wp, w1, w2)]
    scratch.append(pltpu.VMEM((length, length), F32))
    scratch += [pltpu.VMEM((2, 2, length, length) if n == 2 else shape, kind) for n, (shape, kind) in enumerate(stored[:10])]
    scratch += [pltpu.VMEM((length, width), F32), pltpu.VMEM((length, width), F32), pltpu.VMEM((length, width), BF16)]
    scratch += [pltpu.VMEM((2, length // 2, width), F32)]
    scratch += [
        pltpu.SemaphoreType.DMA((5,)),
        pltpu.SemaphoreType.DMA((STORED,)),
        pltpu.SemaphoreType.DMA((2,)),
        pltpu.SemaphoreType.DMA((1,)),
    ]
    operands = [pads, patches, received, segments, ext, *vectors, *weights]
    first = len(operands)
    held = STORED + 1 if tick > 0 else 0
    out = pl.pallas_call(
        functools.partial(forward_kernel, tick),
        out_shape=[jax.ShapeDtypeStruct((length, width), BF16), bias]
        + [jax.ShapeDtypeStruct((micro, *shape), kind) for shape, kind in stored],
        in_specs=[pl.BlockSpec(memory_space=pltpu.SMEM)] + hbm_specs(2) + vmem_specs(2 + VECTORS) + hbm_specs(4 + held),
        out_specs=vmem_specs(1) + hbm_specs(STORED + 1),
        scratch_shapes=scratch,
        input_output_aliases={first + n: 1 + n for n in range(held)},
        compiler_params=pltpu.CompilerParams(vmem_limit_bytes=VMEM_BYTES),
        name="forward_layer",
    )(*operands, *(kept if tick > 0 else ()))
    return out[0], out[1:]


def backward_kernel(tick, cotangent_hbm, returned_hbm, *refs):
    vectors, refs = refs[:VECTORS], refs[VECTORS:]
    (wqkv_hbm, wp_hbm, w1_hbm, w2_hbm, qkv_i, prob_i, mixed_i, proj_i, x1_i, slope_i, mlp_i, xin_i) = refs[:12]
    refs = refs[12 + (7 if tick > 0 else 0) :]
    dx_ref, *stores = refs[:8]
    (wqkv, wp, w1, w2, qkv, probs, mixed, proj, x1, slope, mlp, xin, dm, dz, dproj, packed, dx1, total, dmixed, dscore, diag, sums, tables, g_ref, acts, load_sem, store_sem, prob_sem) = refs[8:]
    dm_o, dz_o, dproj_o, packed_o, dx_o, tables_o, sums_o = stores
    length, width = g_ref.shape
    hidden = w1.shape[1]
    blocks = length // LANES
    pairs = width // LANES
    section = lax.axis_index("section")
    slot = tick - 1 + section
    active = (slot >= 0) & (slot < cotangent_hbm.shape[0])
    factor = HALF ** (-0.5)
    loads = [
        (mlp_i.at[slot], mlp), (w2_hbm, w2), (slope_i.at[slot], slope), (w1_hbm, w1), (x1_i.at[slot], x1),
        (proj_i.at[slot], proj), (wp_hbm, wp), (qkv_i.at[slot], qkv), (mixed_i.at[slot], mixed), (wqkv_hbm, wqkv),
        (xin_i.at[slot], xin),
    ]
    step_rows = 64
    steps = length // step_rows

    def load(number):
        return pltpu.make_async_copy(*loads[number], load_sem.at[number])

    def store(number, source, there):
        return pltpu.make_async_copy(source, there.at[slot], store_sem.at[number])

    def prob_load(pair):
        return pltpu.make_async_copy(
            prob_i.at[slot, pl.ds(2 * pair, 2)], probs.at[pair % 2], prob_sem.at[pair % 2]
        )

    def vector(row):
        return vectors[row][...]

    def put(row, partial):
        sums[row : row + 1, :] = jnp.sum(partial, 0, keepdims=True)

    nothing = jnp.zeros((8, width), F32)

    @pl.when(active)
    def _():
        @pl.when(section == 1)
        def _():
            pltpu.make_async_copy(cotangent_hbm.at[slot], g_ref, load_sem.at[11]).start()

        @pl.when(section == 0)
        def _():
            pltpu.make_async_copy(returned_hbm, g_ref, load_sem.at[11]).start()

        for number in range(len(loads)):
            load(number).start()
        prob_load(0).start()
        pltpu.make_async_copy(returned_hbm, g_ref, load_sem.at[11]).wait()
        load(0).wait()

        def first(step, carry):
            rows = chunk(step, step_rows)
            upstream = g_ref[rows, :].astype(F32)
            low = (upstream * vector(SCALE_M)).astype(BF16)
            dm[rows, :] = low
            return carry[0] + fold(upstream * mlp[rows, :].astype(F32)), carry[1] + fold(low.astype(F32))

        scale_sum, bias_sum = lax.fori_loop(0, steps, first, (nothing, nothing))
        put(SCALE_M, scale_sum)
        put(B2, bias_sum)
        store(0, dm, dm_o).start()
        load(1).wait()
        load(2).wait()
        load(3).wait()
        pieces = [
            (pl.ds(high * (length // 2), length // 2), pl.ds(part * width, width))
            for part in range(hidden // width)
            for high in range(2)
        ]

        def expand(number):
            rows, columns = pieces[number]
            acts[number % 2] = nt(dm[rows, :], w2[columns, :])

        expand(0)
        act_sum = None
        for number, (rows, columns) in enumerate(pieces):
            if number + 1 < len(pieces):
                expand(number + 1)
            low = (acts[number % 2] * slope[rows, columns].astype(F32)).astype(BF16)
            dz[rows, columns] = low
            act_sum = fold(low.astype(F32)) + (nothing if number % 2 == 0 else act_sum)
            if number % 2 == 1:
                put(B1 + number // 2, act_sum)
            more = nt(dz[rows, columns], w1[:, columns])
            total[rows, :] = more if number < 2 else total[rows, :] + more
        store(1, dz, dz_o).start()
        load(4).wait()
        load(5).wait()

        def second(step, carry):
            rows = chunk(step, step_rows)
            upper = total[rows, :]
            scaled, inverse = normalize(x1[rows, :])
            resid = g_ref[rows, :].astype(F32) + norm_back(upper * vector(GAIN2), scaled, inverse)
            dx1[rows, :] = resid
            low = (resid * vector(SCALE_A)).astype(BF16)
            dproj[rows, :] = low
            terms = (upper * scaled, upper, resid * proj[rows, :].astype(F32), low.astype(F32))
            return tuple(old + fold(term) for old, term in zip(carry, terms))

        for row, partial in zip((GAIN2, SHIFT2, SCALE_A, PBIAS), lax.fori_loop(0, steps, second, (nothing,) * 4)):
            put(row, partial)
        store(2, dproj, dproj_o).start()
        load(6).wait()
        dmixed[...] = nt(dproj[...], wp[...]).astype(BF16)
        load(7).wait()
        load(8).wait()

        @pl.loop(0, pairs)
        def _(pair):
            prob_load(pair).wait()

            @pl.when(pair + 1 < pairs)
            def _():
                prob_load(pair + 1).start()

            side = pair % 2
            columns = chunk(pair, LANES)
            key_columns = pl.ds(pl.multiple_of(width + pair * LANES, LANES), LANES)
            value_columns = pl.ds(pl.multiple_of(2 * width + pair * LANES, LANES), LANES)
            values = qkv[:, value_columns]
            above = dmixed[:, columns]
            queries_t = qkv[:, columns].T
            keys_t = qkv[:, key_columns].T
            above_t = above.T
            products = (above.astype(F32) * mixed[:, columns]).T
            grads = [], [], []
            for which in range(2):
                half = slice(which * HALF, (which + 1) * HALF)
                delta = jnp.sum(products[half], 0, keepdims=True)
                own_values = jnp.where(half_mask(values.shape, which), values, jnp.zeros_like(values))
                edge = (blocks - 1) * LANES
                diag[which, :edge, :] = jnp.zeros((edge, LANES), F32)
                for wide in range(blocks // 2):
                    prob_grad = nt(own_values, above[2 * LANES * wide : 2 * LANES * (wide + 1)])
                    for part in range(2):
                        place = 2 * wide + part
                        low, high = key_rows(place, blocks)
                        lanes = pl.ds(place * LANES, LANES)
                        first_row = (blocks - 1 - place) * LANES
                        here = probs[side, which, low:high, lanes].astype(F32) * (
                            prob_grad[low:high, part * LANES : (part + 1) * LANES]
                            - delta[:, place * LANES : (place + 1) * LANES]
                        )
                        dscore[which, low:high, lanes] = here.astype(BF16)
                        if low > 0:
                            dscore[which, :low, lanes] = jnp.zeros((low, LANES), BF16)
                        if high < length:
                            dscore[which, high:, lanes] = jnp.zeros((length - high, LANES), BF16)
                        there = pl.ds(first_row + low, high - low)
                        if place == 0:
                            diag[which, there, :] = here
                            diag[which, edge + high :, :] = jnp.zeros((length - high, LANES), F32)
                        else:
                            diag[which, there, :] = diag[which, there, :] + here
                tables[pl.ds(2 * pair + which, 1), :] = gather_diagonals(diag.at[which])[:, REACH : REACH + tables.shape[1]]
                grads[0].append(nn(keys_t[half], dscore[which]))
                grads[1].append(nt(queries_t[half], dscore[which]))
                grads[2].append(nt(above_t[half], probs[side, which]))
            for found, where, scale in zip(grads, (columns, key_columns, value_columns), (factor, None, None)):
                low = jnp.concatenate(found, 0).astype(BF16)
                if scale is not None:
                    low = (low.astype(F32) * scale).astype(BF16)
                packed[:, where] = low.T

        store(3, packed, packed_o).start()
        load(9).wait()
        total[...] = nt(packed[...], wqkv[...])
        load(10).wait()

        def third(step, carry):
            rows = chunk(step, step_rows)
            upper = total[rows, :]
            scaled, inverse = normalize(xin[rows, :].astype(F32))
            dx_ref[rows, :] = (dx1[rows, :] + norm_back(upper * vector(GAIN1), scaled, inverse)).astype(BF16)
            terms = (
                upper * scaled,
                upper,
                packed[rows, :width].astype(F32),
                packed[rows, 2 * width :].astype(F32),
            )
            return tuple(old + fold(term) for old, term in zip(carry, terms))

        for row, partial in zip((GAIN1, SHIFT1, QBIAS, VBIAS), lax.fori_loop(0, steps, third, (nothing,) * 4)):
            put(row, partial)
        store(4, dx_ref, dx_o).start()
        store(5, tables, tables_o).start()
        store(6, sums, sums_o).start()
        ends = {0: (dm, dm_o), 1: (dz, dz_o), 2: (dproj, dproj_o), 3: (packed, packed_o), 4: (dx_ref, dx_o), 5: (tables, tables_o), 6: (sums, sums_o)}
        for number, (source, there) in ends.items():
            store(number, source, there).wait()


def backward(tick, cotangent, returned, vectors, weights, saved, kept):
    micro, length, width = cotangent.shape
    wqkv, wp, w1, w2 = weights
    hidden = w1.shape[1]
    bias, h1, qkv, probs, mixed, proj, x1, h2, act, slope, mlp, y, xin, wide = saved
    heads = probs.shape[1]
    span = 2 * length - LANES
    summed = (16, width)
    table = (heads, 5 * LANES)
    stored = [
        ((length, width), BF16),
        ((length, hidden), BF16),
        ((length, width), BF16),
        ((length, 3 * width), BF16),
        ((length, width), BF16),
        (table, F32),
        (summed, F32),
    ]
    reads = [qkv, probs, wide, proj, x1, slope, mlp, xin]
    scratch = [pltpu.VMEM(x.shape, x.dtype) for x in weights]
    scratch += [pltpu.VMEM((2, 2, length, length) if x is probs else x.shape[1:], x.dtype) for x in reads]
    scratch += [pltpu.VMEM(shape, kind) for shape, kind in stored[:4]]
    scratch += [
        pltpu.VMEM((length, width), F32),
        pltpu.VMEM((length, width), F32),
        pltpu.VMEM((length, width), BF16),
        pltpu.VMEM((2, length, length), BF16),
        pltpu.VMEM((2, span, LANES), F32),
        pltpu.VMEM(summed, F32),
        pltpu.VMEM(table, F32),
        pltpu.VMEM((length, width), BF16),
        pltpu.VMEM((2, length // 2, width), F32),
        pltpu.SemaphoreType.DMA((12,)),
        pltpu.SemaphoreType.DMA((7,)),
        pltpu.SemaphoreType.DMA((2,)),
    ]
    operands = [cotangent, returned, *vectors, *weights, *reads]
    first = len(operands)
    held = 7 if tick > 0 else 0
    out = pl.pallas_call(
        functools.partial(backward_kernel, tick),
        out_shape=[jax.ShapeDtypeStruct((length, width), BF16)]
        + [jax.ShapeDtypeStruct((micro, *shape), kind) for shape, kind in stored],
        in_specs=hbm_specs(2) + vmem_specs(VECTORS) + hbm_specs(12 + held),
        out_specs=vmem_specs(1) + hbm_specs(7),
        scratch_shapes=scratch,
        input_output_aliases={first + n: 1 + n for n in range(held)},
        compiler_params=pltpu.CompilerParams(vmem_limit_bytes=VMEM_BYTES),
        name="backward_layer",
    )(*operands, *(kept if tick > 0 else ()))
    return out[0], out[1:]


def small_lines(width):
    lines = width // LANES
    places = [(row, tile, row * lines + tile) for row in range(10) for tile in range(lines)]
    return places + [(B1, tile, B1 * lines + tile) for tile in range(4 * lines)]


def widen_kernel(per_side, sum_ref, small_ref, *refs):
    step = pl.program_id(0)
    block = step // per_side
    bigs, vectors, table_ref = refs[:4], refs[4:-1], refs[-1]
    for target, low, high in zip(bigs, (0, 4, 8, 11), (4, 8, 11, 12)):

        @pl.when((block >= low) & (block < high))
        def _():
            target[...] = sum_ref[...].astype(F32)

    @pl.when(step == 0)
    def _():
        places = small_lines(vectors[0].shape[1])
        for row, tile, line in places:
            vectors[row][:, tile * LANES : (tile + 1) * LANES] = small_ref[line : line + 1, :]
        first = len(places)
        heads, columns = table_ref.shape
        tiles = columns // LANES
        for head in range(heads):
            for tile in range(tiles):
                line = first + head * tiles + tile
                table_ref[head : head + 1, tile * LANES : (tile + 1) * LANES] = small_ref[line : line + 1, :]


def widen(summed, small, width, heads, per_side):
    part = (width // per_side, width)
    shapes = [(4 * width, width), (width, 4 * width), (width, 3 * width), (width, width)]
    shapes += [(1, width)] * 10 + [(1, 4 * width), (heads, 5 * LANES)]

    def lying(first, count):
        def place(step):
            local = jnp.clip(step - first * per_side, 0, count * per_side - 1)
            return (local % per_side, local // per_side)

        return place

    return pl.pallas_call(
        functools.partial(widen_kernel, per_side),
        grid=(12 * per_side,),
        out_shape=[jax.ShapeDtypeStruct(shape, F32) for shape in shapes],
        in_specs=[pl.BlockSpec(part, lambda s: (s, 0)), pl.BlockSpec(small.shape, lambda s: (0, 0))],
        out_specs=[
            pl.BlockSpec(part, lambda s: (jnp.minimum(s, 4 * per_side - 1), 0)),
            pl.BlockSpec(part, lying(4, 4)),
            pl.BlockSpec(part, lying(8, 3)),
            pl.BlockSpec(part, lying(11, 1)),
        ]
        + [pl.BlockSpec(shape, lambda s: (0, 0)) for shape in shapes[4:]],
        compiler_params=pltpu.CompilerParams(vmem_limit_bytes=VMEM_BYTES),
        name="widen",
    )(summed, small)


BLOCK = 256
LAG = 3


def reduce_kernel(
    bits, chunks, blocks, lag, *refs
):
    (a_ref, dm_ref, h2_ref, dz_ref, h1_ref, dp_ref, o_ref, dproj_ref, sums_ref, tables_ref, out_ref, small_out_ref) = refs[:12]
    (lhs, rhs, grads, total, small_ref, small_total, *received) = refs[12 : 18 + 2 * bits]
    (load_sem, send_sem, recv_sem, small_send, small_recv, store_sem) = refs[18 + 2 * bits :]
    small_received = received[bits:]
    me = lax.axis_index("dp")
    rows = BLOCK * blocks
    width = grads.shape[1]
    per_side = width // BLOCK
    last = 2 * bits

    barrier = pltpu.get_barrier_semaphore()
    for place in range(bits):
        stride = 1 << place
        other = me + stride * (1 - 2 * ((me // stride) % 2))
        pl.semaphore_signal(barrier, inc=1, device_id={"dp": other}, device_id_type=MESH)
    pl.semaphore_wait(barrier, bits)

    families = (
        (a_ref, dm_ref, 4 * per_side, True),
        (h2_ref, dz_ref, 4 * per_side, False),
        (h1_ref, dp_ref, 3 * per_side, False),
        (o_ref, dproj_ref, per_side, False),
    )
    n_blocks = 12 * per_side

    def load(block):
        slot = block % 2
        first = 0
        for left, right, count, walks in families:
            @pl.when((block >= first) & (block < first + count))
            def _():
                local = block - first
                if walks:
                    left_column = local * BLOCK
                    right_column = 0
                else:
                    left_column = (local % per_side) * BLOCK
                    right_column = (local // per_side) * width
                pltpu.make_async_copy(
                    left.at[:, pl.ds(pl.multiple_of(left_column, BLOCK), BLOCK)],
                    lhs.at[slot],
                    load_sem.at[0, slot],
                ).start()
                pltpu.make_async_copy(
                    right.at[:, pl.ds(pl.multiple_of(right_column, BLOCK), width)],
                    rhs.at[slot],
                    load_sem.at[1, slot],
                ).start()
            first += count

    def produce(block):
        slot = block % 2
        pltpu.make_async_copy(lhs.at[slot], lhs.at[slot], load_sem.at[0, slot]).wait()
        pltpu.make_async_copy(rhs.at[slot], rhs.at[slot], load_sem.at[1, slot]).wait()

        @pl.when(block + 1 < n_blocks)
        def _():
            load(block + 1)

        grads[pl.ds(pl.multiple_of(block * BLOCK, BLOCK), BLOCK), :] = lax.dot_general(
            lhs[slot], rhs[slot], (((0,), (0,)), ((), ())), preferred_element_type=jnp.float32
        ).astype(jnp.bfloat16)

    def turn(chunk):
        place = chunk % 9
        return place % 2 + place // 5 - place // 6

    def partner(rotation, stage):
        stride = lax.shift_left(jnp.int32(1), (stage + rotation) % bits)
        mine = (me // stride) % 2
        return mine, me + stride * (1 - 2 * mine)

    def offset(base, height, rotation, stage):
        for earlier in range(stage):
            mine, _ = partner(rotation, earlier)
            base = base + mine * (height >> (earlier + 1))
        return base

    def piece(ref, start, size):
        return ref.at[pl.ds(pl.multiple_of(start, size), size)]

    def send(position, base, height, rotation, source, landing, result, slot, sems):
        send_at, recv_at = sems
        if position < bits:
            stage = position
            half = height >> (stage + 1)
            mine, other = partner(rotation, stage)
            start = offset(base, height, rotation, stage) + (1 - mine) * half
            src, dst = piece(source, start, half), landing[stage].at[slot]
        else:
            stage = last - 1 - position
            half = height >> (stage + 1)
            mine, other = partner(rotation, stage)
            start = offset(base, height, rotation, stage + 1)
            src = dst = piece(result, start, half)
        return pltpu.make_async_remote_copy(
            src_ref=src,
            dst_ref=dst,
            send_sem=send_at.at[position],
            recv_sem=recv_at.at[position, slot],
            device_id={"dp": other},
            device_id_type=MESH,
        )

    def take(position, base, height, rotation, source, landing, result, slot, sems):
        send(position - 1, base, height, rotation, source, landing, result, slot, sems).wait_recv()
        stage = position - 1
        if stage < bits:
            half = height >> (stage + 1)
            start = pl.multiple_of(offset(base, height, rotation, stage + 1), half)
            keep = pl.ds(start, half)
            value = source[keep, :].astype(jnp.float32) + landing[stage][slot].astype(jnp.float32)
            target = result if stage == bits - 1 else source
            target[keep, :] = value.astype(target.dtype)

    def step(position, *way):
        if position > 0:
            take(position, *way)
        if position < last:
            send(position, *way).start()

    main = (grads, received[:bits], total)
    main_sems = (send_sem, recv_sem)

    def walk(position, chunk):
        if position == 0:
            for sub in range(blocks):
                block = chunk * blocks + sub

                @pl.when(block < n_blocks)
                def _():
                    produce(block)

        base = chunk * rows
        step(position, base, rows, turn(chunk), *main, chunk, main_sems)
        if position == last:
            there = pl.ds(pl.multiple_of(base, rows), rows)
            pltpu.make_async_copy(total.at[there], out_ref.at[there], store_sem.at[0]).start()

    def walk_small(position):
        height = small_ref.shape[0]
        way = (0, height, 0, small_ref, small_received, small_total, 0, (small_send, small_recv))
        step(position, *way)

    load(jnp.int32(0))
    small_ref[...] = jnp.zeros_like(small_ref)
    places = small_lines(width)
    for row, tile, line in places:
        if row == B1:
            row, tile = B1 + tile // (width // LANES), tile % (width // LANES)
        lanes = slice(tile * LANES, (tile + 1) * LANES)
        small_ref[line : line + 1, :] = sums_ref[0, row : row + 1, lanes] + sums_ref[1, row : row + 1, lanes]
    line = len(places)
    for head in range(tables_ref.shape[1]):
        for tile in range(tables_ref.shape[2] // LANES):
            lanes = slice(tile * LANES, (tile + 1) * LANES)
            small_ref[line : line + 1, :] = tables_ref[0, head : head + 1, lanes] + tables_ref[1, head : head + 1, lanes]
            line += 1

    @pl.loop(0, chunks + lag * last)
    def _(tick):
        for position in range(last + 1):
            chunk = tick - lag * position

            @pl.when((chunk >= 0) & (chunk < chunks))
            def _():
                walk(position, chunk)

            @pl.when(tick == lag * position)
            def _():
                walk_small(position)

    small_out_ref[...] = small_total[...]
    for position in range(last):
        stage = position if position < bits else last - 1 - position
        size = received[stage]
        pltpu.make_async_copy(size, size, send_sem.at[position]).wait()
        size = small_received[stage]
        pltpu.make_async_copy(size, size, small_send.at[position]).wait()
    pltpu.make_async_copy(total, out_ref, store_sem.at[0]).wait()


def reduce_gradients(a, dm, h2, dz, h1, packed, o, dproj, sums, tables):
    parts = lax.axis_size("dp")
    bits = parts.bit_length() - 1
    blocks = max(1, 16 * parts // BLOCK)
    tokens, width = h1.shape
    n_blocks = 12 * width // BLOCK
    chunks = -(-n_blocks // blocks)
    rows = BLOCK * blocks
    lines = len(small_lines(width)) + tables.shape[1] * tables.shape[2] // LANES
    height = -(-lines // (8 * parts)) * 8 * parts
    small = jax.ShapeDtypeStruct((height, LANES), jnp.float32)
    bf16 = jnp.bfloat16
    return pl.pallas_call(
        functools.partial(reduce_kernel, bits, chunks, blocks, LAG),
        out_shape=(
            jax.ShapeDtypeStruct((chunks * rows, width), bf16),
            jax.ShapeDtypeStruct(small.shape, jnp.float32),
        ),
        in_specs=[pl.BlockSpec(memory_space=pl.ANY)] * 8 + [pl.BlockSpec(memory_space=pltpu.VMEM)] * 2,
        out_specs=(pl.BlockSpec(memory_space=pl.ANY), pl.BlockSpec(memory_space=pltpu.VMEM)),
        scratch_shapes=[
            pltpu.VMEM((2, tokens, BLOCK), bf16),
            pltpu.VMEM((2, tokens, width), bf16),
            pltpu.VMEM((chunks * rows, width), bf16),
            pltpu.VMEM((chunks * rows, width), bf16),
            pltpu.VMEM(small.shape, jnp.float32),
            pltpu.VMEM(small.shape, jnp.float32),
            *[pltpu.VMEM((chunks, rows >> (s + 1), width), bf16) for s in range(bits)],
            *[pltpu.VMEM((1, height >> (s + 1), 128), jnp.float32) for s in range(bits)],
            pltpu.SemaphoreType.DMA((2, 2)),
            pltpu.SemaphoreType.DMA((2 * bits,)),
            pltpu.SemaphoreType.DMA((2 * bits, chunks)),
            pltpu.SemaphoreType.DMA((2 * bits,)),
            pltpu.SemaphoreType.DMA((2 * bits, 1)),
            pltpu.SemaphoreType.DMA((1,)),
        ],
        compiler_params=pltpu.CompilerParams(
            collective_id=0, has_side_effects=True, vmem_limit_bytes=60 * 1024 * 1024
        ),
        name="reduce_gradients",
    )(a, dm, h2, dz, h1, packed, o, dproj, sums, tables)


def shifted(block, axis, distance):
    devices = range(lax.axis_size(axis))
    route = [(i - distance, i) for i in devices if i - distance in devices]
    return lax.ppermute(block, axis, route)


def per_device(
    patches,
    segment_ids,
    pad_counts,
    norm1_gain,
    norm1_bias,
    qkv_weight,
    query_bias,
    value_bias,
    rel_table,
    proj_weight,
    proj_bias,
    scale_attn,
    norm2_gain,
    norm2_bias,
    fc1_weight,
    fc1_bias,
    fc2_weight,
    fc2_bias,
    scale_mlp,
    cotangent,
):
    micro, length, width = patches.shape
    vectors = (
        norm1_gain,
        norm1_bias,
        query_bias,
        value_bias,
        proj_bias,
        scale_attn,
        norm2_gain,
        norm2_bias,
        fc2_bias,
        scale_mlp,
        fc1_bias,
    )
    weights = (qkv_weight[0], proj_weight[0], fc1_weight[0], fc2_weight[0])
    entries = rel_table.shape[2]
    before = REACH
    after = 2 * length - before - entries
    ext = jnp.pad(rel_table[0, :, ::-1], ((0, 0), (before, after)))
    received = patches[0]
    saved = None
    for tick in range(micro + 1):
        result, saved = forward(
            tick, pad_counts, patches, received, segment_ids, ext, vectors, weights, saved
        )
        if tick < micro:
            received = shifted(result, "section", 1)
    returned = received
    kept = None
    for tick in range(micro + 1):
        input_grad, kept = backward(tick, cotangent, returned, vectors, weights, saved, kept)
        if tick < micro:
            returned = shifted(input_grad, "section", -1)
    dm, dz, dproj, packed, in_grads, tables, sums = kept
    h1, mixed, h2, act, outputs = saved[1], saved[4], saved[7], saved[8], saved[11]
    left = [x.reshape(micro * length, -1) for x in (act, dm, h2, dz, h1, packed, mixed, dproj)]
    summed, small = reduce_gradients(*left, sums, tables)
    fc2_grad, fc1_grad, qkv_grad, proj_grad, *small_grads = widen(summed, small, width, tables.shape[1], 2)
    table_grad = small_grads[VECTORS][:, :entries][:, ::-1]
    return (
        outputs[None],
        in_grads[None],
        small_grads[GAIN1],
        small_grads[SHIFT1],
        qkv_grad[None],
        small_grads[QBIAS],
        small_grads[VBIAS],
        table_grad[None],
        proj_grad[None],
        small_grads[PBIAS],
        small_grads[SCALE_A],
        small_grads[GAIN2],
        small_grads[SHIFT2],
        fc1_grad[None],
        small_grads[B1],
        fc2_grad[None],
        small_grads[B2],
        small_grads[SCALE_M],
    )


def solution(mesh):
    placed = (
        P("dp", None, None),
        P("dp", None),
        P("dp"),
        P("section", None),
        P("section", None),
        P("section", None, None),
        P("section", None),
        P("section", None),
        P("section", None, None),
        P("section", None, None),
        P("section", None),
        P("section", None),
        P("section", None),
        P("section", None),
        P("section", None, None),
        P("section", None),
        P("section", None, None),
        P("section", None),
        P("section", None),
        P("dp", None, None),
    )
    return jax.shard_map(
        per_device,
        mesh=mesh,
        in_specs=placed,
        out_specs=(
            P("section", "dp", None, None),
            P("section", "dp", None, None),
            P("section", None),
            P("section", None),
            P("section", None, None),
            P("section", None),
            P("section", None),
            P("section", None, None),
            P("section", None, None),
            P("section", None),
            P("section", None),
            P("section", None),
            P("section", None),
            P("section", None, None),
            P("section", None),
            P("section", None, None),
            P("section", None),
            P("section", None),
        ),
        check_vma=False,
    )
```

```python
import functools
import math

import jax
import jax.numpy as jnp
from jax import lax
from jax.experimental import pallas as pl
from jax.experimental.pallas import tpu as pltpu
from jax.sharding import PartitionSpec as P

MESH = pl.DeviceIdType.MESH
BF16, F32 = jnp.bfloat16, jnp.float32
VMEM_BYTES = 60 * 1024 * 1024
LANES = 128
TAIL = (
    0.11652249842882156,
    0.06748615205287933,
    0.2689361274242401,
    -0.23702505230903625,
    0.3898930847644806,
    -0.10581281781196594,
)
HALF = 64
REACH = 2 * LANES
GAIN1, SHIFT1, QBIAS, VBIAS, PBIAS, SCALE_A, GAIN2, SHIFT2, B2, SCALE_M, B1 = range(11)
VECTORS = 11
STORED = 14
STRIP = 16


def dot(left, right, left_dim, right_dim):
    return lax.dot_general(
        left, right, (((left_dim,), (right_dim,)), ((), ())), preferred_element_type=F32
    )


def nn(left, right):
    return dot(left, right, 1, 0)


def nt(left, right):
    return dot(left, right, 1, 1)


def normalize(values):
    centered = values - jnp.mean(values, -1, keepdims=True)
    inverse = lax.rsqrt(jnp.mean(centered * centered, -1, keepdims=True) + 1e-06)
    return centered * inverse, inverse


def norm_back(upper, scaled, inverse):
    return inverse * (
        upper
        - jnp.mean(upper, -1, keepdims=True)
        - scaled * jnp.mean(upper * scaled, -1, keepdims=True)
    )


def fold(values):
    return jnp.sum(values.reshape(values.shape[0] // 8, 8, values.shape[1]), 0)


def half_mask(shape, which):
    return lax.broadcasted_iota(jnp.int32, shape, 1) // HALF == which


def strips(first, last, size):
    return [slice(start, start + size) for start in range(first, last, size)]


def chunk(index, size):
    return pl.ds(pl.multiple_of(index * size, size), size)


def skew_bias(reversed_row, target):
    span, lanes = target.shape
    rows = pltpu.roll(jnp.broadcast_to(reversed_row, (8, reversed_row.shape[1])), 0, 1, stride=1, stride_axis=0)
    tiles = span // lanes
    for fine in range(lanes // 8):
        moved = rows if fine == 0 else pltpu.roll(rows, 8 * fine, 1)
        for coarse in range(tiles):
            place = 8 * (fine + lanes // 8 * coarse)
            target[place : place + 8, :] = moved[:, lanes * (tiles - coarse) : lanes * (tiles - coarse + 1)]


def gather_diagonals(source):
    span, lanes = source.shape
    tiles = span // lanes
    width = span + lanes
    blank = jnp.zeros((8, lanes), F32)
    found = None
    for fine in range(lanes // 8):
        places = [8 * (fine + lanes // 8 * coarse) for coarse in reversed(range(tiles))]
        line = jnp.concatenate([blank] + [source[place : place + 8, :] for place in places], 1)
        if fine > 0:
            line = pltpu.roll(line, width - 8 * fine, 1)
        found = line if found is None else found + line
    row = lax.broadcasted_iota(jnp.int32, found.shape, 0)
    for place in range(3):
        moved = pltpu.roll(found, width - (1 << place), 1)
        found = jnp.where((row // (1 << place)) % 2 == 1, moved, found)
    return jnp.sum(found, 0, keepdims=True)


def normal_tail(size, expo):
    ratio = 1.0 / (1.0 + 0.28 * size)
    value = TAIL[-1]
    for coefficient in TAIL[-2::-1]:
        value = value * ratio + coefficient
    return value * ratio * expo


def key_rows(query_block, blocks):
    reach = REACH // LANES
    return max(0, query_block - reach) * LANES, min(blocks, query_block + reach + 1) * LANES


def forward_kernel(tick, pads, patches_hbm, received_hbm, seg_ref, ext_ref, *refs):
    vectors, refs = refs[:VECTORS], refs[VECTORS:]
    wqkv_hbm, wp_hbm, w1_hbm, w2_hbm = refs[:4]
    refs = refs[4 + (STORED + 1 if tick > 0 else 0) :]
    y_ref, bias_o, *stores = refs[: STORED + 2]
    (bias, wqkv, wp, w1, w2, mask, h1, qkv, probs, mixed, proj, x1, h2, act, slope, mlp, wide_mixed, scales, xin, held, load_sem, store_sem, prob_sem, bias_sem) = refs[STORED + 2 :]
    h1_o, qkv_o, prob_o, mixed_o, proj_o, x1_o, h2_o, act_o, slope_o, mlp_o, y_o, xin_o, wide_o, scales_o = stores
    length, width = xin.shape
    hidden = w1.shape[1]
    heads = bias.shape[0]
    blocks = length // LANES
    section = lax.axis_index("section")
    slot = tick - section
    active = (slot >= 0) & (slot < seg_ref.shape[0])
    factor = HALF ** (-0.5)
    loads = [(wqkv_hbm, wqkv), (wp_hbm, wp), (w1_hbm, w1), (w2_hbm, w2)]

    def load(number):
        return pltpu.make_async_copy(*loads[number], load_sem.at[number])

    def store(number, source, there):
        return pltpu.make_async_copy(source, there.at[slot], store_sem.at[number])

    def vector(row):
        return vectors[row][...]

    def bias_load():
        return pltpu.make_async_copy(bias_o, bias, bias_sem.at[0])

    def bias_store():
        return pltpu.make_async_copy(bias, bias_o, bias_sem.at[0])

    @pl.when(active)
    def _():
        @pl.when(section == 0)
        def _():
            pltpu.make_async_copy(patches_hbm.at[slot], xin, load_sem.at[4]).start()

        if tick > 0:

            @pl.when(section == 1)
            def _():
                pltpu.make_async_copy(received_hbm, xin, load_sem.at[4]).start()

        for number in range(len(loads)):
            load(number).start()
        if tick > 0:
            bias_load().start()

    if tick == 0:

        @pl.loop(0, heads)
        def _(head):
            skew_bias(ext_ref[pl.ds(head, 1), :], bias.at[head])

        bias_store().start()

    @pl.when(active)
    def _():
        pltpu.make_async_copy(xin, xin, load_sem.at[4]).wait()
        segment = seg_ref[pl.ds(slot, 1), :].astype(F32)
        key_segment = jnp.broadcast_to(segment, (LANES, length)).T

        for rows in strips(0, length, STRIP):
            scaled, _ = normalize(xin[rows, :].astype(F32))
            h1[rows, :] = (scaled * vector(GAIN1) + vector(SHIFT1)).astype(BF16)

        alive = length - pads[slot]
        for place in range(blocks):
            lanes = slice(place * LANES, (place + 1) * LANES)
            for rows in strips(0, length, 64):
                key = lax.broadcasted_iota(jnp.int32, (64, LANES), 0) + rows.start
                query = lax.broadcasted_iota(jnp.int32, (64, LANES), 1) + place * LANES
                allowed = ((key_segment[rows] == segment[:, lanes]) & (key < alive)) | (key == query)
                mask[rows, lanes] = jnp.where(allowed, 0.0, -1000000000.0)

        store(0, h1, h1_o).start()
        store(11, xin, xin_o).start()
        load(0).wait()
        for part in range(3):
            columns = pl.ds(part * width, width)
            result = nn(h1[...], wqkv[:, columns])
            for rows in strips(0, length, STRIP):
                piece = result[rows]
                if part == 0:
                    piece = (piece + vector(QBIAS)) * factor
                if part == 2:
                    piece = piece + vector(VBIAS)
                qkv[rows, columns] = piece.astype(BF16)
        store(1, qkv, qkv_o).start()
        if tick > 0:
            bias_load().wait()

        def prob_store(pair):
            return pltpu.make_async_copy(
                probs.at[pair % 2], prob_o.at[slot, pl.ds(2 * pair, 2)], prob_sem.at[pair % 2]
            )

        @pl.loop(0, width // LANES)
        def _(pair):
            @pl.when(pair >= 2)
            def _():
                prob_store(pair - 2).wait()

            side = pair % 2
            columns = chunk(pair, LANES)
            queries = qkv[:, columns]
            keys = qkv[:, pl.ds(pl.multiple_of(width + pair * LANES, LANES), LANES)]
            values = qkv[:, pl.ds(pl.multiple_of(2 * width + pair * LANES, LANES), LANES)].T
            outs = []
            for which in range(2):
                own_keys = jnp.where(half_mask(keys.shape, which), keys, jnp.zeros_like(keys))
                lines = []
                for wide in range(blocks // 2):
                    scores = nt(own_keys, queries[2 * LANES * wide : 2 * LANES * (wide + 1)])
                    for part in range(2):
                        place = 2 * wide + part
                        low, high = key_rows(place, blocks)
                        lanes = slice(place * LANES, (place + 1) * LANES)
                        first = (blocks - 1 - place) * LANES
                        spare = which * blocks + place
                        highest = None
                        for rows in strips(low, high, 64):
                            here = (
                                scores[rows, part * LANES : (part + 1) * LANES]
                                + bias[2 * pair + which, first + rows.start : first + rows.stop, :]
                                + mask[rows, lanes]
                            )
                            held[spare, rows, :] = here
                            top = jnp.max(here.reshape(8, 8, LANES), 0)
                            highest = top if highest is None else jnp.maximum(highest, top)
                        highest = jnp.max(highest, 0, keepdims=True)
                        sums = jnp.zeros((8, LANES), F32)
                        for rows in strips(low, high, 64):
                            expo = jnp.exp(held[spare, rows, :] - highest)
                            probs[side, which, rows, lanes] = expo.astype(BF16)
                            sums = sums + fold(expo)
                        lines.append(1.0 / jnp.sum(sums, 0, keepdims=True))
                        if low > 0:
                            probs[side, which, :low, lanes] = jnp.zeros((low, LANES), BF16)
                        if high < length:
                            probs[side, which, high:, lanes] = jnp.zeros((length - high, LANES), BF16)
                scale = jnp.concatenate(lines, 1)
                scales[pl.ds(2 * pair + which, 1), :] = scale
                outs.append(nn(values[which * HALF : (which + 1) * HALF], probs[side, which]) * scale)
            out = jnp.concatenate(outs, 0).T
            wide_mixed[:, columns] = out
            mixed[:, columns] = out.astype(BF16)
            prob_store(pair).start()

        store(3, mixed, mixed_o).start()
        store(12, wide_mixed, wide_o).start()
        store(13, scales, scales_o).start()
        load(1).wait()

        result = nn(mixed[...], wp[...])
        for rows in strips(0, length, STRIP):
            out = result[rows] + vector(PBIAS)
            proj[rows, :] = out.astype(BF16)
            resid = xin[rows, :].astype(F32) + vector(SCALE_A) * out
            x1[rows, :] = resid
            scaled, _ = normalize(resid)
            h2[rows, :] = (scaled * vector(GAIN2) + vector(SHIFT2)).astype(BF16)

        store(4, proj, proj_o).start()
        store(5, x1, x1_o).start()
        store(6, h2, h2_o).start()
        load(2).wait()
        load(3).wait()
        pieces = [
            (pl.ds(high * (length // 2), length // 2), pl.ds(part * width, width))
            for part in range(hidden // width)
            for high in range(2)
        ]

        def expand(number):
            rows, columns = pieces[number]
            return nn(h2[rows, :], w1[:, columns])

        coming = expand(0)
        totals = [None, None]
        for number, (rows, columns) in enumerate(pieces):
            current = coming
            if number + 1 < len(pieces):
                coming = expand(number + 1)
            for strip in strips(0, length // 2, STRIP):
                there = pl.ds(rows.start + strip.start, STRIP)
                here = current[strip] + vectors[B1][:, columns]
                expo = jnp.exp(-0.5 * here * here)
                tail = normal_tail(jnp.abs(here), expo)
                normal = jnp.where(here < 0.0, tail, 1.0 - tail)
                act[there, columns] = (here * normal).astype(BF16)
                slope[there, columns] = (normal + here * (expo * (1.0 / math.sqrt(2.0 * math.pi)))).astype(BF16)
            more = nn(act[rows, columns], w2[columns, :])
            totals[number % 2] = more if number < 2 else totals[number % 2] + more
        store(7, act, act_o).start()
        store(8, slope, slope_o).start()

        for half in range(2):
            for strip in strips(0, length // 2, STRIP):
                rows = pl.ds(half * (length // 2) + strip.start, STRIP)
                out = totals[half][strip] + vector(B2)
                mlp[rows, :] = out.astype(BF16)
                y_ref[rows, :] = (x1[rows, :] + vector(SCALE_M) * out).astype(BF16)

        store(9, mlp, mlp_o).start()
        store(10, y_ref, y_o).start()
        for pair in (width // LANES - 2, width // LANES - 1):
            prob_store(pair).wait()
        ends = {0: (h1, h1_o), 1: (qkv, qkv_o), 3: (mixed, mixed_o), 4: (proj, proj_o), 5: (x1, x1_o), 6: (h2, h2_o),
                7: (act, act_o), 8: (slope, slope_o), 9: (mlp, mlp_o), 10: (y_ref, y_o), 11: (xin, xin_o), 12: (wide_mixed, wide_o), 13: (scales, scales_o)}
        for number, (source, there) in ends.items():
            store(number, source, there).wait()

    if tick == 0:
        bias_store().wait()


def hbm_specs(count):
    return [pl.BlockSpec(memory_space=pl.ANY)] * count


def vmem_specs(count):
    return [pl.BlockSpec(memory_space=pltpu.VMEM)] * count


def forward(tick, pads, patches, received, segments, ext, vectors, weights, kept):
    micro, length, width = patches.shape
    wqkv, wp, w1, w2 = weights
    hidden = w1.shape[1]
    heads = ext.shape[0]
    stored = [
        ((length, width), BF16),
        ((length, 3 * width), BF16),
        ((heads, length, length), BF16),
        ((length, width), BF16),
        ((length, width), BF16),
        ((length, width), F32),
        ((length, width), BF16),
        ((length, hidden), BF16),
        ((length, hidden), BF16),
        ((length, width), BF16),
        ((length, width), BF16),
        ((length, width), BF16),
        ((length, width), F32),
        ((heads, length), F32),
    ]
    bias = jax.ShapeDtypeStruct((heads, 2 * length - LANES, LANES), F32)
    scratch = [pltpu.VMEM(x.shape, x.dtype) for x in (bias, wqkv, wp, w1, w2)]
    scratch.append(pltpu.VMEM((length, length), F32))
    scratch += [pltpu.VMEM((2, 2, length, length) if n == 2 else shape, kind) for n, (shape, kind) in enumerate(stored[:10])]
    scratch += [pltpu.VMEM((length, width), F32), pltpu.VMEM((heads, length), F32), pltpu.VMEM((length, width), BF16)]
    scratch += [pltpu.VMEM((2 * length // LANES, length, LANES), F32)]
    scratch += [
        pltpu.SemaphoreType.DMA((5,)),
        pltpu.SemaphoreType.DMA((STORED,)),
        pltpu.SemaphoreType.DMA((2,)),
        pltpu.SemaphoreType.DMA((1,)),
    ]
    operands = [pads, patches, received, segments, ext, *vectors, *weights]
    first = len(operands)
    held = STORED + 1 if tick > 0 else 0
    out = pl.pallas_call(
        functools.partial(forward_kernel, tick),
        out_shape=[jax.ShapeDtypeStruct((length, width), BF16), bias]
        + [jax.ShapeDtypeStruct((micro, *shape), kind) for shape, kind in stored],
        in_specs=[pl.BlockSpec(memory_space=pltpu.SMEM)] + hbm_specs(1) + (vmem_specs(1) if tick > 0 else hbm_specs(1)) + vmem_specs(2 + VECTORS) + hbm_specs(4 + held),
        out_specs=vmem_specs(1) + hbm_specs(STORED + 1),
        scratch_shapes=scratch,
        input_output_aliases={first + n: 1 + n for n in range(held)},
        compiler_params=pltpu.CompilerParams(vmem_limit_bytes=VMEM_BYTES),
        name="forward_layer",
    )(*operands, *(kept if tick > 0 else ()))
    return out[0], out[1:]


def backward_kernel(tick, cotangent_hbm, returned_hbm, *refs):
    vectors, refs = refs[:VECTORS], refs[VECTORS:]
    (wqkv_hbm, wp_hbm, w1_hbm, w2_hbm, qkv_i, prob_i, mixed_i, proj_i, x1_i, slope_i, mlp_i, xin_i, scales_i) = refs[:13]
    refs = refs[13 + (7 if tick > 0 else 0) :]
    dx_ref, *stores = refs[:8]
    (wqkv, wp, w1, w2, qkv, probs, mixed, proj, x1, slope, mlp, xin, scales, dm, dz, dproj, packed, dx1, dmixed, dscore, diag, sums, tables, g_ref, load_sem, store_sem, prob_sem) = refs[8:]
    dm_o, dz_o, dproj_o, packed_o, dx_o, tables_o, sums_o = stores
    length, width = g_ref.shape
    hidden = w1.shape[1]
    blocks = length // LANES
    pairs = width // LANES
    section = lax.axis_index("section")
    slot = tick - 1 + section
    active = (slot >= 0) & (slot < cotangent_hbm.shape[0])
    factor = HALF ** (-0.5)
    loads = [
        (mlp_i.at[slot], mlp), (w2_hbm, w2), (slope_i.at[slot], slope), (w1_hbm, w1), (x1_i.at[slot], x1),
        (proj_i.at[slot], proj), (wp_hbm, wp), (qkv_i.at[slot], qkv), (mixed_i.at[slot], mixed), (wqkv_hbm, wqkv),
        (xin_i.at[slot], xin), (scales_i.at[slot], scales),
    ]

    def load(number):
        return pltpu.make_async_copy(*loads[number], load_sem.at[number])

    def store(number, source, there):
        return pltpu.make_async_copy(source, there.at[slot], store_sem.at[number])

    def prob_load(pair):
        return pltpu.make_async_copy(
            prob_i.at[slot, pl.ds(2 * pair, 2)], probs.at[pair % 2], prob_sem.at[pair % 2]
        )

    def vector(row):
        return vectors[row][...]

    def put(row, partial):
        sums[row : row + 1, :] = jnp.sum(partial, 0, keepdims=True)

    nothing = jnp.zeros((8, width), F32)

    @pl.when(active)
    def _():
        @pl.when(section == 1)
        def _():
            pltpu.make_async_copy(cotangent_hbm.at[slot], g_ref, load_sem.at[12]).start()

        if tick > 0:

            @pl.when(section == 0)
            def _():
                pltpu.make_async_copy(returned_hbm, g_ref, load_sem.at[12]).start()

        for number in range(len(loads)):
            load(number).start()
        prob_load(0).start()
        pltpu.make_async_copy(g_ref, g_ref, load_sem.at[12]).wait()
        load(0).wait()

        scale_sum = bias_sum = nothing
        for rows in strips(0, length, STRIP):
            upstream = g_ref[rows, :].astype(F32)
            low = (upstream * vector(SCALE_M)).astype(BF16)
            dm[rows, :] = low
            scale_sum = scale_sum + fold(upstream * mlp[rows, :].astype(F32))
            bias_sum = bias_sum + fold(low.astype(F32))
        put(SCALE_M, scale_sum)
        put(B2, bias_sum)
        store(0, dm, dm_o).start()
        load(1).wait()
        load(2).wait()
        load(3).wait()
        pieces = [
            (pl.ds(high * (length // 2), length // 2), pl.ds(part * width, width))
            for part in range(hidden // width)
            for high in range(2)
        ]

        def expand(number):
            rows, columns = pieces[number]
            return nt(dm[rows, :], w2[columns, :])

        coming = expand(0)
        totals = [None, None]
        act_sum = nothing
        for number, (rows, columns) in enumerate(pieces):
            current = coming
            if number + 1 < len(pieces):
                coming = expand(number + 1)
            for strip in strips(0, length // 2, STRIP):
                there = pl.ds(rows.start + strip.start, STRIP)
                low = (current[strip] * slope[there, columns].astype(F32)).astype(BF16)
                dz[there, columns] = low
                act_sum = act_sum + fold(low.astype(F32))
            if number % 2 == 1:
                put(B1 + number // 2, act_sum)
                act_sum = nothing
            more = nt(dz[rows, columns], w1[:, columns])
            totals[number % 2] = more if number < 2 else totals[number % 2] + more
        store(1, dz, dz_o).start()
        load(4).wait()
        load(5).wait()

        found = [nothing] * 4
        for half in range(2):
            for strip in strips(0, length // 2, STRIP):
                rows = pl.ds(half * (length // 2) + strip.start, STRIP)
                upper = totals[half][strip]
                scaled, inverse = normalize(x1[rows, :])
                resid = g_ref[rows, :].astype(F32) + norm_back(upper * vector(GAIN2), scaled, inverse)
                dx1[rows, :] = resid
                low = (resid * vector(SCALE_A)).astype(BF16)
                dproj[rows, :] = low
                terms = (upper * scaled, upper, resid * proj[rows, :].astype(F32), low.astype(F32))
                found = [old + fold(term) for old, term in zip(found, terms)]
        for row, partial in zip((GAIN2, SHIFT2, SCALE_A, PBIAS), found):
            put(row, partial)
        store(2, dproj, dproj_o).start()
        load(6).wait()
        dmixed[...] = nt(dproj[...], wp[...]).astype(BF16)
        load(7).wait()
        load(8).wait()
        load(11).wait()

        @pl.loop(0, pairs)
        def _(pair):
            prob_load(pair).wait()

            @pl.when(pair + 1 < pairs)
            def _():
                prob_load(pair + 1).start()

            side = pair % 2
            columns = chunk(pair, LANES)
            key_columns = pl.ds(pl.multiple_of(width + pair * LANES, LANES), LANES)
            value_columns = pl.ds(pl.multiple_of(2 * width + pair * LANES, LANES), LANES)
            values = qkv[:, value_columns]
            above = dmixed[:, columns]
            queries_t = qkv[:, columns].T
            keys_t = qkv[:, key_columns].T
            above_t = above.astype(F32).T
            products = (above.astype(F32) * mixed[:, columns]).T
            grads = [], [], []
            for which in range(2):
                half = slice(which * HALF, (which + 1) * HALF)
                delta = jnp.sum(products[half], 0, keepdims=True)
                scale = scales[pl.ds(2 * pair + which, 1), :]
                own_values = jnp.where(half_mask(values.shape, which), values, jnp.zeros_like(values))
                edge = (blocks - 1) * LANES
                diag[which, :edge, :] = jnp.zeros((edge, LANES), F32)
                for wide in range(blocks // 2):
                    prob_grad = nt(own_values, above[2 * LANES * wide : 2 * LANES * (wide + 1)])
                    for part in range(2):
                        place = 2 * wide + part
                        low, high = key_rows(place, blocks)
                        lanes = slice(place * LANES, (place + 1) * LANES)
                        first_row = (blocks - 1 - place) * LANES
                        for rows in strips(low, high, 64):
                            here = (probs[side, which, rows, lanes].astype(F32) * scale[:, lanes]) * (
                                prob_grad[rows, part * LANES : (part + 1) * LANES] - delta[:, lanes]
                            )
                            dscore[which, rows, lanes] = here.astype(BF16)
                            there = slice(first_row + rows.start, first_row + rows.stop)
                            diag[which, there, :] = here if place == 0 else diag[which, there, :] + here
                        if low > 0:
                            dscore[which, :low, lanes] = jnp.zeros((low, LANES), BF16)
                        if high < length:
                            dscore[which, high:, lanes] = jnp.zeros((length - high, LANES), BF16)
                        if place == 0:
                            diag[which, edge + high :, :] = jnp.zeros((length - high, LANES), F32)
                line = gather_diagonals(diag.at[which])
                most = tables.shape[1] - LANES
                tables[pl.ds(2 * pair + which, 1), :] = jnp.concatenate(
                    [line[:, REACH + 1 : REACH + 1 + most], line[:, REACH : REACH + LANES]], 1
                )
                grads[0].append(nn(keys_t[half], dscore[which]))
                grads[1].append(nt(queries_t[half], dscore[which]))
                grads[2].append(nt((above_t[half] * scale).astype(BF16), probs[side, which]))
            for found, where, scale in zip(grads, (columns, key_columns, value_columns), (factor, None, None)):
                low = jnp.concatenate(found, 0).astype(BF16)
                if scale is not None:
                    low = (low.astype(F32) * scale).astype(BF16)
                packed[:, where] = low.T

        store(3, packed, packed_o).start()
        load(9).wait()
        result = nt(packed[...], wqkv[...])
        load(10).wait()
        found = [nothing] * 4
        for rows in strips(0, length, STRIP):
            upper = result[rows]
            scaled, inverse = normalize(xin[rows, :].astype(F32))
            dx_ref[rows, :] = (dx1[rows, :] + norm_back(upper * vector(GAIN1), scaled, inverse)).astype(BF16)
            terms = (
                upper * scaled,
                upper,
                packed[rows, :width].astype(F32),
                packed[rows, 2 * width :].astype(F32),
            )
            found = [old + fold(term) for old, term in zip(found, terms)]
        for row, partial in zip((GAIN1, SHIFT1, QBIAS, VBIAS), found):
            put(row, partial)
        store(4, dx_ref, dx_o).start()
        store(5, tables, tables_o).start()
        store(6, sums, sums_o).start()
        ends = {0: (dm, dm_o), 1: (dz, dz_o), 2: (dproj, dproj_o), 3: (packed, packed_o), 4: (dx_ref, dx_o), 5: (tables, tables_o), 6: (sums, sums_o)}
        for number, (source, there) in ends.items():
            store(number, source, there).wait()


def backward(tick, cotangent, returned, vectors, weights, saved, kept):
    micro, length, width = cotangent.shape
    wqkv, wp, w1, w2 = weights
    hidden = w1.shape[1]
    bias, h1, qkv, probs, mixed, proj, x1, h2, act, slope, mlp, y, xin, wide, scales = saved
    heads = probs.shape[1]
    span = 2 * length - LANES
    summed = (16, width)
    table = (heads, 5 * LANES)
    stored = [
        ((length, width), BF16),
        ((length, hidden), BF16),
        ((length, width), BF16),
        ((length, 3 * width), BF16),
        ((length, width), BF16),
        (table, F32),
        (summed, F32),
    ]
    reads = [qkv, probs, wide, proj, x1, slope, mlp, xin, scales]
    scratch = [pltpu.VMEM(x.shape, x.dtype) for x in weights]
    scratch += [pltpu.VMEM((2, 2, length, length) if x is probs else x.shape[1:], x.dtype) for x in reads]
    scratch += [pltpu.VMEM(shape, kind) for shape, kind in stored[:4]]
    scratch += [
        pltpu.VMEM((length, width), F32),
        pltpu.VMEM((length, width), BF16),
        pltpu.VMEM((2, length, length), BF16),
        pltpu.VMEM((2, span, LANES), F32),
        pltpu.VMEM(summed, F32),
        pltpu.VMEM(table, F32),
        pltpu.VMEM((length, width), BF16),
        pltpu.SemaphoreType.DMA((13,)),
        pltpu.SemaphoreType.DMA((7,)),
        pltpu.SemaphoreType.DMA((2,)),
    ]
    operands = [cotangent, returned, *vectors, *weights, *reads]
    first = len(operands)
    held = 7 if tick > 0 else 0
    out = pl.pallas_call(
        functools.partial(backward_kernel, tick),
        out_shape=[jax.ShapeDtypeStruct((length, width), BF16)]
        + [jax.ShapeDtypeStruct((micro, *shape), kind) for shape, kind in stored],
        in_specs=hbm_specs(1) + (vmem_specs(1) if tick > 0 else hbm_specs(1)) + vmem_specs(VECTORS) + hbm_specs(13 + held),
        out_specs=vmem_specs(1) + hbm_specs(7),
        scratch_shapes=scratch,
        input_output_aliases={first + n: 1 + n for n in range(held)},
        compiler_params=pltpu.CompilerParams(vmem_limit_bytes=VMEM_BYTES),
        name="backward_layer",
    )(*operands, *(kept if tick > 0 else ()))
    return out[0], out[1:]


def small_lines(width):
    lines = width // LANES
    places = [(row, tile, row * lines + tile) for row in range(10) for tile in range(lines)]
    return places + [(B1, tile, B1 * lines + tile) for tile in range(4 * lines)]


def reverse_lanes(values):
    lane = lax.broadcasted_iota(jnp.int32, values.shape, 1)
    for place in range(LANES.bit_length() - 1):
        step = 1 << place
        up, down = pltpu.roll(values, step, 1), pltpu.roll(values, LANES - step, 1)
        values = jnp.where((lane // step) % 2 == 1, up, down)
    return values


def widen_kernel(sum_hbm, small_ref, *refs):
    bigs, vectors, table_ref = refs[:4], refs[4 : 4 + VECTORS], refs[4 + VECTORS]
    narrow, wide, load_sem, store_sem = refs[5 + VECTORS :]
    depth, width = narrow.shape[:2]
    blocks = [(0, slice(b * width, (b + 1) * width), slice(0, width)) for b in range(4)]
    for target, count in ((1, 4), (2, 3), (3, 1)):
        blocks += [(target, slice(0, width), slice(b * width, (b + 1) * width)) for b in range(count)]

    def load(block):
        rows = pl.ds(block * width, width)
        return pltpu.make_async_copy(sum_hbm.at[rows, :], narrow.at[block % depth], load_sem.at[block % depth])

    def store(block):
        target, rows, columns = blocks[block]
        there = bigs[target].at[rows, columns]
        return pltpu.make_async_copy(wide.at[block % depth], there, store_sem.at[block % depth])

    for block in range(depth):
        load(block).start()
    for block in range(len(blocks)):
        load(block).wait()
        if block >= depth:
            store(block - depth).wait()
        for rows in strips(0, width, 64):
            wide[block % depth, rows, :] = narrow[block % depth, rows, :].astype(F32)
        store(block).start()
        if block + depth < len(blocks):
            load(block + depth).start()
    places = small_lines(width)
    for row, tile, line in places:
        vectors[row][:, tile * LANES : (tile + 1) * LANES] = small_ref[line : line + 1, :]
    first = len(places)
    heads, entries = table_ref.shape
    tiles = -(-entries // LANES)
    flipped = reverse_lanes(small_ref[first : first + heads * tiles, :])
    for head in range(heads):
        for tile in range(tiles - 1):
            line = head * tiles + tile
            there = (tiles - 2 - tile) * LANES
            table_ref[head : head + 1, there : there + LANES] = flipped[line : line + 1]
        line = first + head * tiles + tiles - 1
        table_ref[head : head + 1, entries - 1 :] = small_ref[line : line + 1, 0:1]
    for block in range(len(blocks) - depth, len(blocks)):
        store(block).wait()


def widen(summed, small, width, heads, entries):
    shapes = [(4 * width, width), (width, 4 * width), (width, 3 * width), (width, width)]
    shapes += [(1, width)] * 10 + [(1, 4 * width), (heads, entries)]
    return pl.pallas_call(
        widen_kernel,
        out_shape=[jax.ShapeDtypeStruct(shape, F32) for shape in shapes],
        in_specs=hbm_specs(1) + vmem_specs(1),
        out_specs=hbm_specs(4) + vmem_specs(VECTORS + 1),
        scratch_shapes=[
            pltpu.VMEM((3, width, width), BF16),
            pltpu.VMEM((3, width, width), F32),
            pltpu.SemaphoreType.DMA((3,)),
            pltpu.SemaphoreType.DMA((3,)),
        ],
        compiler_params=pltpu.CompilerParams(vmem_limit_bytes=VMEM_BYTES),
        name="widen",
    )(summed, small)


BLOCK = 256
LAG = 3


def reduce_kernel(
    bits, chunks, blocks, lag, *refs
):
    (a_ref, dm_ref, h2_ref, dz_ref, h1_ref, dp_ref, o_ref, dproj_ref, sums_ref, tables_ref, out_ref, small_out_ref) = refs[:12]
    (lhs, rhs, grads, total, small_ref, small_total, *received) = refs[12 : 18 + 2 * bits]
    (load_sem, send_sem, recv_sem, small_send, small_recv, store_sem) = refs[18 + 2 * bits :]
    small_received = received[bits:]
    me = lax.axis_index("dp")
    rows = BLOCK * blocks
    width = grads.shape[1]
    per_side = width // BLOCK
    last = 2 * bits

    barrier = pltpu.get_barrier_semaphore()
    for place in range(bits):
        stride = 1 << place
        other = me + stride * (1 - 2 * ((me // stride) % 2))
        pl.semaphore_signal(barrier, inc=1, device_id={"dp": other}, device_id_type=MESH)
    pl.semaphore_wait(barrier, bits)

    families = (
        (a_ref, dm_ref, 4 * per_side, True),
        (h2_ref, dz_ref, 4 * per_side, False),
        (h1_ref, dp_ref, 3 * per_side, False),
        (o_ref, dproj_ref, per_side, False),
    )
    n_blocks = 12 * per_side

    def load(block):
        slot = block % 2
        first = 0
        for left, right, count, walks in families:
            @pl.when((block >= first) & (block < first + count))
            def _():
                local = block - first
                if walks:
                    left_column = local * BLOCK
                    right_column = 0
                else:
                    left_column = (local % per_side) * BLOCK
                    right_column = (local // per_side) * width
                pltpu.make_async_copy(
                    left.at[:, pl.ds(pl.multiple_of(left_column, BLOCK), BLOCK)],
                    lhs.at[slot],
                    load_sem.at[0, slot],
                ).start()
                pltpu.make_async_copy(
                    right.at[:, pl.ds(pl.multiple_of(right_column, BLOCK), width)],
                    rhs.at[slot],
                    load_sem.at[1, slot],
                ).start()
            first += count

    def produce(block):
        slot = block % 2
        pltpu.make_async_copy(lhs.at[slot], lhs.at[slot], load_sem.at[0, slot]).wait()
        pltpu.make_async_copy(rhs.at[slot], rhs.at[slot], load_sem.at[1, slot]).wait()

        @pl.when(block + 1 < n_blocks)
        def _():
            load(block + 1)

        grads[pl.ds(pl.multiple_of(block * BLOCK, BLOCK), BLOCK), :] = lax.dot_general(
            lhs[slot], rhs[slot], (((0,), (0,)), ((), ())), preferred_element_type=jnp.float32
        ).astype(jnp.bfloat16)

    def turn(chunk):
        place = chunk % 9
        return place % 2 + place // 5 - place // 6

    def partner(rotation, stage):
        stride = lax.shift_left(jnp.int32(1), (stage + rotation) % bits)
        mine = (me // stride) % 2
        return mine, me + stride * (1 - 2 * mine)

    def offset(base, height, rotation, stage):
        for earlier in range(stage):
            mine, _ = partner(rotation, earlier)
            base = base + mine * (height >> (earlier + 1))
        return base

    def piece(ref, start, size):
        return ref.at[pl.ds(pl.multiple_of(start, size), size)]

    def send(position, base, height, rotation, source, landing, result, slot, sems):
        send_at, recv_at = sems
        if position < bits:
            stage = position
            half = height >> (stage + 1)
            mine, other = partner(rotation, stage)
            start = offset(base, height, rotation, stage) + (1 - mine) * half
            src, dst = piece(source, start, half), landing[stage].at[slot]
        else:
            stage = last - 1 - position
            half = height >> (stage + 1)
            mine, other = partner(rotation, stage)
            start = offset(base, height, rotation, stage + 1)
            src = dst = piece(result, start, half)
        return pltpu.make_async_remote_copy(
            src_ref=src,
            dst_ref=dst,
            send_sem=send_at.at[position],
            recv_sem=recv_at.at[position, slot],
            device_id={"dp": other},
            device_id_type=MESH,
        )

    def take(position, base, height, rotation, source, landing, result, slot, sems):
        send(position - 1, base, height, rotation, source, landing, result, slot, sems).wait_recv()
        stage = position - 1
        if stage < bits:
            half = height >> (stage + 1)
            start = pl.multiple_of(offset(base, height, rotation, stage + 1), half)
            keep = pl.ds(start, half)
            value = source[keep, :].astype(jnp.float32) + landing[stage][slot].astype(jnp.float32)
            target = result if stage == bits - 1 else source
            target[keep, :] = value.astype(target.dtype)

    def step(position, *way):
        if position > 0:
            take(position, *way)
        if position < last:
            send(position, *way).start()

    main = (grads, received[:bits], total)
    main_sems = (send_sem, recv_sem)

    def walk(position, chunk):
        if position == 0:
            for sub in range(blocks):
                block = chunk * blocks + sub

                @pl.when(block < n_blocks)
                def _():
                    produce(block)

        base = chunk * rows
        step(position, base, rows, turn(chunk), *main, chunk, main_sems)
        if position == last:
            there = pl.ds(pl.multiple_of(base, rows), rows)
            pltpu.make_async_copy(total.at[there], out_ref.at[there], store_sem.at[0]).start()

    def walk_small(position):
        height = small_ref.shape[0]
        way = (0, height, 0, small_ref, small_received, small_total, 0, (small_send, small_recv))
        step(position, *way)

    load(jnp.int32(0))
    small_ref[...] = jnp.zeros_like(small_ref)
    places = small_lines(width)
    for row, tile, line in places:
        if row == B1:
            row, tile = B1 + tile // (width // LANES), tile % (width // LANES)
        lanes = slice(tile * LANES, (tile + 1) * LANES)
        small_ref[line : line + 1, :] = sums_ref[0, row : row + 1, lanes] + sums_ref[1, row : row + 1, lanes]
    line = len(places)
    for head in range(tables_ref.shape[1]):
        for tile in range(tables_ref.shape[2] // LANES):
            lanes = slice(tile * LANES, (tile + 1) * LANES)
            small_ref[line : line + 1, :] = tables_ref[0, head : head + 1, lanes] + tables_ref[1, head : head + 1, lanes]
            line += 1

    @pl.loop(0, chunks + lag * last)
    def _(tick):
        for position in range(last + 1):
            chunk = tick - lag * position

            @pl.when((chunk >= 0) & (chunk < chunks))
            def _():
                walk(position, chunk)

            @pl.when(tick == lag * position)
            def _():
                walk_small(position)

    small_out_ref[...] = small_total[...]
    for position in range(last):
        stage = position if position < bits else last - 1 - position
        size = received[stage]
        pltpu.make_async_copy(size, size, send_sem.at[position]).wait()
        size = small_received[stage]
        pltpu.make_async_copy(size, size, small_send.at[position]).wait()
    pltpu.make_async_copy(total, out_ref, store_sem.at[0]).wait()


def reduce_gradients(a, dm, h2, dz, h1, packed, o, dproj, sums, tables):
    parts = lax.axis_size("dp")
    bits = parts.bit_length() - 1
    blocks = max(1, 16 * parts // BLOCK)
    tokens, width = h1.shape
    n_blocks = 12 * width // BLOCK
    chunks = -(-n_blocks // blocks)
    rows = BLOCK * blocks
    lines = len(small_lines(width)) + tables.shape[1] * tables.shape[2] // LANES
    height = -(-lines // (8 * parts)) * 8 * parts
    small = jax.ShapeDtypeStruct((height, LANES), jnp.float32)
    bf16 = jnp.bfloat16
    return pl.pallas_call(
        functools.partial(reduce_kernel, bits, chunks, blocks, LAG),
        out_shape=(
            jax.ShapeDtypeStruct((chunks * rows, width), bf16),
            jax.ShapeDtypeStruct(small.shape, jnp.float32),
        ),
        in_specs=[pl.BlockSpec(memory_space=pl.ANY)] * 8 + [pl.BlockSpec(memory_space=pltpu.VMEM)] * 2,
        out_specs=(pl.BlockSpec(memory_space=pl.ANY), pl.BlockSpec(memory_space=pltpu.VMEM)),
        scratch_shapes=[
            pltpu.VMEM((2, tokens, BLOCK), bf16),
            pltpu.VMEM((2, tokens, width), bf16),
            pltpu.VMEM((chunks * rows, width), bf16),
            pltpu.VMEM((chunks * rows, width), bf16),
            pltpu.VMEM(small.shape, jnp.float32),
            pltpu.VMEM(small.shape, jnp.float32),
            *[pltpu.VMEM((chunks, rows >> (s + 1), width), bf16) for s in range(bits)],
            *[pltpu.VMEM((1, height >> (s + 1), 128), jnp.float32) for s in range(bits)],
            pltpu.SemaphoreType.DMA((2, 2)),
            pltpu.SemaphoreType.DMA((2 * bits,)),
            pltpu.SemaphoreType.DMA((2 * bits, chunks)),
            pltpu.SemaphoreType.DMA((2 * bits,)),
            pltpu.SemaphoreType.DMA((2 * bits, 1)),
            pltpu.SemaphoreType.DMA((1,)),
        ],
        compiler_params=pltpu.CompilerParams(
            collective_id=0, has_side_effects=True, vmem_limit_bytes=60 * 1024 * 1024
        ),
        name="reduce_gradients",
    )(a, dm, h2, dz, h1, packed, o, dproj, sums, tables)


def shifted(block, axis, distance):
    devices = range(lax.axis_size(axis))
    route = [(i - distance, i) for i in devices if i - distance in devices]
    return lax.ppermute(block, axis, route)


def per_device(
    patches,
    segment_ids,
    pad_counts,
    norm1_gain,
    norm1_bias,
    qkv_weight,
    query_bias,
    value_bias,
    rel_table,
    proj_weight,
    proj_bias,
    scale_attn,
    norm2_gain,
    norm2_bias,
    fc1_weight,
    fc1_bias,
    fc2_weight,
    fc2_bias,
    scale_mlp,
    cotangent,
):
    micro, length, width = patches.shape
    vectors = (
        norm1_gain,
        norm1_bias,
        query_bias,
        value_bias,
        proj_bias,
        scale_attn,
        norm2_gain,
        norm2_bias,
        fc2_bias,
        scale_mlp,
        fc1_bias,
    )
    weights = (qkv_weight[0], proj_weight[0], fc1_weight[0], fc2_weight[0])
    entries = rel_table.shape[2]
    before = REACH
    after = 2 * length - before - entries
    ext = jnp.pad(rel_table[0, :, ::-1], ((0, 0), (before, after)))
    received = patches
    saved = None
    for tick in range(micro + 1):
        result, saved = forward(
            tick, pad_counts, patches, received, segment_ids, ext, vectors, weights, saved
        )
        if tick < micro:
            received = shifted(result, "section", 1)
    returned = cotangent
    kept = None
    for tick in range(micro + 1):
        input_grad, kept = backward(tick, cotangent, returned, vectors, weights, saved, kept)
        if tick < micro:
            returned = shifted(input_grad, "section", -1)
    dm, dz, dproj, packed, in_grads, tables, sums = kept
    h1, mixed, h2, act, outputs = saved[1], saved[4], saved[7], saved[8], saved[11]
    left = [x.reshape(micro * length, -1) for x in (act, dm, h2, dz, h1, packed, mixed, dproj)]
    summed, small = reduce_gradients(*left, sums, tables)
    fc2_grad, fc1_grad, qkv_grad, proj_grad, *small_grads = widen(
        summed, small, width, tables.shape[1], entries
    )
    table_grad = small_grads[VECTORS]
    return (
        outputs[None],
        in_grads[None],
        small_grads[GAIN1],
        small_grads[SHIFT1],
        qkv_grad[None],
        small_grads[QBIAS],
        small_grads[VBIAS],
        table_grad[None],
        proj_grad[None],
        small_grads[PBIAS],
        small_grads[SCALE_A],
        small_grads[GAIN2],
        small_grads[SHIFT2],
        fc1_grad[None],
        small_grads[B1],
        fc2_grad[None],
        small_grads[B2],
        small_grads[SCALE_M],
    )


def solution(mesh):
    placed = (
        P("dp", None, None),
        P("dp", None),
        P("dp"),
        P("section", None),
        P("section", None),
        P("section", None, None),
        P("section", None),
        P("section", None),
        P("section", None, None),
        P("section", None, None),
        P("section", None),
        P("section", None),
        P("section", None),
        P("section", None),
        P("section", None, None),
        P("section", None),
        P("section", None, None),
        P("section", None),
        P("section", None),
        P("dp", None, None),
    )
    return jax.shard_map(
        per_device,
        mesh=mesh,
        in_specs=placed,
        out_specs=(
            P("section", "dp", None, None),
            P("section", "dp", None, None),
            P("section", None),
            P("section", None),
            P("section", None, None),
            P("section", None),
            P("section", None),
            P("section", None, None),
            P("section", None, None),
            P("section", None),
            P("section", None),
            P("section", None),
            P("section", None),
            P("section", None, None),
            P("section", None),
            P("section", None, None),
            P("section", None),
            P("section", None),
        ),
        check_vma=False,
    )
```

```python
import functools
import math

import jax
import jax.numpy as jnp
from jax import lax
from jax.experimental import pallas as pl
from jax.experimental.pallas import tpu as pltpu
from jax.sharding import PartitionSpec as P

MESH = pl.DeviceIdType.MESH
BF16, F32 = jnp.bfloat16, jnp.float32
VMEM_BYTES = 60 * 1024 * 1024
LANES = 128
TAIL = (
    0.11652249842882156,
    0.06748615205287933,
    0.2689361274242401,
    -0.23702505230903625,
    0.3898930847644806,
    -0.10581281781196594,
)
HALF = 64
REACH = 2 * LANES
GAIN1, SHIFT1, QBIAS, VBIAS, PBIAS, SCALE_A, GAIN2, SHIFT2, B2, SCALE_M, B1 = range(11)
VECTORS = 11
STORED = 14
STRIP = 16


def dot(left, right, left_dim, right_dim):
    return lax.dot_general(
        left, right, (((left_dim,), (right_dim,)), ((), ())), preferred_element_type=F32
    )


def nn(left, right):
    return dot(left, right, 1, 0)


def nt(left, right):
    return dot(left, right, 1, 1)


def normalize(values):
    centered = values - jnp.mean(values, -1, keepdims=True)
    inverse = lax.rsqrt(jnp.mean(centered * centered, -1, keepdims=True) + 1e-06)
    return centered * inverse, inverse


def norm_back(upper, scaled, inverse):
    return inverse * (
        upper
        - jnp.mean(upper, -1, keepdims=True)
        - scaled * jnp.mean(upper * scaled, -1, keepdims=True)
    )


def fold(values):
    return jnp.sum(values.reshape(values.shape[0] // 8, 8, values.shape[1]), 0)


def half_mask(shape, which):
    return lax.broadcasted_iota(jnp.int32, shape, 1) // HALF == which


def strips(first, last, size):
    return [slice(start, start + size) for start in range(first, last, size)]


def chunk(index, size):
    return pl.ds(pl.multiple_of(index * size, size), size)


def skew_bias(reversed_row, target):
    span, lanes = target.shape
    rows = pltpu.roll(jnp.broadcast_to(reversed_row, (8, reversed_row.shape[1])), 0, 1, stride=1, stride_axis=0)
    tiles = span // lanes
    for fine in range(lanes // 8):
        moved = rows if fine == 0 else pltpu.roll(rows, 8 * fine, 1)
        for coarse in range(tiles):
            place = 8 * (fine + lanes // 8 * coarse)
            target[place : place + 8, :] = moved[:, lanes * (tiles - coarse) : lanes * (tiles - coarse + 1)]


def gather_diagonals(source):
    span, lanes = source.shape
    tiles = span // lanes
    width = span + lanes
    blank = jnp.zeros((8, lanes), F32)
    found = None
    for fine in range(lanes // 8):
        places = [8 * (fine + lanes // 8 * coarse) for coarse in reversed(range(tiles))]
        line = jnp.concatenate([blank] + [source[place : place + 8, :] for place in places], 1)
        if fine > 0:
            line = pltpu.roll(line, width - 8 * fine, 1)
        found = line if found is None else found + line
    row = lax.broadcasted_iota(jnp.int32, found.shape, 0)
    for place in range(3):
        moved = pltpu.roll(found, width - (1 << place), 1)
        found = jnp.where((row // (1 << place)) % 2 == 1, moved, found)
    return jnp.sum(found, 0, keepdims=True)


def normal_tail(size, expo):
    ratio = 1.0 / (1.0 + 0.28 * size)
    value = TAIL[-1]
    for coefficient in TAIL[-2::-1]:
        value = value * ratio + coefficient
    return value * ratio * expo


def key_rows(query_block, blocks):
    reach = REACH // LANES
    return max(0, query_block - reach) * LANES, min(blocks, query_block + reach + 1) * LANES


def forward_kernel(tick, pads, patches_hbm, received_hbm, seg_ref, ext_ref, *refs):
    vectors, refs = refs[:VECTORS], refs[VECTORS:]
    wqkv_hbm, wp_hbm, w1_hbm, w2_hbm = refs[:4]
    refs = refs[4 + (STORED + 1 if tick > 0 else 0) :]
    y_ref, bias_o, *stores = refs[: STORED + 2]
    (bias, wqkv, wp, w1, w2, mask, h1, qkv, probs, mixed, proj, x1, h2, act, slope, mlp, wide_mixed, scales, xin, held, load_sem, store_sem, prob_sem, bias_sem) = refs[STORED + 2 :]
    h1_o, qkv_o, prob_o, mixed_o, proj_o, x1_o, h2_o, act_o, slope_o, mlp_o, y_o, xin_o, wide_o, scales_o = stores
    length, width = xin.shape
    hidden = w1.shape[1]
    heads = bias.shape[0]
    blocks = length // LANES
    section = lax.axis_index("section")
    slot = tick - section
    active = (slot >= 0) & (slot < seg_ref.shape[0])
    factor = HALF ** (-0.5)
    thirds = [pl.ds(part * width, width) for part in range(3)]
    loads = [(wqkv_hbm.at[:, columns], wqkv.at[:, columns]) for columns in thirds]
    loads += [(wp_hbm, wp), (w1_hbm, w1), (w2_hbm, w2)]

    def load(number):
        return pltpu.make_async_copy(*loads[number], load_sem.at[number])

    def store(number, source, there):
        return pltpu.make_async_copy(source, there.at[slot], store_sem.at[number])

    def vector(row):
        return vectors[row][...]

    def bias_load():
        return pltpu.make_async_copy(bias_o, bias, bias_sem.at[0])

    def bias_store():
        return pltpu.make_async_copy(bias, bias_o, bias_sem.at[0])

    @pl.when(active)
    def _():
        @pl.when(section == 0)
        def _():
            pltpu.make_async_copy(patches_hbm.at[slot], xin, load_sem.at[6]).start()

        if tick > 0:

            @pl.when(section == 1)
            def _():
                pltpu.make_async_copy(received_hbm, xin, load_sem.at[6]).start()

        for number in range(3):
            load(number).start()

    if tick == 0:

        @pl.loop(0, heads)
        def _(head):
            skew_bias(ext_ref[pl.ds(head, 1), :], bias.at[head])

        bias_store().start()

    @pl.when(active)
    def _():
        pltpu.make_async_copy(xin, xin, load_sem.at[6]).wait()
        if tick > 0:
            bias_load().start()
        segment = seg_ref[pl.ds(slot, 1), :].astype(F32)
        key_segment = jnp.broadcast_to(segment, (LANES, length)).T

        for rows in strips(0, length, STRIP):
            scaled, _ = normalize(xin[rows, :].astype(F32))
            h1[rows, :] = (scaled * vector(GAIN1) + vector(SHIFT1)).astype(BF16)

        alive = length - pads[slot]
        for place in range(blocks):
            lanes = slice(place * LANES, (place + 1) * LANES)
            for rows in strips(0, length, 64):
                key = lax.broadcasted_iota(jnp.int32, (64, LANES), 0) + rows.start
                query = lax.broadcasted_iota(jnp.int32, (64, LANES), 1) + place * LANES
                allowed = ((key_segment[rows] == segment[:, lanes]) & (key < alive)) | (key == query)
                mask[rows, lanes] = jnp.where(allowed, 0.0, -1000000000.0)

        store(0, h1, h1_o).start()
        store(11, xin, xin_o).start()
        for part in range(3):
            load(part).wait()
            columns = thirds[part]
            result = nn(h1[...], wqkv[:, columns])
            for rows in strips(0, length, STRIP):
                piece = result[rows]
                if part == 0:
                    piece = (piece + vector(QBIAS)) * factor
                if part == 2:
                    piece = piece + vector(VBIAS)
                qkv[rows, columns] = piece.astype(BF16)
        store(1, qkv, qkv_o).start()
        if tick > 0:
            bias_load().wait()
        for number in (3, 4, 5):
            load(number).start()

        def prob_store(pair):
            return pltpu.make_async_copy(
                probs.at[pair % 2], prob_o.at[slot, pl.ds(2 * pair, 2)], prob_sem.at[pair % 2]
            )

        @pl.loop(0, width // LANES)
        def _(pair):
            @pl.when(pair >= 2)
            def _():
                prob_store(pair - 2).wait()

            side = pair % 2
            columns = chunk(pair, LANES)
            queries = qkv[:, columns]
            keys = qkv[:, pl.ds(pl.multiple_of(width + pair * LANES, LANES), LANES)]
            values = qkv[:, pl.ds(pl.multiple_of(2 * width + pair * LANES, LANES), LANES)].T
            outs = []
            for which in range(2):
                own_keys = jnp.where(half_mask(keys.shape, which), keys, jnp.zeros_like(keys))
                lines = []
                for wide in range(blocks // 2):
                    scores = nt(own_keys, queries[2 * LANES * wide : 2 * LANES * (wide + 1)])
                    for part in range(2):
                        place = 2 * wide + part
                        low, high = key_rows(place, blocks)
                        lanes = slice(place * LANES, (place + 1) * LANES)
                        first = (blocks - 1 - place) * LANES
                        spare = which * blocks + place
                        highest = None
                        for rows in strips(low, high, 64):
                            here = (
                                scores[rows, part * LANES : (part + 1) * LANES]
                                + bias[2 * pair + which, first + rows.start : first + rows.stop, :]
                                + mask[rows, lanes]
                            )
                            held[spare, rows, :] = here
                            top = jnp.max(here.reshape(8, 8, LANES), 0)
                            highest = top if highest is None else jnp.maximum(highest, top)
                        highest = jnp.max(highest, 0, keepdims=True)
                        sums = jnp.zeros((8, LANES), F32)
                        for rows in strips(low, high, 64):
                            expo = jnp.exp(held[spare, rows, :] - highest)
                            probs[side, which, rows, lanes] = expo.astype(BF16)
                            sums = sums + fold(expo)
                        lines.append(1.0 / jnp.sum(sums, 0, keepdims=True))
                        if low > 0:
                            probs[side, which, :low, lanes] = jnp.zeros((low, LANES), BF16)
                        if high < length:
                            probs[side, which, high:, lanes] = jnp.zeros((length - high, LANES), BF16)
                scale = jnp.concatenate(lines, 1)
                scales[pl.ds(2 * pair + which, 1), :] = scale
                outs.append(nn(values[which * HALF : (which + 1) * HALF], probs[side, which]) * scale)
            out = jnp.concatenate(outs, 0).T
            wide_mixed[:, columns] = out
            mixed[:, columns] = out.astype(BF16)
            prob_store(pair).start()

        store(3, mixed, mixed_o).start()
        store(12, wide_mixed, wide_o).start()
        store(13, scales, scales_o).start()
        load(3).wait()

        result = nn(mixed[...], wp[...])
        for rows in strips(0, length, STRIP):
            out = result[rows] + vector(PBIAS)
            proj[rows, :] = out.astype(BF16)
            resid = xin[rows, :].astype(F32) + vector(SCALE_A) * out
            x1[rows, :] = resid
            scaled, _ = normalize(resid)
            h2[rows, :] = (scaled * vector(GAIN2) + vector(SHIFT2)).astype(BF16)

        store(4, proj, proj_o).start()
        store(5, x1, x1_o).start()
        store(6, h2, h2_o).start()
        load(4).wait()
        load(5).wait()
        pieces = [
            (pl.ds(high * (length // 2), length // 2), pl.ds(part * width, width))
            for part in range(hidden // width)
            for high in range(2)
        ]

        def expand(number):
            rows, columns = pieces[number]
            return nn(h2[rows, :], w1[:, columns])

        coming = expand(0)
        totals = [None, None]
        for number, (rows, columns) in enumerate(pieces):
            current = coming
            if number + 1 < len(pieces):
                coming = expand(number + 1)
            for strip in strips(0, length // 2, STRIP):
                there = pl.ds(rows.start + strip.start, STRIP)
                here = current[strip] + vectors[B1][:, columns]
                expo = jnp.exp(-0.5 * here * here)
                tail = normal_tail(jnp.abs(here), expo)
                normal = jnp.where(here < 0.0, tail, 1.0 - tail)
                act[there, columns] = (here * normal).astype(BF16)
                slope[there, columns] = (normal + here * (expo * (1.0 / math.sqrt(2.0 * math.pi)))).astype(BF16)
            more = nn(act[rows, columns], w2[columns, :])
            totals[number % 2] = more if number < 2 else totals[number % 2] + more
        store(7, act, act_o).start()
        store(8, slope, slope_o).start()

        for half in range(2):
            for strip in strips(0, length // 2, STRIP):
                rows = pl.ds(half * (length // 2) + strip.start, STRIP)
                out = totals[half][strip] + vector(B2)
                mlp[rows, :] = out.astype(BF16)
                y_ref[rows, :] = (x1[rows, :] + vector(SCALE_M) * out).astype(BF16)

        store(9, mlp, mlp_o).start()
        store(10, y_ref, y_o).start()
        for pair in (width // LANES - 2, width // LANES - 1):
            prob_store(pair).wait()
        ends = {0: (h1, h1_o), 1: (qkv, qkv_o), 3: (mixed, mixed_o), 4: (proj, proj_o), 5: (x1, x1_o), 6: (h2, h2_o),
                7: (act, act_o), 8: (slope, slope_o), 9: (mlp, mlp_o), 10: (y_ref, y_o), 11: (xin, xin_o), 12: (wide_mixed, wide_o), 13: (scales, scales_o)}
        for number, (source, there) in ends.items():
            store(number, source, there).wait()

    if tick == 0:
        bias_store().wait()


def hbm_specs(count):
    return [pl.BlockSpec(memory_space=pl.ANY)] * count


def vmem_specs(count):
    return [pl.BlockSpec(memory_space=pltpu.VMEM)] * count


def forward(tick, pads, patches, received, segments, ext, vectors, weights, kept):
    micro, length, width = patches.shape
    wqkv, wp, w1, w2 = weights
    hidden = w1.shape[1]
    heads = ext.shape[0]
    stored = [
        ((length, width), BF16),
        ((length, 3 * width), BF16),
        ((heads, length, length), BF16),
        ((length, width), BF16),
        ((length, width), BF16),
        ((length, width), F32),
        ((length, width), BF16),
        ((length, hidden), BF16),
        ((length, hidden), BF16),
        ((length, width), BF16),
        ((length, width), BF16),
        ((length, width), BF16),
        ((length, width), F32),
        ((heads, length), F32),
    ]
    bias = jax.ShapeDtypeStruct((heads, 2 * length - LANES, LANES), F32)
    scratch = [pltpu.VMEM(x.shape, x.dtype) for x in (bias, wqkv, wp, w1, w2)]
    scratch.append(pltpu.VMEM((length, length), F32))
    scratch += [pltpu.VMEM((2, 2, length, length) if n == 2 else shape, kind) for n, (shape, kind) in enumerate(stored[:10])]
    scratch += [pltpu.VMEM((length, width), F32), pltpu.VMEM((heads, length), F32), pltpu.VMEM((length, width), BF16)]
    scratch += [pltpu.VMEM((2 * length // LANES, length, LANES), F32)]
    scratch += [
        pltpu.SemaphoreType.DMA((7,)),
        pltpu.SemaphoreType.DMA((STORED,)),
        pltpu.SemaphoreType.DMA((2,)),
        pltpu.SemaphoreType.DMA((1,)),
    ]
    operands = [pads, patches, received, segments, ext, *vectors, *weights]
    first = len(operands)
    held = STORED + 1 if tick > 0 else 0
    out = pl.pallas_call(
        functools.partial(forward_kernel, tick),
        out_shape=[jax.ShapeDtypeStruct((length, width), BF16), bias]
        + [jax.ShapeDtypeStruct((micro, *shape), kind) for shape, kind in stored],
        in_specs=[pl.BlockSpec(memory_space=pltpu.SMEM)] + hbm_specs(1) + (vmem_specs(1) if tick > 0 else hbm_specs(1)) + vmem_specs(2 + VECTORS) + hbm_specs(4 + held),
        out_specs=vmem_specs(1) + hbm_specs(STORED + 1),
        scratch_shapes=scratch,
        input_output_aliases={first + n: 1 + n for n in range(held)},
        compiler_params=pltpu.CompilerParams(vmem_limit_bytes=VMEM_BYTES),
        name="forward_layer",
    )(*operands, *(kept if tick > 0 else ()))
    return out[0], out[1:]


def backward_kernel(tick, cotangent_hbm, returned_hbm, *refs):
    vectors, refs = refs[:VECTORS], refs[VECTORS:]
    (wqkv_hbm, wp_hbm, w1_hbm, w2_hbm, qkv_i, prob_i, mixed_i, proj_i, x1_i, slope_i, mlp_i, xin_i, scales_i) = refs[:13]
    refs = refs[13 + (7 if tick > 0 else 0) :]
    dx_ref, *stores = refs[:8]
    (wqkv, wp, w1, w2, qkv, probs, mixed, proj, x1, slope, mlp, xin, scales, dm, dz, dproj, packed, dx1, dmixed, dscore, diag, sums, tables, g_ref, load_sem, store_sem, prob_sem) = refs[8:]
    dm_o, dz_o, dproj_o, packed_o, dx_o, tables_o, sums_o = stores
    length, width = g_ref.shape
    hidden = w1.shape[1]
    blocks = length // LANES
    pairs = width // LANES
    section = lax.axis_index("section")
    slot = tick - 1 + section
    active = (slot >= 0) & (slot < cotangent_hbm.shape[0])
    factor = HALF ** (-0.5)
    parts = [pl.ds(part * width, width) for part in range(hidden // width)]
    loads = [(mlp_i.at[slot], mlp)]
    loads += [(w2_hbm.at[part, :], w2.at[part, :]) for part in parts]
    loads += [(slope_i.at[slot], slope)]
    loads += [(w1_hbm.at[:, part], w1.at[:, part]) for part in parts]
    early = len(loads)
    loads += [
        (x1_i.at[slot], x1), (proj_i.at[slot], proj), (wp_hbm, wp), (qkv_i.at[slot], qkv), (mixed_i.at[slot], mixed),
        (scales_i.at[slot], scales), (wqkv_hbm, wqkv), (xin_i.at[slot], xin),
    ]
    upstream_sem = load_sem.at[len(loads)]
    def load(number):
        return pltpu.make_async_copy(*loads[number], load_sem.at[number])

    def store(number, source, there):
        return pltpu.make_async_copy(source, there.at[slot], store_sem.at[number])

    def prob_load(pair):
        return pltpu.make_async_copy(
            prob_i.at[slot, pl.ds(2 * pair, 2)], probs.at[pair % 2], prob_sem.at[pair % 2]
        )

    def vector(row):
        return vectors[row][...]

    def put(row, partial):
        sums[row : row + 1, :] = jnp.sum(partial, 0, keepdims=True)

    nothing = jnp.zeros((8, width), F32)

    @pl.when(active)
    def _():
        @pl.when(section == 1)
        def _():
            pltpu.make_async_copy(cotangent_hbm.at[slot], g_ref, upstream_sem).start()

        if tick > 0:

            @pl.when(section == 0)
            def _():
                pltpu.make_async_copy(returned_hbm, g_ref, upstream_sem).start()

        for number in range(1 + len(parts)):
            load(number).start()
        pltpu.make_async_copy(g_ref, g_ref, upstream_sem).wait()
        load(0).wait()
        for number in range(1 + len(parts), early):
            load(number).start()

        scale_sum = bias_sum = nothing
        for rows in strips(0, length, STRIP):
            upstream = g_ref[rows, :].astype(F32)
            low = (upstream * vector(SCALE_M)).astype(BF16)
            dm[rows, :] = low
            scale_sum = scale_sum + fold(upstream * mlp[rows, :].astype(F32))
            bias_sum = bias_sum + fold(low.astype(F32))
        put(SCALE_M, scale_sum)
        put(B2, bias_sum)
        store(0, dm, dm_o).start()
        pieces = [
            (pl.ds(high * (length // 2), length // 2), pl.ds(part * width, width))
            for part in range(hidden // width)
            for high in range(2)
        ]

        def expand(number):
            rows, columns = pieces[number]
            if number % 2 == 0:
                load(1 + number // 2).wait()
            return nt(dm[rows, :], w2[columns, :])

        coming = expand(0)
        totals = [None, None]
        act_sum = nothing
        load(1 + len(parts)).wait()
        for number, (rows, columns) in enumerate(pieces):
            if number == 2:
                for later in range(early, len(loads)):
                    load(later).start()
                prob_load(0).start()
            if number % 2 == 0:
                load(2 + len(parts) + number // 2).wait()
            current = coming
            if number + 1 < len(pieces):
                coming = expand(number + 1)
            for strip in strips(0, length // 2, STRIP):
                there = pl.ds(rows.start + strip.start, STRIP)
                low = (current[strip] * slope[there, columns].astype(F32)).astype(BF16)
                dz[there, columns] = low
                act_sum = act_sum + fold(low.astype(F32))
            if number % 2 == 1:
                put(B1 + number // 2, act_sum)
                act_sum = nothing
            more = nt(dz[rows, columns], w1[:, columns])
            totals[number % 2] = more if number < 2 else totals[number % 2] + more
        store(1, dz, dz_o).start()
        load(early).wait()
        load(early + 1).wait()
        found = [nothing] * 4
        for half in range(2):
            for strip in strips(0, length // 2, STRIP):
                rows = pl.ds(half * (length // 2) + strip.start, STRIP)
                upper = totals[half][strip]
                scaled, inverse = normalize(x1[rows, :])
                resid = g_ref[rows, :].astype(F32) + norm_back(upper * vector(GAIN2), scaled, inverse)
                dx1[rows, :] = resid
                low = (resid * vector(SCALE_A)).astype(BF16)
                dproj[rows, :] = low
                terms = (upper * scaled, upper, resid * proj[rows, :].astype(F32), low.astype(F32))
                found = [old + fold(term) for old, term in zip(found, terms)]
        for row, partial in zip((GAIN2, SHIFT2, SCALE_A, PBIAS), found):
            put(row, partial)
        store(2, dproj, dproj_o).start()
        load(early + 2).wait()
        dmixed[...] = nt(dproj[...], wp[...]).astype(BF16)
        for number in range(early + 3, early + 6):
            load(number).wait()

        @pl.loop(0, pairs)
        def _(pair):
            prob_load(pair).wait()

            @pl.when(pair + 1 < pairs)
            def _():
                prob_load(pair + 1).start()

            side = pair % 2
            columns = chunk(pair, LANES)
            key_columns = pl.ds(pl.multiple_of(width + pair * LANES, LANES), LANES)
            value_columns = pl.ds(pl.multiple_of(2 * width + pair * LANES, LANES), LANES)
            values = qkv[:, value_columns]
            above = dmixed[:, columns]
            queries_t = qkv[:, columns].T
            keys_t = qkv[:, key_columns].T
            above_t = above.astype(F32).T
            products = (above.astype(F32) * mixed[:, columns]).T
            grads = [], [], []
            for which in range(2):
                half = slice(which * HALF, (which + 1) * HALF)
                delta = jnp.sum(products[half], 0, keepdims=True)
                scale = scales[pl.ds(2 * pair + which, 1), :]
                own_values = jnp.where(half_mask(values.shape, which), values, jnp.zeros_like(values))
                edge = (blocks - 1) * LANES
                diag[which, :edge, :] = jnp.zeros((edge, LANES), F32)
                for wide in range(blocks // 2):
                    prob_grad = nt(own_values, above[2 * LANES * wide : 2 * LANES * (wide + 1)])
                    for part in range(2):
                        place = 2 * wide + part
                        low, high = key_rows(place, blocks)
                        lanes = slice(place * LANES, (place + 1) * LANES)
                        first_row = (blocks - 1 - place) * LANES
                        for rows in strips(low, high, 64):
                            here = (probs[side, which, rows, lanes].astype(F32) * scale[:, lanes]) * (
                                prob_grad[rows, part * LANES : (part + 1) * LANES] - delta[:, lanes]
                            )
                            dscore[which, rows, lanes] = here.astype(BF16)
                            there = slice(first_row + rows.start, first_row + rows.stop)
                            diag[which, there, :] = here if place == 0 else diag[which, there, :] + here
                        if low > 0:
                            dscore[which, :low, lanes] = jnp.zeros((low, LANES), BF16)
                        if high < length:
                            dscore[which, high:, lanes] = jnp.zeros((length - high, LANES), BF16)
                        if place == 0:
                            diag[which, edge + high :, :] = jnp.zeros((length - high, LANES), F32)
                line = gather_diagonals(diag.at[which])
                most = tables.shape[1] - LANES
                tables[pl.ds(2 * pair + which, 1), :] = jnp.concatenate(
                    [line[:, REACH + 1 : REACH + 1 + most], line[:, REACH : REACH + LANES]], 1
                )
                grads[0].append(nn(keys_t[half], dscore[which]))
                grads[1].append(nt(queries_t[half], dscore[which]))
                grads[2].append(nt((above_t[half] * scale).astype(BF16), probs[side, which]))
            for found, where, scale in zip(grads, (columns, key_columns, value_columns), (factor, None, None)):
                low = jnp.concatenate(found, 0).astype(BF16)
                if scale is not None:
                    low = (low.astype(F32) * scale).astype(BF16)
                packed[:, where] = low.T

        store(3, packed, packed_o).start()
        load(early + 6).wait()
        result = nt(packed[...], wqkv[...])
        load(early + 7).wait()
        found = [nothing] * 4
        for rows in strips(0, length, STRIP):
            upper = result[rows]
            scaled, inverse = normalize(xin[rows, :].astype(F32))
            dx_ref[rows, :] = (dx1[rows, :] + norm_back(upper * vector(GAIN1), scaled, inverse)).astype(BF16)
            terms = (
                upper * scaled,
                upper,
                packed[rows, :width].astype(F32),
                packed[rows, 2 * width :].astype(F32),
            )
            found = [old + fold(term) for old, term in zip(found, terms)]
        for row, partial in zip((GAIN1, SHIFT1, QBIAS, VBIAS), found):
            put(row, partial)
        store(4, dx_ref, dx_o).start()
        store(5, tables, tables_o).start()
        store(6, sums, sums_o).start()
        ends = {0: (dm, dm_o), 1: (dz, dz_o), 2: (dproj, dproj_o), 3: (packed, packed_o), 4: (dx_ref, dx_o), 5: (tables, tables_o), 6: (sums, sums_o)}
        for number, (source, there) in ends.items():
            store(number, source, there).wait()


def backward(tick, cotangent, returned, vectors, weights, saved, kept):
    micro, length, width = cotangent.shape
    wqkv, wp, w1, w2 = weights
    hidden = w1.shape[1]
    bias, h1, qkv, probs, mixed, proj, x1, h2, act, slope, mlp, y, xin, wide, scales = saved
    heads = probs.shape[1]
    span = 2 * length - LANES
    summed = (16, width)
    table = (heads, 5 * LANES)
    stored = [
        ((length, width), BF16),
        ((length, hidden), BF16),
        ((length, width), BF16),
        ((length, 3 * width), BF16),
        ((length, width), BF16),
        (table, F32),
        (summed, F32),
    ]
    reads = [qkv, probs, wide, proj, x1, slope, mlp, xin, scales]
    scratch = [pltpu.VMEM(x.shape, x.dtype) for x in weights]
    scratch += [pltpu.VMEM((2, 2, length, length) if x is probs else x.shape[1:], x.dtype) for x in reads]
    scratch += [pltpu.VMEM(shape, kind) for shape, kind in stored[:4]]
    scratch += [
        pltpu.VMEM((length, width), F32),
        pltpu.VMEM((length, width), BF16),
        pltpu.VMEM((2, length, length), BF16),
        pltpu.VMEM((2, span, LANES), F32),
        pltpu.VMEM(summed, F32),
        pltpu.VMEM(table, F32),
        pltpu.VMEM((length, width), BF16),
        pltpu.SemaphoreType.DMA((19,)),
        pltpu.SemaphoreType.DMA((7,)),
        pltpu.SemaphoreType.DMA((2,)),
    ]
    operands = [cotangent, returned, *vectors, *weights, *reads]
    first = len(operands)
    held = 7 if tick > 0 else 0
    out = pl.pallas_call(
        functools.partial(backward_kernel, tick),
        out_shape=[jax.ShapeDtypeStruct((length, width), BF16)]
        + [jax.ShapeDtypeStruct((micro, *shape), kind) for shape, kind in stored],
        in_specs=hbm_specs(1) + (vmem_specs(1) if tick > 0 else hbm_specs(1)) + vmem_specs(VECTORS) + hbm_specs(13 + held),
        out_specs=vmem_specs(1) + hbm_specs(7),
        scratch_shapes=scratch,
        input_output_aliases={first + n: 1 + n for n in range(held)},
        compiler_params=pltpu.CompilerParams(vmem_limit_bytes=VMEM_BYTES),
        name="backward_layer",
    )(*operands, *(kept if tick > 0 else ()))
    return out[0], out[1:]


def small_lines(width):
    lines = width // LANES
    places = [(row, tile, row * lines + tile) for row in range(10) for tile in range(lines)]
    return places + [(B1, tile, B1 * lines + tile) for tile in range(4 * lines)]


def reverse_lanes(values):
    lane = lax.broadcasted_iota(jnp.int32, values.shape, 1)
    for place in range(LANES.bit_length() - 1):
        step = 1 << place
        up, down = pltpu.roll(values, step, 1), pltpu.roll(values, LANES - step, 1)
        values = jnp.where((lane // step) % 2 == 1, up, down)
    return values


def widen_kernel(sum_hbm, small_ref, *refs):
    bigs, vectors, table_ref = refs[:4], refs[4 : 4 + VECTORS], refs[4 + VECTORS]
    narrow, wide, load_sem, store_sem = refs[5 + VECTORS :]
    depth, width = narrow.shape[:2]
    blocks = [(0, slice(b * width, (b + 1) * width), slice(0, width)) for b in range(4)]
    for target, count in ((1, 4), (2, 3), (3, 1)):
        blocks += [(target, slice(0, width), slice(b * width, (b + 1) * width)) for b in range(count)]

    def load(block):
        rows = pl.ds(block * width, width)
        return pltpu.make_async_copy(sum_hbm.at[rows, :], narrow.at[block % depth], load_sem.at[block % depth])

    def store(block):
        target, rows, columns = blocks[block]
        there = bigs[target].at[rows, columns]
        return pltpu.make_async_copy(wide.at[block % depth], there, store_sem.at[block % depth])

    for block in range(depth):
        load(block).start()
    for block in range(len(blocks)):
        load(block).wait()
        if block >= depth:
            store(block - depth).wait()
        for rows in strips(0, width, 64):
            wide[block % depth, rows, :] = narrow[block % depth, rows, :].astype(F32)
        store(block).start()
        if block + depth < len(blocks):
            load(block + depth).start()
    places = small_lines(width)
    for row, tile, line in places:
        vectors[row][:, tile * LANES : (tile + 1) * LANES] = small_ref[line : line + 1, :]
    first = len(places)
    heads, entries = table_ref.shape
    tiles = -(-entries // LANES)
    flipped = reverse_lanes(small_ref[first : first + heads * tiles, :])
    for head in range(heads):
        for tile in range(tiles - 1):
            line = head * tiles + tile
            there = (tiles - 2 - tile) * LANES
            table_ref[head : head + 1, there : there + LANES] = flipped[line : line + 1]
        line = first + head * tiles + tiles - 1
        table_ref[head : head + 1, entries - 1 :] = small_ref[line : line + 1, 0:1]
    for block in range(len(blocks) - depth, len(blocks)):
        store(block).wait()


def widen(summed, small, width, heads, entries):
    shapes = [(4 * width, width), (width, 4 * width), (width, 3 * width), (width, width)]
    shapes += [(1, width)] * 10 + [(1, 4 * width), (heads, entries)]
    return pl.pallas_call(
        widen_kernel,
        out_shape=[jax.ShapeDtypeStruct(shape, F32) for shape in shapes],
        in_specs=hbm_specs(1) + vmem_specs(1),
        out_specs=hbm_specs(4) + vmem_specs(VECTORS + 1),
        scratch_shapes=[
            pltpu.VMEM((3, width, width), BF16),
            pltpu.VMEM((3, width, width), F32),
            pltpu.SemaphoreType.DMA((3,)),
            pltpu.SemaphoreType.DMA((3,)),
        ],
        compiler_params=pltpu.CompilerParams(vmem_limit_bytes=VMEM_BYTES),
        name="widen",
    )(summed, small)


BLOCK = 256
LAG = 3


def reduce_kernel(
    bits, chunks, blocks, lag, *refs
):
    (a_ref, dm_ref, h2_ref, dz_ref, h1_ref, dp_ref, o_ref, dproj_ref, sums_ref, tables_ref, out_ref, small_out_ref) = refs[:12]
    (lhs, rhs, grads, total, small_ref, small_total, *received) = refs[12 : 18 + 2 * bits]
    (load_sem, send_sem, recv_sem, small_send, small_recv, store_sem) = refs[18 + 2 * bits :]
    small_received = received[bits:]
    me = lax.axis_index("dp")
    rows = BLOCK * blocks
    width = grads.shape[1]
    per_side = width // BLOCK
    last = 2 * bits

    barrier = pltpu.get_barrier_semaphore()
    for place in range(bits):
        stride = 1 << place
        other = me + stride * (1 - 2 * ((me // stride) % 2))
        pl.semaphore_signal(barrier, inc=1, device_id={"dp": other}, device_id_type=MESH)
    pl.semaphore_wait(barrier, bits)

    families = (
        (a_ref, dm_ref, 4 * per_side, True),
        (h2_ref, dz_ref, 4 * per_side, False),
        (h1_ref, dp_ref, 3 * per_side, False),
        (o_ref, dproj_ref, per_side, False),
    )
    n_blocks = 12 * per_side

    def load(block):
        slot = block % 2
        first = 0
        for left, right, count, walks in families:
            @pl.when((block >= first) & (block < first + count))
            def _():
                local = block - first
                if walks:
                    left_column = local * BLOCK
                    right_column = 0
                else:
                    left_column = (local % per_side) * BLOCK
                    right_column = (local // per_side) * width
                pltpu.make_async_copy(
                    left.at[:, pl.ds(pl.multiple_of(left_column, BLOCK), BLOCK)],
                    lhs.at[slot],
                    load_sem.at[0, slot],
                ).start()
                pltpu.make_async_copy(
                    right.at[:, pl.ds(pl.multiple_of(right_column, BLOCK), width)],
                    rhs.at[slot],
                    load_sem.at[1, slot],
                ).start()
            first += count

    def produce(block):
        slot = block % 2
        pltpu.make_async_copy(lhs.at[slot], lhs.at[slot], load_sem.at[0, slot]).wait()
        pltpu.make_async_copy(rhs.at[slot], rhs.at[slot], load_sem.at[1, slot]).wait()

        @pl.when(block + 1 < n_blocks)
        def _():
            load(block + 1)

        grads[pl.ds(pl.multiple_of(block * BLOCK, BLOCK), BLOCK), :] = lax.dot_general(
            lhs[slot], rhs[slot], (((0,), (0,)), ((), ())), preferred_element_type=jnp.float32
        ).astype(jnp.bfloat16)

    def turn(chunk):
        place = chunk % 9
        return place % 2 + place // 5 - place // 6

    def partner(rotation, stage):
        stride = lax.shift_left(jnp.int32(1), (stage + rotation) % bits)
        mine = (me // stride) % 2
        return mine, me + stride * (1 - 2 * mine)

    def offset(base, height, rotation, stage):
        for earlier in range(stage):
            mine, _ = partner(rotation, earlier)
            base = base + mine * (height >> (earlier + 1))
        return base

    def piece(ref, start, size):
        return ref.at[pl.ds(pl.multiple_of(start, size), size)]

    def send(position, base, height, rotation, source, landing, result, slot, sems):
        send_at, recv_at = sems
        if position < bits:
            stage = position
            half = height >> (stage + 1)
            mine, other = partner(rotation, stage)
            start = offset(base, height, rotation, stage) + (1 - mine) * half
            src, dst = piece(source, start, half), landing[stage].at[slot]
        else:
            stage = last - 1 - position
            half = height >> (stage + 1)
            mine, other = partner(rotation, stage)
            start = offset(base, height, rotation, stage + 1)
            src = dst = piece(result, start, half)
        return pltpu.make_async_remote_copy(
            src_ref=src,
            dst_ref=dst,
            send_sem=send_at.at[position],
            recv_sem=recv_at.at[position, slot],
            device_id={"dp": other},
            device_id_type=MESH,
        )

    def take(position, base, height, rotation, source, landing, result, slot, sems):
        send(position - 1, base, height, rotation, source, landing, result, slot, sems).wait_recv()
        stage = position - 1
        if stage < bits:
            half = height >> (stage + 1)
            start = pl.multiple_of(offset(base, height, rotation, stage + 1), half)
            keep = pl.ds(start, half)
            value = source[keep, :].astype(jnp.float32) + landing[stage][slot].astype(jnp.float32)
            target = result if stage == bits - 1 else source
            target[keep, :] = value.astype(target.dtype)

    def step(position, *way):
        if position > 0:
            take(position, *way)
        if position < last:
            send(position, *way).start()

    main = (grads, received[:bits], total)
    main_sems = (send_sem, recv_sem)

    def walk(position, chunk):
        if position == 0:
            for sub in range(blocks):
                block = chunk * blocks + sub

                @pl.when(block < n_blocks)
                def _():
                    produce(block)

        base = chunk * rows
        step(position, base, rows, turn(chunk), *main, chunk, main_sems)
        if position == last:
            there = pl.ds(pl.multiple_of(base, rows), rows)
            pltpu.make_async_copy(total.at[there], out_ref.at[there], store_sem.at[0]).start()

    def walk_small(position):
        height = small_ref.shape[0]
        way = (0, height, 0, small_ref, small_received, small_total, 0, (small_send, small_recv))
        step(position, *way)

    load(jnp.int32(0))
    small_ref[...] = jnp.zeros_like(small_ref)
    places = small_lines(width)
    for row, tile, line in places:
        if row == B1:
            row, tile = B1 + tile // (width // LANES), tile % (width // LANES)
        lanes = slice(tile * LANES, (tile + 1) * LANES)
        small_ref[line : line + 1, :] = sums_ref[0, row : row + 1, lanes] + sums_ref[1, row : row + 1, lanes]
    line = len(places)
    for head in range(tables_ref.shape[1]):
        for tile in range(tables_ref.shape[2] // LANES):
            lanes = slice(tile * LANES, (tile + 1) * LANES)
            small_ref[line : line + 1, :] = tables_ref[0, head : head + 1, lanes] + tables_ref[1, head : head + 1, lanes]
            line += 1

    @pl.loop(0, chunks + lag * last)
    def _(tick):
        for position in range(last + 1):
            chunk = tick - lag * position

            @pl.when((chunk >= 0) & (chunk < chunks))
            def _():
                walk(position, chunk)

            @pl.when(tick == lag * position)
            def _():
                walk_small(position)

    small_out_ref[...] = small_total[...]
    for position in range(last):
        stage = position if position < bits else last - 1 - position
        size = received[stage]
        pltpu.make_async_copy(size, size, send_sem.at[position]).wait()
        size = small_received[stage]
        pltpu.make_async_copy(size, size, small_send.at[position]).wait()
    pltpu.make_async_copy(total, out_ref, store_sem.at[0]).wait()


def reduce_gradients(a, dm, h2, dz, h1, packed, o, dproj, sums, tables):
    parts = lax.axis_size("dp")
    bits = parts.bit_length() - 1
    blocks = max(2, 16 * parts // BLOCK)
    tokens, width = h1.shape
    n_blocks = 12 * width // BLOCK
    chunks = -(-n_blocks // blocks)
    rows = BLOCK * blocks
    lines = len(small_lines(width)) + tables.shape[1] * tables.shape[2] // LANES
    height = -(-lines // (8 * parts)) * 8 * parts
    small = jax.ShapeDtypeStruct((height, LANES), jnp.float32)
    bf16 = jnp.bfloat16
    return pl.pallas_call(
        functools.partial(reduce_kernel, bits, chunks, blocks, LAG),
        out_shape=(
            jax.ShapeDtypeStruct((chunks * rows, width), bf16),
            jax.ShapeDtypeStruct(small.shape, jnp.float32),
        ),
        in_specs=[pl.BlockSpec(memory_space=pl.ANY)] * 8 + [pl.BlockSpec(memory_space=pltpu.VMEM)] * 2,
        out_specs=(pl.BlockSpec(memory_space=pl.ANY), pl.BlockSpec(memory_space=pltpu.VMEM)),
        scratch_shapes=[
            pltpu.VMEM((2, tokens, BLOCK), bf16),
            pltpu.VMEM((2, tokens, width), bf16),
            pltpu.VMEM((chunks * rows, width), bf16),
            pltpu.VMEM((chunks * rows, width), bf16),
            pltpu.VMEM(small.shape, jnp.float32),
            pltpu.VMEM(small.shape, jnp.float32),
            *[pltpu.VMEM((chunks, rows >> (s + 1), width), bf16) for s in range(bits)],
            *[pltpu.VMEM((1, height >> (s + 1), 128), jnp.float32) for s in range(bits)],
            pltpu.SemaphoreType.DMA((2, 2)),
            pltpu.SemaphoreType.DMA((2 * bits,)),
            pltpu.SemaphoreType.DMA((2 * bits, chunks)),
            pltpu.SemaphoreType.DMA((2 * bits,)),
            pltpu.SemaphoreType.DMA((2 * bits, 1)),
            pltpu.SemaphoreType.DMA((1,)),
        ],
        compiler_params=pltpu.CompilerParams(
            collective_id=0, has_side_effects=True, vmem_limit_bytes=60 * 1024 * 1024
        ),
        name="reduce_gradients",
    )(a, dm, h2, dz, h1, packed, o, dproj, sums, tables)


def shifted(block, axis, distance):
    devices = range(lax.axis_size(axis))
    route = [(i - distance, i) for i in devices if i - distance in devices]
    return lax.ppermute(block, axis, route)


def per_device(
    patches,
    segment_ids,
    pad_counts,
    norm1_gain,
    norm1_bias,
    qkv_weight,
    query_bias,
    value_bias,
    rel_table,
    proj_weight,
    proj_bias,
    scale_attn,
    norm2_gain,
    norm2_bias,
    fc1_weight,
    fc1_bias,
    fc2_weight,
    fc2_bias,
    scale_mlp,
    cotangent,
):
    micro, length, width = patches.shape
    vectors = (
        norm1_gain,
        norm1_bias,
        query_bias,
        value_bias,
        proj_bias,
        scale_attn,
        norm2_gain,
        norm2_bias,
        fc2_bias,
        scale_mlp,
        fc1_bias,
    )
    weights = (qkv_weight[0], proj_weight[0], fc1_weight[0], fc2_weight[0])
    entries = rel_table.shape[2]
    before = REACH
    after = 2 * length - before - entries
    ext = jnp.pad(rel_table[0, :, ::-1], ((0, 0), (before, after)))
    received = patches
    saved = None
    for tick in range(micro + 1):
        result, saved = forward(
            tick, pad_counts, patches, received, segment_ids, ext, vectors, weights, saved
        )
        if tick < micro:
            received = shifted(result, "section", 1)
    returned = cotangent
    kept = None
    for tick in range(micro + 1):
        input_grad, kept = backward(tick, cotangent, returned, vectors, weights, saved, kept)
        if tick < micro:
            returned = shifted(input_grad, "section", -1)
    dm, dz, dproj, packed, in_grads, tables, sums = kept
    h1, mixed, h2, act, outputs = saved[1], saved[4], saved[7], saved[8], saved[11]
    left = [x.reshape(micro * length, -1) for x in (act, dm, h2, dz, h1, packed, mixed, dproj)]
    summed, small = reduce_gradients(*left, sums, tables)
    fc2_grad, fc1_grad, qkv_grad, proj_grad, *small_grads = widen(
        summed, small, width, tables.shape[1], entries
    )
    table_grad = small_grads[VECTORS]
    return (
        outputs[None],
        in_grads[None],
        small_grads[GAIN1],
        small_grads[SHIFT1],
        qkv_grad[None],
        small_grads[QBIAS],
        small_grads[VBIAS],
        table_grad[None],
        proj_grad[None],
        small_grads[PBIAS],
        small_grads[SCALE_A],
        small_grads[GAIN2],
        small_grads[SHIFT2],
        fc1_grad[None],
        small_grads[B1],
        fc2_grad[None],
        small_grads[B2],
        small_grads[SCALE_M],
    )


def solution(mesh):
    placed = (
        P("dp", None, None),
        P("dp", None),
        P("dp"),
        P("section", None),
        P("section", None),
        P("section", None, None),
        P("section", None),
        P("section", None),
        P("section", None, None),
        P("section", None, None),
        P("section", None),
        P("section", None),
        P("section", None),
        P("section", None),
        P("section", None, None),
        P("section", None),
        P("section", None, None),
        P("section", None),
        P("section", None),
        P("dp", None, None),
    )
    return jax.shard_map(
        per_device,
        mesh=mesh,
        in_specs=placed,
        out_specs=(
            P("section", "dp", None, None),
            P("section", "dp", None, None),
            P("section", None),
            P("section", None),
            P("section", None, None),
            P("section", None),
            P("section", None),
            P("section", None, None),
            P("section", None, None),
            P("section", None),
            P("section", None),
            P("section", None),
            P("section", None),
            P("section", None, None),
            P("section", None),
            P("section", None, None),
            P("section", None),
            P("section", None),
        ),
        check_vma=False,
    )
```

```python
import functools
import math

import jax
import jax.numpy as jnp
from jax import lax
from jax.experimental import pallas as pl
from jax.experimental.pallas import tpu as pltpu
from jax.sharding import PartitionSpec as P

MESH = pl.DeviceIdType.MESH
BF16, F32 = jnp.bfloat16, jnp.float32
VMEM_BYTES = 60 * 1024 * 1024
LANES = 128
HALF = 64
REACH = 2 * LANES
GAIN1, SHIFT1, QBIAS, VBIAS, PBIAS, SCALE_A, GAIN2, SHIFT2, B2, SCALE_M, B1 = range(11)
VECTORS = 11
STORED = 14
STRIP = 16
GROUP = 2


def dot(left, right, left_dim, right_dim):
    return lax.dot_general(
        left, right, (((left_dim,), (right_dim,)), ((), ())), preferred_element_type=F32
    )


def nn(left, right):
    return dot(left, right, 1, 0)


def nt(left, right):
    return dot(left, right, 1, 1)


def normalize(values):
    centered = values - jnp.mean(values, -1, keepdims=True)
    inverse = lax.rsqrt(jnp.mean(centered * centered, -1, keepdims=True) + 1e-06)
    return centered * inverse, inverse


def norm_back(upper, scaled, inverse):
    return inverse * (
        upper
        - jnp.mean(upper, -1, keepdims=True)
        - scaled * jnp.mean(upper * scaled, -1, keepdims=True)
    )


def fold(values):
    return jnp.sum(values.reshape(values.shape[0] // 8, 8, values.shape[1]), 0)


def half_mask(shape, which):
    return lax.broadcasted_iota(jnp.int32, shape, 1) // HALF == which


def strips(first, last, size):
    return [slice(start, start + size) for start in range(first, last, size)]


def chunk(index, size):
    return pl.ds(pl.multiple_of(index * size, size), size)


def skew_bias(reversed_row, target):
    span, lanes = target.shape
    rows = pltpu.roll(jnp.broadcast_to(reversed_row, (8, reversed_row.shape[1])), 0, 1, stride=1, stride_axis=0)
    tiles = span // lanes
    for fine in range(lanes // 8):
        moved = rows if fine == 0 else pltpu.roll(rows, 8 * fine, 1)
        for coarse in range(tiles):
            place = 8 * (fine + lanes // 8 * coarse)
            target[place : place + 8, :] = moved[:, lanes * (tiles - coarse) : lanes * (tiles - coarse + 1)]


def gather_diagonals(source):
    span, lanes = source.shape
    tiles = span // lanes
    width = span + lanes
    blank = jnp.zeros((8, lanes), F32)
    found = None
    for fine in range(lanes // 8):
        places = [8 * (fine + lanes // 8 * coarse) for coarse in reversed(range(tiles))]
        line = jnp.concatenate([blank] + [source[place : place + 8, :] for place in places], 1)
        if fine > 0:
            line = pltpu.roll(line, width - 8 * fine, 1)
        found = line if found is None else found + line
    row = lax.broadcasted_iota(jnp.int32, found.shape, 0)
    for place in range(3):
        moved = pltpu.roll(found, width - (1 << place), 1)
        found = jnp.where((row // (1 << place)) % 2 == 1, moved, found)
    return jnp.sum(found, 0, keepdims=True)


def key_rows(query_block, blocks):
    reach = REACH // LANES
    return max(0, query_block - reach) * LANES, min(blocks, query_block + reach + 1) * LANES


def forward_kernel(tick, pads, patches_hbm, received_hbm, seg_ref, ext_ref, *refs):
    vectors, refs = refs[:VECTORS], refs[VECTORS:]
    wqkv_hbm, wp_hbm, w1_hbm, w2_hbm = refs[:4]
    refs = refs[4 + (STORED + 1 if tick > 0 else 0) :]
    y_ref, bias_o, *stores = refs[: STORED + 2]
    (bias, wqkv, wp, w1, w2, mask, h1, qkv, probs, mixed, proj, x1, h2, act, slope, mlp, wide_mixed, scales, xin, held, load_sem, store_sem, prob_sem, bias_sem) = refs[STORED + 2 :]
    h1_o, qkv_o, prob_o, mixed_o, proj_o, x1_o, h2_o, act_o, slope_o, mlp_o, y_o, xin_o, wide_o, scales_o = stores
    length, width = xin.shape
    hidden = w1.shape[1]
    heads = bias.shape[0]
    blocks = length // LANES
    section = lax.axis_index("section")
    slot = tick - section
    active = (slot >= 0) & (slot < seg_ref.shape[0])
    factor = HALF ** (-0.5)
    thirds = [pl.ds(part * width, width) for part in range(3)]
    loads = [(wqkv_hbm.at[:, columns], wqkv.at[:, columns]) for columns in thirds]
    loads += [(wp_hbm, wp), (w1_hbm, w1), (w2_hbm, w2)]

    def load(number):
        return pltpu.make_async_copy(*loads[number], load_sem.at[number])

    def store(number, source, there):
        return pltpu.make_async_copy(source, there.at[slot], store_sem.at[number])

    def vector(row):
        return vectors[row][...]

    def bias_load():
        return pltpu.make_async_copy(bias_o, bias, bias_sem.at[0])

    def bias_store():
        return pltpu.make_async_copy(bias, bias_o, bias_sem.at[0])

    @pl.when(active)
    def _():
        @pl.when(section == 0)
        def _():
            pltpu.make_async_copy(patches_hbm.at[slot], xin, load_sem.at[6]).start()

        if tick > 0:

            @pl.when(section == 1)
            def _():
                pltpu.make_async_copy(received_hbm, xin, load_sem.at[6]).start()

        for number in range(3):
            load(number).start()

    if tick == 0:

        @pl.loop(0, heads)
        def _(head):
            skew_bias(ext_ref[pl.ds(head, 1), :], bias.at[head])

        bias_store().start()

    @pl.when(active)
    def _():
        pltpu.make_async_copy(xin, xin, load_sem.at[6]).wait()
        if tick > 0:
            bias_load().start()
        segment = seg_ref[pl.ds(slot, 1), :].astype(F32)
        key_segment = jnp.broadcast_to(segment, (LANES, length)).T

        for rows in strips(0, length, STRIP):
            scaled, _ = normalize(xin[rows, :].astype(F32))
            h1[rows, :] = (scaled * vector(GAIN1) + vector(SHIFT1)).astype(BF16)

        alive = length - pads[slot]
        for place in range(blocks):
            lanes = slice(place * LANES, (place + 1) * LANES)
            for rows in strips(0, length, 64):
                key = lax.broadcasted_iota(jnp.int32, (64, LANES), 0) + rows.start
                query = lax.broadcasted_iota(jnp.int32, (64, LANES), 1) + place * LANES
                allowed = ((key_segment[rows] == segment[:, lanes]) & (key < alive)) | (key == query)
                mask[rows, lanes] = jnp.where(allowed, 0.0, -1000000000.0)

        store(0, h1, h1_o).start()
        store(11, xin, xin_o).start()
        for part in range(3):
            load(part).wait()
            columns = thirds[part]
            result = nn(h1[...], wqkv[:, columns])
            for rows in strips(0, length, STRIP):
                piece = result[rows]
                if part == 0:
                    piece = (piece + vector(QBIAS)) * factor
                if part == 2:
                    piece = piece + vector(VBIAS)
                qkv[rows, columns] = piece.astype(BF16)
        store(1, qkv, qkv_o).start()
        if tick > 0:
            bias_load().wait()
        for number in (3, 4, 5):
            load(number).start()

        together = 2 * GROUP

        def prob_store(group):
            return pltpu.make_async_copy(
                probs.at[group % 2], prob_o.at[slot, pl.ds(together * group, together)], prob_sem.at[group % 2]
            )

        def attend(side, within, pair):
            columns = chunk(pair, LANES)
            queries = qkv[:, columns]
            keys = qkv[:, pl.ds(pl.multiple_of(width + pair * LANES, LANES), LANES)]
            values = qkv[:, pl.ds(pl.multiple_of(2 * width + pair * LANES, LANES), LANES)].T
            outs = []
            for which in range(2):
                own_keys = jnp.where(half_mask(keys.shape, which), keys, jnp.zeros_like(keys))
                lines = []
                for wide in range(blocks // 2):
                    scores = nt(own_keys, queries[2 * LANES * wide : 2 * LANES * (wide + 1)])
                    for part in range(2):
                        place = 2 * wide + part
                        low, high = key_rows(place, blocks)
                        lanes = slice(place * LANES, (place + 1) * LANES)
                        first = (blocks - 1 - place) * LANES
                        spare = (2 * within + which) * blocks + place
                        highest = None
                        for rows in strips(low, high, 64):
                            here = (
                                scores[rows, part * LANES : (part + 1) * LANES]
                                + bias[2 * pair + which, first + rows.start : first + rows.stop, :]
                                + mask[rows, lanes]
                            )
                            held[spare, rows, :] = here
                            top = jnp.max(here.reshape(8, 8, LANES), 0)
                            highest = top if highest is None else jnp.maximum(highest, top)
                        highest = jnp.max(highest, 0, keepdims=True)
                        sums = jnp.zeros((8, LANES), F32)
                        for rows in strips(low, high, 64):
                            expo = jnp.exp(held[spare, rows, :] - highest)
                            probs[side, 2 * within + which, rows, lanes] = expo.astype(BF16)
                            sums = sums + fold(expo)
                        lines.append(1.0 / jnp.sum(sums, 0, keepdims=True))
                        if low > 0:
                            probs[side, 2 * within + which, :low, lanes] = jnp.zeros((low, LANES), BF16)
                        if high < length:
                            probs[side, 2 * within + which, high:, lanes] = jnp.zeros((length - high, LANES), BF16)
                scale = jnp.concatenate(lines, 1)
                scales[pl.ds(2 * pair + which, 1), :] = scale
                outs.append(nn(values[which * HALF : (which + 1) * HALF], probs[side, 2 * within + which]) * scale)
            out = jnp.concatenate(outs, 0).T
            wide_mixed[:, columns] = out
            mixed[:, columns] = out.astype(BF16)

        @pl.loop(0, heads // together)
        def _(group):
            @pl.when(group >= 2)
            def _():
                prob_store(group - 2).wait()

            for within in range(GROUP):
                attend(group % 2, within, GROUP * group + within)
            prob_store(group).start()

        store(3, mixed, mixed_o).start()
        store(12, wide_mixed, wide_o).start()
        store(13, scales, scales_o).start()
        load(3).wait()

        result = nn(mixed[...], wp[...])
        for rows in strips(0, length, STRIP):
            out = result[rows] + vector(PBIAS)
            proj[rows, :] = out.astype(BF16)
            resid = xin[rows, :].astype(F32) + vector(SCALE_A) * out
            x1[rows, :] = resid
            scaled, _ = normalize(resid)
            h2[rows, :] = (scaled * vector(GAIN2) + vector(SHIFT2)).astype(BF16)

        store(4, proj, proj_o).start()
        store(5, x1, x1_o).start()
        store(6, h2, h2_o).start()
        load(4).wait()
        load(5).wait()
        pieces = [
            (pl.ds(high * (length // 2), length // 2), pl.ds(part * width, width))
            for part in range(hidden // width)
            for high in range(2)
        ]

        def expand(number):
            rows, columns = pieces[number]
            return nn(h2[rows, :], w1[:, columns])

        coming = expand(0)
        totals = [None, None]
        for number, (rows, columns) in enumerate(pieces):
            current = coming
            if number + 1 < len(pieces):
                coming = expand(number + 1)
            for strip in strips(0, length // 2, STRIP):
                there = pl.ds(rows.start + strip.start, STRIP)
                here = current[strip] + vectors[B1][:, columns]
                normal = 0.5 * lax.erf(here * math.sqrt(0.5)) + 0.5
                density = jnp.exp(-0.5 * here * here) * (1.0 / math.sqrt(2.0 * math.pi))
                act[there, columns] = (here * normal).astype(BF16)
                slope[there, columns] = (normal + here * density).astype(BF16)
            more = nn(act[rows, columns], w2[columns, :])
            totals[number % 2] = more if number < 2 else totals[number % 2] + more
        store(7, act, act_o).start()
        store(8, slope, slope_o).start()

        for half in range(2):
            for strip in strips(0, length // 2, STRIP):
                rows = pl.ds(half * (length // 2) + strip.start, STRIP)
                out = totals[half][strip] + vector(B2)
                mlp[rows, :] = out.astype(BF16)
                y_ref[rows, :] = (x1[rows, :] + vector(SCALE_M) * out).astype(BF16)

        store(9, mlp, mlp_o).start()
        store(10, y_ref, y_o).start()
        for group in range(max(0, heads // together - 2), heads // together):
            prob_store(group).wait()
        ends = {0: (h1, h1_o), 1: (qkv, qkv_o), 3: (mixed, mixed_o), 4: (proj, proj_o), 5: (x1, x1_o), 6: (h2, h2_o),
                7: (act, act_o), 8: (slope, slope_o), 9: (mlp, mlp_o), 10: (y_ref, y_o), 11: (xin, xin_o), 12: (wide_mixed, wide_o), 13: (scales, scales_o)}
        for number, (source, there) in ends.items():
            store(number, source, there).wait()

    if tick == 0:
        bias_store().wait()


def hbm_specs(count):
    return [pl.BlockSpec(memory_space=pl.ANY)] * count


def vmem_specs(count):
    return [pl.BlockSpec(memory_space=pltpu.VMEM)] * count


def forward(tick, pads, patches, received, segments, ext, vectors, weights, kept):
    micro, length, width = patches.shape
    wqkv, wp, w1, w2 = weights
    hidden = w1.shape[1]
    heads = ext.shape[0]
    stored = [
        ((length, width), BF16),
        ((length, 3 * width), BF16),
        ((heads, length, length), BF16),
        ((length, width), BF16),
        ((length, width), BF16),
        ((length, width), F32),
        ((length, width), BF16),
        ((length, hidden), BF16),
        ((length, hidden), BF16),
        ((length, width), BF16),
        ((length, width), BF16),
        ((length, width), BF16),
        ((length, width), F32),
        ((heads, length), F32),
    ]
    bias = jax.ShapeDtypeStruct((heads, 2 * length - LANES, LANES), F32)
    scratch = [pltpu.VMEM(x.shape, x.dtype) for x in (bias, wqkv, wp, w1, w2)]
    scratch.append(pltpu.VMEM((length, length), F32))
    scratch += [pltpu.VMEM((2, 2 * GROUP, length, length) if n == 2 else shape, kind) for n, (shape, kind) in enumerate(stored[:10])]
    scratch += [pltpu.VMEM((length, width), F32), pltpu.VMEM((heads, length), F32), pltpu.VMEM((length, width), BF16)]
    scratch += [pltpu.VMEM((2 * GROUP * length // LANES, length, LANES), F32)]
    scratch += [
        pltpu.SemaphoreType.DMA((7,)),
        pltpu.SemaphoreType.DMA((STORED,)),
        pltpu.SemaphoreType.DMA((2,)),
        pltpu.SemaphoreType.DMA((1,)),
    ]
    operands = [pads, patches, received, segments, ext, *vectors, *weights]
    first = len(operands)
    held = STORED + 1 if tick > 0 else 0
    out = pl.pallas_call(
        functools.partial(forward_kernel, tick),
        out_shape=[jax.ShapeDtypeStruct((length, width), BF16), bias]
        + [jax.ShapeDtypeStruct((micro, *shape), kind) for shape, kind in stored],
        in_specs=[pl.BlockSpec(memory_space=pltpu.SMEM)] + hbm_specs(1) + (vmem_specs(1) if tick > 0 else hbm_specs(1)) + vmem_specs(2 + VECTORS) + hbm_specs(4 + held),
        out_specs=vmem_specs(1) + hbm_specs(STORED + 1),
        scratch_shapes=scratch,
        input_output_aliases={first + n: 1 + n for n in range(held)},
        compiler_params=pltpu.CompilerParams(vmem_limit_bytes=VMEM_BYTES),
        name="forward_layer",
    )(*operands, *(kept if tick > 0 else ()))
    return out[0], out[1:]


def backward_kernel(tick, cotangent_hbm, returned_hbm, *refs):
    vectors, refs = refs[:VECTORS], refs[VECTORS:]
    (wqkv_hbm, wp_hbm, w1_hbm, w2_hbm, qkv_i, prob_i, mixed_i, proj_i, x1_i, slope_i, mlp_i, xin_i, scales_i) = refs[:13]
    refs = refs[13 + (7 if tick > 0 else 0) :]
    dx_ref, *stores = refs[:8]
    (wqkv, wp, w1, w2, qkv, probs, mixed, proj, x1, slope, mlp, xin, scales, dm, dz, dproj, packed, dx1, dmixed, dscore, diag, sums, tables, g_ref, load_sem, store_sem, prob_sem) = refs[8:]
    dm_o, dz_o, dproj_o, packed_o, dx_o, tables_o, sums_o = stores
    length, width = g_ref.shape
    hidden = w1.shape[1]
    blocks = length // LANES
    pairs = width // LANES
    section = lax.axis_index("section")
    slot = tick - 1 + section
    active = (slot >= 0) & (slot < cotangent_hbm.shape[0])
    factor = HALF ** (-0.5)
    parts = [pl.ds(part * width, width) for part in range(hidden // width)]
    loads = [(mlp_i.at[slot], mlp)]
    loads += [(w2_hbm.at[part, :], w2.at[part, :]) for part in parts]
    loads += [(slope_i.at[slot], slope)]
    loads += [(w1_hbm.at[:, part], w1.at[:, part]) for part in parts]
    early = len(loads)
    loads += [
        (x1_i.at[slot], x1), (proj_i.at[slot], proj), (wp_hbm, wp), (qkv_i.at[slot], qkv), (mixed_i.at[slot], mixed),
        (scales_i.at[slot], scales), (wqkv_hbm, wqkv), (xin_i.at[slot], xin),
    ]
    upstream_sem = load_sem.at[len(loads)]
    def load(number):
        return pltpu.make_async_copy(*loads[number], load_sem.at[number])

    def store(number, source, there):
        return pltpu.make_async_copy(source, there.at[slot], store_sem.at[number])

    together = 2 * GROUP

    def prob_load(group):
        return pltpu.make_async_copy(
            prob_i.at[slot, pl.ds(together * group, together)], probs.at[group % 2], prob_sem.at[group % 2]
        )

    def vector(row):
        return vectors[row][...]

    def put(row, partial):
        sums[row : row + 1, :] = jnp.sum(partial, 0, keepdims=True)

    nothing = jnp.zeros((8, width), F32)

    @pl.when(active)
    def _():
        @pl.when(section == 1)
        def _():
            pltpu.make_async_copy(cotangent_hbm.at[slot], g_ref, upstream_sem).start()

        if tick > 0:

            @pl.when(section == 0)
            def _():
                pltpu.make_async_copy(returned_hbm, g_ref, upstream_sem).start()

        for number in range(1 + len(parts)):
            load(number).start()
        pltpu.make_async_copy(g_ref, g_ref, upstream_sem).wait()
        load(0).wait()
        for number in range(1 + len(parts), early):
            load(number).start()

        scale_sum = bias_sum = nothing
        for rows in strips(0, length, STRIP):
            upstream = g_ref[rows, :].astype(F32)
            low = (upstream * vector(SCALE_M)).astype(BF16)
            dm[rows, :] = low
            scale_sum = scale_sum + fold(upstream * mlp[rows, :].astype(F32))
            bias_sum = bias_sum + fold(low.astype(F32))
        put(SCALE_M, scale_sum)
        put(B2, bias_sum)
        store(0, dm, dm_o).start()
        pieces = [
            (pl.ds(high * (length // 2), length // 2), pl.ds(part * width, width))
            for part in range(hidden // width)
            for high in range(2)
        ]

        def expand(number):
            rows, columns = pieces[number]
            if number % 2 == 0:
                load(1 + number // 2).wait()
            return nt(dm[rows, :], w2[columns, :])

        coming = expand(0)
        totals = [None, None]
        act_sum = nothing
        load(1 + len(parts)).wait()
        for number, (rows, columns) in enumerate(pieces):
            if number == 2:
                for later in range(early, len(loads)):
                    load(later).start()
                prob_load(0).start()
            if number % 2 == 0:
                load(2 + len(parts) + number // 2).wait()
            current = coming
            if number + 1 < len(pieces):
                coming = expand(number + 1)
            for strip in strips(0, length // 2, STRIP):
                there = pl.ds(rows.start + strip.start, STRIP)
                low = (current[strip] * slope[there, columns].astype(F32)).astype(BF16)
                dz[there, columns] = low
                act_sum = act_sum + fold(low.astype(F32))
            if number % 2 == 1:
                put(B1 + number // 2, act_sum)
                act_sum = nothing
            more = nt(dz[rows, columns], w1[:, columns])
            totals[number % 2] = more if number < 2 else totals[number % 2] + more
        store(1, dz, dz_o).start()
        load(early).wait()
        load(early + 1).wait()
        found = [nothing] * 4
        for half in range(2):
            for strip in strips(0, length // 2, STRIP):
                rows = pl.ds(half * (length // 2) + strip.start, STRIP)
                upper = totals[half][strip]
                scaled, inverse = normalize(x1[rows, :])
                resid = g_ref[rows, :].astype(F32) + norm_back(upper * vector(GAIN2), scaled, inverse)
                dx1[rows, :] = resid
                low = (resid * vector(SCALE_A)).astype(BF16)
                dproj[rows, :] = low
                terms = (upper * scaled, upper, resid * proj[rows, :].astype(F32), low.astype(F32))
                found = [old + fold(term) for old, term in zip(found, terms)]
        for row, partial in zip((GAIN2, SHIFT2, SCALE_A, PBIAS), found):
            put(row, partial)
        store(2, dproj, dproj_o).start()
        load(early + 2).wait()
        dmixed[...] = nt(dproj[...], wp[...]).astype(BF16)
        for number in range(early + 3, early + 6):
            load(number).wait()

        def attend(side, within, pair):
            columns = chunk(pair, LANES)
            key_columns = pl.ds(pl.multiple_of(width + pair * LANES, LANES), LANES)
            value_columns = pl.ds(pl.multiple_of(2 * width + pair * LANES, LANES), LANES)
            values = qkv[:, value_columns]
            above = dmixed[:, columns]
            queries_t = qkv[:, columns].T
            keys_t = qkv[:, key_columns].T
            above_t = above.astype(F32).T
            products = (above.astype(F32) * mixed[:, columns]).T
            grads = [], [], []
            for which in range(2):
                place_in = 2 * within + which
                half = slice(which * HALF, (which + 1) * HALF)
                delta = jnp.sum(products[half], 0, keepdims=True)
                scale = scales[pl.ds(2 * pair + which, 1), :]
                own_values = jnp.where(half_mask(values.shape, which), values, jnp.zeros_like(values))
                edge = (blocks - 1) * LANES
                diag[place_in, :edge, :] = jnp.zeros((edge, LANES), F32)
                for wide in range(blocks // 2):
                    prob_grad = nt(own_values, above[2 * LANES * wide : 2 * LANES * (wide + 1)])
                    for part in range(2):
                        place = 2 * wide + part
                        low, high = key_rows(place, blocks)
                        lanes = slice(place * LANES, (place + 1) * LANES)
                        first_row = (blocks - 1 - place) * LANES
                        for rows in strips(low, high, 64):
                            here = (probs[side, place_in, rows, lanes].astype(F32) * scale[:, lanes]) * (
                                prob_grad[rows, part * LANES : (part + 1) * LANES] - delta[:, lanes]
                            )
                            dscore[place_in, rows, lanes] = here.astype(BF16)
                            there = slice(first_row + rows.start, first_row + rows.stop)
                            diag[place_in, there, :] = here if place == 0 else diag[place_in, there, :] + here
                        if low > 0:
                            dscore[place_in, :low, lanes] = jnp.zeros((low, LANES), BF16)
                        if high < length:
                            dscore[place_in, high:, lanes] = jnp.zeros((length - high, LANES), BF16)
                        if place == 0:
                            diag[place_in, edge + high :, :] = jnp.zeros((length - high, LANES), F32)
                line = gather_diagonals(diag.at[place_in])
                most = tables.shape[1] - LANES
                tables[pl.ds(2 * pair + which, 1), :] = jnp.concatenate(
                    [line[:, REACH + 1 : REACH + 1 + most], line[:, REACH : REACH + LANES]], 1
                )
                grads[0].append(nn(keys_t[half], dscore[place_in]))
                grads[1].append(nt(queries_t[half], dscore[place_in]))
                grads[2].append(nt((above_t[half] * scale).astype(BF16), probs[side, place_in]))
            for found, where, scale in zip(grads, (columns, key_columns, value_columns), (factor, None, None)):
                low = jnp.concatenate(found, 0).astype(BF16)
                if scale is not None:
                    low = (low.astype(F32) * scale).astype(BF16)
                packed[:, where] = low.T

        @pl.loop(0, pairs // GROUP)
        def _(group):
            prob_load(group).wait()

            @pl.when(group + 1 < pairs // GROUP)
            def _():
                prob_load(group + 1).start()

            for within in range(GROUP):
                attend(group % 2, within, GROUP * group + within)

        store(3, packed, packed_o).start()
        load(early + 6).wait()
        result = nt(packed[...], wqkv[...])
        load(early + 7).wait()
        found = [nothing] * 4
        for rows in strips(0, length, STRIP):
            upper = result[rows]
            scaled, inverse = normalize(xin[rows, :].astype(F32))
            dx_ref[rows, :] = (dx1[rows, :] + norm_back(upper * vector(GAIN1), scaled, inverse)).astype(BF16)
            terms = (
                upper * scaled,
                upper,
                packed[rows, :width].astype(F32),
                packed[rows, 2 * width :].astype(F32),
            )
            found = [old + fold(term) for old, term in zip(found, terms)]
        for row, partial in zip((GAIN1, SHIFT1, QBIAS, VBIAS), found):
            put(row, partial)
        store(4, dx_ref, dx_o).start()
        store(5, tables, tables_o).start()
        store(6, sums, sums_o).start()
        ends = {0: (dm, dm_o), 1: (dz, dz_o), 2: (dproj, dproj_o), 3: (packed, packed_o), 4: (dx_ref, dx_o), 5: (tables, tables_o), 6: (sums, sums_o)}
        for number, (source, there) in ends.items():
            store(number, source, there).wait()


def backward(tick, cotangent, returned, vectors, weights, saved, kept):
    micro, length, width = cotangent.shape
    wqkv, wp, w1, w2 = weights
    hidden = w1.shape[1]
    bias, h1, qkv, probs, mixed, proj, x1, h2, act, slope, mlp, y, xin, wide, scales = saved
    heads = probs.shape[1]
    span = 2 * length - LANES
    summed = (16, width)
    table = (heads, 5 * LANES)
    stored = [
        ((length, width), BF16),
        ((length, hidden), BF16),
        ((length, width), BF16),
        ((length, 3 * width), BF16),
        ((length, width), BF16),
        (table, F32),
        (summed, F32),
    ]
    reads = [qkv, probs, wide, proj, x1, slope, mlp, xin, scales]
    scratch = [pltpu.VMEM(x.shape, x.dtype) for x in weights]
    scratch += [pltpu.VMEM((2, 2 * GROUP, length, length) if x is probs else x.shape[1:], x.dtype) for x in reads]
    scratch += [pltpu.VMEM(shape, kind) for shape, kind in stored[:4]]
    scratch += [
        pltpu.VMEM((length, width), F32),
        pltpu.VMEM((length, width), BF16),
        pltpu.VMEM((2 * GROUP, length, length), BF16),
        pltpu.VMEM((2 * GROUP, span, LANES), F32),
        pltpu.VMEM(summed, F32),
        pltpu.VMEM(table, F32),
        pltpu.VMEM((length, width), BF16),
        pltpu.SemaphoreType.DMA((19,)),
        pltpu.SemaphoreType.DMA((7,)),
        pltpu.SemaphoreType.DMA((2,)),
    ]
    operands = [cotangent, returned, *vectors, *weights, *reads]
    first = len(operands)
    held = 7 if tick > 0 else 0
    out = pl.pallas_call(
        functools.partial(backward_kernel, tick),
        out_shape=[jax.ShapeDtypeStruct((length, width), BF16)]
        + [jax.ShapeDtypeStruct((micro, *shape), kind) for shape, kind in stored],
        in_specs=hbm_specs(1) + (vmem_specs(1) if tick > 0 else hbm_specs(1)) + vmem_specs(VECTORS) + hbm_specs(13 + held),
        out_specs=vmem_specs(1) + hbm_specs(7),
        scratch_shapes=scratch,
        input_output_aliases={first + n: 1 + n for n in range(held)},
        compiler_params=pltpu.CompilerParams(vmem_limit_bytes=VMEM_BYTES),
        name="backward_layer",
    )(*operands, *(kept if tick > 0 else ()))
    return out[0], out[1:]


def small_lines(width):
    lines = width // LANES
    places = [(row, tile, row * lines + tile) for row in range(10) for tile in range(lines)]
    return places + [(B1, tile, B1 * lines + tile) for tile in range(4 * lines)]


def reverse_lanes(values):
    lane = lax.broadcasted_iota(jnp.int32, values.shape, 1)
    for place in range(LANES.bit_length() - 1):
        step = 1 << place
        up, down = pltpu.roll(values, step, 1), pltpu.roll(values, LANES - step, 1)
        values = jnp.where((lane // step) % 2 == 1, up, down)
    return values


def widen_kernel(sum_hbm, small_ref, *refs):
    bigs, vectors, table_ref = refs[:4], refs[4 : 4 + VECTORS], refs[4 + VECTORS]
    narrow, wide, load_sem, store_sem = refs[5 + VECTORS :]
    depth, width = narrow.shape[:2]
    blocks = [(0, slice(b * width, (b + 1) * width), slice(0, width)) for b in range(4)]
    for target, count in ((1, 4), (2, 3), (3, 1)):
        blocks += [(target, slice(0, width), slice(b * width, (b + 1) * width)) for b in range(count)]

    def load(block):
        rows = pl.ds(block * width, width)
        return pltpu.make_async_copy(sum_hbm.at[rows, :], narrow.at[block % depth], load_sem.at[block % depth])

    def store(block):
        target, rows, columns = blocks[block]
        there = bigs[target].at[rows, columns]
        return pltpu.make_async_copy(wide.at[block % depth], there, store_sem.at[block % depth])

    for block in range(depth):
        load(block).start()
    for block in range(len(blocks)):
        load(block).wait()
        if block >= depth:
            store(block - depth).wait()
        for rows in strips(0, width, 64):
            wide[block % depth, rows, :] = narrow[block % depth, rows, :].astype(F32)
        store(block).start()
        if block + depth < len(blocks):
            load(block + depth).start()
    places = small_lines(width)
    for row, tile, line in places:
        vectors[row][:, tile * LANES : (tile + 1) * LANES] = small_ref[line : line + 1, :]
    first = len(places)
    heads, entries = table_ref.shape
    tiles = -(-entries // LANES)
    flipped = reverse_lanes(small_ref[first : first + heads * tiles, :])
    for head in range(heads):
        for tile in range(tiles - 1):
            line = head * tiles + tile
            there = (tiles - 2 - tile) * LANES
            table_ref[head : head + 1, there : there + LANES] = flipped[line : line + 1]
        line = first + head * tiles + tiles - 1
        table_ref[head : head + 1, entries - 1 :] = small_ref[line : line + 1, 0:1]
    for block in range(len(blocks) - depth, len(blocks)):
        store(block).wait()


def widen(summed, small, width, heads, entries):
    shapes = [(4 * width, width), (width, 4 * width), (width, 3 * width), (width, width)]
    shapes += [(1, width)] * 10 + [(1, 4 * width), (heads, entries)]
    return pl.pallas_call(
        widen_kernel,
        out_shape=[jax.ShapeDtypeStruct(shape, F32) for shape in shapes],
        in_specs=hbm_specs(1) + vmem_specs(1),
        out_specs=hbm_specs(4) + vmem_specs(VECTORS + 1),
        scratch_shapes=[
            pltpu.VMEM((3, width, width), BF16),
            pltpu.VMEM((3, width, width), F32),
            pltpu.SemaphoreType.DMA((3,)),
            pltpu.SemaphoreType.DMA((3,)),
        ],
        compiler_params=pltpu.CompilerParams(vmem_limit_bytes=VMEM_BYTES),
        name="widen",
    )(summed, small)


BLOCK = 256
LAG = 5


def reduce_kernel(
    bits, chunks, blocks, lag, *refs
):
    (a_ref, dm_ref, h2_ref, dz_ref, h1_ref, dp_ref, o_ref, dproj_ref, sums_ref, tables_ref, out_ref, small_out_ref) = refs[:12]
    (lhs, rhs, grads, total, small_ref, small_total, *received) = refs[12 : 18 + 2 * bits]
    (load_sem, send_sem, recv_sem, small_send, small_recv, store_sem) = refs[18 + 2 * bits :]
    small_received = received[bits:]
    me = lax.axis_index("dp")
    rows = BLOCK * blocks
    width = grads.shape[1]
    per_side = width // BLOCK
    last = 2 * bits

    barrier = pltpu.get_barrier_semaphore()
    for place in range(bits):
        stride = 1 << place
        other = me + stride * (1 - 2 * ((me // stride) % 2))
        pl.semaphore_signal(barrier, inc=1, device_id={"dp": other}, device_id_type=MESH)
    pl.semaphore_wait(barrier, bits)

    families = (
        (a_ref, dm_ref, 4 * per_side, True),
        (h2_ref, dz_ref, 4 * per_side, False),
        (h1_ref, dp_ref, 3 * per_side, False),
        (o_ref, dproj_ref, per_side, False),
    )
    n_blocks = 12 * per_side

    def load(block):
        slot = block % 2
        first = 0
        for left, right, count, walks in families:
            @pl.when((block >= first) & (block < first + count))
            def _():
                local = block - first
                if walks:
                    left_column = local * BLOCK
                    right_column = 0
                else:
                    left_column = (local % per_side) * BLOCK
                    right_column = (local // per_side) * width
                pltpu.make_async_copy(
                    left.at[:, pl.ds(pl.multiple_of(left_column, BLOCK), BLOCK)],
                    lhs.at[slot],
                    load_sem.at[0, slot],
                ).start()
                pltpu.make_async_copy(
                    right.at[:, pl.ds(pl.multiple_of(right_column, BLOCK), width)],
                    rhs.at[slot],
                    load_sem.at[1, slot],
                ).start()
            first += count

    def produce(block):
        slot = block % 2
        pltpu.make_async_copy(lhs.at[slot], lhs.at[slot], load_sem.at[0, slot]).wait()
        pltpu.make_async_copy(rhs.at[slot], rhs.at[slot], load_sem.at[1, slot]).wait()

        @pl.when(block + 1 < n_blocks)
        def _():
            load(block + 1)

        grads[pl.ds(pl.multiple_of(block * BLOCK, BLOCK), BLOCK), :] = lax.dot_general(
            lhs[slot], rhs[slot], (((0,), (0,)), ((), ())), preferred_element_type=jnp.float32
        ).astype(jnp.bfloat16)

    def turn(chunk):
        place = chunk % 9
        return place % 2 + place // 5 - place // 6

    def partner(rotation, stage):
        stride = lax.shift_left(jnp.int32(1), (stage + rotation) % bits)
        mine = (me // stride) % 2
        return mine, me + stride * (1 - 2 * mine)

    def offset(base, height, rotation, stage):
        for earlier in range(stage):
            mine, _ = partner(rotation, earlier)
            base = base + mine * (height >> (earlier + 1))
        return base

    def piece(ref, start, size):
        return ref.at[pl.ds(pl.multiple_of(start, size), size)]

    def send(position, base, height, rotation, source, landing, result, slot, sems):
        send_at, recv_at = sems
        if position < bits:
            stage = position
            half = height >> (stage + 1)
            mine, other = partner(rotation, stage)
            start = offset(base, height, rotation, stage) + (1 - mine) * half
            src, dst = piece(source, start, half), landing[stage].at[slot]
        else:
            stage = last - 1 - position
            half = height >> (stage + 1)
            mine, other = partner(rotation, stage)
            start = offset(base, height, rotation, stage + 1)
            src = dst = piece(result, start, half)
        return pltpu.make_async_remote_copy(
            src_ref=src,
            dst_ref=dst,
            send_sem=send_at.at[position],
            recv_sem=recv_at.at[position, slot],
            device_id={"dp": other},
            device_id_type=MESH,
        )

    def take(position, base, height, rotation, source, landing, result, slot, sems):
        send(position - 1, base, height, rotation, source, landing, result, slot, sems).wait_recv()
        stage = position - 1
        if stage < bits:
            half = height >> (stage + 1)
            start = pl.multiple_of(offset(base, height, rotation, stage + 1), half)
            keep = pl.ds(start, half)
            value = source[keep, :].astype(jnp.float32) + landing[stage][slot].astype(jnp.float32)
            target = result if stage == bits - 1 else source
            target[keep, :] = value.astype(target.dtype)

    def step(position, *way):
        if position > 0:
            take(position, *way)
        if position < last:
            send(position, *way).start()

    main = (grads, received[:bits], total)
    main_sems = (send_sem, recv_sem)

    def walk(position, chunk):
        if position == 0:
            for sub in range(blocks):
                block = chunk * blocks + sub

                @pl.when(block < n_blocks)
                def _():
                    produce(block)

        base = chunk * rows
        step(position, base, rows, turn(chunk), *main, chunk, main_sems)
        if position == last:
            there = pl.ds(pl.multiple_of(base, rows), rows)
            pltpu.make_async_copy(total.at[there], out_ref.at[there], store_sem.at[0]).start()

    def walk_small(position):
        height = small_ref.shape[0]
        way = (0, height, 0, small_ref, small_received, small_total, 0, (small_send, small_recv))
        step(position, *way)

    load(jnp.int32(0))
    small_ref[...] = jnp.zeros_like(small_ref)
    places = small_lines(width)
    for row, tile, line in places:
        if row == B1:
            row, tile = B1 + tile // (width // LANES), tile % (width // LANES)
        lanes = slice(tile * LANES, (tile + 1) * LANES)
        small_ref[line : line + 1, :] = sums_ref[0, row : row + 1, lanes] + sums_ref[1, row : row + 1, lanes]
    line = len(places)
    for head in range(tables_ref.shape[1]):
        for tile in range(tables_ref.shape[2] // LANES):
            lanes = slice(tile * LANES, (tile + 1) * LANES)
            small_ref[line : line + 1, :] = tables_ref[0, head : head + 1, lanes] + tables_ref[1, head : head + 1, lanes]
            line += 1

    @pl.loop(0, chunks + lag * last)
    def _(tick):
        for position in range(last + 1):
            chunk = tick - lag * position

            @pl.when((chunk >= 0) & (chunk < chunks))
            def _():
                walk(position, chunk)

            @pl.when(tick == lag * position)
            def _():
                walk_small(position)

    small_out_ref[...] = small_total[...]
    for position in range(last):
        stage = position if position < bits else last - 1 - position
        size = received[stage]
        pltpu.make_async_copy(size, size, send_sem.at[position]).wait()
        size = small_received[stage]
        pltpu.make_async_copy(size, size, small_send.at[position]).wait()
    pltpu.make_async_copy(total, out_ref, store_sem.at[0]).wait()


def reduce_gradients(a, dm, h2, dz, h1, packed, o, dproj, sums, tables):
    parts = lax.axis_size("dp")
    bits = parts.bit_length() - 1
    blocks = max(1, 16 * parts // BLOCK)
    tokens, width = h1.shape
    n_blocks = 12 * width // BLOCK
    chunks = -(-n_blocks // blocks)
    rows = BLOCK * blocks
    lines = len(small_lines(width)) + tables.shape[1] * tables.shape[2] // LANES
    height = -(-lines // (8 * parts)) * 8 * parts
    small = jax.ShapeDtypeStruct((height, LANES), jnp.float32)
    bf16 = jnp.bfloat16
    return pl.pallas_call(
        functools.partial(reduce_kernel, bits, chunks, blocks, LAG),
        out_shape=(
            jax.ShapeDtypeStruct((chunks * rows, width), bf16),
            jax.ShapeDtypeStruct(small.shape, jnp.float32),
        ),
        in_specs=[pl.BlockSpec(memory_space=pl.ANY)] * 8 + [pl.BlockSpec(memory_space=pltpu.VMEM)] * 2,
        out_specs=(pl.BlockSpec(memory_space=pl.ANY), pl.BlockSpec(memory_space=pltpu.VMEM)),
        scratch_shapes=[
            pltpu.VMEM((2, tokens, BLOCK), bf16),
            pltpu.VMEM((2, tokens, width), bf16),
            pltpu.VMEM((chunks * rows, width), bf16),
            pltpu.VMEM((chunks * rows, width), bf16),
            pltpu.VMEM(small.shape, jnp.float32),
            pltpu.VMEM(small.shape, jnp.float32),
            *[pltpu.VMEM((chunks, rows >> (s + 1), width), bf16) for s in range(bits)],
            *[pltpu.VMEM((1, height >> (s + 1), 128), jnp.float32) for s in range(bits)],
            pltpu.SemaphoreType.DMA((2, 2)),
            pltpu.SemaphoreType.DMA((2 * bits,)),
            pltpu.SemaphoreType.DMA((2 * bits, chunks)),
            pltpu.SemaphoreType.DMA((2 * bits,)),
            pltpu.SemaphoreType.DMA((2 * bits, 1)),
            pltpu.SemaphoreType.DMA((1,)),
        ],
        compiler_params=pltpu.CompilerParams(
            collective_id=0, has_side_effects=True, vmem_limit_bytes=60 * 1024 * 1024
        ),
        name="reduce_gradients",
    )(a, dm, h2, dz, h1, packed, o, dproj, sums, tables)


def shifted(block, axis, distance):
    devices = range(lax.axis_size(axis))
    route = [(i - distance, i) for i in devices if i - distance in devices]
    return lax.ppermute(block, axis, route)


def per_device(
    patches,
    segment_ids,
    pad_counts,
    norm1_gain,
    norm1_bias,
    qkv_weight,
    query_bias,
    value_bias,
    rel_table,
    proj_weight,
    proj_bias,
    scale_attn,
    norm2_gain,
    norm2_bias,
    fc1_weight,
    fc1_bias,
    fc2_weight,
    fc2_bias,
    scale_mlp,
    cotangent,
):
    micro, length, width = patches.shape
    vectors = (
        norm1_gain,
        norm1_bias,
        query_bias,
        value_bias,
        proj_bias,
        scale_attn,
        norm2_gain,
        norm2_bias,
        fc2_bias,
        scale_mlp,
        fc1_bias,
    )
    weights = (qkv_weight[0], proj_weight[0], fc1_weight[0], fc2_weight[0])
    entries = rel_table.shape[2]
    before = REACH
    after = 2 * length - before - entries
    ext = jnp.pad(rel_table[0, :, ::-1], ((0, 0), (before, after)))
    received = patches
    saved = None
    for tick in range(micro + 1):
        result, saved = forward(
            tick, pad_counts, patches, received, segment_ids, ext, vectors, weights, saved
        )
        if tick < micro:
            received = shifted(result, "section", 1)
    returned = cotangent
    kept = None
    for tick in range(micro + 1):
        input_grad, kept = backward(tick, cotangent, returned, vectors, weights, saved, kept)
        if tick < micro:
            returned = shifted(input_grad, "section", -1)
    dm, dz, dproj, packed, in_grads, tables, sums = kept
    h1, mixed, h2, act, outputs = saved[1], saved[4], saved[7], saved[8], saved[11]
    left = [x.reshape(micro * length, -1) for x in (act, dm, h2, dz, h1, packed, mixed, dproj)]
    summed, small = reduce_gradients(*left, sums, tables)
    fc2_grad, fc1_grad, qkv_grad, proj_grad, *small_grads = widen(
        summed, small, width, tables.shape[1], entries
    )
    table_grad = small_grads[VECTORS]
    return (
        outputs[None],
        in_grads[None],
        small_grads[GAIN1],
        small_grads[SHIFT1],
        qkv_grad[None],
        small_grads[QBIAS],
        small_grads[VBIAS],
        table_grad[None],
        proj_grad[None],
        small_grads[PBIAS],
        small_grads[SCALE_A],
        small_grads[GAIN2],
        small_grads[SHIFT2],
        fc1_grad[None],
        small_grads[B1],
        fc2_grad[None],
        small_grads[B2],
        small_grads[SCALE_M],
    )


def solution(mesh):
    placed = (
        P("dp", None, None),
        P("dp", None),
        P("dp"),
        P("section", None),
        P("section", None),
        P("section", None, None),
        P("section", None),
        P("section", None),
        P("section", None, None),
        P("section", None, None),
        P("section", None),
        P("section", None),
        P("section", None),
        P("section", None),
        P("section", None, None),
        P("section", None),
        P("section", None, None),
        P("section", None),
        P("section", None),
        P("dp", None, None),
    )
    return jax.shard_map(
        per_device,
        mesh=mesh,
        in_specs=placed,
        out_specs=(
            P("section", "dp", None, None),
            P("section", "dp", None, None),
            P("section", None),
            P("section", None),
            P("section", None, None),
            P("section", None),
            P("section", None),
            P("section", None, None),
            P("section", None, None),
            P("section", None),
            P("section", None),
            P("section", None),
            P("section", None),
            P("section", None, None),
            P("section", None),
            P("section", None, None),
            P("section", None),
            P("section", None),
        ),
        check_vma=False,
    )
```

```python
import functools
import math

import jax
import jax.numpy as jnp
from jax import lax
from jax.experimental import pallas as pl
from jax.experimental.pallas import tpu as pltpu
from jax.sharding import PartitionSpec as P

MESH = pl.DeviceIdType.MESH
BF16, F32 = jnp.bfloat16, jnp.float32
VMEM_BYTES = 60 * 1024 * 1024
LANES = 128
HALF = 64
REACH = 2 * LANES
GAIN1, SHIFT1, QBIAS, VBIAS, PBIAS, SCALE_A, GAIN2, SHIFT2, B2, SCALE_M, B1 = range(11)
VECTORS = 10
ATTEND = 10
EXPAND = 4
STRIP = 16
GROUP = 2


def dot(left, right, left_dim, right_dim):
    return lax.dot_general(
        left, right, (((left_dim,), (right_dim,)), ((), ())), preferred_element_type=F32
    )


def nn(left, right):
    return dot(left, right, 1, 0)


def nt(left, right):
    return dot(left, right, 1, 1)


def normalize(values):
    centered = values - jnp.mean(values, -1, keepdims=True)
    inverse = lax.rsqrt(jnp.mean(centered * centered, -1, keepdims=True) + 1e-06)
    return centered * inverse, inverse


def norm_back(upper, scaled, inverse):
    return inverse * (
        upper
        - jnp.mean(upper, -1, keepdims=True)
        - scaled * jnp.mean(upper * scaled, -1, keepdims=True)
    )


def fold(values):
    return jnp.sum(values.reshape(values.shape[0] // 8, 8, values.shape[1]), 0)


def half_mask(shape, which):
    return lax.broadcasted_iota(jnp.int32, shape, 1) // HALF == which


def strips(first, last, size):
    return [slice(start, start + size) for start in range(first, last, size)]


def chunk(index, size):
    return pl.ds(pl.multiple_of(index * size, size), size)


def skew_bias(reversed_row, target):
    span, lanes = target.shape
    rows = pltpu.roll(jnp.broadcast_to(reversed_row, (8, reversed_row.shape[1])), 0, 1, stride=1, stride_axis=0)
    tiles = span // lanes
    for fine in range(lanes // 8):
        moved = rows if fine == 0 else pltpu.roll(rows, 8 * fine, 1)
        for coarse in range(tiles):
            place = 8 * (fine + lanes // 8 * coarse)
            target[place : place + 8, :] = moved[:, lanes * (tiles - coarse) : lanes * (tiles - coarse + 1)]


def gather_diagonals(source):
    span, lanes = source.shape
    tiles = span // lanes
    width = span + lanes
    blank = jnp.zeros((8, lanes), F32)
    found = None
    for fine in range(lanes // 8):
        places = [8 * (fine + lanes // 8 * coarse) for coarse in reversed(range(tiles))]
        line = jnp.concatenate([blank] + [source[place : place + 8, :] for place in places], 1)
        if fine > 0:
            line = pltpu.roll(line, width - 8 * fine, 1)
        found = line if found is None else found + line
    row = lax.broadcasted_iota(jnp.int32, found.shape, 0)
    for place in range(3):
        moved = pltpu.roll(found, width - (1 << place), 1)
        found = jnp.where((row // (1 << place)) % 2 == 1, moved, found)
    return jnp.sum(found, 0, keepdims=True)


def key_rows(query_block, blocks):
    reach = REACH // LANES
    return max(0, query_block - reach) * LANES, min(blocks, query_block + reach + 1) * LANES


def pick(mine, own, other, act):
    @pl.when(mine)
    def _():
        act(own)

    @pl.when(jnp.logical_not(mine))
    def _():
        act(other)


def bands_kernel(own_ref, other_ref, packs_ref, bands_hbm, band, store_sem):
    section = lax.axis_index("section")
    heads = band.shape[1]
    tables = own_ref.shape[0] - heads
    edge = jnp.zeros((1, REACH), F32)

    def store(layer):
        return pltpu.make_async_copy(band.at[layer], bands_hbm.at[layer], store_sem.at[layer])

    for layer in range(2):

        def fill(source):
            packs_ref[layer] = source[...]

        pick(section == layer, own_ref, other_ref, fill)

        @pl.loop(0, heads)
        def _(head):
            kept = packs_ref[layer, pl.ds(tables + head, 1), :]
            skew_bias(jnp.concatenate([edge, kept], 1), band.at[layer, head])

        store(layer).start()
    for layer in range(2):
        store(layer).wait()


def bands(own, other, heads, length):
    shape = (2, heads, 2 * length - LANES, LANES)
    return pl.pallas_call(
        bands_kernel,
        out_shape=[jax.ShapeDtypeStruct((2, *own.shape), F32), jax.ShapeDtypeStruct(shape, F32)],
        in_specs=vmem_specs(2),
        out_specs=vmem_specs(1) + hbm_specs(1),
        scratch_shapes=[pltpu.VMEM(shape, F32), pltpu.SemaphoreType.DMA((2,))],
        compiler_params=pltpu.CompilerParams(vmem_limit_bytes=VMEM_BYTES),
        name="bias_bands",
    )(own, other)


def attend_kernel(layer, pads, x_hbm, seg_ref, packs_ref, bands_hbm, *refs):
    wqkv_own, wqkv_other, wp_own, wp_other = refs[:4]
    refs = refs[4 + (ATTEND if layer > 0 else 0) :]
    stores = refs[:ATTEND]
    (bias, wqkv, wp, mask, h1, qkv, probs, mixed, proj, x1, h2, xin, wide_mixed, scales, held, load_sem, store_sem, prob_sem) = refs[ATTEND:]
    h1_o, qkv_o, prob_o, mixed_o, proj_o, x1_o, h2_o, xin_o, wide_o, scales_o = stores
    length, width = xin.shape
    heads = bias.shape[0]
    blocks = length // LANES
    section = lax.axis_index("section")
    mine = section == layer
    factor = HALF ** (-0.5)
    thirds = [pl.ds(part * width, width) for part in range(3)]

    def load(number):
        if number < 3:
            part = thirds[number]
            return wqkv_own.at[:, part], wqkv_other.at[:, part], wqkv.at[:, part], load_sem.at[number]
        return wp_own, wp_other, wp, load_sem.at[3]

    def start(number):
        own, other, target, sem = load(number)
        pick(mine, own, other, lambda source: pltpu.make_async_copy(source, target, sem).start())

    def wait(number):
        own, other, target, sem = load(number)
        pltpu.make_async_copy(target, target, sem).wait()

    def store(number, source, there):
        return pltpu.make_async_copy(source, there.at[layer], store_sem.at[number])

    def vector(row):
        return packs_ref[layer, row : row + 1, :]

    row = section if layer == 0 else 0
    pltpu.make_async_copy(x_hbm.at[row], xin, load_sem.at[4]).start()
    for number in range(3):
        start(number)
    pltpu.make_async_copy(xin, xin, load_sem.at[4]).wait()
    pltpu.make_async_copy(bands_hbm.at[layer], bias, load_sem.at[5]).start()
    segment = seg_ref[pl.ds(section, 1), :].astype(F32)
    key_segment = jnp.broadcast_to(segment, (LANES, length)).T

    for rows in strips(0, length, STRIP):
        scaled, _ = normalize(xin[rows, :].astype(F32))
        h1[rows, :] = (scaled * vector(GAIN1) + vector(SHIFT1)).astype(BF16)

    alive = length - pads[section]
    for place in range(blocks):
        lanes = slice(place * LANES, (place + 1) * LANES)
        for rows in strips(0, length, 64):
            key = lax.broadcasted_iota(jnp.int32, (64, LANES), 0) + rows.start
            query = lax.broadcasted_iota(jnp.int32, (64, LANES), 1) + place * LANES
            allowed = ((key_segment[rows] == segment[:, lanes]) & (key < alive)) | (key == query)
            mask[rows, lanes] = jnp.where(allowed, 0.0, -1000000000.0)

    store(0, h1, h1_o).start()
    store(7, xin, xin_o).start()
    for part in range(3):
        wait(part)
        columns = thirds[part]
        result = nn(h1[...], wqkv[:, columns])
        for rows in strips(0, length, STRIP):
            piece = result[rows]
            if part == 0:
                piece = (piece + vector(QBIAS)) * factor
            if part == 2:
                piece = piece + vector(VBIAS)
            qkv[rows, columns] = piece.astype(BF16)
    store(1, qkv, qkv_o).start()
    pltpu.make_async_copy(bias, bias, load_sem.at[5]).wait()
    start(3)
    together = 2 * GROUP

    def prob_store(group):
        return pltpu.make_async_copy(
            probs.at[group % 2], prob_o.at[layer, pl.ds(together * group, together)], prob_sem.at[group % 2]
        )

    def attend(side, within, pair):
        columns = chunk(pair, LANES)
        queries = qkv[:, columns]
        keys = qkv[:, pl.ds(pl.multiple_of(width + pair * LANES, LANES), LANES)]
        values = qkv[:, pl.ds(pl.multiple_of(2 * width + pair * LANES, LANES), LANES)].T
        outs = []
        for which in range(2):
            own_keys = jnp.where(half_mask(keys.shape, which), keys, jnp.zeros_like(keys))
            lines = []
            for wide in range(blocks // 2):
                scores = nt(own_keys, queries[2 * LANES * wide : 2 * LANES * (wide + 1)])
                for part in range(2):
                    place = 2 * wide + part
                    low, high = key_rows(place, blocks)
                    lanes = slice(place * LANES, (place + 1) * LANES)
                    first = (blocks - 1 - place) * LANES
                    spare = (2 * within + which) * blocks + place
                    highest = None
                    for rows in strips(low, high, 64):
                        here = (
                            scores[rows, part * LANES : (part + 1) * LANES]
                            + bias[2 * pair + which, first + rows.start : first + rows.stop, :]
                            + mask[rows, lanes]
                        )
                        held[spare, rows, :] = here
                        top = jnp.max(here.reshape(8, 8, LANES), 0)
                        highest = top if highest is None else jnp.maximum(highest, top)
                    highest = jnp.max(highest, 0, keepdims=True)
                    sums = jnp.zeros((8, LANES), F32)
                    for rows in strips(low, high, 64):
                        expo = jnp.exp(held[spare, rows, :] - highest)
                        probs[side, 2 * within + which, rows, lanes] = expo.astype(BF16)
                        sums = sums + fold(expo)
                    lines.append(1.0 / jnp.sum(sums, 0, keepdims=True))
                    if low > 0:
                        probs[side, 2 * within + which, :low, lanes] = jnp.zeros((low, LANES), BF16)
                    if high < length:
                        probs[side, 2 * within + which, high:, lanes] = jnp.zeros((length - high, LANES), BF16)
            scale = jnp.concatenate(lines, 1)
            scales[pl.ds(2 * pair + which, 1), :] = scale
            outs.append(nn(values[which * HALF : (which + 1) * HALF], probs[side, 2 * within + which]) * scale)
        out = jnp.concatenate(outs, 0).T
        wide_mixed[:, columns] = out
        mixed[:, columns] = out.astype(BF16)

    @pl.loop(0, heads // together)
    def _(group):
        @pl.when(group >= 2)
        def _():
            prob_store(group - 2).wait()

        for within in range(GROUP):
            attend(group % 2, within, GROUP * group + within)
        prob_store(group).start()

    store(3, mixed, mixed_o).start()
    store(8, wide_mixed, wide_o).start()
    store(9, scales, scales_o).start()
    wait(3)

    result = nn(mixed[...], wp[...])
    for rows in strips(0, length, STRIP):
        out = result[rows] + vector(PBIAS)
        proj[rows, :] = out.astype(BF16)
        resid = xin[rows, :].astype(F32) + vector(SCALE_A) * out
        x1[rows, :] = resid
        scaled, _ = normalize(resid)
        h2[rows, :] = (scaled * vector(GAIN2) + vector(SHIFT2)).astype(BF16)

    store(4, proj, proj_o).start()
    store(5, x1, x1_o).start()
    store(6, h2, h2_o).start()
    for group in range(max(0, heads // together - 2), heads // together):
        prob_store(group).wait()
    ends = {0: (h1, h1_o), 1: (qkv, qkv_o), 3: (mixed, mixed_o), 4: (proj, proj_o), 5: (x1, x1_o), 6: (h2, h2_o),
            7: (xin, xin_o), 8: (wide_mixed, wide_o), 9: (scales, scales_o)}
    for number, (source, there) in ends.items():
        store(number, source, there).wait()


def expand_kernel(layer, packs_ref, x1_hbm, h2_hbm, w1_own, w1_other, w2_own, w2_other, *refs):
    refs = refs[EXPAND if layer > 0 else 0 :]
    act_o, slope_o, mlp_o, y_o = refs[:EXPAND]
    (w1, w2, x1, h2, act, slope, mlp, out_row, load_sem, store_sem) = refs[EXPAND:]
    length, width = x1.shape
    hidden = w1.shape[1]
    mine = lax.axis_index("section") == layer

    def load(number):
        part = pl.ds((number % 4) * width, width)
        if number < 4:
            return w1_own.at[:, part], w1_other.at[:, part], w1.at[:, part], load_sem.at[number]
        return w2_own.at[part, :], w2_other.at[part, :], w2.at[part, :], load_sem.at[number]

    def start(number):
        own, other, target, sem = load(number)
        pick(mine, own, other, lambda source: pltpu.make_async_copy(source, target, sem).start())

    def wait(number):
        own, other, target, sem = load(number)
        pltpu.make_async_copy(target, target, sem).wait()

    def store(number, source, there):
        return pltpu.make_async_copy(source, there.at[layer], store_sem.at[number])

    def vector(row):
        return packs_ref[layer, row : row + 1, :]

    pltpu.make_async_copy(h2_hbm.at[layer], h2, load_sem.at[8]).start()
    for number in range(4):
        start(number)
    pltpu.make_async_copy(h2, h2, load_sem.at[8]).wait()
    for number in range(4, 8):
        start(number)
    pltpu.make_async_copy(x1_hbm.at[layer], x1, load_sem.at[9]).start()
    pieces = [
        (pl.ds(high * (length // 2), length // 2), pl.ds(part * width, width))
        for part in range(hidden // width)
        for high in range(2)
    ]

    def expand(number):
        rows, columns = pieces[number]
        if number % 2 == 0:
            wait(number // 2)
        return nn(h2[rows, :], w1[:, columns])

    coming = expand(0)
    totals = [None, None]
    for number, (rows, columns) in enumerate(pieces):
        current = coming
        if number + 1 < len(pieces):
            coming = expand(number + 1)
        for strip in strips(0, length // 2, STRIP):
            there = pl.ds(rows.start + strip.start, STRIP)
            here = current[strip] + vector(B1 + number // 2)
            normal = 0.5 * lax.erf(here * math.sqrt(0.5)) + 0.5
            density = jnp.exp(-0.5 * here * here) * (1.0 / math.sqrt(2.0 * math.pi))
            act[there, columns] = (here * normal).astype(BF16)
            slope[there, columns] = (normal + here * density).astype(BF16)
        if number % 2 == 0:
            wait(4 + number // 2)
        more = nn(act[rows, columns], w2[columns, :])
        totals[number % 2] = more if number < 2 else totals[number % 2] + more
    store(0, act, act_o).start()
    store(1, slope, slope_o).start()

    pltpu.make_async_copy(x1, x1, load_sem.at[9]).wait()
    for half in range(2):
        for strip in strips(0, length // 2, STRIP):
            rows = pl.ds(half * (length // 2) + strip.start, STRIP)
            out = totals[half][strip] + vector(B2)
            mlp[rows, :] = out.astype(BF16)
            out_row[rows, :] = (x1[rows, :] + vector(SCALE_M) * out).astype(BF16)

    store(2, mlp, mlp_o).start()
    store(3, out_row, y_o).start()
    for number, (source, there) in enumerate(((act, act_o), (slope, slope_o), (mlp, mlp_o), (out_row, y_o))):
        store(number, source, there).wait()


def hbm_specs(count):
    return [pl.BlockSpec(memory_space=pl.ANY)] * count


def vmem_specs(count):
    return [pl.BlockSpec(memory_space=pltpu.VMEM)] * count


def stacked(stored):
    return [jax.ShapeDtypeStruct((2, *shape), kind) for shape, kind in stored]


def attend(layer, pads, rows, segments, packs, band, weights, kept):
    length, width = rows.shape[1:]
    heads = band.shape[1]
    stored = [
        ((length, width), BF16),
        ((length, 3 * width), BF16),
        ((heads, length, length), BF16),
        ((length, width), BF16),
        ((length, width), BF16),
        ((length, width), F32),
        ((length, width), BF16),
        ((length, width), BF16),
        ((length, width), F32),
        ((heads, length), F32),
    ]
    scratch = [pltpu.VMEM(band.shape[1:], F32)] + [pltpu.VMEM(pair[0].shape, BF16) for pair in weights]
    scratch.append(pltpu.VMEM((length, length), F32))
    scratch += [
        pltpu.VMEM((2, 2 * GROUP, length, length) if n == 2 else shape, kind)
        for n, (shape, kind) in enumerate(stored)
    ]
    scratch += [
        pltpu.VMEM((2 * GROUP * length // LANES, length, LANES), F32),
        pltpu.SemaphoreType.DMA((6,)),
        pltpu.SemaphoreType.DMA((ATTEND,)),
        pltpu.SemaphoreType.DMA((2,)),
    ]
    operands = [pads, rows, segments, packs, band, *[x for pair in weights for x in pair]]
    held = ATTEND if layer > 0 else 0
    return pl.pallas_call(
        functools.partial(attend_kernel, layer),
        out_shape=stacked(stored),
        in_specs=[pl.BlockSpec(memory_space=pltpu.SMEM)] + hbm_specs(1) + vmem_specs(2) + hbm_specs(5 + held),
        out_specs=hbm_specs(ATTEND),
        scratch_shapes=scratch,
        input_output_aliases={len(operands) + n: n for n in range(held)},
        compiler_params=pltpu.CompilerParams(vmem_limit_bytes=VMEM_BYTES),
        name="forward_attention",
    )(*operands, *(kept if layer > 0 else ()))


def expand(layer, packs, x1, h2, weights, kept):
    length, width = x1.shape[1:]
    hidden = weights[0][0].shape[1]
    stored = [((length, hidden), BF16), ((length, hidden), BF16), ((length, width), BF16), ((length, width), BF16)]
    scratch = [pltpu.VMEM(pair[0].shape, BF16) for pair in weights]
    scratch += [pltpu.VMEM((length, width), F32), pltpu.VMEM((length, width), BF16)]
    scratch += [pltpu.VMEM(shape, kind) for shape, kind in stored]
    scratch += [pltpu.SemaphoreType.DMA((10,)), pltpu.SemaphoreType.DMA((EXPAND,))]
    operands = [packs, x1, h2, *[x for pair in weights for x in pair]]
    held = EXPAND if layer > 0 else 0
    return pl.pallas_call(
        functools.partial(expand_kernel, layer),
        out_shape=stacked(stored),
        in_specs=vmem_specs(1) + hbm_specs(6 + held),
        out_specs=hbm_specs(EXPAND),
        scratch_shapes=scratch,
        input_output_aliases={len(operands) + n: n for n in range(held)},
        compiler_params=pltpu.CompilerParams(vmem_limit_bytes=VMEM_BYTES),
        name="forward_mlp",
    )(*operands, *(kept if layer > 0 else ()))


def backward_kernel(layer, cotangent_hbm, packs_ref, *refs):
    weights, refs = refs[:8], refs[8:]
    (qkv_i, prob_i, mixed_i, proj_i, x1_i, slope_i, mlp_i, xin_i, scales_i) = refs[:9]
    refs = refs[9 + (7 if layer == 0 else 0) :]
    stores = refs[:7]
    (wqkv, wp, w1, w2, qkv, probs, mixed, proj, x1, slope, mlp, xin, scales, dm, dz, dproj, packed, dx_ref, dx1, dmixed, dscore, diag, sums, tables, g_ref, load_sem, store_sem, prob_sem) = refs[7:]
    dm_o, dz_o, dproj_o, packed_o, dx_o, tables_o, sums_o = stores
    wqkv_hbm, wp_hbm, w1_hbm, w2_hbm = zip(weights[::2], weights[1::2])
    length, width = g_ref.shape
    hidden = w1.shape[1]
    blocks = length // LANES
    pairs = width // LANES
    section = lax.axis_index("section")
    mine = section == layer
    factor = HALF ** (-0.5)
    parts = [pl.ds(part * width, width) for part in range(hidden // width)]
    loads = [(mlp_i.at[layer], mlp)]
    loads += [(tuple(x.at[part, :] for x in w2_hbm), w2.at[part, :]) for part in parts]
    loads += [(slope_i.at[layer], slope)]
    loads += [(tuple(x.at[:, part] for x in w1_hbm), w1.at[:, part]) for part in parts]
    early = len(loads)
    loads += [
        (x1_i.at[layer], x1), (proj_i.at[layer], proj), (wp_hbm, wp), (qkv_i.at[layer], qkv), (mixed_i.at[layer], mixed),
        (scales_i.at[layer], scales), (wqkv_hbm, wqkv), (xin_i.at[layer], xin),
    ]
    upstream_sem = load_sem.at[len(loads)]

    def start(number):
        source, target = loads[number]

        def go(ref):
            pltpu.make_async_copy(ref, target, load_sem.at[number]).start()

        if isinstance(source, tuple):
            pick(mine, *source, go)
        else:
            go(source)

    def load(number):
        target = loads[number][1]
        return pltpu.make_async_copy(target, target, load_sem.at[number])

    def store(number, source, there):
        return pltpu.make_async_copy(source, there.at[layer], store_sem.at[number])

    together = 2 * GROUP

    def prob_load(group):
        return pltpu.make_async_copy(
            prob_i.at[layer, pl.ds(together * group, together)], probs.at[group % 2], prob_sem.at[group % 2]
        )

    def vector(row):
        return packs_ref[layer, row : row + 1, :]

    def put(row, partial):
        sums[row : row + 1, :] = jnp.sum(partial, 0, keepdims=True)

    nothing = jnp.zeros((8, width), F32)

    upstream_hbm = cotangent_hbm.at[section] if layer == 1 else dx_o.at[1]
    pltpu.make_async_copy(upstream_hbm, g_ref, upstream_sem).start()
    for number in range(1 + len(parts)):
        start(number)
    pltpu.make_async_copy(g_ref, g_ref, upstream_sem).wait()
    load(0).wait()
    for number in range(1 + len(parts), early):
        start(number)
    scale_sum = bias_sum = nothing
    for rows in strips(0, length, STRIP):
        upstream = g_ref[rows, :].astype(F32)
        low = (upstream * vector(SCALE_M)).astype(BF16)
        dm[rows, :] = low
        scale_sum = scale_sum + fold(upstream * mlp[rows, :].astype(F32))
        bias_sum = bias_sum + fold(low.astype(F32))
    put(SCALE_M, scale_sum)
    put(B2, bias_sum)
    store(0, dm, dm_o).start()
    pieces = [
        (pl.ds(high * (length // 2), length // 2), pl.ds(part * width, width))
        for part in range(hidden // width)
        for high in range(2)
    ]

    def expand(number):
        rows, columns = pieces[number]
        if number % 2 == 0:
            load(1 + number // 2).wait()
        return nt(dm[rows, :], w2[columns, :])

    coming = expand(0)
    totals = [None, None]
    act_sum = nothing
    load(1 + len(parts)).wait()
    for number, (rows, columns) in enumerate(pieces):
        if number == 2:
            for later in range(early, len(loads)):
                start(later)
            prob_load(0).start()
        if number % 2 == 0:
            load(2 + len(parts) + number // 2).wait()
        current = coming
        if number + 1 < len(pieces):
            coming = expand(number + 1)
        for strip in strips(0, length // 2, STRIP):
            there = pl.ds(rows.start + strip.start, STRIP)
            low = (current[strip] * slope[there, columns].astype(F32)).astype(BF16)
            dz[there, columns] = low
            act_sum = act_sum + fold(low.astype(F32))
        if number % 2 == 1:
            put(B1 + number // 2, act_sum)
            act_sum = nothing
        more = nt(dz[rows, columns], w1[:, columns])
        totals[number % 2] = more if number < 2 else totals[number % 2] + more
    store(1, dz, dz_o).start()
    load(early).wait()
    load(early + 1).wait()
    found = [nothing] * 4
    for half in range(2):
        for strip in strips(0, length // 2, STRIP):
            rows = pl.ds(half * (length // 2) + strip.start, STRIP)
            upper = totals[half][strip]
            scaled, inverse = normalize(x1[rows, :])
            resid = g_ref[rows, :].astype(F32) + norm_back(upper * vector(GAIN2), scaled, inverse)
            dx1[rows, :] = resid
            low = (resid * vector(SCALE_A)).astype(BF16)
            dproj[rows, :] = low
            terms = (upper * scaled, upper, resid * proj[rows, :].astype(F32), low.astype(F32))
            found = [old + fold(term) for old, term in zip(found, terms)]
    for row, partial in zip((GAIN2, SHIFT2, SCALE_A, PBIAS), found):
        put(row, partial)
    store(2, dproj, dproj_o).start()
    load(early + 2).wait()
    dmixed[...] = nt(dproj[...], wp[...]).astype(BF16)
    for number in range(early + 3, early + 6):
        load(number).wait()

    def attend(side, within, pair):
        columns = chunk(pair, LANES)
        key_columns = pl.ds(pl.multiple_of(width + pair * LANES, LANES), LANES)
        value_columns = pl.ds(pl.multiple_of(2 * width + pair * LANES, LANES), LANES)
        values = qkv[:, value_columns]
        above = dmixed[:, columns]
        queries_t = qkv[:, columns].T
        keys_t = qkv[:, key_columns].T
        above_t = above.astype(F32).T
        products = (above.astype(F32) * mixed[:, columns]).T
        grads = [], [], []
        for which in range(2):
            place_in = 2 * within + which
            half = slice(which * HALF, (which + 1) * HALF)
            delta = jnp.sum(products[half], 0, keepdims=True)
            scale = scales[pl.ds(2 * pair + which, 1), :]
            own_values = jnp.where(half_mask(values.shape, which), values, jnp.zeros_like(values))
            edge = (blocks - 1) * LANES
            diag[place_in, :edge, :] = jnp.zeros((edge, LANES), F32)
            for wide in range(blocks // 2):
                prob_grad = nt(own_values, above[2 * LANES * wide : 2 * LANES * (wide + 1)])
                for part in range(2):
                    place = 2 * wide + part
                    low, high = key_rows(place, blocks)
                    lanes = slice(place * LANES, (place + 1) * LANES)
                    first_row = (blocks - 1 - place) * LANES
                    for rows in strips(low, high, 64):
                        here = (probs[side, place_in, rows, lanes].astype(F32) * scale[:, lanes]) * (
                            prob_grad[rows, part * LANES : (part + 1) * LANES] - delta[:, lanes]
                        )
                        dscore[place_in, rows, lanes] = here.astype(BF16)
                        there = slice(first_row + rows.start, first_row + rows.stop)
                        diag[place_in, there, :] = here if place == 0 else diag[place_in, there, :] + here
                    if low > 0:
                        dscore[place_in, :low, lanes] = jnp.zeros((low, LANES), BF16)
                    if high < length:
                        dscore[place_in, high:, lanes] = jnp.zeros((length - high, LANES), BF16)
                    if place == 0:
                        diag[place_in, edge + high :, :] = jnp.zeros((length - high, LANES), F32)
            line = gather_diagonals(diag.at[place_in])
            most = tables.shape[1] - LANES
            tables[pl.ds(2 * pair + which, 1), :] = jnp.concatenate(
                [line[:, REACH + 1 : REACH + 1 + most], line[:, REACH : REACH + LANES]], 1
            )
            grads[0].append(nn(keys_t[half], dscore[place_in]))
            grads[1].append(nt(queries_t[half], dscore[place_in]))
            grads[2].append(nt((above_t[half] * scale).astype(BF16), probs[side, place_in]))
        for found, where, scale in zip(grads, (columns, key_columns, value_columns), (factor, None, None)):
            low = jnp.concatenate(found, 0).astype(BF16)
            if scale is not None:
                low = (low.astype(F32) * scale).astype(BF16)
            packed[:, where] = low.T

    @pl.loop(0, pairs // GROUP)
    def _(group):
        prob_load(group).wait()

        @pl.when(group + 1 < pairs // GROUP)
        def _():
            prob_load(group + 1).start()

        for within in range(GROUP):
            attend(group % 2, within, GROUP * group + within)

    store(3, packed, packed_o).start()
    load(early + 6).wait()
    result = nt(packed[...], wqkv[...])
    load(early + 7).wait()
    found = [nothing] * 4
    for rows in strips(0, length, STRIP):
        upper = result[rows]
        scaled, inverse = normalize(xin[rows, :].astype(F32))
        dx_ref[rows, :] = (dx1[rows, :] + norm_back(upper * vector(GAIN1), scaled, inverse)).astype(BF16)
        terms = (
            upper * scaled,
            upper,
            packed[rows, :width].astype(F32),
            packed[rows, 2 * width :].astype(F32),
        )
        found = [old + fold(term) for old, term in zip(found, terms)]
    for row, partial in zip((GAIN1, SHIFT1, QBIAS, VBIAS), found):
        put(row, partial)
    store(4, dx_ref, dx_o).start()
    store(5, tables, tables_o).start()
    store(6, sums, sums_o).start()
    ends = {0: (dm, dm_o), 1: (dz, dz_o), 2: (dproj, dproj_o), 3: (packed, packed_o), 4: (dx_ref, dx_o), 5: (tables, tables_o), 6: (sums, sums_o)}
    for number, (source, there) in ends.items():
        store(number, source, there).wait()


def backward(layer, cotangent, packs, weights, saved, kept):
    length, width = cotangent.shape[1:]
    hidden = weights[2][0].shape[1]
    h1, qkv, probs, mixed, proj, x1, h2, xin, wide, scales, act, slope, mlp, y = saved
    heads = probs.shape[1]
    span = 2 * length - LANES
    summed = (16, width)
    table = (heads, 5 * LANES)
    stored = [
        ((length, width), BF16),
        ((length, hidden), BF16),
        ((length, width), BF16),
        ((length, 3 * width), BF16),
        ((length, width), BF16),
        (table, F32),
        (summed, F32),
    ]
    reads = [qkv, probs, wide, proj, x1, slope, mlp, xin, scales]
    scratch = [pltpu.VMEM(pair[0].shape, BF16) for pair in weights]
    scratch += [pltpu.VMEM((2, 2 * GROUP, length, length) if x is probs else x.shape[1:], x.dtype) for x in reads]
    scratch += [pltpu.VMEM(shape, kind) for shape, kind in stored[:5]]
    scratch += [
        pltpu.VMEM((length, width), F32),
        pltpu.VMEM((length, width), BF16),
        pltpu.VMEM((2 * GROUP, length, length), BF16),
        pltpu.VMEM((2 * GROUP, span, LANES), F32),
        pltpu.VMEM(summed, F32),
        pltpu.VMEM(table, F32),
        pltpu.VMEM((length, width), BF16),
        pltpu.SemaphoreType.DMA((19,)),
        pltpu.SemaphoreType.DMA((7,)),
        pltpu.SemaphoreType.DMA((2,)),
    ]
    operands = [cotangent, packs, *[x for pair in weights for x in pair], *reads]
    held = 7 if layer == 0 else 0
    return pl.pallas_call(
        functools.partial(backward_kernel, layer),
        out_shape=stacked(stored),
        in_specs=hbm_specs(1) + vmem_specs(1) + hbm_specs(8 + len(reads) + held),
        out_specs=hbm_specs(7),
        scratch_shapes=scratch,
        input_output_aliases={len(operands) + n: n for n in range(held)},
        compiler_params=pltpu.CompilerParams(vmem_limit_bytes=VMEM_BYTES),
        name="backward_layer",
    )(*operands, *(kept if layer == 0 else ()))


def small_lines(width):
    lines = width // LANES
    places = [(row, tile, row * lines + tile) for row in range(10) for tile in range(lines)]
    return places + [(B1, tile, B1 * lines + tile) for tile in range(4 * lines)]


def reverse_lanes(values):
    lane = lax.broadcasted_iota(jnp.int32, values.shape, 1)
    for place in range(LANES.bit_length() - 1):
        step = 1 << place
        up, down = pltpu.roll(values, step, 1), pltpu.roll(values, LANES - step, 1)
        values = jnp.where((lane // step) % 2 == 1, up, down)
    return values


def widen_kernel(sum_hbm, small_ref, *refs):
    bigs, vectors, table_ref = refs[:4], refs[4 : 5 + VECTORS], refs[5 + VECTORS]
    narrow, wide, load_sem, store_sem = refs[6 + VECTORS :]
    depth, width = narrow.shape[:2]
    blocks = [(0, slice(b * width, (b + 1) * width), slice(0, width)) for b in range(4)]
    for target, count in ((1, 4), (2, 3), (3, 1)):
        blocks += [(target, slice(0, width), slice(b * width, (b + 1) * width)) for b in range(count)]

    def load(block):
        rows = pl.ds(block * width, width)
        return pltpu.make_async_copy(sum_hbm.at[rows, :], narrow.at[block % depth], load_sem.at[block % depth])

    def store(block):
        target, rows, columns = blocks[block]
        there = bigs[target].at[rows, columns]
        return pltpu.make_async_copy(wide.at[block % depth], there, store_sem.at[block % depth])

    for block in range(depth):
        load(block).start()
    for block in range(len(blocks)):
        load(block).wait()
        if block >= depth:
            store(block - depth).wait()
        for rows in strips(0, width, 64):
            wide[block % depth, rows, :] = narrow[block % depth, rows, :].astype(F32)
        store(block).start()
        if block + depth < len(blocks):
            load(block + depth).start()
    places = small_lines(width)
    for row, tile, line in places:
        vectors[row][:, tile * LANES : (tile + 1) * LANES] = small_ref[line : line + 1, :]
    first = len(places)
    heads, entries = table_ref.shape
    tiles = -(-entries // LANES)
    flipped = reverse_lanes(small_ref[first : first + heads * tiles, :])
    for head in range(heads):
        for tile in range(tiles - 1):
            line = head * tiles + tile
            there = (tiles - 2 - tile) * LANES
            table_ref[head : head + 1, there : there + LANES] = flipped[line : line + 1]
        line = first + head * tiles + tiles - 1
        table_ref[head : head + 1, entries - 1 :] = small_ref[line : line + 1, 0:1]
    for block in range(len(blocks) - depth, len(blocks)):
        store(block).wait()


def widen(summed, small, width, heads, entries):
    shapes = [(4 * width, width), (width, 4 * width), (width, 3 * width), (width, width)]
    shapes += [(1, width)] * 10 + [(1, 4 * width), (heads, entries)]
    return pl.pallas_call(
        widen_kernel,
        out_shape=[jax.ShapeDtypeStruct(shape, F32) for shape in shapes],
        in_specs=hbm_specs(1) + vmem_specs(1),
        out_specs=hbm_specs(4) + vmem_specs(VECTORS + 2),
        scratch_shapes=[
            pltpu.VMEM((3, width, width), BF16),
            pltpu.VMEM((3, width, width), F32),
            pltpu.SemaphoreType.DMA((3,)),
            pltpu.SemaphoreType.DMA((3,)),
        ],
        compiler_params=pltpu.CompilerParams(vmem_limit_bytes=VMEM_BYTES),
        name="widen",
    )(summed, small)


BLOCK = 256
LAG = 3


def reduce_kernel(bits, chunks, blocks, lags, window, *refs):
    (a_ref, dm_ref, h2_ref, dz_ref, h1_ref, dp_ref, o_ref, dproj_ref, y_ref, dx_ref, sums_ref, tables_ref) = refs[:12]
    out_ref, small_out_ref, y_out, dx_out = refs[12:16]
    refs = refs[16:]
    (lhs, rhs, grads, total, crossing, landed, smalls, small_ref, small_landed, small_total, *received) = refs[: 10 + 2 * bits]
    (load_sem, send_sem, recv_sem, small_send, small_recv, store_sem, cross_send, cross_recv, row_sem, credit) = refs[10 + 2 * bits :]
    small_received = received[bits:]
    me = lax.axis_index("dp")
    section = lax.axis_index("section")
    beside = 1 - section
    rows = BLOCK * blocks
    width = grads.shape[1]
    per_side = width // BLOCK
    last = 2 * bits
    starts = [0] + [lags[0] + lags[1] * place for place in range(last + 1)]

    barrier = pltpu.get_barrier_semaphore()
    for place in range(bits):
        stride = 1 << place
        other = me + stride * (1 - 2 * ((me // stride) % 2))
        pl.semaphore_signal(barrier, inc=1, device_id={"dp": other}, device_id_type=MESH)
    pl.semaphore_signal(barrier, inc=1, device_id={"section": beside}, device_id_type=MESH)
    pl.semaphore_wait(barrier, bits + 1)

    def across(source, target, number):
        return pltpu.make_async_remote_copy(
            src_ref=source,
            dst_ref=target,
            send_sem=cross_send.at[number],
            recv_sem=cross_recv.at[number],
            device_id={"section": beside},
            device_id_type=MESH,
        )

    def row_copy(number):
        source, target = ((y_ref, y_out), (dx_ref, dx_out))[number]
        return pltpu.make_async_copy(source.at[section], target.at[section], row_sem.at[number])

    def row_across(number):
        source, target = ((y_ref, y_out), (dx_ref, dx_out))[number]
        return across(source.at[beside], target.at[section], window + 1 + number)

    families = (
        (a_ref, dm_ref, 4 * per_side, True),
        (h2_ref, dz_ref, 4 * per_side, False),
        (h1_ref, dp_ref, 3 * per_side, False),
        (o_ref, dproj_ref, per_side, False),
    )
    n_blocks = 12 * per_side

    def load(block):
        slot = block % 2
        first = 0
        for left, right, count, walks in families:
            @pl.when((block >= first) & (block < first + count))
            def _():
                local = block - first
                if walks:
                    left_column = local * BLOCK
                    right_column = 0
                else:
                    left_column = (local % per_side) * BLOCK
                    right_column = (local // per_side) * width
                for number, layer in enumerate((section, beside)):
                    pltpu.make_async_copy(
                        left.at[layer, :, pl.ds(pl.multiple_of(left_column, BLOCK), BLOCK)],
                        lhs.at[slot, number],
                        load_sem.at[0, slot],
                    ).start()
                    pltpu.make_async_copy(
                        right.at[layer, :, pl.ds(pl.multiple_of(right_column, BLOCK), width)],
                        rhs.at[slot, number],
                        load_sem.at[1, slot],
                    ).start()
            first += count

    def produce(block, sub, side):
        slot = block % 2
        pltpu.make_async_copy(lhs.at[slot], lhs.at[slot], load_sem.at[0, slot]).wait()
        pltpu.make_async_copy(rhs.at[slot], rhs.at[slot], load_sem.at[1, slot]).wait()

        @pl.when(block + 1 < n_blocks)
        def _():
            load(block + 1)

        crossing[side, sub * BLOCK : (sub + 1) * BLOCK, :] = dot(lhs[slot, 1], rhs[slot, 1], 0, 0).astype(BF16)
        grads[chunk(block, BLOCK), :] = dot(lhs[slot, 0], rhs[slot, 0], 0, 0).astype(BF16)

    def turn(chunk):
        place = chunk % 9
        return place % 2 + place // 5 - place // 6

    def partner(rotation, stage):
        stride = lax.shift_left(jnp.int32(1), (stage + rotation) % bits)
        mine = (me // stride) % 2
        return mine, me + stride * (1 - 2 * mine)

    def offset(base, height, rotation, stage):
        for earlier in range(stage):
            mine, _ = partner(rotation, earlier)
            base = base + mine * (height >> (earlier + 1))
        return base

    def piece(ref, start, size):
        return ref.at[pl.ds(pl.multiple_of(start, size), size)]

    def send(position, base, height, rotation, source, landing, result, slot, sems):
        send_at, recv_at = sems
        if position < bits:
            stage = position
            half = height >> (stage + 1)
            mine, other = partner(rotation, stage)
            start = offset(base, height, rotation, stage) + (1 - mine) * half
            src, dst = piece(source, start, half), landing[stage].at[slot]
        else:
            stage = last - 1 - position
            half = height >> (stage + 1)
            mine, other = partner(rotation, stage)
            start = offset(base, height, rotation, stage + 1)
            src = dst = piece(result, start, half)
        return pltpu.make_async_remote_copy(
            src_ref=src,
            dst_ref=dst,
            send_sem=send_at.at[position],
            recv_sem=recv_at.at[position, slot],
            device_id={"dp": other},
            device_id_type=MESH,
        )

    def take(position, base, height, rotation, source, landing, result, slot, sems):
        send(position - 1, base, height, rotation, source, landing, result, slot, sems).wait_recv()
        stage = position - 1
        if stage < bits:
            half = height >> (stage + 1)
            start = pl.multiple_of(offset(base, height, rotation, stage + 1), half)
            keep = pl.ds(start, half)
            value = source[keep, :].astype(jnp.float32) + landing[stage][slot].astype(jnp.float32)
            target = result if stage == bits - 1 else source
            target[keep, :] = value.astype(target.dtype)

    def step(position, *way):
        if position > 0:
            take(position, *way)
        if position < last:
            send(position, *way).start()

    main = (grads, received[:bits], total)
    main_sems = (send_sem, recv_sem)

    def cross(side):
        return across(crossing.at[side], landed.at[side], side)

    def give(part):
        side = part % window

        @pl.when(part >= window)
        def _():
            cross(side).wait_send()
            pl.semaphore_wait(credit, 1)

        for sub in range(blocks):
            block = part * blocks + sub

            @pl.when(block < n_blocks)
            def _():
                produce(block, sub, side)

        cross(side).start()

    def join(part):
        side = part % window
        cross(side).wait_recv()
        there = chunk(part, rows)
        grads[there, :] = (grads[there, :].astype(F32) + landed[side].astype(F32)).astype(BF16)

        @pl.when(part < chunks - window)
        def _():
            pl.semaphore_signal(credit, inc=1, device_id={"section": beside}, device_id_type=MESH)

    def walk(position, part):
        if position == 0:
            join(part)
        base = part * rows
        step(position, base, rows, turn(part), *main, part, main_sems)
        if position == last:
            there = pl.ds(pl.multiple_of(base, rows), rows)
            pltpu.make_async_copy(total.at[there], out_ref.at[there], store_sem.at[0]).start()

    def small_cross():
        return across(smalls.at[beside], small_landed, window)

    def walk_small(position):
        height = small_ref.shape[0]
        if position == 0:
            small_cross().wait_recv()
            small_ref[...] = smalls[section] + small_landed[...]
        way = (0, height, 0, small_ref, small_received, small_total, 0, (small_send, small_recv))
        step(position, *way)

    load(jnp.int32(0))
    smalls[...] = jnp.zeros_like(smalls)
    places = small_lines(width)
    for layer in range(2):
        for row, tile, line in places:
            if row == B1:
                row, tile = B1 + tile // (width // LANES), tile % (width // LANES)
            smalls[layer, line : line + 1, :] = sums_ref[layer, row : row + 1, tile * LANES : (tile + 1) * LANES]
        line = len(places)
        for head in range(tables_ref.shape[1]):
            for tile in range(tables_ref.shape[2] // LANES):
                lanes = slice(tile * LANES, (tile + 1) * LANES)
                smalls[layer, line : line + 1, :] = tables_ref[layer, head : head + 1, lanes]
                line += 1
    small_cross().start()
    for number in range(2):
        row_copy(number).start()
        row_across(number).start()

    @pl.loop(0, chunks + starts[-1])
    def _(tick):
        @pl.when(tick < chunks)
        def _():
            give(tick)

        for position in range(last + 1):
            part = tick - starts[position + 1]

            @pl.when((part >= 0) & (part < chunks))
            def _():
                walk(position, part)

            @pl.when(part == 0)
            def _():
                walk_small(position)

    small_out_ref[...] = small_total[...]
    for position in range(last):
        stage = position if position < bits else last - 1 - position
        size = received[stage]
        pltpu.make_async_copy(size, size, send_sem.at[position]).wait()
        size = small_received[stage]
        pltpu.make_async_copy(size, size, small_send.at[position]).wait()
    for side in range(window):
        cross(side).wait_send()
    small_cross().wait_send()
    for number in range(2):
        row_copy(number).wait()
        row_across(number).wait()
    pltpu.make_async_copy(total, out_ref, store_sem.at[0]).wait()


def reduce_gradients(a, dm, h2, dz, h1, packed, o, dproj, y, dx, sums, tables):
    parts = lax.axis_size("dp")
    bits = parts.bit_length() - 1
    blocks = max(1, 16 * parts // BLOCK)
    layers, length, width = h1.shape
    n_blocks = 12 * width // BLOCK
    chunks = -(-n_blocks // blocks)
    rows = BLOCK * blocks
    lags, window = ((2, LAG), 4) if blocks == 1 else ((0, LAG), 1)
    lines = len(small_lines(width)) + tables.shape[1] * tables.shape[2] // LANES
    height = -(-lines // (8 * parts)) * 8 * parts
    small = (height, LANES)
    return pl.pallas_call(
        functools.partial(reduce_kernel, bits, chunks, blocks, lags, window),
        out_shape=(
            jax.ShapeDtypeStruct((chunks * rows, width), BF16),
            jax.ShapeDtypeStruct(small, F32),
            jax.ShapeDtypeStruct(y.shape, BF16),
            jax.ShapeDtypeStruct(dx.shape, BF16),
        ),
        in_specs=hbm_specs(10) + vmem_specs(2),
        out_specs=hbm_specs(1) + vmem_specs(1) + hbm_specs(2),
        scratch_shapes=[
            pltpu.VMEM((2, layers, length, BLOCK), BF16),
            pltpu.VMEM((2, layers, length, width), BF16),
            pltpu.VMEM((chunks * rows, width), BF16),
            pltpu.VMEM((chunks * rows, width), BF16),
            pltpu.VMEM((window, rows, width), BF16),
            pltpu.VMEM((window, rows, width), BF16),
            pltpu.VMEM((layers, *small), F32),
            pltpu.VMEM(small, F32),
            pltpu.VMEM(small, F32),
            pltpu.VMEM(small, F32),
            *[pltpu.VMEM((chunks, rows >> (s + 1), width), BF16) for s in range(bits)],
            *[pltpu.VMEM((1, height >> (s + 1), LANES), F32) for s in range(bits)],
            pltpu.SemaphoreType.DMA((2, 2)),
            pltpu.SemaphoreType.DMA((2 * bits,)),
            pltpu.SemaphoreType.DMA((2 * bits, chunks)),
            pltpu.SemaphoreType.DMA((2 * bits,)),
            pltpu.SemaphoreType.DMA((2 * bits, 1)),
            pltpu.SemaphoreType.DMA((1,)),
            pltpu.SemaphoreType.DMA((window + 3,)),
            pltpu.SemaphoreType.DMA((window + 3,)),
            pltpu.SemaphoreType.DMA((2,)),
            pltpu.SemaphoreType.REGULAR,
        ],
        compiler_params=pltpu.CompilerParams(
            collective_id=0, has_side_effects=True, vmem_limit_bytes=VMEM_BYTES
        ),
        name="reduce_gradients",
    )(a, dm, h2, dz, h1, packed, o, dproj, y, dx, sums, tables)


def swapped(block):
    return lax.ppermute(block, "section", [(0, 1), (1, 0)])


def per_device(
    patches,
    segment_ids,
    pad_counts,
    norm1_gain,
    norm1_bias,
    qkv_weight,
    query_bias,
    value_bias,
    rel_table,
    proj_weight,
    proj_bias,
    scale_attn,
    norm2_gain,
    norm2_bias,
    fc1_weight,
    fc1_bias,
    fc2_weight,
    fc2_bias,
    scale_mlp,
    cotangent,
):
    micro, length, width = patches.shape
    heads, entries = rel_table.shape[1:]
    own = jnp.concatenate(
        [
            norm1_gain,
            norm1_bias,
            query_bias,
            value_bias,
            proj_bias,
            scale_attn,
            norm2_gain,
            norm2_bias,
            fc2_bias,
            scale_mlp,
            fc1_bias.reshape(-1, width),
            jnp.pad(rel_table[0, :, ::-1], ((0, 0), (0, width - entries))),
        ],
        0,
    )
    own_weights = (qkv_weight[0], proj_weight[0], fc1_weight[0], fc2_weight[0])
    other = swapped(own)
    weights = [(x, swapped(x)) for x in own_weights]
    packs, band = bands(own, other, heads, length)
    attended = expanded = None
    rows = patches
    for layer in range(2):
        attended = attend(layer, pad_counts, rows, segment_ids, packs, band, weights[:2], attended)
        expanded = expand(layer, packs, attended[5], attended[6], weights[2:], expanded)
        rows = expanded[3]
    saved = [*attended, *expanded]
    kept = None
    for layer in (1, 0):
        kept = backward(layer, cotangent, packs, weights, saved, kept)
    dm, dz, dproj, packed, dx, tables, sums = kept
    h1, mixed, h2, act, y = saved[0], saved[3], saved[6], saved[10], saved[13]
    summed, small, outputs, in_grads = reduce_gradients(
        act, dm, h2, dz, h1, packed, mixed, dproj, y, dx, sums, tables
    )
    fc2_grad, fc1_grad, qkv_grad, proj_grad, *small_grads = widen(
        summed, small, width, heads, entries
    )
    table_grad = small_grads[VECTORS + 1]
    return (
        outputs[None],
        in_grads[None],
        small_grads[GAIN1],
        small_grads[SHIFT1],
        qkv_grad[None],
        small_grads[QBIAS],
        small_grads[VBIAS],
        table_grad[None],
        proj_grad[None],
        small_grads[PBIAS],
        small_grads[SCALE_A],
        small_grads[GAIN2],
        small_grads[SHIFT2],
        fc1_grad[None],
        small_grads[B1],
        fc2_grad[None],
        small_grads[B2],
        small_grads[SCALE_M],
    )


def solution(mesh):
    placed = (
        P("dp", None, None),
        P("dp", None),
        P("dp"),
        P("section", None),
        P("section", None),
        P("section", None, None),
        P("section", None),
        P("section", None),
        P("section", None, None),
        P("section", None, None),
        P("section", None),
        P("section", None),
        P("section", None),
        P("section", None),
        P("section", None, None),
        P("section", None),
        P("section", None, None),
        P("section", None),
        P("section", None),
        P("dp", None, None),
    )
    return jax.shard_map(
        per_device,
        mesh=mesh,
        in_specs=placed,
        out_specs=(
            P("section", "dp", None, None),
            P("section", "dp", None, None),
            P("section", None),
            P("section", None),
            P("section", None, None),
            P("section", None),
            P("section", None),
            P("section", None, None),
            P("section", None, None),
            P("section", None),
            P("section", None),
            P("section", None),
            P("section", None),
            P("section", None, None),
            P("section", None),
            P("section", None, None),
            P("section", None),
            P("section", None),
        ),
        check_vma=False,
    )
```

```python
import functools
import math

import jax
import jax.numpy as jnp
from jax import lax
from jax.experimental import pallas as pl
from jax.experimental.pallas import tpu as pltpu
from jax.sharding import PartitionSpec as P

MESH = pl.DeviceIdType.MESH
BF16, F32 = jnp.bfloat16, jnp.float32
VMEM_BYTES = 60 * 1024 * 1024
LANES = 128
HALF = 64
REACH = 2 * LANES
GAIN1, SHIFT1, QBIAS, VBIAS, PBIAS, SCALE_A, GAIN2, SHIFT2, B2, SCALE_M, B1 = range(11)
VECTORS = 10
STORED = 14
STRIP = 16
GROUP = 2


def dot(left, right, left_dim, right_dim):
    return lax.dot_general(
        left, right, (((left_dim,), (right_dim,)), ((), ())), preferred_element_type=F32
    )


def nn(left, right):
    return dot(left, right, 1, 0)


def nt(left, right):
    return dot(left, right, 1, 1)


def normalize(values):
    centered = values - jnp.mean(values, -1, keepdims=True)
    inverse = lax.rsqrt(jnp.mean(centered * centered, -1, keepdims=True) + 1e-06)
    return centered * inverse, inverse


def norm_back(upper, scaled, inverse):
    return inverse * (
        upper
        - jnp.mean(upper, -1, keepdims=True)
        - scaled * jnp.mean(upper * scaled, -1, keepdims=True)
    )


def fold(values):
    return jnp.sum(values.reshape(values.shape[0] // 8, 8, values.shape[1]), 0)


def half_mask(shape, which):
    return lax.broadcasted_iota(jnp.int32, shape, 1) // HALF == which


def strips(first, last, size):
    return [slice(start, start + size) for start in range(first, last, size)]


def chunk(index, size):
    return pl.ds(pl.multiple_of(index * size, size), size)


def skew_bias(reversed_row, target):
    span, lanes = target.shape
    rows = pltpu.roll(jnp.broadcast_to(reversed_row, (8, reversed_row.shape[1])), 1, 1, stride=1, stride_axis=0)
    tiles = span // lanes
    for fine in range(lanes // 8):
        moved = rows if fine == 0 else pltpu.roll(rows, 8 * fine, 1)
        for coarse in range(tiles):
            place = 8 * (fine + lanes // 8 * coarse)
            target[place : place + 8, :] = moved[:, lanes * (tiles - coarse) : lanes * (tiles - coarse + 1)]


def gather_diagonals(source):
    span, lanes = source.shape
    tiles = span // lanes
    width = span + lanes
    blank = jnp.zeros((8, lanes), F32)
    found = None
    for fine in range(lanes // 8):
        places = [8 * (fine + lanes // 8 * coarse) for coarse in reversed(range(tiles))]
        line = jnp.concatenate([blank] + [source[place : place + 8, :] for place in places], 1)
        if fine > 0:
            line = pltpu.roll(line, width - 8 * fine, 1)
        found = line if found is None else found + line
    row = lax.broadcasted_iota(jnp.int32, found.shape, 0)
    for place in range(3):
        moved = pltpu.roll(found, width - (1 << place), 1)
        found = jnp.where((row // (1 << place)) % 2 == 1, moved, found)
    return jnp.sum(found, 0, keepdims=True)


def key_rows(query_block, blocks):
    reach = REACH // LANES
    return max(0, query_block - reach) * LANES, min(blocks, query_block + reach + 1) * LANES


def pick(mine, own, other, act):
    @pl.when(mine)
    def _():
        act(own)

    @pl.when(jnp.logical_not(mine))
    def _():
        act(other)


def pack_kernel(*refs):
    *vectors, bias_ref, table_ref, pack_ref = refs
    width = pack_ref.shape[1]
    heads, entries = table_ref.shape[1:]
    pack_ref[...] = jnp.zeros_like(pack_ref)
    for row, vector in enumerate(vectors):
        pack_ref[row : row + 1, :] = vector[...]
    for part in range(bias_ref.shape[1] // width):
        pack_ref[B1 + part : B1 + part + 1, :] = bias_ref[:, part * width : (part + 1) * width]
    first = pack_ref.shape[0] - heads
    tiles = entries // LANES
    lane = lax.broadcasted_iota(jnp.int32, (heads, LANES), 1)
    ending = jnp.broadcast_to(table_ref[0, :, entries - 1 :], (heads, LANES))
    pack_ref[first:, :LANES] = jnp.where(lane == LANES - 1, ending, 0.0)
    for tile in range(tiles):
        there = (tiles - tile) * LANES
        pack_ref[first:, there : there + LANES] = reverse_lanes(table_ref[0, :, tile * LANES : (tile + 1) * LANES])


def pack(vectors, rel_table):
    heads = rel_table.shape[1]
    return pl.pallas_call(
        pack_kernel,
        out_shape=jax.ShapeDtypeStruct((16 + heads, vectors[0].shape[1]), F32),
        in_specs=vmem_specs(len(vectors) + 1),
        out_specs=pl.BlockSpec(memory_space=pltpu.VMEM),
        name="pack_vectors",
    )(*vectors, rel_table)


def bands_kernel(own_ref, other_ref, packs_ref, bands_hbm, band, store_sem):
    section = lax.axis_index("section")
    heads = band.shape[1]
    tables = own_ref.shape[0] - heads
    edge = jnp.zeros((1, LANES), F32)

    def store(layer):
        return pltpu.make_async_copy(band.at[layer], bands_hbm.at[layer], store_sem.at[layer])

    for layer in range(2):

        def fill(source):
            packs_ref[layer] = source[...]

        pick(section == layer, own_ref, other_ref, fill)

        @pl.loop(0, heads // 4)
        def _(group):
            for within in range(4):
                head = 4 * group + within
                kept = packs_ref[layer, pl.ds(tables + head, 1), :]
                skew_bias(jnp.concatenate([edge, kept, edge], 1), band.at[layer, head])

        store(layer).start()
    for layer in range(2):
        store(layer).wait()


def bands(own, other, heads, length):
    shape = (2, heads, 2 * length - LANES, LANES)
    return pl.pallas_call(
        bands_kernel,
        out_shape=[jax.ShapeDtypeStruct((2, *own.shape), F32), jax.ShapeDtypeStruct(shape, F32)],
        in_specs=vmem_specs(2),
        out_specs=vmem_specs(1) + hbm_specs(1),
        scratch_shapes=[pltpu.VMEM(shape, F32), pltpu.SemaphoreType.DMA((2,))],
        compiler_params=pltpu.CompilerParams(vmem_limit_bytes=VMEM_BYTES),
        name="bias_bands",
    )(own, other)


def forward_kernel(layer, pads, x_hbm, seg_ref, packs_ref, bands_hbm, *refs):
    wqkv_own, wqkv_other, wp_own, wp_other, w1_own, w1_other, w2_own, w2_other = refs[:8]
    refs = refs[8 + (STORED if layer > 0 else 0) :]
    stores = refs[:STORED]
    (bias, wqkv, wp, w1, w2, mask, h1, qkv, probs, mixed, proj, x1, h2, xin, wide_mixed, scales, act, slope, mlp, out_row, held, load_sem, store_sem, prob_sem) = refs[STORED:]
    h1_o, qkv_o, prob_o, mixed_o, proj_o, x1_o, h2_o, xin_o, wide_o, scales_o, act_o, slope_o, mlp_o, y_o = stores
    hidden = w1.shape[1]
    length, width = xin.shape
    heads = bias.shape[0]
    blocks = length // LANES
    section = lax.axis_index("section")
    mine = section == layer
    factor = HALF ** (-0.5)
    thirds = [pl.ds(part * width, width) for part in range(3)]

    def load(number):
        if number < 3:
            part = thirds[number]
            return wqkv_own.at[:, part], wqkv_other.at[:, part], wqkv.at[:, part], load_sem.at[number]
        if number == 3:
            return wp_own, wp_other, wp, load_sem.at[3]
        part = pl.ds((number % 4) * width, width)
        if number < 8:
            return w1_own.at[:, part], w1_other.at[:, part], w1.at[:, part], load_sem.at[number]
        return w2_own.at[part, :], w2_other.at[part, :], w2.at[part, :], load_sem.at[number]

    def start(number):
        own, other, target, sem = load(number)
        pick(mine, own, other, lambda source: pltpu.make_async_copy(source, target, sem).start())

    def wait(number):
        own, other, target, sem = load(number)
        pltpu.make_async_copy(target, target, sem).wait()

    def store(number, source, there):
        return pltpu.make_async_copy(source, there.at[layer], store_sem.at[number])

    def part_store(number, source, there, columns):
        return pltpu.make_async_copy(source.at[:, columns], there.at[layer, :, columns], store_sem.at[number])

    def vector(row):
        return packs_ref[layer, row : row + 1, :]

    source = x_hbm.at[section] if layer == 0 else y_o.at[0]
    pltpu.make_async_copy(source, xin, load_sem.at[12]).start()
    for number in range(3):
        start(number)
    pltpu.make_async_copy(xin, xin, load_sem.at[12]).wait()
    pltpu.make_async_copy(bands_hbm.at[layer], bias, load_sem.at[13]).start()
    segment = seg_ref[pl.ds(section, 1), :].astype(F32)
    key_segment = jnp.broadcast_to(segment, (LANES, length)).T

    for rows in strips(0, length, STRIP):
        scaled, _ = normalize(xin[rows, :].astype(F32))
        h1[rows, :] = (scaled * vector(GAIN1) + vector(SHIFT1)).astype(BF16)

    alive = length - pads[section]
    for place in range(blocks):
        lanes = slice(place * LANES, (place + 1) * LANES)
        for rows in strips(0, length, 64):
            key = lax.broadcasted_iota(jnp.int32, (64, LANES), 0) + rows.start
            query = lax.broadcasted_iota(jnp.int32, (64, LANES), 1) + place * LANES
            allowed = ((key_segment[rows] == segment[:, lanes]) & (key < alive)) | (key == query)
            mask[rows, lanes] = jnp.where(allowed, 0.0, -1000000000.0)

    store(0, h1, h1_o).start()
    store(7, xin, xin_o).start()
    for part in range(3):
        wait(part)
        columns = thirds[part]
        result = nn(h1[...], wqkv[:, columns])
        for rows in strips(0, length, STRIP):
            piece = result[rows]
            if part == 0:
                piece = (piece + vector(QBIAS)) * factor
            if part == 2:
                piece = piece + vector(VBIAS)
            qkv[rows, columns] = piece.astype(BF16)
    store(1, qkv, qkv_o).start()
    pltpu.make_async_copy(bias, bias, load_sem.at[13]).wait()
    for number in range(3, 12):
        start(number)
    together = 2 * GROUP

    def prob_store(group):
        return pltpu.make_async_copy(
            probs.at[group % 2], prob_o.at[layer, pl.ds(together * group, together)], prob_sem.at[group % 2]
        )

    def attend(side, within, pair):
        columns = chunk(pair, LANES)
        queries = qkv[:, columns]
        keys = qkv[:, pl.ds(pl.multiple_of(width + pair * LANES, LANES), LANES)]
        values = qkv[:, pl.ds(pl.multiple_of(2 * width + pair * LANES, LANES), LANES)].T
        outs = []
        for which in range(2):
            own_keys = jnp.where(half_mask(keys.shape, which), keys, jnp.zeros_like(keys))
            lines = []
            for wide in range(blocks // 2):
                scores = nt(own_keys, queries[2 * LANES * wide : 2 * LANES * (wide + 1)])
                for part in range(2):
                    place = 2 * wide + part
                    low, high = key_rows(place, blocks)
                    lanes = slice(place * LANES, (place + 1) * LANES)
                    first = (blocks - 1 - place) * LANES
                    spare = (2 * within + which) * blocks + place
                    highest = None
                    for rows in strips(low, high, 64):
                        here = (
                            scores[rows, part * LANES : (part + 1) * LANES]
                            + bias[2 * pair + which, first + rows.start : first + rows.stop, :]
                            + mask[rows, lanes]
                        )
                        held[spare, rows, :] = here
                        top = jnp.max(here.reshape(8, 8, LANES), 0)
                        highest = top if highest is None else jnp.maximum(highest, top)
                    highest = jnp.max(highest, 0, keepdims=True)
                    sums = jnp.zeros((8, LANES), F32)
                    for rows in strips(low, high, 64):
                        expo = jnp.exp(held[spare, rows, :] - highest)
                        probs[side, 2 * within + which, rows, lanes] = expo.astype(BF16)
                        sums = sums + fold(expo)
                    lines.append(1.0 / jnp.sum(sums, 0, keepdims=True))
                    if low > 0:
                        probs[side, 2 * within + which, :low, lanes] = jnp.zeros((low, LANES), BF16)
                    if high < length:
                        probs[side, 2 * within + which, high:, lanes] = jnp.zeros((length - high, LANES), BF16)
            scale = jnp.concatenate(lines, 1)
            scales[pl.ds(2 * pair + which, 1), :] = scale
            outs.append(nn(values[which * HALF : (which + 1) * HALF], probs[side, 2 * within + which]) * scale)
        out = jnp.concatenate(outs, 0).T
        wide_mixed[:, columns] = out
        mixed[:, columns] = out.astype(BF16)

    @pl.loop(0, heads // together)
    def _(group):
        @pl.when(group >= 2)
        def _():
            prob_store(group - 2).wait()

        for within in range(GROUP):
            attend(group % 2, within, GROUP * group + within)
        prob_store(group).start()

    store(3, mixed, mixed_o).start()
    store(8, wide_mixed, wide_o).start()
    store(9, scales, scales_o).start()
    wait(3)

    result = nn(mixed[...], wp[...])
    for rows in strips(0, length, STRIP):
        out = result[rows] + vector(PBIAS)
        proj[rows, :] = out.astype(BF16)
        resid = xin[rows, :].astype(F32) + vector(SCALE_A) * out
        x1[rows, :] = resid
        scaled, _ = normalize(resid)
        h2[rows, :] = (scaled * vector(GAIN2) + vector(SHIFT2)).astype(BF16)

    store(4, proj, proj_o).start()
    store(5, x1, x1_o).start()
    store(6, h2, h2_o).start()
    pieces = [pl.ds(part * width, width) for part in range(hidden // width)]

    def expand(number):
        wait(4 + number)
        return nn(h2[...], w1[:, pieces[number]])

    coming = expand(0)
    result = None
    for number, columns in enumerate(pieces):
        current = coming
        if number + 1 < len(pieces):
            coming = expand(number + 1)
        for there in strips(0, length, STRIP):
            here = current[there] + vector(B1 + number)
            normal = 0.5 * lax.erf(here * math.sqrt(0.5)) + 0.5
            density = jnp.exp(-0.5 * here * here) * (1.0 / math.sqrt(2.0 * math.pi))
            act[there, columns] = (here * normal).astype(BF16)
            slope[there, columns] = (normal + here * density).astype(BF16)
        wait(8 + number)
        more = nn(act[:, columns], w2[columns, :])
        result = more if number == 0 else result + more
        part_store(10, act, act_o, columns).start()
        part_store(11, slope, slope_o, columns).start()

    for rows in strips(0, length, STRIP):
        out = result[rows] + vector(B2)
        mlp[rows, :] = out.astype(BF16)
        out_row[rows, :] = (x1[rows, :] + vector(SCALE_M) * out).astype(BF16)

    store(12, mlp, mlp_o).start()
    store(13, out_row, y_o).start()
    for group in range(max(0, heads // together - 2), heads // together):
        prob_store(group).wait()
    ends = {0: (h1, h1_o), 1: (qkv, qkv_o), 3: (mixed, mixed_o), 4: (proj, proj_o), 5: (x1, x1_o), 6: (h2, h2_o),
            7: (xin, xin_o), 8: (wide_mixed, wide_o), 9: (scales, scales_o),
            10: (act, act_o), 11: (slope, slope_o), 12: (mlp, mlp_o), 13: (out_row, y_o)}
    for number, (source, there) in ends.items():
        store(number, source, there).wait()


def hbm_specs(count):
    return [pl.BlockSpec(memory_space=pl.ANY)] * count


def vmem_specs(count):
    return [pl.BlockSpec(memory_space=pltpu.VMEM)] * count


def stacked(stored):
    return [jax.ShapeDtypeStruct((2, *shape), kind) for shape, kind in stored]


def forward(layer, pads, rows, segments, packs, band, weights, kept):
    length, width = rows.shape[1:]
    heads = band.shape[1]
    hidden = weights[2][0].shape[1]
    stored = [
        ((length, width), BF16),
        ((length, 3 * width), BF16),
        ((heads, length, length), BF16),
        ((length, width), BF16),
        ((length, width), BF16),
        ((length, width), F32),
        ((length, width), BF16),
        ((length, width), BF16),
        ((length, width), F32),
        ((heads, length), F32),
        ((length, hidden), BF16),
        ((length, hidden), BF16),
        ((length, width), BF16),
        ((length, width), BF16),
    ]
    scratch = [pltpu.VMEM(band.shape[1:], F32)] + [pltpu.VMEM(pair[0].shape, BF16) for pair in weights]
    scratch.append(pltpu.VMEM((length, length), F32))
    scratch += [
        pltpu.VMEM((2, 2 * GROUP, length, length) if n == 2 else shape, kind)
        for n, (shape, kind) in enumerate(stored)
    ]
    scratch += [
        pltpu.VMEM((2 * GROUP * length // LANES, length, LANES), F32),
        pltpu.SemaphoreType.DMA((14,)),
        pltpu.SemaphoreType.DMA((STORED,)),
        pltpu.SemaphoreType.DMA((2,)),
    ]
    operands = [pads, rows, segments, packs, band, *[x for pair in weights for x in pair]]
    held = STORED if layer > 0 else 0
    return pl.pallas_call(
        functools.partial(forward_kernel, layer),
        out_shape=stacked(stored),
        in_specs=[pl.BlockSpec(memory_space=pltpu.SMEM)] + hbm_specs(1) + vmem_specs(2) + hbm_specs(9 + held),
        out_specs=hbm_specs(STORED),
        scratch_shapes=scratch,
        input_output_aliases={len(operands) + n: n for n in range(held)},
        compiler_params=pltpu.CompilerParams(vmem_limit_bytes=VMEM_BYTES),
        name="forward_layer",
    )(*operands, *(kept if layer > 0 else ()))


def backward_kernel(layer, cotangent_hbm, packs_ref, *refs):
    weights, refs = refs[:8], refs[8:]
    (qkv_i, prob_i, mixed_i, proj_i, x1_i, slope_i, mlp_i, xin_i, scales_i) = refs[:9]
    refs = refs[9 + (7 if layer == 0 else 0) :]
    stores = refs[:7]
    (wqkv, wp, w1, w2, qkv, probs, mixed, proj, x1, slope, mlp, xin, scales, dm, dz, dproj, packed, dx_ref, dx1, dmixed, dscore, diag, sums, tables, g_ref, load_sem, store_sem, prob_sem) = refs[7:]
    dm_o, dz_o, dproj_o, packed_o, dx_o, tables_o, sums_o = stores
    wqkv_hbm, wp_hbm, w1_hbm, w2_hbm = zip(weights[::2], weights[1::2])
    length, width = g_ref.shape
    hidden = w1.shape[1]
    blocks = length // LANES
    pairs = width // LANES
    section = lax.axis_index("section")
    mine = section == layer
    factor = HALF ** (-0.5)
    parts = [pl.ds(part * width, width) for part in range(hidden // width)]
    loads = [(mlp_i.at[layer], mlp)]
    loads += [(tuple(x.at[part, :] for x in w2_hbm), w2.at[part, :]) for part in parts]
    loads += [(slope_i.at[layer], slope)]
    loads += [(tuple(x.at[:, part] for x in w1_hbm), w1.at[:, part]) for part in parts]
    early = len(loads)
    loads += [
        (x1_i.at[layer], x1), (proj_i.at[layer], proj), (wp_hbm, wp), (qkv_i.at[layer], qkv), (mixed_i.at[layer], mixed),
        (scales_i.at[layer], scales), (wqkv_hbm, wqkv), (xin_i.at[layer], xin),
    ]
    upstream_sem = load_sem.at[len(loads)]

    def start(number):
        source, target = loads[number]

        def go(ref):
            pltpu.make_async_copy(ref, target, load_sem.at[number]).start()

        if isinstance(source, tuple):
            pick(mine, *source, go)
        else:
            go(source)

    def load(number):
        target = loads[number][1]
        return pltpu.make_async_copy(target, target, load_sem.at[number])

    def store(number, source, there):
        return pltpu.make_async_copy(source, there.at[layer], store_sem.at[number])

    together = 2 * GROUP

    def prob_load(group):
        return pltpu.make_async_copy(
            prob_i.at[layer, pl.ds(together * group, together)], probs.at[group % 2], prob_sem.at[group % 2]
        )

    def vector(row):
        return packs_ref[layer, row : row + 1, :]

    def put(row, partial):
        sums[row : row + 1, :] = jnp.sum(partial, 0, keepdims=True)

    nothing = jnp.zeros((8, width), F32)

    upstream_hbm = cotangent_hbm.at[section] if layer == 1 else dx_o.at[1]
    pltpu.make_async_copy(upstream_hbm, g_ref, upstream_sem).start()
    for number in range(1 + len(parts)):
        start(number)
    pltpu.make_async_copy(g_ref, g_ref, upstream_sem).wait()
    load(0).wait()
    for number in range(1 + len(parts), early):
        start(number)
    scale_sum = bias_sum = nothing
    for rows in strips(0, length, STRIP):
        upstream = g_ref[rows, :].astype(F32)
        low = (upstream * vector(SCALE_M)).astype(BF16)
        dm[rows, :] = low
        scale_sum = scale_sum + fold(upstream * mlp[rows, :].astype(F32))
        bias_sum = bias_sum + fold(low.astype(F32))
    put(SCALE_M, scale_sum)
    put(B2, bias_sum)
    store(0, dm, dm_o).start()
    pieces = [pl.ds(part * width, width) for part in range(hidden // width)]

    def expand(number):
        load(1 + number).wait()
        return nt(dm[...], w2[pieces[number], :])

    coming = expand(0)
    upper_sum = None
    load(1 + len(parts)).wait()
    for number, columns in enumerate(pieces):
        if number == 1:
            for later in range(early, len(loads)):
                start(later)
            prob_load(0).start()
        load(2 + len(parts) + number).wait()
        current = coming
        if number + 1 < len(pieces):
            coming = expand(number + 1)
        act_sum = nothing
        for there in strips(0, length, STRIP):
            low = (current[there] * slope[there, columns].astype(F32)).astype(BF16)
            dz[there, columns] = low
            act_sum = act_sum + fold(low.astype(F32))
        put(B1 + number, act_sum)
        more = nt(dz[:, columns], w1[:, columns])
        upper_sum = more if number == 0 else upper_sum + more
    store(1, dz, dz_o).start()
    load(early).wait()
    load(early + 1).wait()
    found = [nothing] * 4
    for rows in strips(0, length, STRIP):
        upper = upper_sum[rows]
        scaled, inverse = normalize(x1[rows, :])
        resid = g_ref[rows, :].astype(F32) + norm_back(upper * vector(GAIN2), scaled, inverse)
        dx1[rows, :] = resid
        low = (resid * vector(SCALE_A)).astype(BF16)
        dproj[rows, :] = low
        terms = (upper * scaled, upper, resid * proj[rows, :].astype(F32), low.astype(F32))
        found = [old + fold(term) for old, term in zip(found, terms)]
    for row, partial in zip((GAIN2, SHIFT2, SCALE_A, PBIAS), found):
        put(row, partial)
    store(2, dproj, dproj_o).start()
    load(early + 2).wait()
    dmixed[...] = nt(dproj[...], wp[...]).astype(BF16)
    for number in range(early + 3, early + 6):
        load(number).wait()

    def attend(side, within, pair):
        columns = chunk(pair, LANES)
        key_columns = pl.ds(pl.multiple_of(width + pair * LANES, LANES), LANES)
        value_columns = pl.ds(pl.multiple_of(2 * width + pair * LANES, LANES), LANES)
        values = qkv[:, value_columns]
        above = dmixed[:, columns]
        queries_t = qkv[:, columns].T
        keys_t = qkv[:, key_columns].T
        above_t = above.astype(F32).T
        products = (above.astype(F32) * mixed[:, columns]).T
        grads = [], [], []
        for which in range(2):
            place_in = 2 * within + which
            half = slice(which * HALF, (which + 1) * HALF)
            delta = jnp.sum(products[half], 0, keepdims=True)
            scale = scales[pl.ds(2 * pair + which, 1), :]
            own_values = jnp.where(half_mask(values.shape, which), values, jnp.zeros_like(values))
            edge = (blocks - 1) * LANES
            diag[place_in, :edge, :] = jnp.zeros((edge, LANES), F32)
            for wide in range(blocks // 2):
                prob_grad = nt(own_values, above[2 * LANES * wide : 2 * LANES * (wide + 1)])
                for part in range(2):
                    place = 2 * wide + part
                    low, high = key_rows(place, blocks)
                    lanes = slice(place * LANES, (place + 1) * LANES)
                    first_row = (blocks - 1 - place) * LANES
                    for rows in strips(low, high, 64):
                        here = (probs[side, place_in, rows, lanes].astype(F32) * scale[:, lanes]) * (
                            prob_grad[rows, part * LANES : (part + 1) * LANES] - delta[:, lanes]
                        )
                        dscore[place_in, rows, lanes] = here.astype(BF16)
                        there = slice(first_row + rows.start, first_row + rows.stop)
                        diag[place_in, there, :] = here if place == 0 else diag[place_in, there, :] + here
                    if low > 0:
                        dscore[place_in, :low, lanes] = jnp.zeros((low, LANES), BF16)
                    if high < length:
                        dscore[place_in, high:, lanes] = jnp.zeros((length - high, LANES), BF16)
                    if place == 0:
                        diag[place_in, edge + high :, :] = jnp.zeros((length - high, LANES), F32)
            line = gather_diagonals(diag.at[place_in])
            most = tables.shape[1] - LANES
            tables[pl.ds(2 * pair + which, 1), :] = jnp.concatenate(
                [line[:, REACH + 1 : REACH + 1 + most], line[:, REACH : REACH + LANES]], 1
            )
            grads[0].append(nn(keys_t[half], dscore[place_in]))
            grads[1].append(nt(queries_t[half], dscore[place_in]))
            grads[2].append(nt((above_t[half] * scale).astype(BF16), probs[side, place_in]))
        for found, where, scale in zip(grads, (columns, key_columns, value_columns), (factor, None, None)):
            low = jnp.concatenate(found, 0).astype(BF16)
            if scale is not None:
                low = (low.astype(F32) * scale).astype(BF16)
            packed[:, where] = low.T

    @pl.loop(0, pairs // GROUP)
    def _(group):
        prob_load(group).wait()

        @pl.when(group + 1 < pairs // GROUP)
        def _():
            prob_load(group + 1).start()

        for within in range(GROUP):
            attend(group % 2, within, GROUP * group + within)

    store(3, packed, packed_o).start()
    load(early + 6).wait()
    result = nt(packed[...], wqkv[...])
    load(early + 7).wait()
    found = [nothing] * 4
    for rows in strips(0, length, STRIP):
        upper = result[rows]
        scaled, inverse = normalize(xin[rows, :].astype(F32))
        dx_ref[rows, :] = (dx1[rows, :] + norm_back(upper * vector(GAIN1), scaled, inverse)).astype(BF16)
        terms = (
            upper * scaled,
            upper,
            packed[rows, :width].astype(F32),
            packed[rows, 2 * width :].astype(F32),
        )
        found = [old + fold(term) for old, term in zip(found, terms)]
    for row, partial in zip((GAIN1, SHIFT1, QBIAS, VBIAS), found):
        put(row, partial)
    store(4, dx_ref, dx_o).start()
    store(5, tables, tables_o).start()
    store(6, sums, sums_o).start()
    ends = {0: (dm, dm_o), 1: (dz, dz_o), 2: (dproj, dproj_o), 3: (packed, packed_o), 4: (dx_ref, dx_o), 5: (tables, tables_o), 6: (sums, sums_o)}
    for number, (source, there) in ends.items():
        store(number, source, there).wait()


def backward(layer, cotangent, packs, weights, saved, kept):
    length, width = cotangent.shape[1:]
    hidden = weights[2][0].shape[1]
    h1, qkv, probs, mixed, proj, x1, h2, xin, wide, scales, act, slope, mlp, y = saved
    heads = probs.shape[1]
    span = 2 * length - LANES
    summed = (16, width)
    table = (heads, 5 * LANES)
    stored = [
        ((length, width), BF16),
        ((length, hidden), BF16),
        ((length, width), BF16),
        ((length, 3 * width), BF16),
        ((length, width), BF16),
        (table, F32),
        (summed, F32),
    ]
    reads = [qkv, probs, wide, proj, x1, slope, mlp, xin, scales]
    scratch = [pltpu.VMEM(pair[0].shape, BF16) for pair in weights]
    scratch += [pltpu.VMEM((2, 2 * GROUP, length, length) if x is probs else x.shape[1:], x.dtype) for x in reads]
    scratch += [pltpu.VMEM(shape, kind) for shape, kind in stored[:5]]
    scratch += [
        pltpu.VMEM((length, width), F32),
        pltpu.VMEM((length, width), BF16),
        pltpu.VMEM((2 * GROUP, length, length), BF16),
        pltpu.VMEM((2 * GROUP, span, LANES), F32),
        pltpu.VMEM(summed, F32),
        pltpu.VMEM(table, F32),
        pltpu.VMEM((length, width), BF16),
        pltpu.SemaphoreType.DMA((19,)),
        pltpu.SemaphoreType.DMA((7,)),
        pltpu.SemaphoreType.DMA((2,)),
    ]
    operands = [cotangent, packs, *[x for pair in weights for x in pair], *reads]
    held = 7 if layer == 0 else 0
    return pl.pallas_call(
        functools.partial(backward_kernel, layer),
        out_shape=stacked(stored),
        in_specs=hbm_specs(1) + vmem_specs(1) + hbm_specs(8 + len(reads) + held),
        out_specs=hbm_specs(7),
        scratch_shapes=scratch,
        input_output_aliases={len(operands) + n: n for n in range(held)},
        compiler_params=pltpu.CompilerParams(vmem_limit_bytes=VMEM_BYTES),
        name="backward_layer",
    )(*operands, *(kept if layer == 0 else ()))


def small_lines(width):
    lines = width // LANES
    places = [(row, tile, row * lines + tile) for row in range(10) for tile in range(lines)]
    return places + [(B1, tile, B1 * lines + tile) for tile in range(4 * lines)]


def reverse_lanes(values):
    lane = lax.broadcasted_iota(jnp.int32, values.shape, 1)
    for place in range(LANES.bit_length() - 1):
        step = 1 << place
        up, down = pltpu.roll(values, step, 1), pltpu.roll(values, LANES - step, 1)
        values = jnp.where((lane // step) % 2 == 1, up, down)
    return values


def widen_kernel(sum_hbm, small_ref, *refs):
    bigs, vectors, table_ref = refs[:4], refs[4 : 5 + VECTORS], refs[5 + VECTORS]
    narrow, wide, load_sem, store_sem = refs[6 + VECTORS :]
    depth, width = narrow.shape[:2]
    blocks = [(0, slice(b * width, (b + 1) * width), slice(0, width)) for b in range(4)]
    for target, count in ((1, 4), (2, 3), (3, 1)):
        blocks += [(target, slice(0, width), slice(b * width, (b + 1) * width)) for b in range(count)]

    def load(block):
        rows = pl.ds(block * width, width)
        return pltpu.make_async_copy(sum_hbm.at[rows, :], narrow.at[block % depth], load_sem.at[block % depth])

    def store(block):
        target, rows, columns = blocks[block]
        there = bigs[target].at[rows, columns]
        return pltpu.make_async_copy(wide.at[block % depth], there, store_sem.at[block % depth])

    for block in range(depth):
        load(block).start()
    for block in range(len(blocks)):
        load(block).wait()
        if block >= depth:
            store(block - depth).wait()
        for rows in strips(0, width, 64):
            wide[block % depth, rows, :] = narrow[block % depth, rows, :].astype(F32)
        store(block).start()
        if block + depth < len(blocks):
            load(block + depth).start()
    places = small_lines(width)
    for row, tile, line in places:
        vectors[row][:, tile * LANES : (tile + 1) * LANES] = small_ref[line : line + 1, :]
    first = len(places)
    heads, entries = table_ref.shape
    tiles = -(-entries // LANES)
    flipped = reverse_lanes(small_ref[first : first + heads * tiles, :])
    for head in range(heads):
        for tile in range(tiles - 1):
            line = head * tiles + tile
            there = (tiles - 2 - tile) * LANES
            table_ref[head : head + 1, there : there + LANES] = flipped[line : line + 1]
        line = first + head * tiles + tiles - 1
        table_ref[head : head + 1, entries - 1 :] = small_ref[line : line + 1, 0:1]
    for block in range(len(blocks) - depth, len(blocks)):
        store(block).wait()


def widen(summed, small, width, heads, entries):
    shapes = [(4 * width, width), (width, 4 * width), (width, 3 * width), (width, width)]
    shapes += [(1, width)] * 10 + [(1, 4 * width), (heads, entries)]
    return pl.pallas_call(
        widen_kernel,
        out_shape=[jax.ShapeDtypeStruct(shape, F32) for shape in shapes],
        in_specs=hbm_specs(1) + vmem_specs(1),
        out_specs=hbm_specs(4) + vmem_specs(VECTORS + 2),
        scratch_shapes=[
            pltpu.VMEM((3, width, width), BF16),
            pltpu.VMEM((3, width, width), F32),
            pltpu.SemaphoreType.DMA((3,)),
            pltpu.SemaphoreType.DMA((3,)),
        ],
        compiler_params=pltpu.CompilerParams(vmem_limit_bytes=VMEM_BYTES),
        name="widen",
    )(summed, small)


BLOCK = 256
LAG = 3


def reduce_kernel(bits, chunks, blocks, lags, window, *refs):
    (a_ref, dm_ref, h2_ref, dz_ref, h1_ref, dp_ref, o_ref, dproj_ref, y_ref, dx_ref, sums_ref, tables_ref) = refs[:12]
    out_ref, small_out_ref, y_out, dx_out = refs[12:16]
    refs = refs[16:]
    (lhs, rhs, grads, total, crossing, landed, smalls, small_ref, small_landed, small_total, *received) = refs[: 10 + 2 * bits]
    (load_sem, send_sem, recv_sem, small_send, small_recv, store_sem, cross_send, cross_recv, row_sem, credit) = refs[10 + 2 * bits :]
    small_received = received[bits:]
    me = lax.axis_index("dp")
    section = lax.axis_index("section")
    beside = 1 - section
    rows = BLOCK * blocks
    width = grads.shape[1]
    per_side = width // BLOCK
    last = 2 * bits
    starts = [0] + [lags[0] + lags[1] * place for place in range(last + 1)]

    barrier = pltpu.get_barrier_semaphore()
    for place in range(bits):
        stride = 1 << place
        other = me + stride * (1 - 2 * ((me // stride) % 2))
        pl.semaphore_signal(barrier, inc=1, device_id={"dp": other}, device_id_type=MESH)
    pl.semaphore_signal(barrier, inc=1, device_id={"section": beside}, device_id_type=MESH)
    pl.semaphore_wait(barrier, bits + 1)

    def across(source, target, number):
        return pltpu.make_async_remote_copy(
            src_ref=source,
            dst_ref=target,
            send_sem=cross_send.at[number],
            recv_sem=cross_recv.at[number],
            device_id={"section": beside},
            device_id_type=MESH,
        )

    def row_copy(number):
        source, target = ((y_ref, y_out), (dx_ref, dx_out))[number]
        return pltpu.make_async_copy(source.at[section], target.at[section], row_sem.at[number])

    def row_across(number):
        source, target = ((y_ref, y_out), (dx_ref, dx_out))[number]
        return across(source.at[beside], target.at[section], window + 1 + number)

    families = (
        (a_ref, dm_ref, 4 * per_side, True),
        (h2_ref, dz_ref, 4 * per_side, False),
        (h1_ref, dp_ref, 3 * per_side, False),
        (o_ref, dproj_ref, per_side, False),
    )
    n_blocks = 12 * per_side

    def load(block):
        slot = block % 2
        first = 0
        for left, right, count, walks in families:
            @pl.when((block >= first) & (block < first + count))
            def _():
                local = block - first
                if walks:
                    left_column = local * BLOCK
                    right_column = 0
                else:
                    left_column = (local % per_side) * BLOCK
                    right_column = (local // per_side) * width
                for number, layer in enumerate((section, beside)):
                    pltpu.make_async_copy(
                        left.at[layer, :, pl.ds(pl.multiple_of(left_column, BLOCK), BLOCK)],
                        lhs.at[slot, number],
                        load_sem.at[0, slot],
                    ).start()
                    pltpu.make_async_copy(
                        right.at[layer, :, pl.ds(pl.multiple_of(right_column, BLOCK), width)],
                        rhs.at[slot, number],
                        load_sem.at[1, slot],
                    ).start()
            first += count

    def produce(block, sub, side):
        slot = block % 2
        pltpu.make_async_copy(lhs.at[slot], lhs.at[slot], load_sem.at[0, slot]).wait()
        pltpu.make_async_copy(rhs.at[slot], rhs.at[slot], load_sem.at[1, slot]).wait()

        @pl.when(block + 1 < n_blocks)
        def _():
            load(block + 1)

        crossing[side, sub * BLOCK : (sub + 1) * BLOCK, :] = dot(lhs[slot, 1], rhs[slot, 1], 0, 0).astype(BF16)
        grads[chunk(block, BLOCK), :] = dot(lhs[slot, 0], rhs[slot, 0], 0, 0).astype(BF16)

    def turn(chunk):
        place = chunk % 9
        return place % 2 + place // 5 - place // 6

    def partner(rotation, stage):
        stride = lax.shift_left(jnp.int32(1), (stage + rotation) % bits)
        mine = (me // stride) % 2
        return mine, me + stride * (1 - 2 * mine)

    def offset(base, height, rotation, stage):
        for earlier in range(stage):
            mine, _ = partner(rotation, earlier)
            base = base + mine * (height >> (earlier + 1))
        return base

    def piece(ref, start, size):
        return ref.at[pl.ds(pl.multiple_of(start, size), size)]

    def send(position, base, height, rotation, source, landing, result, slot, sems):
        send_at, recv_at = sems
        if position < bits:
            stage = position
            half = height >> (stage + 1)
            mine, other = partner(rotation, stage)
            start = offset(base, height, rotation, stage) + (1 - mine) * half
            src, dst = piece(source, start, half), landing[stage].at[slot]
        else:
            stage = last - 1 - position
            half = height >> (stage + 1)
            mine, other = partner(rotation, stage)
            start = offset(base, height, rotation, stage + 1)
            src = dst = piece(result, start, half)
        return pltpu.make_async_remote_copy(
            src_ref=src,
            dst_ref=dst,
            send_sem=send_at.at[position],
            recv_sem=recv_at.at[position, slot],
            device_id={"dp": other},
            device_id_type=MESH,
        )

    def take(position, base, height, rotation, source, landing, result, slot, sems):
        send(position - 1, base, height, rotation, source, landing, result, slot, sems).wait_recv()
        stage = position - 1
        if stage < bits:
            half = height >> (stage + 1)
            start = pl.multiple_of(offset(base, height, rotation, stage + 1), half)
            keep = pl.ds(start, half)
            value = source[keep, :].astype(jnp.float32) + landing[stage][slot].astype(jnp.float32)
            target = result if stage == bits - 1 else source
            target[keep, :] = value.astype(target.dtype)

    def step(position, *way):
        if position > 0:
            take(position, *way)
        if position < last:
            send(position, *way).start()

    main = (grads, received[:bits], total)
    main_sems = (send_sem, recv_sem)

    def cross(side):
        return across(crossing.at[side], landed.at[side], side)

    def give(part):
        side = part % window

        @pl.when(part >= window)
        def _():
            cross(side).wait_send()
            pl.semaphore_wait(credit, 1)

        for sub in range(blocks):
            block = part * blocks + sub

            @pl.when(block < n_blocks)
            def _():
                produce(block, sub, side)

        cross(side).start()

    def join(part):
        side = part % window
        cross(side).wait_recv()
        there = chunk(part, rows)
        grads[there, :] = (grads[there, :].astype(F32) + landed[side].astype(F32)).astype(BF16)

        @pl.when(part < chunks - window)
        def _():
            pl.semaphore_signal(credit, inc=1, device_id={"section": beside}, device_id_type=MESH)

    def walk(position, part):
        if position == 0:
            join(part)
        base = part * rows
        step(position, base, rows, turn(part), *main, part, main_sems)
        if position == last:
            there = pl.ds(pl.multiple_of(base, rows), rows)
            pltpu.make_async_copy(total.at[there], out_ref.at[there], store_sem.at[0]).start()

    def small_cross():
        return across(smalls.at[beside], small_landed, window)

    def walk_small(position):
        height = small_ref.shape[0]
        if position == 0:
            small_cross().wait_recv()
            small_ref[...] = smalls[section] + small_landed[...]
        way = (0, height, 0, small_ref, small_received, small_total, 0, (small_send, small_recv))
        step(position, *way)

    load(jnp.int32(0))
    smalls[...] = jnp.zeros_like(smalls)
    places = small_lines(width)
    for layer in range(2):
        for row, tile, line in places:
            if row == B1:
                row, tile = B1 + tile // (width // LANES), tile % (width // LANES)
            smalls[layer, line : line + 1, :] = sums_ref[layer, row : row + 1, tile * LANES : (tile + 1) * LANES]
        line = len(places)
        for head in range(tables_ref.shape[1]):
            for tile in range(tables_ref.shape[2] // LANES):
                lanes = slice(tile * LANES, (tile + 1) * LANES)
                smalls[layer, line : line + 1, :] = tables_ref[layer, head : head + 1, lanes]
                line += 1
    small_cross().start()
    for number in range(2):
        row_copy(number).start()
        row_across(number).start()

    @pl.loop(0, chunks + starts[-1])
    def _(tick):
        @pl.when(tick < chunks)
        def _():
            give(tick)

        for position in range(last + 1):
            part = tick - starts[position + 1]

            @pl.when((part >= 0) & (part < chunks))
            def _():
                walk(position, part)

            @pl.when(part == 0)
            def _():
                walk_small(position)

    small_out_ref[...] = small_total[...]
    for position in range(last):
        stage = position if position < bits else last - 1 - position
        size = received[stage]
        pltpu.make_async_copy(size, size, send_sem.at[position]).wait()
        size = small_received[stage]
        pltpu.make_async_copy(size, size, small_send.at[position]).wait()
    for side in range(window):
        cross(side).wait_send()
    small_cross().wait_send()
    for number in range(2):
        row_copy(number).wait()
        row_across(number).wait()
    pltpu.make_async_copy(total, out_ref, store_sem.at[0]).wait()


def reduce_gradients(a, dm, h2, dz, h1, packed, o, dproj, y, dx, sums, tables):
    parts = lax.axis_size("dp")
    bits = parts.bit_length() - 1
    blocks = max(1, 16 * parts // BLOCK)
    layers, length, width = h1.shape
    n_blocks = 12 * width // BLOCK
    chunks = -(-n_blocks // blocks)
    rows = BLOCK * blocks
    lags, window = ((2, LAG), 4) if blocks == 1 else ((0, LAG), 1)
    lines = len(small_lines(width)) + tables.shape[1] * tables.shape[2] // LANES
    height = -(-lines // (8 * parts)) * 8 * parts
    small = (height, LANES)
    return pl.pallas_call(
        functools.partial(reduce_kernel, bits, chunks, blocks, lags, window),
        out_shape=(
            jax.ShapeDtypeStruct((chunks * rows, width), BF16),
            jax.ShapeDtypeStruct(small, F32),
            jax.ShapeDtypeStruct(y.shape, BF16),
            jax.ShapeDtypeStruct(dx.shape, BF16),
        ),
        in_specs=hbm_specs(10) + vmem_specs(2),
        out_specs=hbm_specs(1) + vmem_specs(1) + hbm_specs(2),
        scratch_shapes=[
            pltpu.VMEM((2, layers, length, BLOCK), BF16),
            pltpu.VMEM((2, layers, length, width), BF16),
            pltpu.VMEM((chunks * rows, width), BF16),
            pltpu.VMEM((chunks * rows, width), BF16),
            pltpu.VMEM((window, rows, width), BF16),
            pltpu.VMEM((window, rows, width), BF16),
            pltpu.VMEM((layers, *small), F32),
            pltpu.VMEM(small, F32),
            pltpu.VMEM(small, F32),
            pltpu.VMEM(small, F32),
            *[pltpu.VMEM((chunks, rows >> (s + 1), width), BF16) for s in range(bits)],
            *[pltpu.VMEM((1, height >> (s + 1), LANES), F32) for s in range(bits)],
            pltpu.SemaphoreType.DMA((2, 2)),
            pltpu.SemaphoreType.DMA((2 * bits,)),
            pltpu.SemaphoreType.DMA((2 * bits, chunks)),
            pltpu.SemaphoreType.DMA((2 * bits,)),
            pltpu.SemaphoreType.DMA((2 * bits, 1)),
            pltpu.SemaphoreType.DMA((1,)),
            pltpu.SemaphoreType.DMA((window + 3,)),
            pltpu.SemaphoreType.DMA((window + 3,)),
            pltpu.SemaphoreType.DMA((2,)),
            pltpu.SemaphoreType.REGULAR,
        ],
        compiler_params=pltpu.CompilerParams(
            collective_id=0, has_side_effects=True, vmem_limit_bytes=VMEM_BYTES
        ),
        name="reduce_gradients",
    )(a, dm, h2, dz, h1, packed, o, dproj, y, dx, sums, tables)


def swapped(block):
    return lax.ppermute(block, "section", [(0, 1), (1, 0)])


def per_device(
    patches,
    segment_ids,
    pad_counts,
    norm1_gain,
    norm1_bias,
    qkv_weight,
    query_bias,
    value_bias,
    rel_table,
    proj_weight,
    proj_bias,
    scale_attn,
    norm2_gain,
    norm2_bias,
    fc1_weight,
    fc1_bias,
    fc2_weight,
    fc2_bias,
    scale_mlp,
    cotangent,
):
    micro, length, width = patches.shape
    heads, entries = rel_table.shape[1:]
    vectors = (
        norm1_gain,
        norm1_bias,
        query_bias,
        value_bias,
        proj_bias,
        scale_attn,
        norm2_gain,
        norm2_bias,
        fc2_bias,
        scale_mlp,
        fc1_bias,
    )
    own = pack(vectors, rel_table)
    own_weights = (qkv_weight[0], proj_weight[0], fc1_weight[0], fc2_weight[0])
    other = swapped(own)
    weights = [(x, swapped(x)) for x in own_weights]
    packs, band = bands(own, other, heads, length)
    saved = None
    rows = patches
    for layer in range(2):
        saved = forward(layer, pad_counts, rows, segment_ids, packs, band, weights, saved)
    kept = None
    for layer in (1, 0):
        kept = backward(layer, cotangent, packs, weights, saved, kept)
    dm, dz, dproj, packed, dx, tables, sums = kept
    h1, mixed, h2, act, y = saved[0], saved[3], saved[6], saved[10], saved[13]
    summed, small, outputs, in_grads = reduce_gradients(
        act, dm, h2, dz, h1, packed, mixed, dproj, y, dx, sums, tables
    )
    fc2_grad, fc1_grad, qkv_grad, proj_grad, *small_grads = widen(
        summed, small, width, heads, entries
    )
    table_grad = small_grads[VECTORS + 1]
    return (
        outputs[None],
        in_grads[None],
        small_grads[GAIN1],
        small_grads[SHIFT1],
        qkv_grad[None],
        small_grads[QBIAS],
        small_grads[VBIAS],
        table_grad[None],
        proj_grad[None],
        small_grads[PBIAS],
        small_grads[SCALE_A],
        small_grads[GAIN2],
        small_grads[SHIFT2],
        fc1_grad[None],
        small_grads[B1],
        fc2_grad[None],
        small_grads[B2],
        small_grads[SCALE_M],
    )


def solution(mesh):
    placed = (
        P("dp", None, None),
        P("dp", None),
        P("dp"),
        P("section", None),
        P("section", None),
        P("section", None, None),
        P("section", None),
        P("section", None),
        P("section", None, None),
        P("section", None, None),
        P("section", None),
        P("section", None),
        P("section", None),
        P("section", None),
        P("section", None, None),
        P("section", None),
        P("section", None, None),
        P("section", None),
        P("section", None),
        P("dp", None, None),
    )
    return jax.shard_map(
        per_device,
        mesh=mesh,
        in_specs=placed,
        out_specs=(
            P("section", "dp", None, None),
            P("section", "dp", None, None),
            P("section", None),
            P("section", None),
            P("section", None, None),
            P("section", None),
            P("section", None),
            P("section", None, None),
            P("section", None, None),
            P("section", None),
            P("section", None),
            P("section", None),
            P("section", None),
            P("section", None, None),
            P("section", None),
            P("section", None, None),
            P("section", None),
            P("section", None),
        ),
        check_vma=False,
    )
```

```python
import functools
import math

import jax
import jax.numpy as jnp
from jax import lax
from jax.experimental import pallas as pl
from jax.experimental.pallas import tpu as pltpu
from jax.sharding import PartitionSpec as P

MESH = pl.DeviceIdType.MESH
BF16, F32 = jnp.bfloat16, jnp.float32
VMEM_BYTES = 60 * 1024 * 1024
LANES = 128
HALF = 64
REACH = 2 * LANES
GAIN1, SHIFT1, QBIAS, VBIAS, PBIAS, SCALE_A, GAIN2, SHIFT2, B2, SCALE_M, B1 = range(11)
VECTORS = 10
STORED = 14
STRIP = 16
GROUP = 2


def dot(left, right, left_dim, right_dim):
    return lax.dot_general(
        left, right, (((left_dim,), (right_dim,)), ((), ())), preferred_element_type=F32
    )


def nn(left, right):
    return dot(left, right, 1, 0)


def nt(left, right):
    return dot(left, right, 1, 1)


def normalize(values):
    centered = values - jnp.mean(values, -1, keepdims=True)
    inverse = lax.rsqrt(jnp.mean(centered * centered, -1, keepdims=True) + 1e-06)
    return centered * inverse, inverse


def norm_back(upper, scaled, inverse):
    return inverse * (
        upper
        - jnp.mean(upper, -1, keepdims=True)
        - scaled * jnp.mean(upper * scaled, -1, keepdims=True)
    )


def fold(values):
    return jnp.sum(values.reshape(values.shape[0] // 8, 8, values.shape[1]), 0)


def half_mask(shape, which):
    return lax.broadcasted_iota(jnp.int32, shape, 1) // HALF == which


def strips(first, last, size):
    return [slice(start, start + size) for start in range(first, last, size)]


def chunk(index, size):
    return pl.ds(pl.multiple_of(index * size, size), size)


def skew_bias(reversed_row, target):
    span, lanes = target.shape
    rows = pltpu.roll(jnp.broadcast_to(reversed_row, (8, reversed_row.shape[1])), 1, 1, stride=1, stride_axis=0)
    tiles = span // lanes
    for fine in range(lanes // 8):
        moved = rows if fine == 0 else pltpu.roll(rows, 8 * fine, 1)
        for coarse in range(tiles):
            place = 8 * (fine + lanes // 8 * coarse)
            target[place : place + 8, :] = moved[:, lanes * (tiles - coarse) : lanes * (tiles - coarse + 1)]


def gather_diagonals(source):
    span, lanes = source.shape
    tiles = span // lanes
    width = span + lanes
    blank = jnp.zeros((8, lanes), F32)
    found = None
    for fine in range(lanes // 8):
        places = [8 * (fine + lanes // 8 * coarse) for coarse in reversed(range(tiles))]
        line = jnp.concatenate([blank] + [source[place : place + 8, :] for place in places], 1)
        if fine > 0:
            line = pltpu.roll(line, width - 8 * fine, 1)
        found = line if found is None else found + line
    row = lax.broadcasted_iota(jnp.int32, found.shape, 0)
    for place in range(3):
        moved = pltpu.roll(found, width - (1 << place), 1)
        found = jnp.where((row // (1 << place)) % 2 == 1, moved, found)
    return jnp.sum(found, 0, keepdims=True)


def key_rows(query_block, blocks):
    reach = REACH // LANES
    return max(0, query_block - reach) * LANES, min(blocks, query_block + reach + 1) * LANES


def pick(mine, own, other, act):
    @pl.when(mine)
    def _():
        act(own)

    @pl.when(jnp.logical_not(mine))
    def _():
        act(other)


def pack_kernel(*refs):
    *vectors, bias_ref, table_ref, pack_ref = refs
    width = pack_ref.shape[1]
    heads, _, entries = table_ref.shape
    pack_ref[...] = jnp.zeros_like(pack_ref)
    for row, vector in enumerate(vectors):
        pack_ref[row : row + 1, :] = vector[...]
    for part in range(bias_ref.shape[1] // width):
        pack_ref[B1 + part : B1 + part + 1, :] = bias_ref[:, part * width : (part + 1) * width]
    first = pack_ref.shape[0] - heads
    tiles = entries // LANES
    lane = lax.broadcasted_iota(jnp.int32, (heads, LANES), 1)
    ending = jnp.broadcast_to(table_ref[:, 0, entries - 1 :], (heads, LANES))
    pack_ref[first:, :LANES] = jnp.where(lane == LANES - 1, ending, 0.0)
    for tile in range(tiles):
        there = (tiles - tile) * LANES
        pack_ref[first:, there : there + LANES] = reverse_lanes(table_ref[:, 0, tile * LANES : (tile + 1) * LANES])


def pack(vectors, rel_table):
    heads = rel_table.shape[0]
    return pl.pallas_call(
        pack_kernel,
        out_shape=jax.ShapeDtypeStruct((16 + heads, vectors[0].shape[1]), F32),
        in_specs=vmem_specs(len(vectors) + 1),
        out_specs=pl.BlockSpec(memory_space=pltpu.VMEM),
        name="pack_vectors",
    )(*vectors, rel_table)


def fill(target, source):
    target[...] = source[...]


def band_kernel(pack_ref, band_hbm, band, store_sem):
    heads = band.shape[0]
    tables = pack_ref.shape[0] - heads
    edge = jnp.zeros((1, LANES), F32)

    @pl.loop(0, heads // 4)
    def _(group):
        for within in range(4):
            head = 4 * group + within
            kept = pack_ref[pl.ds(tables + head, 1), :]
            skew_bias(jnp.concatenate([edge, kept, edge], 1), band.at[head])

    there = pltpu.make_async_copy(band, band_hbm, store_sem.at[0])
    there.start()
    there.wait()


def bias_band(packed, heads, length):
    shape = (heads, 2 * length - LANES, LANES)
    return pl.pallas_call(
        band_kernel,
        out_shape=jax.ShapeDtypeStruct(shape, F32),
        in_specs=vmem_specs(1),
        out_specs=pl.BlockSpec(memory_space=pl.ANY),
        scratch_shapes=[pltpu.VMEM(shape, F32), pltpu.SemaphoreType.DMA((1,))],
        compiler_params=pltpu.CompilerParams(vmem_limit_bytes=VMEM_BYTES),
        name="bias_band",
    )(packed)


def forward_kernel(layer, pads, x_hbm, seg_ref, own_pack, other_pack, own_band, other_band, *refs):
    wqkv_own, wqkv_other, wp_own, wp_other, w1_own, w1_other, w2_own, w2_other = refs[:8]
    refs = refs[8 + (STORED if layer > 0 else 0) :]
    stores = refs[:STORED]
    (bias, wqkv, wp, w1, w2, mask, h1, qkv, probs, mixed, proj, x1, h2, xin, wide_mixed, scales, act, slope, mlp, out_row, held, pack_ref, load_sem, store_sem, prob_sem) = refs[STORED:]
    h1_o, qkv_o, prob_o, mixed_o, proj_o, x1_o, h2_o, xin_o, wide_o, scales_o, act_o, slope_o, mlp_o, y_o = stores
    hidden = w1.shape[1]
    length, width = xin.shape
    heads = bias.shape[0]
    blocks = length // LANES
    section = lax.axis_index("section")
    mine = section == layer
    factor = HALF ** (-0.5)
    thirds = [pl.ds(part * width, width) for part in range(3)]

    def load(number):
        if number < 3:
            part = thirds[number]
            return wqkv_own.at[:, part], wqkv_other.at[:, part], wqkv.at[:, part], load_sem.at[number]
        if number == 3:
            return wp_own, wp_other, wp, load_sem.at[3]
        part = pl.ds((number % 4) * width, width)
        if number < 8:
            return w1_own.at[:, part], w1_other.at[:, part], w1.at[:, part], load_sem.at[number]
        return w2_own.at[part, :], w2_other.at[part, :], w2.at[part, :], load_sem.at[number]

    def start(number):
        own, other, target, sem = load(number)
        pick(mine, own, other, lambda source: pltpu.make_async_copy(source, target, sem).start())

    def wait(number):
        own, other, target, sem = load(number)
        pltpu.make_async_copy(target, target, sem).wait()

    def store(number, source, there):
        return pltpu.make_async_copy(source, there.at[layer], store_sem.at[number])

    def part_store(number, source, there, columns):
        return pltpu.make_async_copy(source.at[:, columns], there.at[layer, :, columns], store_sem.at[number])

    def vector(row):
        return pack_ref[row : row + 1, :]

    source = x_hbm.at[section] if layer == 0 else y_o.at[0]
    pltpu.make_async_copy(source, xin, load_sem.at[12]).start()
    for number in range(3):
        start(number)
    pltpu.make_async_copy(xin, xin, load_sem.at[12]).wait()
    pick(mine, own_band, other_band, lambda source: pltpu.make_async_copy(source, bias, load_sem.at[13]).start())
    pick(mine, own_pack, other_pack, functools.partial(fill, pack_ref))
    segment = seg_ref[pl.ds(section, 1), :].astype(F32)
    key_segment = jnp.broadcast_to(segment, (LANES, length)).T

    for rows in strips(0, length, STRIP):
        scaled, _ = normalize(xin[rows, :].astype(F32))
        h1[rows, :] = (scaled * vector(GAIN1) + vector(SHIFT1)).astype(BF16)

    alive = length - pads[section]
    for place in range(blocks):
        lanes = slice(place * LANES, (place + 1) * LANES)
        for rows in strips(0, length, 64):
            key = lax.broadcasted_iota(jnp.int32, (64, LANES), 0) + rows.start
            query = lax.broadcasted_iota(jnp.int32, (64, LANES), 1) + place * LANES
            allowed = ((key_segment[rows] == segment[:, lanes]) & (key < alive)) | (key == query)
            mask[rows, lanes] = jnp.where(allowed, 0.0, -1000000000.0)

    store(0, h1, h1_o).start()
    store(7, xin, xin_o).start()
    for part in range(3):
        wait(part)
        columns = thirds[part]
        result = nn(h1[...], wqkv[:, columns])
        for rows in strips(0, length, STRIP):
            piece = result[rows]
            if part == 0:
                piece = (piece + vector(QBIAS)) * factor
            if part == 2:
                piece = piece + vector(VBIAS)
            qkv[rows, columns] = piece.astype(BF16)
    store(1, qkv, qkv_o).start()
    pltpu.make_async_copy(bias, bias, load_sem.at[13]).wait()
    for number in range(3, 12):
        start(number)
    together = 2 * GROUP

    def prob_store(group):
        return pltpu.make_async_copy(
            probs.at[group % 2], prob_o.at[layer, pl.ds(together * group, together)], prob_sem.at[group % 2]
        )

    def attend(side, within, pair):
        columns = chunk(pair, LANES)
        queries = qkv[:, columns]
        keys = qkv[:, pl.ds(pl.multiple_of(width + pair * LANES, LANES), LANES)]
        values = qkv[:, pl.ds(pl.multiple_of(2 * width + pair * LANES, LANES), LANES)].T
        outs = []
        for which in range(2):
            own_keys = jnp.where(half_mask(keys.shape, which), keys, jnp.zeros_like(keys))
            lines = []
            for wide in range(blocks // 2):
                scores = nt(own_keys, queries[2 * LANES * wide : 2 * LANES * (wide + 1)])
                for part in range(2):
                    place = 2 * wide + part
                    low, high = key_rows(place, blocks)
                    lanes = slice(place * LANES, (place + 1) * LANES)
                    first = (blocks - 1 - place) * LANES
                    spare = (2 * within + which) * blocks + place
                    highest = None
                    for rows in strips(low, high, 64):
                        here = (
                            scores[rows, part * LANES : (part + 1) * LANES]
                            + bias[2 * pair + which, first + rows.start : first + rows.stop, :]
                            + mask[rows, lanes]
                        )
                        held[spare, rows, :] = here
                        top = jnp.max(here.reshape(8, 8, LANES), 0)
                        highest = top if highest is None else jnp.maximum(highest, top)
                    highest = jnp.max(highest, 0, keepdims=True)
                    sums = jnp.zeros((8, LANES), F32)
                    for rows in strips(low, high, 64):
                        expo = jnp.exp(held[spare, rows, :] - highest)
                        probs[side, 2 * within + which, rows, lanes] = expo.astype(BF16)
                        sums = sums + fold(expo)
                    lines.append(1.0 / jnp.sum(sums, 0, keepdims=True))
                    if low > 0:
                        probs[side, 2 * within + which, :low, lanes] = jnp.zeros((low, LANES), BF16)
                    if high < length:
                        probs[side, 2 * within + which, high:, lanes] = jnp.zeros((length - high, LANES), BF16)
            scale = jnp.concatenate(lines, 1)
            scales[pl.ds(2 * pair + which, 1), :] = scale
            outs.append(nn(values[which * HALF : (which + 1) * HALF], probs[side, 2 * within + which]) * scale)
        out = jnp.concatenate(outs, 0).T
        wide_mixed[:, columns] = out
        mixed[:, columns] = out.astype(BF16)

    @pl.loop(0, heads // together)
    def _(group):
        @pl.when(group >= 2)
        def _():
            prob_store(group - 2).wait()

        for within in range(GROUP):
            attend(group % 2, within, GROUP * group + within)
        prob_store(group).start()

    store(3, mixed, mixed_o).start()
    store(8, wide_mixed, wide_o).start()
    store(9, scales, scales_o).start()
    wait(3)

    result = nn(mixed[...], wp[...])
    for rows in strips(0, length, STRIP):
        out = result[rows] + vector(PBIAS)
        proj[rows, :] = out.astype(BF16)
        resid = xin[rows, :].astype(F32) + vector(SCALE_A) * out
        x1[rows, :] = resid
        scaled, _ = normalize(resid)
        h2[rows, :] = (scaled * vector(GAIN2) + vector(SHIFT2)).astype(BF16)

    store(4, proj, proj_o).start()
    store(5, x1, x1_o).start()
    store(6, h2, h2_o).start()
    pieces = [
        (pl.ds(high * (length // 2), length // 2), pl.ds(part * width, width))
        for part in range(hidden // width)
        for high in range(2)
    ]

    def expand(number):
        rows, columns = pieces[number]
        if number % 2 == 0:
            wait(4 + number // 2)
        return nn(h2[rows, :], w1[:, columns])

    coming = expand(0)
    totals = [None, None]
    for number, (rows, columns) in enumerate(pieces):
        current = coming
        if number + 1 < len(pieces):
            coming = expand(number + 1)
        for strip in strips(0, length // 2, STRIP):
            there = pl.ds(rows.start + strip.start, STRIP)
            here = current[strip] + vector(B1 + number // 2)
            normal = 0.5 * lax.erf(here * math.sqrt(0.5)) + 0.5
            density = jnp.exp(-0.5 * here * here) * (1.0 / math.sqrt(2.0 * math.pi))
            act[there, columns] = (here * normal).astype(BF16)
            slope[there, columns] = (normal + here * density).astype(BF16)
        if number % 2 == 0:
            wait(8 + number // 2)
        more = nn(act[rows, columns], w2[columns, :])
        totals[number % 2] = more if number < 2 else totals[number % 2] + more
        if number % 2 == 1:
            part_store(10, act, act_o, columns).start()
            part_store(11, slope, slope_o, columns).start()

    for half in range(2):
        for strip in strips(0, length // 2, STRIP):
            rows = pl.ds(half * (length // 2) + strip.start, STRIP)
            out = totals[half][strip] + vector(B2)
            mlp[rows, :] = out.astype(BF16)
            out_row[rows, :] = (x1[rows, :] + vector(SCALE_M) * out).astype(BF16)

    store(12, mlp, mlp_o).start()
    store(13, out_row, y_o).start()
    for group in range(max(0, heads // together - 2), heads // together):
        prob_store(group).wait()
    ends = {0: (h1, h1_o), 1: (qkv, qkv_o), 3: (mixed, mixed_o), 4: (proj, proj_o), 5: (x1, x1_o), 6: (h2, h2_o),
            7: (xin, xin_o), 8: (wide_mixed, wide_o), 9: (scales, scales_o),
            10: (act, act_o), 11: (slope, slope_o), 12: (mlp, mlp_o), 13: (out_row, y_o)}
    for number, (source, there) in ends.items():
        store(number, source, there).wait()


def hbm_specs(count):
    return [pl.BlockSpec(memory_space=pl.ANY)] * count


def vmem_specs(count):
    return [pl.BlockSpec(memory_space=pltpu.VMEM)] * count


def stacked(stored):
    return [jax.ShapeDtypeStruct((2, *shape), kind) for shape, kind in stored]


def forward(layer, pads, rows, segments, packs, band, weights, kept):
    length, width = rows.shape[1:]
    heads = band[0].shape[0]
    hidden = weights[2][0].shape[1]
    stored = [
        ((length, width), BF16),
        ((length, 3 * width), BF16),
        ((heads, length, length), BF16),
        ((length, width), BF16),
        ((length, width), BF16),
        ((length, width), F32),
        ((length, width), BF16),
        ((length, width), BF16),
        ((length, width), F32),
        ((heads, length), F32),
        ((length, hidden), BF16),
        ((length, hidden), BF16),
        ((length, width), BF16),
        ((length, width), BF16),
    ]
    scratch = [pltpu.VMEM(band[0].shape, F32)] + [pltpu.VMEM(pair[0].shape, BF16) for pair in weights]
    scratch.append(pltpu.VMEM((length, length), F32))
    scratch += [
        pltpu.VMEM((2, 2 * GROUP, length, length) if n == 2 else shape, kind)
        for n, (shape, kind) in enumerate(stored)
    ]
    scratch += [
        pltpu.VMEM((2 * GROUP * length // LANES, length, LANES), F32),
        pltpu.VMEM(packs[0].shape, F32),
        pltpu.SemaphoreType.DMA((14,)),
        pltpu.SemaphoreType.DMA((STORED,)),
        pltpu.SemaphoreType.DMA((2,)),
    ]
    operands = [pads, rows, segments, *packs, *band, *[x for pair in weights for x in pair]]
    held = STORED if layer > 0 else 0
    return pl.pallas_call(
        functools.partial(forward_kernel, layer),
        out_shape=stacked(stored),
        in_specs=[pl.BlockSpec(memory_space=pltpu.SMEM)] + hbm_specs(1) + vmem_specs(3) + hbm_specs(10 + held),
        out_specs=hbm_specs(STORED),
        scratch_shapes=scratch,
        input_output_aliases={len(operands) + n: n for n in range(held)},
        compiler_params=pltpu.CompilerParams(vmem_limit_bytes=VMEM_BYTES),
        name="forward_layer",
    )(*operands, *(kept if layer > 0 else ()))


def backward_kernel(layer, cotangent_hbm, own_pack, other_pack, *refs):
    weights, refs = refs[:8], refs[8:]
    (qkv_i, prob_i, mixed_i, proj_i, x1_i, slope_i, mlp_i, xin_i, scales_i) = refs[:9]
    refs = refs[9 + (7 if layer == 0 else 0) :]
    stores = refs[:7]
    (wqkv, wp, w1, w2, qkv, probs, mixed, proj, x1, slope, mlp, xin, scales, dm, dz, dproj, packed, dx_ref, dx1, dmixed, dscore, diag, sums, tables, g_ref, pack_ref, load_sem, store_sem, prob_sem) = refs[7:]
    dm_o, dz_o, dproj_o, packed_o, dx_o, tables_o, sums_o = stores
    wqkv_hbm, wp_hbm, w1_hbm, w2_hbm = zip(weights[::2], weights[1::2])
    length, width = g_ref.shape
    hidden = w1.shape[1]
    blocks = length // LANES
    pairs = width // LANES
    section = lax.axis_index("section")
    mine = section == layer
    factor = HALF ** (-0.5)
    parts = [pl.ds(part * width, width) for part in range(hidden // width)]
    loads = [(mlp_i.at[layer], mlp)]
    loads += [(tuple(x.at[part, :] for x in w2_hbm), w2.at[part, :]) for part in parts]
    loads += [(slope_i.at[layer], slope)]
    loads += [(tuple(x.at[:, part] for x in w1_hbm), w1.at[:, part]) for part in parts]
    early = len(loads)
    loads += [
        (x1_i.at[layer], x1), (proj_i.at[layer], proj), (wp_hbm, wp), (qkv_i.at[layer], qkv), (mixed_i.at[layer], mixed),
        (scales_i.at[layer], scales), (wqkv_hbm, wqkv), (xin_i.at[layer], xin),
    ]
    upstream_sem = load_sem.at[len(loads)]

    def start(number):
        source, target = loads[number]

        def go(ref):
            pltpu.make_async_copy(ref, target, load_sem.at[number]).start()

        if isinstance(source, tuple):
            pick(mine, *source, go)
        else:
            go(source)

    def load(number):
        target = loads[number][1]
        return pltpu.make_async_copy(target, target, load_sem.at[number])

    def store(number, source, there):
        return pltpu.make_async_copy(source, there.at[layer], store_sem.at[number])

    together = 2 * GROUP

    def prob_load(group):
        return pltpu.make_async_copy(
            prob_i.at[layer, pl.ds(together * group, together)], probs.at[group % 2], prob_sem.at[group % 2]
        )

    def vector(row):
        return pack_ref[row : row + 1, :]

    def put(row, partial):
        sums[row : row + 1, :] = jnp.sum(partial, 0, keepdims=True)

    nothing = jnp.zeros((8, width), F32)

    upstream_hbm = cotangent_hbm.at[section] if layer == 1 else dx_o.at[1]
    pltpu.make_async_copy(upstream_hbm, g_ref, upstream_sem).start()
    pick(mine, own_pack, other_pack, functools.partial(fill, pack_ref))
    for number in range(1 + len(parts)):
        start(number)
    pltpu.make_async_copy(g_ref, g_ref, upstream_sem).wait()
    load(0).wait()
    for number in range(1 + len(parts), early):
        start(number)
    scale_sum = bias_sum = nothing
    for rows in strips(0, length, STRIP):
        upstream = g_ref[rows, :].astype(F32)
        low = (upstream * vector(SCALE_M)).astype(BF16)
        dm[rows, :] = low
        scale_sum = scale_sum + fold(upstream * mlp[rows, :].astype(F32))
        bias_sum = bias_sum + fold(low.astype(F32))
    put(SCALE_M, scale_sum)
    put(B2, bias_sum)
    store(0, dm, dm_o).start()
    pieces = [pl.ds(part * width, width) for part in range(hidden // width)]

    def expand(number):
        load(1 + number).wait()
        return nt(dm[...], w2[pieces[number], :])

    coming = expand(0)
    upper_sum = None
    load(1 + len(parts)).wait()
    for number, columns in enumerate(pieces):
        if number == 1:
            for later in range(early, len(loads)):
                start(later)
            prob_load(0).start()
        load(2 + len(parts) + number).wait()
        current = coming
        if number + 1 < len(pieces):
            coming = expand(number + 1)
        act_sum = nothing
        for there in strips(0, length, STRIP):
            low = (current[there] * slope[there, columns].astype(F32)).astype(BF16)
            dz[there, columns] = low
            act_sum = act_sum + fold(low.astype(F32))
        put(B1 + number, act_sum)
        more = nt(dz[:, columns], w1[:, columns])
        upper_sum = more if number == 0 else upper_sum + more
    store(1, dz, dz_o).start()
    load(early).wait()
    load(early + 1).wait()
    found = [nothing] * 4
    for rows in strips(0, length, STRIP):
        upper = upper_sum[rows]
        scaled, inverse = normalize(x1[rows, :])
        resid = g_ref[rows, :].astype(F32) + norm_back(upper * vector(GAIN2), scaled, inverse)
        dx1[rows, :] = resid
        low = (resid * vector(SCALE_A)).astype(BF16)
        dproj[rows, :] = low
        terms = (upper * scaled, upper, resid * proj[rows, :].astype(F32), low.astype(F32))
        found = [old + fold(term) for old, term in zip(found, terms)]
    for row, partial in zip((GAIN2, SHIFT2, SCALE_A, PBIAS), found):
        put(row, partial)
    store(2, dproj, dproj_o).start()
    load(early + 2).wait()
    dmixed[...] = nt(dproj[...], wp[...]).astype(BF16)
    for number in range(early + 3, early + 6):
        load(number).wait()

    def attend(side, within, pair):
        columns = chunk(pair, LANES)
        key_columns = pl.ds(pl.multiple_of(width + pair * LANES, LANES), LANES)
        value_columns = pl.ds(pl.multiple_of(2 * width + pair * LANES, LANES), LANES)
        values = qkv[:, value_columns]
        above = dmixed[:, columns]
        queries_t = qkv[:, columns].T
        keys_t = qkv[:, key_columns].T
        above_t = above.astype(F32).T
        products = (above.astype(F32) * mixed[:, columns]).T
        grads = [], [], []
        for which in range(2):
            place_in = 2 * within + which
            half = slice(which * HALF, (which + 1) * HALF)
            delta = jnp.sum(products[half], 0, keepdims=True)
            scale = scales[pl.ds(2 * pair + which, 1), :]
            own_values = jnp.where(half_mask(values.shape, which), values, jnp.zeros_like(values))
            edge = (blocks - 1) * LANES
            diag[place_in, :edge, :] = jnp.zeros((edge, LANES), F32)
            for wide in range(blocks // 2):
                prob_grad = nt(own_values, above[2 * LANES * wide : 2 * LANES * (wide + 1)])
                for part in range(2):
                    place = 2 * wide + part
                    low, high = key_rows(place, blocks)
                    lanes = slice(place * LANES, (place + 1) * LANES)
                    first_row = (blocks - 1 - place) * LANES
                    for rows in strips(low, high, 64):
                        here = (probs[side, place_in, rows, lanes].astype(F32) * scale[:, lanes]) * (
                            prob_grad[rows, part * LANES : (part + 1) * LANES] - delta[:, lanes]
                        )
                        dscore[place_in, rows, lanes] = here.astype(BF16)
                        there = slice(first_row + rows.start, first_row + rows.stop)
                        diag[place_in, there, :] = here if place == 0 else diag[place_in, there, :] + here
                    if low > 0:
                        dscore[place_in, :low, lanes] = jnp.zeros((low, LANES), BF16)
                    if high < length:
                        dscore[place_in, high:, lanes] = jnp.zeros((length - high, LANES), BF16)
                    if place == 0:
                        diag[place_in, edge + high :, :] = jnp.zeros((length - high, LANES), F32)
            line = gather_diagonals(diag.at[place_in])
            most = tables.shape[1] - LANES
            tables[pl.ds(2 * pair + which, 1), :] = jnp.concatenate(
                [line[:, REACH + 1 : REACH + 1 + most], line[:, REACH : REACH + LANES]], 1
            )
            grads[0].append(nn(keys_t[half], dscore[place_in]))
            grads[1].append(nt(queries_t[half], dscore[place_in]))
            grads[2].append(nt((above_t[half] * scale).astype(BF16), probs[side, place_in]))
        for found, where, scale in zip(grads, (columns, key_columns, value_columns), (factor, None, None)):
            low = jnp.concatenate(found, 0).astype(BF16)
            if scale is not None:
                low = (low.astype(F32) * scale).astype(BF16)
            packed[:, where] = low.T

    @pl.loop(0, pairs // GROUP)
    def _(group):
        prob_load(group).wait()

        @pl.when(group + 1 < pairs // GROUP)
        def _():
            prob_load(group + 1).start()

        for within in range(GROUP):
            attend(group % 2, within, GROUP * group + within)

    store(3, packed, packed_o).start()
    load(early + 6).wait()
    result = nt(packed[...], wqkv[...])
    load(early + 7).wait()
    found = [nothing] * 4
    for rows in strips(0, length, STRIP):
        upper = result[rows]
        scaled, inverse = normalize(xin[rows, :].astype(F32))
        dx_ref[rows, :] = (dx1[rows, :] + norm_back(upper * vector(GAIN1), scaled, inverse)).astype(BF16)
        terms = (
            upper * scaled,
            upper,
            packed[rows, :width].astype(F32),
            packed[rows, 2 * width :].astype(F32),
        )
        found = [old + fold(term) for old, term in zip(found, terms)]
    for row, partial in zip((GAIN1, SHIFT1, QBIAS, VBIAS), found):
        put(row, partial)
    store(4, dx_ref, dx_o).start()
    store(5, tables, tables_o).start()
    store(6, sums, sums_o).start()
    ends = {0: (dm, dm_o), 1: (dz, dz_o), 2: (dproj, dproj_o), 3: (packed, packed_o), 4: (dx_ref, dx_o), 5: (tables, tables_o), 6: (sums, sums_o)}
    for number, (source, there) in ends.items():
        store(number, source, there).wait()


def backward(layer, cotangent, packs, weights, saved, kept):
    length, width = cotangent.shape[1:]
    hidden = weights[2][0].shape[1]
    h1, qkv, probs, mixed, proj, x1, h2, xin, wide, scales, act, slope, mlp, y = saved
    heads = probs.shape[1]
    span = 2 * length - LANES
    summed = (16, width)
    table = (heads, 5 * LANES)
    stored = [
        ((length, width), BF16),
        ((length, hidden), BF16),
        ((length, width), BF16),
        ((length, 3 * width), BF16),
        ((length, width), BF16),
        (table, F32),
        (summed, F32),
    ]
    reads = [qkv, probs, wide, proj, x1, slope, mlp, xin, scales]
    scratch = [pltpu.VMEM(pair[0].shape, BF16) for pair in weights]
    scratch += [pltpu.VMEM((2, 2 * GROUP, length, length) if x is probs else x.shape[1:], x.dtype) for x in reads]
    scratch += [pltpu.VMEM(shape, kind) for shape, kind in stored[:5]]
    scratch += [
        pltpu.VMEM((length, width), F32),
        pltpu.VMEM((length, width), BF16),
        pltpu.VMEM((2 * GROUP, length, length), BF16),
        pltpu.VMEM((2 * GROUP, span, LANES), F32),
        pltpu.VMEM(summed, F32),
        pltpu.VMEM(table, F32),
        pltpu.VMEM((length, width), BF16),
        pltpu.VMEM(packs[0].shape, F32),
        pltpu.SemaphoreType.DMA((19,)),
        pltpu.SemaphoreType.DMA((7,)),
        pltpu.SemaphoreType.DMA((2,)),
    ]
    operands = [cotangent, *packs, *[x for pair in weights for x in pair], *reads]
    held = 7 if layer == 0 else 0
    return pl.pallas_call(
        functools.partial(backward_kernel, layer),
        out_shape=stacked(stored),
        in_specs=hbm_specs(1) + vmem_specs(2) + hbm_specs(8 + len(reads) + held),
        out_specs=hbm_specs(7),
        scratch_shapes=scratch,
        input_output_aliases={len(operands) + n: n for n in range(held)},
        compiler_params=pltpu.CompilerParams(vmem_limit_bytes=VMEM_BYTES),
        name="backward_layer",
    )(*operands, *(kept if layer == 0 else ()))


def small_lines(width):
    lines = width // LANES
    places = [(row, tile, row * lines + tile) for row in range(10) for tile in range(lines)]
    return places + [(B1, tile, B1 * lines + tile) for tile in range(4 * lines)]


def reverse_lanes(values):
    lane = lax.broadcasted_iota(jnp.int32, values.shape, 1)
    for place in range(LANES.bit_length() - 1):
        step = 1 << place
        up, down = pltpu.roll(values, step, 1), pltpu.roll(values, LANES - step, 1)
        values = jnp.where((lane // step) % 2 == 1, up, down)
    return values


def widen_kernel(sum_hbm, y_hbm, dx_hbm, small_ref, *refs):
    bigs, rows_out, vectors, table_ref = refs[:4], refs[4:6], refs[6 : 7 + VECTORS], refs[7 + VECTORS]
    narrow, wide, passing, load_sem, store_sem, pass_sem = refs[8 + VECTORS :]
    depth, width = narrow.shape[:2]
    blocks = [(0, slice(b * width, (b + 1) * width), slice(0, width)) for b in range(4)]
    for target, count in ((1, 4), (2, 3), (3, 1)):
        blocks += [(target, slice(0, width), slice(b * width, (b + 1) * width)) for b in range(count)]

    def load(block):
        rows = pl.ds(block * width, width)
        return pltpu.make_async_copy(sum_hbm.at[rows, :], narrow.at[block % depth], load_sem.at[block % depth])

    def store(block):
        target, rows, columns = blocks[block]
        there = bigs[target].at[rows, columns]
        return pltpu.make_async_copy(wide.at[block % depth], there, store_sem.at[block % depth])

    def fetch(number):
        return pltpu.make_async_copy((y_hbm, dx_hbm)[number], passing.at[number], pass_sem.at[0, number])

    def put(number):
        return pltpu.make_async_copy(passing.at[number], rows_out[number], pass_sem.at[1, number])

    for block in range(depth):
        load(block).start()
    for number in range(2):
        fetch(number).start()
    for block in range(len(blocks)):
        if block == depth:
            for number in range(2):
                fetch(number).wait()
                put(number).start()
        load(block).wait()
        if block >= depth:
            store(block - depth).wait()
        for rows in strips(0, width, 64):
            wide[block % depth, rows, :] = narrow[block % depth, rows, :].astype(F32)
        store(block).start()
        if block + depth < len(blocks):
            load(block + depth).start()
    places = small_lines(width)
    for row, tile, line in places:
        vectors[row][:, tile * LANES : (tile + 1) * LANES] = small_ref[line : line + 1, :]
    first = len(places)
    heads, _, entries = table_ref.shape
    tiles = -(-entries // LANES)
    flipped = reverse_lanes(small_ref[first : first + heads * tiles, :])
    for head in range(heads):
        for tile in range(tiles - 1):
            line = head * tiles + tile
            there = (tiles - 2 - tile) * LANES
            table_ref[head, :, there : there + LANES] = flipped[line : line + 1]
        line = first + head * tiles + tiles - 1
        table_ref[head, :, entries - 1 :] = small_ref[line : line + 1, 0:1]
    for block in range(len(blocks) - depth, len(blocks)):
        store(block).wait()
    for number in range(2):
        put(number).wait()


def widen(summed, small, y, dx, width, heads, entries):
    bigs = [(4 * width, width), (width, 4 * width), (width, 3 * width), (width, width)]
    shapes = [(1, width)] * 10 + [(1, 4 * width), (heads, 1, entries)]
    return pl.pallas_call(
        widen_kernel,
        out_shape=[jax.ShapeDtypeStruct(shape, F32) for shape in bigs]
        + [jax.ShapeDtypeStruct(y.shape, BF16)] * 2
        + [jax.ShapeDtypeStruct(shape, F32) for shape in shapes],
        in_specs=hbm_specs(3) + vmem_specs(1),
        out_specs=hbm_specs(6) + vmem_specs(VECTORS + 2),
        scratch_shapes=[
            pltpu.VMEM((3, width, width), BF16),
            pltpu.VMEM((3, width, width), F32),
            pltpu.VMEM((2, *y.shape), BF16),
            pltpu.SemaphoreType.DMA((3,)),
            pltpu.SemaphoreType.DMA((3,)),
            pltpu.SemaphoreType.DMA((2, 2)),
        ],
        compiler_params=pltpu.CompilerParams(vmem_limit_bytes=VMEM_BYTES),
        name="widen",
    )(summed, y, dx, small)


BLOCK = 256
LAG = 3


def reduce_kernel(bits, chunks, blocks, lags, window, lined, *refs):
    (a_ref, dm_ref, h2_ref, dz_ref, h1_ref, dp_ref, o_ref, dproj_ref, y_ref, dx_ref, sums_ref, tables_ref) = refs[:12]
    out_ref, small_out_ref, y_out, dx_out = refs[12:16]
    refs = refs[16:]
    (lhs, rhs, grads, total, crossing, landed, smalls, small_ref, small_landed, small_total) = refs[:10]
    small_received, received = refs[10 : 10 + bits], refs[10 + bits : -10]
    (load_sem, send_sem, recv_sem, small_send, small_recv, store_sem, cross_send, cross_recv, row_sem, credit) = refs[-10:]
    me = lax.axis_index("dp")
    section = lax.axis_index("section")
    beside = 1 - section
    rows = BLOCK * blocks
    width = grads.shape[1]
    per_side = width // BLOCK
    last = 2 * bits
    steps = 10 if lined else last
    starts = [0] + [lags[0] + lags[1] * place for place in range(steps + 1)]

    barrier = pltpu.get_barrier_semaphore()
    for place in range(bits):
        stride = 1 << place
        other = me + stride * (1 - 2 * ((me // stride) % 2))
        pl.semaphore_signal(barrier, inc=1, device_id={"dp": other}, device_id_type=MESH)
    pl.semaphore_signal(barrier, inc=1, device_id={"section": beside}, device_id_type=MESH)
    pl.semaphore_wait(barrier, bits + 1)

    def across(source, target, number):
        return pltpu.make_async_remote_copy(
            src_ref=source,
            dst_ref=target,
            send_sem=cross_send.at[number],
            recv_sem=cross_recv.at[number],
            device_id={"section": beside},
            device_id_type=MESH,
        )

    def row_copy(number):
        source, target = ((y_ref, y_out), (dx_ref, dx_out))[number]
        return pltpu.make_async_copy(source.at[section], target.at[section], row_sem.at[number])

    def row_across(number):
        source, target = ((y_ref, y_out), (dx_ref, dx_out))[number]
        return across(source.at[beside], target.at[section], window + 1 + number)

    families = (
        (a_ref, dm_ref, 4 * per_side, True),
        (h2_ref, dz_ref, 4 * per_side, False),
        (h1_ref, dp_ref, 3 * per_side, False),
        (o_ref, dproj_ref, per_side, False),
    )
    n_blocks = 12 * per_side

    def load(block):
        slot = block % 2
        first = 0
        for left, right, count, walks in families:
            @pl.when((block >= first) & (block < first + count))
            def _():
                local = block - first
                if walks:
                    left_column = local * BLOCK
                    right_column = 0
                else:
                    left_column = (local % per_side) * BLOCK
                    right_column = (local // per_side) * width
                for number, layer in enumerate((section, beside)):
                    pltpu.make_async_copy(
                        left.at[layer, :, pl.ds(pl.multiple_of(left_column, BLOCK), BLOCK)],
                        lhs.at[slot, number],
                        load_sem.at[0, slot],
                    ).start()
                    pltpu.make_async_copy(
                        right.at[layer, :, pl.ds(pl.multiple_of(right_column, BLOCK), width)],
                        rhs.at[slot, number],
                        load_sem.at[1, slot],
                    ).start()
            first += count

    def produce(block, sub, side):
        slot = block % 2
        pltpu.make_async_copy(lhs.at[slot], lhs.at[slot], load_sem.at[0, slot]).wait()
        pltpu.make_async_copy(rhs.at[slot], rhs.at[slot], load_sem.at[1, slot]).wait()

        @pl.when(block + 1 < n_blocks)
        def _():
            load(block + 1)

        crossing[side, sub * BLOCK : (sub + 1) * BLOCK, :] = dot(lhs[slot, 1], rhs[slot, 1], 0, 0).astype(BF16)
        grads[chunk(block, BLOCK), :] = dot(lhs[slot, 0], rhs[slot, 0], 0, 0).astype(BF16)

    def turn(chunk):
        place = chunk % 9
        return place % 2 + place // 5 - place // 6

    def partner(rotation, stage):
        stride = lax.shift_left(jnp.int32(1), (stage + rotation) % bits)
        mine = (me // stride) % 2
        return mine, me + stride * (1 - 2 * mine)

    def offset(base, height, rotation, stage):
        for earlier in range(stage):
            mine, _ = partner(rotation, earlier)
            base = base + mine * (height >> (earlier + 1))
        return base

    def piece(ref, start, size):
        return ref.at[pl.ds(pl.multiple_of(start, size), size)]

    def send(position, base, height, rotation, source, landing, result, slot, sems):
        send_at, recv_at = sems
        if position < bits:
            stage = position
            half = height >> (stage + 1)
            mine, other = partner(rotation, stage)
            start = offset(base, height, rotation, stage) + (1 - mine) * half
            src, dst = piece(source, start, half), landing[stage].at[slot]
        else:
            stage = last - 1 - position
            half = height >> (stage + 1)
            mine, other = partner(rotation, stage)
            start = offset(base, height, rotation, stage + 1)
            src = dst = piece(result, start, half)
        return pltpu.make_async_remote_copy(
            src_ref=src,
            dst_ref=dst,
            send_sem=send_at.at[position],
            recv_sem=recv_at.at[position, slot],
            device_id={"dp": other},
            device_id_type=MESH,
        )

    def take(position, base, height, rotation, source, landing, result, slot, sems):
        send(position - 1, base, height, rotation, source, landing, result, slot, sems).wait_recv()
        stage = position - 1
        if stage < bits:
            half = height >> (stage + 1)
            start = pl.multiple_of(offset(base, height, rotation, stage + 1), half)
            keep = pl.ds(start, half)
            value = source[keep, :].astype(jnp.float32) + landing[stage][slot].astype(jnp.float32)
            target = result if stage == bits - 1 else source
            target[keep, :] = value.astype(target.dtype)

    def step(position, *way):
        if position > 0:
            take(position, *way)
        if position < last:
            send(position, *way).start()

    main = (grads, received, total)
    main_sems = (send_sem, recv_sem)

    def cross(side):
        return across(crossing.at[side], landed.at[side], side)

    def give(part):
        side = part % window

        @pl.when(part >= window)
        def _():
            cross(side).wait_send()
            pl.semaphore_wait(credit, 1)

        for sub in range(blocks):
            block = part * blocks + sub

            @pl.when(block < n_blocks)
            def _():
                produce(block, sub, side)

        cross(side).start()

    def join(part):
        side = part % window
        cross(side).wait_recv()
        there = chunk(part, rows)
        grads[there, :] = (grads[there, :].astype(F32) + landed[side].astype(F32)).astype(BF16)

        @pl.when(part < chunks - window)
        def _():
            pl.semaphore_signal(credit, inc=1, device_id={"section": beside}, device_id_type=MESH)

    row_z = me // 4
    side_z = row_z // 2
    middle = (row_z + side_z) % 2
    inner, outer = me + 4 * (1 - 2 * side_z), me - 4 * (1 - 2 * side_z)

    def line_plan(early, part):
        place = part % 8
        first = 1 + (place // 3 if early else place % 3)
        second = 3 - first
        mine_first, mine_second = (me // first) % 2, (me // second) % 2
        peer_first = me + first * (1 - 2 * mine_first)
        peer_second = me + second * (1 - 2 * mine_second)
        base = part * rows
        before = (place + 5) // 8 + (place + 2) // 8
        if early:
            slot = 2 * (part // 8) + place // 3
            landing = received[4:]
            quarter = rows // 4
            line = base
            whole = base + row_z * quarter
            size_first = quarter // 2
        else:
            slot = part - 2 * (part // 8) - before
            landing = received[:4]
            whole = base
            size_first = rows // 2
        size_second = size_first // 2
        keep_first = whole + mine_first * size_first
        keep_second = keep_first + mine_second * size_second
        if not early:
            line = keep_second
            quarter = size_second // 4
        everyone = None
        line_land, cross_land, first_land, second_land = [ref.at[slot] for ref in landing]
        mostly = line + quarter * (1 - side_z)
        ending = line + 3 * quarter * side_z
        near, far = line + 2 * quarter * side_z, line + 2 * quarter * (1 - side_z)
        swap_first = (everyone, everyone, peer_first, whole + (1 - mine_first) * size_first, size_first, keep_first, first_land)
        swap_second = (
            everyone, everyone, peer_second, keep_first + (1 - mine_second) * size_second, size_second, keep_second, second_land
        )
        inward = (0, 1, inner, mostly, 3 * quarter, mostly, line_land)
        between = (1, 1, inner, far, 2 * quarter, near, cross_land)
        outward = (1, 0, outer, ending, quarter, ending, line_land.at[pl.ds(0, quarter)])
        back_inward = (0, 1, inner, ending, quarter, None, None)
        back_between = (1, 1, inner, near, 2 * quarter, None, None)
        back_outward = (1, 0, outer, mostly, 3 * quarter, None, None)
        back_first = (everyone, everyone, peer_first, keep_first, size_first, None, None)
        back_second = (everyone, everyone, peer_second, keep_second, size_second, None, None)
        if early:
            return [inward, between, outward, swap_first, swap_second,
                    back_second, back_first, back_inward, back_between, back_outward]
        return [swap_first, swap_second, inward, between, outward,
                back_inward, back_between, back_outward, back_second, back_first]

    def only(role, act):
        if role is None:
            act()
        else:
            pl.when(middle == role)(act)

    def line_step(position, part):
        def run(early):
            plan = line_plan(early, part)

            def copy(number):
                sender, receiver, peer, start, size, arrives, lands = plan[number]
                source = grads if arrives is not None else total
                here = pl.ds(pl.multiple_of(start, 16), size)
                return pltpu.make_async_remote_copy(
                    src_ref=source.at[here],
                    dst_ref=total.at[here] if arrives is None else lands,
                    send_sem=send_sem.at[number],
                    recv_sem=recv_sem.at[number, part],
                    device_id={"dp": peer},
                    device_id_type=MESH,
                )

            def arrive():
                size, arrives, lands = plan[position - 1][4:]
                copy(position - 1).wait_recv()
                if arrives is not None:
                    there = pl.ds(pl.multiple_of(arrives, 16), size)
                    value = (grads[there, :].astype(F32) + lands[...].astype(F32)).astype(BF16)
                    if position == 5:
                        total[there, :] = value
                    else:
                        grads[there, :] = value

            if position > 0:
                only(plan[position - 1][1], arrive)
            if position == 5 and not early:

                def keep():
                    size = rows // 16
                    there = pl.ds(pl.multiple_of(plan[1][5] + row_z * size, 16), size)
                    total[there, :] = grads[there, :]

                only(1, keep)
            if position < 10:
                only(plan[position][0], lambda: copy(position).start())

        early = (part % 8) % 3 == 2

        @pl.when(early)
        def _():
            run(True)

        @pl.when(jnp.logical_not(early))
        def _():
            run(False)

    def line_rows(role):
        ends = ([128, 64, 48, 0, 0, 16, 0, 0, 64, 128], [192, 0, 0, 32, 16, 16, 32, 64, 0, 0])
        middles = ([128, 64, 0, 32, 16, 0, 32, 48, 64, 128], [0, 128, 64, 32, 16, 16, 32, 0, 128, 192])
        late, soon = middles if role else ends
        count = sum(part % 8 % 3 == 2 for part in range(chunks))
        return [(chunks - count) * a + count * b for a, b in zip(late, soon)]

    def walk(position, part):
        if position == 0:
            join(part)
        base = part * rows
        if lined:
            line_step(position, part)
        else:
            step(position, base, rows, turn(part), *main, part, main_sems)
        if position == steps:
            there = pl.ds(pl.multiple_of(base, rows), rows)
            pltpu.make_async_copy(total.at[there], out_ref.at[there], store_sem.at[0]).start()

    def small_cross():
        return across(smalls.at[beside], small_landed, window)

    def walk_small(position):
        height = small_ref.shape[0]
        if position == 0:
            small_cross().wait_recv()
            small_ref[...] = smalls[section] + small_landed[...]
        way = (0, height, 0, small_ref, small_received, small_total, 0, (small_send, small_recv))
        step(position, *way)

    load(jnp.int32(0))
    smalls[...] = jnp.zeros_like(smalls)
    places = small_lines(width)
    for layer in range(2):
        for row, tile, line in places:
            if row == B1:
                row, tile = B1 + tile // (width // LANES), tile % (width // LANES)
            smalls[layer, line : line + 1, :] = sums_ref[layer, row : row + 1, tile * LANES : (tile + 1) * LANES]
        line = len(places)
        for head in range(tables_ref.shape[1]):
            for tile in range(tables_ref.shape[2] // LANES):
                lanes = slice(tile * LANES, (tile + 1) * LANES)
                smalls[layer, line : line + 1, :] = tables_ref[layer, head : head + 1, lanes]
                line += 1
    small_cross().start()
    for number in range(2):
        row_copy(number).start()
        row_across(number).start()

    @pl.loop(0, chunks + starts[-1])
    def _(tick):
        @pl.when(tick < chunks)
        def _():
            give(tick)

        for position in range(steps + 1):
            part = tick - starts[position + 1]

            @pl.when((part >= 0) & (part < chunks))
            def _():
                walk(position, part)

            if position <= last:

                @pl.when(part == 0)
                def _():
                    walk_small(position)

    small_out_ref[...] = small_total[...]
    for position in range(last):
        stage = position if position < bits else last - 1 - position
        size = small_received[stage]
        pltpu.make_async_copy(size, size, small_send.at[position]).wait()
        if not lined:
            size = received[stage]
            pltpu.make_async_copy(size, size, send_sem.at[position]).wait()
    if lined:
        for role in range(2):

            @pl.when(middle == role)
            def _():
                for number, amount in enumerate(line_rows(role)):
                    if amount > 0:
                        size = grads.at[pl.ds(0, amount)]
                        pltpu.make_async_copy(size, size, send_sem.at[number]).wait()
    for side in range(window):
        cross(side).wait_send()
    small_cross().wait_send()
    for number in range(2):
        row_copy(number).wait()
        row_across(number).wait()
    pltpu.make_async_copy(total, out_ref, store_sem.at[0]).wait()


def reduce_gradients(a, dm, h2, dz, h1, packed, o, dproj, y, dx, sums, tables):
    parts = lax.axis_size("dp")
    bits = parts.bit_length() - 1
    blocks = max(1, 16 * parts // BLOCK)
    layers, length, width = h1.shape
    n_blocks = 12 * width // BLOCK
    chunks = -(-n_blocks // blocks)
    rows = BLOCK * blocks
    lags, window = ((2, LAG), 4) if blocks == 1 else ((0, LAG), 1)
    lines = len(small_lines(width)) + tables.shape[1] * tables.shape[2] // LANES
    height = -(-lines // (8 * parts)) * 8 * parts
    small = (height, LANES)
    lined = parts == 16
    if lined:
        early = sum(part % 8 % 3 == 2 for part in range(chunks))
        lands = [(chunks - early, size) for size in (48, 32, 128, 64)] + [(early, size) for size in (192, 128, 32, 16)]
    else:
        lands = [(chunks, rows >> (s + 1)) for s in range(bits)]
    steps = 10 if lined else 2 * bits
    return pl.pallas_call(
        functools.partial(reduce_kernel, bits, chunks, blocks, lags, window, lined),
        out_shape=(
            jax.ShapeDtypeStruct((chunks * rows, width), BF16),
            jax.ShapeDtypeStruct(small, F32),
            jax.ShapeDtypeStruct(y.shape, BF16),
            jax.ShapeDtypeStruct(dx.shape, BF16),
        ),
        in_specs=hbm_specs(10) + vmem_specs(2),
        out_specs=hbm_specs(1) + vmem_specs(1) + hbm_specs(2),
        scratch_shapes=[
            pltpu.VMEM((2, layers, length, BLOCK), BF16),
            pltpu.VMEM((2, layers, length, width), BF16),
            pltpu.VMEM((chunks * rows, width), BF16),
            pltpu.VMEM((chunks * rows, width), BF16),
            pltpu.VMEM((window, rows, width), BF16),
            pltpu.VMEM((window, rows, width), BF16),
            pltpu.VMEM((layers, *small), F32),
            pltpu.VMEM(small, F32),
            pltpu.VMEM(small, F32),
            pltpu.VMEM(small, F32),
            *[pltpu.VMEM((1, height >> (s + 1), LANES), F32) for s in range(bits)],
            *[pltpu.VMEM((*size, width), BF16) for size in lands],
            pltpu.SemaphoreType.DMA((2, 2)),
            pltpu.SemaphoreType.DMA((steps,)),
            pltpu.SemaphoreType.DMA((steps, chunks)),
            pltpu.SemaphoreType.DMA((2 * bits,)),
            pltpu.SemaphoreType.DMA((2 * bits, 1)),
            pltpu.SemaphoreType.DMA((1,)),
            pltpu.SemaphoreType.DMA((window + 3,)),
            pltpu.SemaphoreType.DMA((window + 3,)),
            pltpu.SemaphoreType.DMA((2,)),
            pltpu.SemaphoreType.REGULAR,
        ],
        compiler_params=pltpu.CompilerParams(
            collective_id=0, has_side_effects=True, vmem_limit_bytes=VMEM_BYTES
        ),
        name="reduce_gradients",
    )(a, dm, h2, dz, h1, packed, o, dproj, y, dx, sums, tables)


def swapped(block):
    return lax.ppermute(block, "section", [(0, 1), (1, 0)])


def per_device(
    patches,
    segment_ids,
    pad_counts,
    norm1_gain,
    norm1_bias,
    qkv_weight,
    query_bias,
    value_bias,
    rel_table,
    proj_weight,
    proj_bias,
    scale_attn,
    norm2_gain,
    norm2_bias,
    fc1_weight,
    fc1_bias,
    fc2_weight,
    fc2_bias,
    scale_mlp,
    cotangent,
):
    micro, length, width = patches.shape
    heads, entries = rel_table.shape[1:]
    vectors = (
        norm1_gain,
        norm1_bias,
        query_bias,
        value_bias,
        proj_bias,
        scale_attn,
        norm2_gain,
        norm2_bias,
        fc2_bias,
        scale_mlp,
        fc1_bias,
    )
    own = pack(vectors, rel_table.transpose(1, 0, 2))
    own_band = bias_band(own, heads, length)
    own_weights = (qkv_weight[0], proj_weight[0], fc1_weight[0], fc2_weight[0])
    other = swapped(own)
    weights = [(x, swapped(x)) for x in own_weights]
    other_band = bias_band(other, heads, length)
    packs, band = (own, other), (own_band, other_band)
    saved = None
    rows = patches
    for layer in range(2):
        saved = forward(layer, pad_counts, rows, segment_ids, packs, band, weights, saved)
    kept = None
    for layer in (1, 0):
        kept = backward(layer, cotangent, packs, weights, saved, kept)
    dm, dz, dproj, packed, dx, tables, sums = kept
    h1, mixed, h2, act, y = saved[0], saved[3], saved[6], saved[10], saved[13]
    summed, small, y, dx = reduce_gradients(
        act, dm, h2, dz, h1, packed, mixed, dproj, y, dx, sums, tables
    )
    fc2_grad, fc1_grad, qkv_grad, proj_grad, outputs, in_grads, *small_grads = widen(
        summed, small, y, dx, width, heads, entries
    )
    table_grad = small_grads[VECTORS + 1].transpose(1, 0, 2)
    return (
        outputs[None],
        in_grads[None],
        small_grads[GAIN1],
        small_grads[SHIFT1],
        qkv_grad[None],
        small_grads[QBIAS],
        small_grads[VBIAS],
        table_grad,
        proj_grad[None],
        small_grads[PBIAS],
        small_grads[SCALE_A],
        small_grads[GAIN2],
        small_grads[SHIFT2],
        fc1_grad[None],
        small_grads[B1],
        fc2_grad[None],
        small_grads[B2],
        small_grads[SCALE_M],
    )


def solution(mesh):
    placed = (
        P("dp", None, None),
        P("dp", None),
        P("dp"),
        P("section", None),
        P("section", None),
        P("section", None, None),
        P("section", None),
        P("section", None),
        P("section", None, None),
        P("section", None, None),
        P("section", None),
        P("section", None),
        P("section", None),
        P("section", None),
        P("section", None, None),
        P("section", None),
        P("section", None, None),
        P("section", None),
        P("section", None),
        P("dp", None, None),
    )
    return jax.shard_map(
        per_device,
        mesh=mesh,
        in_specs=placed,
        out_specs=(
            P("section", "dp", None, None),
            P("section", "dp", None, None),
            P("section", None),
            P("section", None),
            P("section", None, None),
            P("section", None),
            P("section", None),
            P("section", None, None),
            P("section", None, None),
            P("section", None),
            P("section", None),
            P("section", None),
            P("section", None),
            P("section", None, None),
            P("section", None),
            P("section", None, None),
            P("section", None),
            P("section", None),
        ),
        check_vma=False,
    )
```

```python
import functools
import math

import jax
import jax.numpy as jnp
from jax import lax
from jax.experimental import pallas as pl
from jax.experimental.pallas import tpu as pltpu
from jax.sharding import PartitionSpec as P

MESH = pl.DeviceIdType.MESH
BF16, F32 = jnp.bfloat16, jnp.float32
VMEM_BYTES = 60 * 1024 * 1024
LANES = 128
HALF = 64
REACH = 2 * LANES
GAIN1, SHIFT1, QBIAS, VBIAS, PBIAS, SCALE_A, GAIN2, SHIFT2, B2, SCALE_M, B1 = range(11)
VECTORS = 10
STORED = 14
STRIP = 16
GROUP = 3


def dot(left, right, left_dim, right_dim):
    return lax.dot_general(
        left, right, (((left_dim,), (right_dim,)), ((), ())), preferred_element_type=F32
    )


def nn(left, right):
    return dot(left, right, 1, 0)


def nt(left, right):
    return dot(left, right, 1, 1)


def normalize(values):
    centered = values - jnp.mean(values, -1, keepdims=True)
    inverse = lax.rsqrt(jnp.mean(centered * centered, -1, keepdims=True) + 1e-06)
    return centered * inverse, inverse


def norm_back(upper, scaled, inverse):
    return inverse * (
        upper
        - jnp.mean(upper, -1, keepdims=True)
        - scaled * jnp.mean(upper * scaled, -1, keepdims=True)
    )


def fold(values):
    return jnp.sum(values.reshape(values.shape[0] // 8, 8, values.shape[1]), 0)


def half_mask(shape, which):
    return lax.broadcasted_iota(jnp.int32, shape, 1) // HALF == which


def strips(first, last, size):
    return [slice(start, start + size) for start in range(first, last, size)]


def chunk(index, size):
    return pl.ds(pl.multiple_of(index * size, size), size)


def skew_bias(reversed_row, target):
    span, lanes = target.shape
    rows = pltpu.roll(jnp.broadcast_to(reversed_row, (8, reversed_row.shape[1])), 1, 1, stride=1, stride_axis=0)
    tiles = span // lanes
    for fine in range(lanes // 8):
        moved = rows if fine == 0 else pltpu.roll(rows, 8 * fine, 1)
        for coarse in range(tiles):
            place = 8 * (fine + lanes // 8 * coarse)
            target[place : place + 8, :] = moved[:, lanes * (tiles - coarse) : lanes * (tiles - coarse + 1)]


def gather_diagonals(source):
    span, lanes = source.shape
    tiles = span // lanes
    width = span + lanes
    blank = jnp.zeros((8, lanes), F32)
    found = None
    for fine in range(lanes // 8):
        places = [8 * (fine + lanes // 8 * coarse) for coarse in reversed(range(tiles))]
        line = jnp.concatenate([blank] + [source[place : place + 8, :] for place in places], 1)
        if fine > 0:
            line = pltpu.roll(line, width - 8 * fine, 1)
        found = line if found is None else found + line
    row = lax.broadcasted_iota(jnp.int32, found.shape, 0)
    for place in range(3):
        moved = pltpu.roll(found, width - (1 << place), 1)
        found = jnp.where((row // (1 << place)) % 2 == 1, moved, found)
    return jnp.sum(found, 0, keepdims=True)


def key_rows(query_block, blocks):
    reach = REACH // LANES
    return max(0, query_block - reach) * LANES, min(blocks, query_block + reach + 1) * LANES


def pick(mine, own, other, act):
    @pl.when(mine)
    def _():
        act(own)

    @pl.when(jnp.logical_not(mine))
    def _():
        act(other)


def pack_kernel(*refs):
    *vectors, bias_ref, table_ref, pack_ref = refs
    width = pack_ref.shape[1]
    heads, _, entries = table_ref.shape
    pack_ref[...] = jnp.zeros_like(pack_ref)
    for row, vector in enumerate(vectors):
        pack_ref[row : row + 1, :] = vector[...]
    for part in range(bias_ref.shape[1] // width):
        pack_ref[B1 + part : B1 + part + 1, :] = bias_ref[:, part * width : (part + 1) * width]
    first = pack_ref.shape[0] - heads
    tiles = entries // LANES
    lane = lax.broadcasted_iota(jnp.int32, (heads, LANES), 1)
    ending = jnp.broadcast_to(table_ref[:, 0, entries - 1 :], (heads, LANES))
    pack_ref[first:, :LANES] = jnp.where(lane == LANES - 1, ending, 0.0)
    for tile in range(tiles):
        there = (tiles - tile) * LANES
        pack_ref[first:, there : there + LANES] = reverse_lanes(table_ref[:, 0, tile * LANES : (tile + 1) * LANES])


def pack(vectors, rel_table):
    heads = rel_table.shape[0]
    return pl.pallas_call(
        pack_kernel,
        out_shape=jax.ShapeDtypeStruct((16 + heads, vectors[0].shape[1]), F32),
        in_specs=vmem_specs(len(vectors) + 1),
        out_specs=pl.BlockSpec(memory_space=pltpu.VMEM),
        name="pack_vectors",
    )(*vectors, rel_table)


def fill(target, source):
    target[...] = source[...]


def band_kernel(pack_ref, band_hbm, band, store_sem):
    heads = band.shape[0]
    tables = pack_ref.shape[0] - heads
    edge = jnp.zeros((1, LANES), F32)

    @pl.loop(0, heads // 4)
    def _(group):
        for within in range(4):
            head = 4 * group + within
            kept = pack_ref[pl.ds(tables + head, 1), :]
            skew_bias(jnp.concatenate([edge, kept, edge], 1), band.at[head])

    there = pltpu.make_async_copy(band, band_hbm, store_sem.at[0])
    there.start()
    there.wait()


def bias_band(packed, heads, length):
    shape = (heads, 2 * length - LANES, LANES)
    return pl.pallas_call(
        band_kernel,
        out_shape=jax.ShapeDtypeStruct(shape, F32),
        in_specs=vmem_specs(1),
        out_specs=pl.BlockSpec(memory_space=pl.ANY),
        scratch_shapes=[pltpu.VMEM(shape, F32), pltpu.SemaphoreType.DMA((1,))],
        compiler_params=pltpu.CompilerParams(vmem_limit_bytes=VMEM_BYTES + 2 * 1024 * 1024),
        name="bias_band",
    )(packed)


def forward_kernel(layer, pads, x_hbm, seg_ref, own_pack, other_pack, own_band, other_band, *refs):
    wqkv_own, wqkv_other, wp_own, wp_other, w1_own, w1_other, w2_own, w2_other = refs[:8]
    refs = refs[8 + (STORED if layer > 0 else 0) :]
    stores = refs[:STORED]
    (bias, wqkv, wp, w1, w2, mask, h1, qkv, probs, mixed, proj, x1, h2, xin, wide_mixed, scales, act, slope, mlp, out_row, held, pack_ref, load_sem, store_sem, prob_sem) = refs[STORED:]
    h1_o, qkv_o, prob_o, mixed_o, proj_o, x1_o, h2_o, xin_o, wide_o, scales_o, act_o, slope_o, mlp_o, y_o = stores
    hidden = w1.shape[1]
    length, width = xin.shape
    heads = bias.shape[0]
    blocks = length // LANES
    section = lax.axis_index("section")
    mine = section == layer
    factor = HALF ** (-0.5)
    thirds = [pl.ds(part * width, width) for part in range(3)]

    def load(number):
        if number < 3:
            part = thirds[number]
            return wqkv_own.at[:, part], wqkv_other.at[:, part], wqkv.at[:, part], load_sem.at[number]
        if number == 3:
            return wp_own, wp_other, wp, load_sem.at[3]
        part = pl.ds((number % 4) * width, width)
        if number < 8:
            return w1_own.at[:, part], w1_other.at[:, part], w1.at[:, part], load_sem.at[number]
        return w2_own.at[part, :], w2_other.at[part, :], w2.at[part, :], load_sem.at[number]

    def start(number):
        own, other, target, sem = load(number)
        pick(mine, own, other, lambda source: pltpu.make_async_copy(source, target, sem).start())

    def wait(number):
        own, other, target, sem = load(number)
        pltpu.make_async_copy(target, target, sem).wait()

    def store(number, source, there):
        return pltpu.make_async_copy(source, there.at[layer], store_sem.at[number])

    def part_store(number, source, there, columns):
        return pltpu.make_async_copy(source.at[:, columns], there.at[layer, :, columns], store_sem.at[number])

    def vector(row):
        return pack_ref[row : row + 1, :]

    source = x_hbm.at[section] if layer == 0 else y_o.at[0]
    pltpu.make_async_copy(source, xin, load_sem.at[12]).start()
    start(0)
    pltpu.make_async_copy(xin, xin, load_sem.at[12]).wait()
    start(1)
    start(2)
    pick(mine, own_band, other_band, lambda source: pltpu.make_async_copy(source, bias, load_sem.at[13]).start())
    pick(mine, own_pack, other_pack, functools.partial(fill, pack_ref))
    segment = seg_ref[pl.ds(section, 1), :].astype(F32)
    key_segment = jnp.broadcast_to(segment, (LANES, length)).T

    for rows in strips(0, length, STRIP):
        scaled, _ = normalize(xin[rows, :].astype(F32))
        h1[rows, :] = (scaled * vector(GAIN1) + vector(SHIFT1)).astype(BF16)
    for part in range(3):
        wait(part)

    alive = length - pads[section]
    for place in range(blocks):
        lanes = slice(place * LANES, (place + 1) * LANES)
        for rows in strips(0, length, 64):
            key = lax.broadcasted_iota(jnp.int32, (64, LANES), 0) + rows.start
            query = lax.broadcasted_iota(jnp.int32, (64, LANES), 1) + place * LANES
            allowed = ((key_segment[rows] == segment[:, lanes]) & (key < alive)) | (key == query)
            mask[rows, lanes] = jnp.where(allowed, 0.0, -1000000000.0)

    store(0, h1, h1_o).start()
    store(7, xin, xin_o).start()
    projections = [(part, pl.ds(high * (length // 2), length // 2)) for part in range(3) for high in range(2)]

    def project(number):
        part, rows = projections[number]
        return nn(h1[rows, :], wqkv[:, thirds[part]])

    coming = project(0)
    for number, (part, rows) in enumerate(projections):
        current = coming
        if number + 1 < len(projections):
            coming = project(number + 1)
        for strip in strips(0, length // 2, STRIP):
            piece = current[strip]
            if part == 0:
                piece = (piece + vector(QBIAS)) * factor
            if part == 2:
                piece = piece + vector(VBIAS)
            qkv[pl.ds(rows.start + strip.start, STRIP), thirds[part]] = piece.astype(BF16)
    store(1, qkv, qkv_o).start()
    pltpu.make_async_copy(bias, bias, load_sem.at[13]).wait()
    for number in range(3, 12):
        start(number)
    together = 2 * GROUP

    def prob_store(group):
        return pltpu.make_async_copy(
            probs.at[group % 2], prob_o.at[layer, pl.ds(together * group, together)], prob_sem.at[group % 2]
        )

    def attend(side, within, pair):
        columns = chunk(pair, LANES)
        queries = qkv[:, columns]
        keys = qkv[:, pl.ds(pl.multiple_of(width + pair * LANES, LANES), LANES)]
        values = qkv[:, pl.ds(pl.multiple_of(2 * width + pair * LANES, LANES), LANES)].T
        outs = []
        for which in range(2):
            own_keys = jnp.where(half_mask(keys.shape, which), keys, jnp.zeros_like(keys))
            lines = []
            for wide in range(blocks // 2):
                scores = nt(own_keys, queries[2 * LANES * wide : 2 * LANES * (wide + 1)])
                for part in range(2):
                    place = 2 * wide + part
                    low, high = key_rows(place, blocks)
                    lanes = slice(place * LANES, (place + 1) * LANES)
                    first = (blocks - 1 - place) * LANES
                    spare = (2 * within + which) * blocks + place
                    highest = None
                    for rows in strips(low, high, 64):
                        here = (
                            scores[rows, part * LANES : (part + 1) * LANES]
                            + bias[2 * pair + which, first + rows.start : first + rows.stop, :]
                            + mask[rows, lanes]
                        )
                        held[spare, rows, :] = here
                        top = jnp.max(here.reshape(8, 8, LANES), 0)
                        highest = top if highest is None else jnp.maximum(highest, top)
                    highest = jnp.max(highest, 0, keepdims=True)
                    sums = jnp.zeros((8, LANES), F32)
                    for rows in strips(low, high, 64):
                        expo = jnp.exp(held[spare, rows, :] - highest)
                        probs[side, 2 * within + which, rows, lanes] = expo.astype(BF16)
                        sums = sums + fold(expo)
                    lines.append(1.0 / jnp.sum(sums, 0, keepdims=True))
                    if low > 0:
                        probs[side, 2 * within + which, :low, lanes] = jnp.zeros((low, LANES), BF16)
                    if high < length:
                        probs[side, 2 * within + which, high:, lanes] = jnp.zeros((length - high, LANES), BF16)
            scale = jnp.concatenate(lines, 1)
            scales[pl.ds(2 * pair + which, 1), :] = scale
            outs.append(nn(values[which * HALF : (which + 1) * HALF], probs[side, 2 * within + which]) * scale)
        out = jnp.concatenate(outs, 0).T
        wide_mixed[:, columns] = out
        mixed[:, columns] = out.astype(BF16)

    @pl.loop(0, heads // together)
    def _(group):
        @pl.when(group >= 2)
        def _():
            prob_store(group - 2).wait()

        for within in range(GROUP):
            attend(group % 2, within, GROUP * group + within)
        prob_store(group).start()

    store(3, mixed, mixed_o).start()
    store(8, wide_mixed, wide_o).start()
    store(9, scales, scales_o).start()
    wait(3)

    results = [nn(mixed[half, :], wp[...]) for half in strips(0, length, length // 2)]
    for rows in strips(0, length, STRIP):
        there = rows.start % (length // 2)
        out = results[rows.start // (length // 2)][there : there + STRIP] + vector(PBIAS)
        proj[rows, :] = out.astype(BF16)
        resid = xin[rows, :].astype(F32) + vector(SCALE_A) * out
        x1[rows, :] = resid
        scaled, _ = normalize(resid)
        h2[rows, :] = (scaled * vector(GAIN2) + vector(SHIFT2)).astype(BF16)

    store(4, proj, proj_o).start()
    store(5, x1, x1_o).start()
    store(6, h2, h2_o).start()
    pieces = [
        (pl.ds(high * (length // 2), length // 2), pl.ds(part * width, width))
        for part in range(hidden // width)
        for high in range(2)
    ]

    def expand(number):
        rows, columns = pieces[number]
        return nn(h2[rows, :], w1[:, columns])

    for number in range(4, 12):
        wait(number)
    coming = expand(0)
    totals = [None, None]
    for number, (rows, columns) in enumerate(pieces):
        current = coming
        if number + 1 < len(pieces):
            coming = expand(number + 1)
        for strip in strips(0, length // 2, STRIP):
            there = pl.ds(rows.start + strip.start, STRIP)
            here = current[strip] + vector(B1 + number // 2)
            normal = 0.5 * lax.erf(here * math.sqrt(0.5)) + 0.5
            density = jnp.exp(-0.5 * here * here) * (1.0 / math.sqrt(2.0 * math.pi))
            act[there, columns] = (here * normal).astype(BF16)
            slope[there, columns] = (normal + here * density).astype(BF16)
        more = nn(act[rows, columns], w2[columns, :])
        totals[number % 2] = more if number < 2 else totals[number % 2] + more
        if number in (len(pieces) // 2 - 1, len(pieces) - 1):
            columns = pl.ds((number // 4) * 2 * width, 2 * width)
            part_store(10, act, act_o, columns).start()
            part_store(11, slope, slope_o, columns).start()

    for half in range(2):
        for strip in strips(0, length // 2, STRIP):
            rows = pl.ds(half * (length // 2) + strip.start, STRIP)
            out = totals[half][strip] + vector(B2)
            mlp[rows, :] = out.astype(BF16)
            out_row[rows, :] = (x1[rows, :] + vector(SCALE_M) * out).astype(BF16)

    store(12, mlp, mlp_o).start()
    store(13, out_row, y_o).start()
    for group in range(max(0, heads // together - 2), heads // together):
        prob_store(group).wait()
    ends = {0: (h1, h1_o), 1: (qkv, qkv_o), 3: (mixed, mixed_o), 4: (proj, proj_o), 5: (x1, x1_o), 6: (h2, h2_o),
            7: (xin, xin_o), 8: (wide_mixed, wide_o), 9: (scales, scales_o),
            10: (act, act_o), 11: (slope, slope_o), 12: (mlp, mlp_o), 13: (out_row, y_o)}
    for number, (source, there) in ends.items():
        store(number, source, there).wait()


def hbm_specs(count):
    return [pl.BlockSpec(memory_space=pl.ANY)] * count


def vmem_specs(count):
    return [pl.BlockSpec(memory_space=pltpu.VMEM)] * count


def stacked(stored):
    return [jax.ShapeDtypeStruct((2, *shape), kind) for shape, kind in stored]


def forward(layer, pads, rows, segments, packs, band, weights, kept):
    length, width = rows.shape[1:]
    heads = band[0].shape[0]
    hidden = weights[2][0].shape[1]
    stored = [
        ((length, width), BF16),
        ((length, 3 * width), BF16),
        ((heads, length, length), BF16),
        ((length, width), BF16),
        ((length, width), BF16),
        ((length, width), F32),
        ((length, width), BF16),
        ((length, width), BF16),
        ((length, width), F32),
        ((heads, length), F32),
        ((length, hidden), BF16),
        ((length, hidden), BF16),
        ((length, width), BF16),
        ((length, width), BF16),
    ]
    scratch = [pltpu.VMEM(band[0].shape, F32)] + [pltpu.VMEM(pair[0].shape, BF16) for pair in weights]
    scratch.append(pltpu.VMEM((length, length), F32))
    scratch += [
        pltpu.VMEM((2, 2 * GROUP, length, length) if n == 2 else shape, kind)
        for n, (shape, kind) in enumerate(stored)
    ]
    scratch += [
        pltpu.VMEM((2 * GROUP * length // LANES, length, LANES), F32),
        pltpu.VMEM(packs[0].shape, F32),
        pltpu.SemaphoreType.DMA((14,)),
        pltpu.SemaphoreType.DMA((STORED,)),
        pltpu.SemaphoreType.DMA((2,)),
    ]
    operands = [pads, rows, segments, *packs, *band, *[x for pair in weights for x in pair]]
    held = STORED if layer > 0 else 0
    return pl.pallas_call(
        functools.partial(forward_kernel, layer),
        out_shape=stacked(stored),
        in_specs=[pl.BlockSpec(memory_space=pltpu.SMEM)] + hbm_specs(1) + vmem_specs(3) + hbm_specs(10 + held),
        out_specs=hbm_specs(STORED),
        scratch_shapes=scratch,
        input_output_aliases={len(operands) + n: n for n in range(held)},
        compiler_params=pltpu.CompilerParams(vmem_limit_bytes=VMEM_BYTES),
        name="forward_layer",
    )(*operands, *(kept if layer > 0 else ()))


def backward_kernel(layer, cotangent_hbm, own_pack, other_pack, *refs):
    weights, refs = refs[:8], refs[8:]
    (qkv_i, prob_i, mixed_i, proj_i, x1_i, slope_i, mlp_i, xin_i, scales_i) = refs[:9]
    refs = refs[9 + (7 if layer == 0 else 0) :]
    stores = refs[:7]
    (wqkv, wp, w1, w2, qkv, probs, mixed, proj, x1, slope, mlp, xin, scales, dm, dz, dproj, packed, dx_ref, dx1, dmixed, dscore, diag, sums, tables, g_ref, pack_ref, load_sem, store_sem, prob_sem) = refs[7:]
    dm_o, dz_o, dproj_o, packed_o, dx_o, tables_o, sums_o = stores
    wqkv_hbm, wp_hbm, w1_hbm, w2_hbm = zip(weights[::2], weights[1::2])
    length, width = g_ref.shape
    hidden = w1.shape[1]
    blocks = length // LANES
    pairs = width // LANES
    section = lax.axis_index("section")
    mine = section == layer
    factor = HALF ** (-0.5)
    parts = [pl.ds(part * width, width) for part in range(hidden // width)]
    loads = [(mlp_i.at[layer], mlp)]
    loads += [(tuple(x.at[part, :] for x in w2_hbm), w2.at[part, :]) for part in parts]
    loads += [(slope_i.at[layer, :, part], slope.at[:, part]) for part in parts]
    loads += [(tuple(x.at[:, part] for x in w1_hbm), w1.at[:, part]) for part in parts]
    early = len(loads)
    loads += [
        (x1_i.at[layer], x1), (proj_i.at[layer], proj), (wp_hbm, wp), (qkv_i.at[layer], qkv), (mixed_i.at[layer], mixed),
        (scales_i.at[layer], scales), (wqkv_hbm, wqkv), (xin_i.at[layer], xin),
    ]
    upstream_sem = load_sem.at[len(loads)]

    def start(number):
        source, target = loads[number]

        def go(ref):
            pltpu.make_async_copy(ref, target, load_sem.at[number]).start()

        if isinstance(source, tuple):
            pick(mine, *source, go)
        else:
            go(source)

    def load(number):
        target = loads[number][1]
        return pltpu.make_async_copy(target, target, load_sem.at[number])

    def store(number, source, there):
        return pltpu.make_async_copy(source, there.at[layer], store_sem.at[number])

    together = 2 * GROUP

    def prob_load(group):
        return pltpu.make_async_copy(
            prob_i.at[layer, pl.ds(together * group, together)], probs.at[group % 2], prob_sem.at[group % 2]
        )

    def vector(row):
        return pack_ref[row : row + 1, :]

    def put(row, partial):
        sums[row : row + 1, :] = jnp.sum(partial, 0, keepdims=True)

    nothing = jnp.zeros((8, width), F32)

    upstream_hbm = cotangent_hbm.at[section] if layer == 1 else dx_o.at[1]
    pltpu.make_async_copy(upstream_hbm, g_ref, upstream_sem).start()
    pick(mine, own_pack, other_pack, functools.partial(fill, pack_ref))
    for number in (0, 1):
        start(number)
    pltpu.make_async_copy(g_ref, g_ref, upstream_sem).wait()
    load(0).wait()
    for number in (5, 9, 2, 6, 10):
        start(number)
    scale_sum = bias_sum = nothing
    for rows in strips(0, length, STRIP):
        upstream = g_ref[rows, :].astype(F32)
        low = (upstream * vector(SCALE_M)).astype(BF16)
        dm[rows, :] = low
        scale_sum = scale_sum + fold(upstream * mlp[rows, :].astype(F32))
        bias_sum = bias_sum + fold(low.astype(F32))
    put(SCALE_M, scale_sum)
    put(B2, bias_sum)
    store(0, dm, dm_o).start()
    pieces = [pl.ds(part * width, width) for part in range(hidden // width)]

    def expand(number):
        load(1 + number).wait()
        return nt(dm[...], w2[pieces[number], :])

    coming = expand(0)
    upper_sum = None
    for number, columns in enumerate(pieces):
        if number == 0:
            for later in (3, 7, 11, 4, 8, 12):
                start(later)
        if number == 2:
            for later in range(early, len(loads)):
                start(later)
            prob_load(0).start()
        load(5 + number).wait()
        load(9 + number).wait()
        current = coming
        if number + 1 < len(pieces):
            coming = expand(number + 1)
        act_sum = nothing
        for there in strips(0, length, STRIP):
            low = (current[there] * slope[there, columns].astype(F32)).astype(BF16)
            dz[there, columns] = low
            act_sum = act_sum + fold(low.astype(F32))
        put(B1 + number, act_sum)
        more = nt(dz[:, columns], w1[:, columns])
        upper_sum = more if number == 0 else upper_sum + more
    store(1, dz, dz_o).start()
    load(early).wait()
    load(early + 1).wait()
    found = [nothing] * 4
    for rows in strips(0, length, STRIP):
        upper = upper_sum[rows]
        scaled, inverse = normalize(x1[rows, :])
        resid = g_ref[rows, :].astype(F32) + norm_back(upper * vector(GAIN2), scaled, inverse)
        dx1[rows, :] = resid
        low = (resid * vector(SCALE_A)).astype(BF16)
        dproj[rows, :] = low
        terms = (upper * scaled, upper, resid * proj[rows, :].astype(F32), low.astype(F32))
        found = [old + fold(term) for old, term in zip(found, terms)]
    for row, partial in zip((GAIN2, SHIFT2, SCALE_A, PBIAS), found):
        put(row, partial)
    store(2, dproj, dproj_o).start()
    load(early + 2).wait()
    dmixed[...] = nt(dproj[...], wp[...]).astype(BF16)
    for number in range(early + 3, early + 6):
        load(number).wait()

    def attend(side, within, pair):
        columns = chunk(pair, LANES)
        key_columns = pl.ds(pl.multiple_of(width + pair * LANES, LANES), LANES)
        value_columns = pl.ds(pl.multiple_of(2 * width + pair * LANES, LANES), LANES)
        values = qkv[:, value_columns]
        above = dmixed[:, columns]
        queries_t = qkv[:, columns].T
        keys_t = qkv[:, key_columns].T
        above_t = above.astype(F32).T
        products = (above.astype(F32) * mixed[:, columns]).T
        grads = [], [], []
        for which in range(2):
            place_in = 2 * within + which
            half = slice(which * HALF, (which + 1) * HALF)
            delta = jnp.sum(products[half], 0, keepdims=True)
            scale = scales[pl.ds(2 * pair + which, 1), :]
            own_values = jnp.where(half_mask(values.shape, which), values, jnp.zeros_like(values))
            edge = (blocks - 1) * LANES
            diag[place_in, :edge, :] = jnp.zeros((edge, LANES), F32)
            for wide in range(blocks // 2):
                prob_grad = nt(own_values, above[2 * LANES * wide : 2 * LANES * (wide + 1)])
                for part in range(2):
                    place = 2 * wide + part
                    low, high = key_rows(place, blocks)
                    lanes = slice(place * LANES, (place + 1) * LANES)
                    first_row = (blocks - 1 - place) * LANES
                    for rows in strips(low, high, 64):
                        here = (probs[side, place_in, rows, lanes].astype(F32) * scale[:, lanes]) * (
                            prob_grad[rows, part * LANES : (part + 1) * LANES] - delta[:, lanes]
                        )
                        dscore[place_in, rows, lanes] = here.astype(BF16)
                        there = slice(first_row + rows.start, first_row + rows.stop)
                        diag[place_in, there, :] = here if place == 0 else diag[place_in, there, :] + here
                    if low > 0:
                        dscore[place_in, :low, lanes] = jnp.zeros((low, LANES), BF16)
                    if high < length:
                        dscore[place_in, high:, lanes] = jnp.zeros((length - high, LANES), BF16)
                    if place == 0:
                        diag[place_in, edge + high :, :] = jnp.zeros((length - high, LANES), F32)
            line = gather_diagonals(diag.at[place_in])
            most = tables.shape[1] - LANES
            tables[pl.ds(2 * pair + which, 1), :] = jnp.concatenate(
                [line[:, REACH + 1 : REACH + 1 + most], line[:, REACH : REACH + LANES]], 1
            )
            grads[0].append(nn(keys_t[half], dscore[place_in]))
            grads[1].append(nt(queries_t[half], dscore[place_in]))
            grads[2].append(nt((above_t[half] * scale).astype(BF16), probs[side, place_in]))
        for found, where, scale in zip(grads, (columns, key_columns, value_columns), (factor, None, None)):
            low = jnp.concatenate(found, 0).astype(BF16)
            if scale is not None:
                low = (low.astype(F32) * scale).astype(BF16)
            packed[:, where] = low.T

    @pl.loop(0, pairs // GROUP)
    def _(group):
        prob_load(group).wait()

        @pl.when(group + 1 < pairs // GROUP)
        def _():
            prob_load(group + 1).start()

        for within in range(GROUP):
            attend(group % 2, within, GROUP * group + within)

    store(3, packed, packed_o).start()
    load(early + 6).wait()
    result = nt(packed[...], wqkv[...])
    load(early + 7).wait()
    found = [nothing] * 4
    for rows in strips(0, length, STRIP):
        upper = result[rows]
        scaled, inverse = normalize(xin[rows, :].astype(F32))
        dx_ref[rows, :] = (dx1[rows, :] + norm_back(upper * vector(GAIN1), scaled, inverse)).astype(BF16)
        terms = (
            upper * scaled,
            upper,
            packed[rows, :width].astype(F32),
            packed[rows, 2 * width :].astype(F32),
        )
        found = [old + fold(term) for old, term in zip(found, terms)]
    for row, partial in zip((GAIN1, SHIFT1, QBIAS, VBIAS), found):
        put(row, partial)
    store(4, dx_ref, dx_o).start()
    store(5, tables, tables_o).start()
    store(6, sums, sums_o).start()
    ends = {0: (dm, dm_o), 1: (dz, dz_o), 2: (dproj, dproj_o), 3: (packed, packed_o), 4: (dx_ref, dx_o), 5: (tables, tables_o), 6: (sums, sums_o)}
    for number, (source, there) in ends.items():
        store(number, source, there).wait()


def backward(layer, cotangent, packs, weights, saved, kept):
    length, width = cotangent.shape[1:]
    hidden = weights[2][0].shape[1]
    h1, qkv, probs, mixed, proj, x1, h2, xin, wide, scales, act, slope, mlp, y = saved
    heads = probs.shape[1]
    span = 2 * length - LANES
    summed = (16, width)
    table = (heads, 5 * LANES)
    stored = [
        ((length, width), BF16),
        ((length, hidden), BF16),
        ((length, width), BF16),
        ((length, 3 * width), BF16),
        ((length, width), BF16),
        (table, F32),
        (summed, F32),
    ]
    reads = [qkv, probs, wide, proj, x1, slope, mlp, xin, scales]
    scratch = [pltpu.VMEM(pair[0].shape, BF16) for pair in weights]
    scratch += [pltpu.VMEM((2, 2 * GROUP, length, length) if x is probs else x.shape[1:], x.dtype) for x in reads]
    scratch += [pltpu.VMEM(shape, kind) for shape, kind in stored[:5]]
    scratch += [
        pltpu.VMEM((length, width), F32),
        pltpu.VMEM((length, width), BF16),
        pltpu.VMEM((2 * GROUP, length, length), BF16),
        pltpu.VMEM((2 * GROUP, span, LANES), F32),
        pltpu.VMEM(summed, F32),
        pltpu.VMEM(table, F32),
        pltpu.VMEM((length, width), BF16),
        pltpu.VMEM(packs[0].shape, F32),
        pltpu.SemaphoreType.DMA((22,)),
        pltpu.SemaphoreType.DMA((7,)),
        pltpu.SemaphoreType.DMA((2,)),
    ]
    operands = [cotangent, *packs, *[x for pair in weights for x in pair], *reads]
    held = 7 if layer == 0 else 0
    return pl.pallas_call(
        functools.partial(backward_kernel, layer),
        out_shape=stacked(stored),
        in_specs=hbm_specs(1) + vmem_specs(2) + hbm_specs(8 + len(reads) + held),
        out_specs=hbm_specs(7),
        scratch_shapes=scratch,
        input_output_aliases={len(operands) + n: n for n in range(held)},
        compiler_params=pltpu.CompilerParams(vmem_limit_bytes=VMEM_BYTES),
        name="backward_layer",
    )(*operands, *(kept if layer == 0 else ()))


def small_lines(width):
    lines = width // LANES
    places = [(row, tile, row * lines + tile) for row in range(10) for tile in range(lines)]
    return places + [(B1, tile, B1 * lines + tile) for tile in range(4 * lines)]


def reverse_lanes(values):
    lane = lax.broadcasted_iota(jnp.int32, values.shape, 1)
    for place in range(LANES.bit_length() - 1):
        step = 1 << place
        up, down = pltpu.roll(values, step, 1), pltpu.roll(values, LANES - step, 1)
        values = jnp.where((lane // step) % 2 == 1, up, down)
    return values


def widen_kernel(sum_hbm, y_hbm, dx_hbm, small_ref, *refs):
    bigs, rows_out, vectors, table_ref = refs[:4], refs[4:6], refs[6 : 7 + VECTORS], refs[7 + VECTORS]
    narrow, wide, passing, load_sem, store_sem, pass_sem = refs[8 + VECTORS :]
    depth, width = narrow.shape[:2]
    blocks = [(0, slice(b * width, (b + 1) * width), slice(0, width)) for b in range(4)]
    for target, count in ((1, 4), (2, 3), (3, 1)):
        blocks += [(target, slice(0, width), slice(b * width, (b + 1) * width)) for b in range(count)]

    def load(block):
        rows = pl.ds(block * width, width)
        return pltpu.make_async_copy(sum_hbm.at[rows, :], narrow.at[block % depth], load_sem.at[block % depth])

    def store(block):
        target, rows, columns = blocks[block]
        there = bigs[target].at[rows, columns]
        return pltpu.make_async_copy(wide.at[block % depth], there, store_sem.at[block % depth])

    def fetch(number):
        return pltpu.make_async_copy((y_hbm, dx_hbm)[number], passing.at[number], pass_sem.at[0, number])

    def put(number):
        return pltpu.make_async_copy(passing.at[number], rows_out[number], pass_sem.at[1, number])

    for block in range(depth):
        load(block).start()
    for number in range(2):
        fetch(number).start()
    for block in range(len(blocks)):
        if block == depth:
            for number in range(2):
                fetch(number).wait()
                put(number).start()
        load(block).wait()
        if block >= depth:
            store(block - depth).wait()
        for rows in strips(0, width, 64):
            wide[block % depth, rows, :] = narrow[block % depth, rows, :].astype(F32)
        store(block).start()
        if block + depth < len(blocks):
            load(block + depth).start()
    places = small_lines(width)
    for row, tile, line in places:
        vectors[row][:, tile * LANES : (tile + 1) * LANES] = small_ref[line : line + 1, :]
    first = len(places)
    heads, _, entries = table_ref.shape
    tiles = -(-entries // LANES)
    flipped = reverse_lanes(small_ref[first : first + heads * tiles, :])
    for head in range(heads):
        for tile in range(tiles - 1):
            line = head * tiles + tile
            there = (tiles - 2 - tile) * LANES
            table_ref[head, :, there : there + LANES] = flipped[line : line + 1]
        line = first + head * tiles + tiles - 1
        table_ref[head, :, entries - 1 :] = small_ref[line : line + 1, 0:1]
    for block in range(len(blocks) - depth, len(blocks)):
        store(block).wait()
    for number in range(2):
        put(number).wait()


def widen(summed, small, y, dx, width, heads, entries):
    bigs = [(4 * width, width), (width, 4 * width), (width, 3 * width), (width, width)]
    shapes = [(1, width)] * 10 + [(1, 4 * width), (heads, 1, entries)]
    return pl.pallas_call(
        widen_kernel,
        out_shape=[jax.ShapeDtypeStruct(shape, F32) for shape in bigs]
        + [jax.ShapeDtypeStruct(y.shape, BF16)] * 2
        + [jax.ShapeDtypeStruct(shape, F32) for shape in shapes],
        in_specs=hbm_specs(3) + vmem_specs(1),
        out_specs=hbm_specs(6) + vmem_specs(VECTORS + 2),
        scratch_shapes=[
            pltpu.VMEM((3, width, width), BF16),
            pltpu.VMEM((3, width, width), F32),
            pltpu.VMEM((2, *y.shape), BF16),
            pltpu.SemaphoreType.DMA((3,)),
            pltpu.SemaphoreType.DMA((3,)),
            pltpu.SemaphoreType.DMA((2, 2)),
        ],
        compiler_params=pltpu.CompilerParams(vmem_limit_bytes=VMEM_BYTES),
        name="widen",
    )(summed, y, dx, small)


BLOCK = 256
LAG = 3


def reduce_kernel(bits, chunks, blocks, lags, window, lined, *refs):
    (a_ref, dm_ref, h2_ref, dz_ref, h1_ref, dp_ref, o_ref, dproj_ref, y_ref, dx_ref, sums_ref, tables_ref) = refs[:12]
    out_ref, small_out_ref, y_out, dx_out = refs[12:16]
    refs = refs[16:]
    (lhs, rhs, grads, total, crossing, landed, smalls, small_ref, small_landed, small_total) = refs[:10]
    small_received, received = refs[10 : 10 + bits], refs[10 + bits : -10]
    (load_sem, send_sem, recv_sem, small_send, small_recv, store_sem, cross_send, cross_recv, row_sem, credit) = refs[-10:]
    me = lax.axis_index("dp")
    section = lax.axis_index("section")
    beside = 1 - section
    rows = BLOCK * blocks
    width = grads.shape[1]
    per_side = width // BLOCK
    last = 2 * bits
    steps = 10 if lined else last
    starts = [0] + [lags[0] + lags[1] * place for place in range(steps + 1)]

    barrier = pltpu.get_barrier_semaphore()
    for place in range(bits):
        stride = 1 << place
        other = me + stride * (1 - 2 * ((me // stride) % 2))
        pl.semaphore_signal(barrier, inc=1, device_id={"dp": other}, device_id_type=MESH)
    pl.semaphore_signal(barrier, inc=1, device_id={"section": beside}, device_id_type=MESH)
    pl.semaphore_wait(barrier, bits + 1)

    def across(source, target, number):
        return pltpu.make_async_remote_copy(
            src_ref=source,
            dst_ref=target,
            send_sem=cross_send.at[number],
            recv_sem=cross_recv.at[number],
            device_id={"section": beside},
            device_id_type=MESH,
        )

    def row_copy(number):
        source, target = ((y_ref, y_out), (dx_ref, dx_out))[number]
        return pltpu.make_async_copy(source.at[section], target.at[section], row_sem.at[number])

    def row_across(number):
        source, target = ((y_ref, y_out), (dx_ref, dx_out))[number]
        return across(source.at[beside], target.at[section], window + 1 + number)

    families = (
        (a_ref, dm_ref, 4 * per_side, True),
        (h2_ref, dz_ref, 4 * per_side, False),
        (h1_ref, dp_ref, 3 * per_side, False),
        (o_ref, dproj_ref, per_side, False),
    )
    n_blocks = 12 * per_side

    def load(block):
        slot = block % 2
        first = 0
        for left, right, count, walks in families:
            @pl.when((block >= first) & (block < first + count))
            def _():
                local = block - first
                if walks:
                    left_column = local * BLOCK
                    right_column = 0
                else:
                    left_column = (local % per_side) * BLOCK
                    right_column = (local // per_side) * width
                for number, layer in enumerate((section, beside)):
                    pltpu.make_async_copy(
                        left.at[layer, :, pl.ds(pl.multiple_of(left_column, BLOCK), BLOCK)],
                        lhs.at[slot, number],
                        load_sem.at[0, slot],
                    ).start()
                    pltpu.make_async_copy(
                        right.at[layer, :, pl.ds(pl.multiple_of(right_column, BLOCK), width)],
                        rhs.at[slot, number],
                        load_sem.at[1, slot],
                    ).start()
            first += count

    def produce(block, sub, side):
        slot = block % 2
        pltpu.make_async_copy(lhs.at[slot], lhs.at[slot], load_sem.at[0, slot]).wait()
        pltpu.make_async_copy(rhs.at[slot], rhs.at[slot], load_sem.at[1, slot]).wait()

        @pl.when(block + 1 < n_blocks)
        def _():
            load(block + 1)

        crossing[side, sub * BLOCK : (sub + 1) * BLOCK, :] = dot(lhs[slot, 1], rhs[slot, 1], 0, 0).astype(BF16)
        grads[chunk(block, BLOCK), :] = dot(lhs[slot, 0], rhs[slot, 0], 0, 0).astype(BF16)

    def turn(chunk):
        place = chunk % 9
        return place % 2 + place // 5 - place // 6

    def partner(rotation, stage):
        stride = lax.shift_left(jnp.int32(1), (stage + rotation) % bits)
        mine = (me // stride) % 2
        return mine, me + stride * (1 - 2 * mine)

    def offset(base, height, rotation, stage):
        for earlier in range(stage):
            mine, _ = partner(rotation, earlier)
            base = base + mine * (height >> (earlier + 1))
        return base

    def piece(ref, start, size):
        return ref.at[pl.ds(pl.multiple_of(start, size), size)]

    def send(position, base, height, rotation, source, landing, result, slot, sems):
        send_at, recv_at = sems
        if position < bits:
            stage = position
            half = height >> (stage + 1)
            mine, other = partner(rotation, stage)
            start = offset(base, height, rotation, stage) + (1 - mine) * half
            src, dst = piece(source, start, half), landing[stage].at[slot]
        else:
            stage = last - 1 - position
            half = height >> (stage + 1)
            mine, other = partner(rotation, stage)
            start = offset(base, height, rotation, stage + 1)
            src = dst = piece(result, start, half)
        return pltpu.make_async_remote_copy(
            src_ref=src,
            dst_ref=dst,
            send_sem=send_at.at[position],
            recv_sem=recv_at.at[position, slot],
            device_id={"dp": other},
            device_id_type=MESH,
        )

    def take(position, base, height, rotation, source, landing, result, slot, sems):
        send(position - 1, base, height, rotation, source, landing, result, slot, sems).wait_recv()
        stage = position - 1
        if stage < bits:
            half = height >> (stage + 1)
            start = pl.multiple_of(offset(base, height, rotation, stage + 1), half)
            keep = pl.ds(start, half)
            value = source[keep, :].astype(jnp.float32) + landing[stage][slot].astype(jnp.float32)
            target = result if stage == bits - 1 else source
            target[keep, :] = value.astype(target.dtype)

    def step(position, *way):
        if position > 0:
            take(position, *way)
        if position < last:
            send(position, *way).start()

    main = (grads, received, total)
    main_sems = (send_sem, recv_sem)

    def cross(side):
        return across(crossing.at[side], landed.at[side], side)

    def give(part):
        side = part % window

        @pl.when(part >= window)
        def _():
            cross(side).wait_send()
            pl.semaphore_wait(credit, 1)

        for sub in range(blocks):
            block = part * blocks + sub

            @pl.when(block < n_blocks)
            def _():
                produce(block, sub, side)

        cross(side).start()

    def join(part):
        side = part % window
        cross(side).wait_recv()
        there = chunk(part, rows)
        grads[there, :] = (grads[there, :].astype(F32) + landed[side].astype(F32)).astype(BF16)

        @pl.when(part < chunks - window)
        def _():
            pl.semaphore_signal(credit, inc=1, device_id={"section": beside}, device_id_type=MESH)

    row_z = me // 4
    side_z = row_z // 2
    middle = (row_z + side_z) % 2
    inner, outer = me + 4 * (1 - 2 * side_z), me - 4 * (1 - 2 * side_z)

    def line_plan(early, part):
        place = part % 8
        first = 1 + (place // 2 if early else place % 2 * ((place + 5) // 8))
        second = 3 - first
        mine_first, mine_second = (me // first) % 2, (me // second) % 2
        peer_first = me + first * (1 - 2 * mine_first)
        peer_second = me + second * (1 - 2 * mine_second)
        base = part * rows
        before = 1 + (place + 5) // 8
        if early:
            slot = 2 * (part // 8) + place // 2
            landing = received[4:]
            quarter = rows // 4
            line = base
            whole = base + row_z * quarter
            size_first = quarter // 2
        else:
            slot = part - 2 * (part // 8) - before
            landing = received[:4]
            whole = base
            size_first = rows // 2
        size_second = size_first // 2
        keep_first = whole + mine_first * size_first
        keep_second = keep_first + mine_second * size_second
        if not early:
            line = keep_second
            quarter = size_second // 4
        everyone = None
        line_land, cross_land, first_land, second_land = [ref.at[slot] for ref in landing]
        mostly = line + quarter * (1 - side_z)
        ending = line + 3 * quarter * side_z
        near, far = line + 2 * quarter * side_z, line + 2 * quarter * (1 - side_z)
        swap_first = (everyone, everyone, peer_first, whole + (1 - mine_first) * size_first, size_first, keep_first, first_land)
        swap_second = (
            everyone, everyone, peer_second, keep_first + (1 - mine_second) * size_second, size_second, keep_second, second_land
        )
        inward = (0, 1, inner, mostly, 3 * quarter, mostly, line_land)
        between = (1, 1, inner, far, 2 * quarter, near, cross_land)
        outward = (1, 0, outer, ending, quarter, ending, line_land.at[pl.ds(0, quarter)])
        back_inward = (0, 1, inner, ending, quarter, None, None)
        back_between = (1, 1, inner, near, 2 * quarter, None, None)
        back_outward = (1, 0, outer, mostly, 3 * quarter, None, None)
        back_first = (everyone, everyone, peer_first, keep_first, size_first, None, None)
        back_second = (everyone, everyone, peer_second, keep_second, size_second, None, None)
        if early:
            return [inward, between, outward, swap_first, swap_second,
                    back_second, back_first, back_inward, back_between, back_outward]
        return [swap_first, swap_second, inward, between, outward,
                back_inward, back_between, back_outward, back_second, back_first]

    def only(role, act):
        if role is None:
            act()
        else:
            pl.when(middle == role)(act)

    def line_step(position, part):
        def run(early):
            plan = line_plan(early, part)

            def copy(number):
                sender, receiver, peer, start, size, arrives, lands = plan[number]
                source = grads if arrives is not None else total
                here = pl.ds(pl.multiple_of(start, 16), size)
                return pltpu.make_async_remote_copy(
                    src_ref=source.at[here],
                    dst_ref=total.at[here] if arrives is None else lands,
                    send_sem=send_sem.at[number],
                    recv_sem=recv_sem.at[number, part],
                    device_id={"dp": peer},
                    device_id_type=MESH,
                )

            def arrive():
                size, arrives, lands = plan[position - 1][4:]
                copy(position - 1).wait_recv()
                if arrives is not None:
                    there = pl.ds(pl.multiple_of(arrives, 16), size)
                    value = (grads[there, :].astype(F32) + lands[...].astype(F32)).astype(BF16)
                    if position == 5:
                        total[there, :] = value
                    else:
                        grads[there, :] = value

            if position > 0:
                only(plan[position - 1][1], arrive)
            if position == 5 and not early:

                def keep():
                    size = rows // 16
                    there = pl.ds(pl.multiple_of(plan[1][5] + row_z * size, 16), size)
                    total[there, :] = grads[there, :]

                only(1, keep)
            if position < 10:
                only(plan[position][0], lambda: copy(position).start())

        early = (part % 8 == 0) | (part % 8 == 2)

        @pl.when(early)
        def _():
            run(True)

        @pl.when(jnp.logical_not(early))
        def _():
            run(False)

    def line_rows(role):
        ends = ([128, 64, 48, 0, 0, 16, 0, 0, 64, 128], [192, 0, 0, 32, 16, 16, 32, 64, 0, 0])
        middles = ([128, 64, 0, 32, 16, 0, 32, 48, 64, 128], [0, 128, 64, 32, 16, 16, 32, 0, 128, 192])
        late, soon = middles if role else ends
        count = sum(part % 8 in (0, 2) for part in range(chunks))
        return [(chunks - count) * a + count * b for a, b in zip(late, soon)]

    def walk(position, part):
        if position == 0:
            join(part)
        base = part * rows
        if lined:
            line_step(position, part)
        else:
            step(position, base, rows, turn(part), *main, part, main_sems)
        if position == steps:
            there = pl.ds(pl.multiple_of(base, rows), rows)
            pltpu.make_async_copy(total.at[there], out_ref.at[there], store_sem.at[0]).start()

    def small_cross():
        return across(smalls.at[beside], small_landed, window)

    def walk_small(position):
        height = small_ref.shape[0]
        if position == 0:
            small_cross().wait_recv()
            small_ref[...] = smalls[section] + small_landed[...]
        way = (0, height, 0, small_ref, small_received, small_total, 0, (small_send, small_recv))
        step(position, *way)

    load(jnp.int32(0))
    smalls[...] = jnp.zeros_like(smalls)
    places = small_lines(width)
    for layer in range(2):
        for row, tile, line in places:
            if row == B1:
                row, tile = B1 + tile // (width // LANES), tile % (width // LANES)
            smalls[layer, line : line + 1, :] = sums_ref[layer, row : row + 1, tile * LANES : (tile + 1) * LANES]
        line = len(places)
        for head in range(tables_ref.shape[1]):
            for tile in range(tables_ref.shape[2] // LANES):
                lanes = slice(tile * LANES, (tile + 1) * LANES)
                smalls[layer, line : line + 1, :] = tables_ref[layer, head : head + 1, lanes]
                line += 1
    small_cross().start()
    for number in range(2):
        row_copy(number).start()
        row_across(number).start()

    @pl.loop(0, chunks + starts[-1])
    def _(tick):
        @pl.when(tick < chunks)
        def _():
            give(tick)

        for position in range(steps + 1):
            part = tick - starts[position + 1]

            @pl.when((part >= 0) & (part < chunks))
            def _():
                walk(position, part)

            if position <= last:

                @pl.when(part == 0)
                def _():
                    walk_small(position)

    small_out_ref[...] = small_total[...]
    for position in range(last):
        stage = position if position < bits else last - 1 - position
        size = small_received[stage]
        pltpu.make_async_copy(size, size, small_send.at[position]).wait()
        if not lined:
            size = received[stage]
            pltpu.make_async_copy(size, size, send_sem.at[position]).wait()
    if lined:
        for role in range(2):

            @pl.when(middle == role)
            def _():
                for number, amount in enumerate(line_rows(role)):
                    if amount > 0:
                        size = grads.at[pl.ds(0, amount)]
                        pltpu.make_async_copy(size, size, send_sem.at[number]).wait()
    for side in range(window):
        cross(side).wait_send()
    small_cross().wait_send()
    for number in range(2):
        row_copy(number).wait()
        row_across(number).wait()
    pltpu.make_async_copy(total, out_ref, store_sem.at[0]).wait()


def reduce_gradients(a, dm, h2, dz, h1, packed, o, dproj, y, dx, sums, tables):
    parts = lax.axis_size("dp")
    bits = parts.bit_length() - 1
    blocks = max(1, 16 * parts // BLOCK)
    layers, length, width = h1.shape
    n_blocks = 12 * width // BLOCK
    chunks = -(-n_blocks // blocks)
    rows = BLOCK * blocks
    lags, window = ((2, LAG), 4) if blocks == 1 else ((0, LAG), 1)
    lines = len(small_lines(width)) + tables.shape[1] * tables.shape[2] // LANES
    height = -(-lines // (8 * parts)) * 8 * parts
    small = (height, LANES)
    lined = parts == 16
    if lined:
        early = sum(part % 8 in (0, 2) for part in range(chunks))
        lands = [(chunks - early, size) for size in (48, 32, 128, 64)] + [(early, size) for size in (192, 128, 32, 16)]
    else:
        lands = [(chunks, rows >> (s + 1)) for s in range(bits)]
    steps = 10 if lined else 2 * bits
    return pl.pallas_call(
        functools.partial(reduce_kernel, bits, chunks, blocks, lags, window, lined),
        out_shape=(
            jax.ShapeDtypeStruct((chunks * rows, width), BF16),
            jax.ShapeDtypeStruct(small, F32),
            jax.ShapeDtypeStruct(y.shape, BF16),
            jax.ShapeDtypeStruct(dx.shape, BF16),
        ),
        in_specs=hbm_specs(10) + vmem_specs(2),
        out_specs=hbm_specs(1) + vmem_specs(1) + hbm_specs(2),
        scratch_shapes=[
            pltpu.VMEM((2, layers, length, BLOCK), BF16),
            pltpu.VMEM((2, layers, length, width), BF16),
            pltpu.VMEM((chunks * rows, width), BF16),
            pltpu.VMEM((chunks * rows, width), BF16),
            pltpu.VMEM((window, rows, width), BF16),
            pltpu.VMEM((window, rows, width), BF16),
            pltpu.VMEM((layers, *small), F32),
            pltpu.VMEM(small, F32),
            pltpu.VMEM(small, F32),
            pltpu.VMEM(small, F32),
            *[pltpu.VMEM((1, height >> (s + 1), LANES), F32) for s in range(bits)],
            *[pltpu.VMEM((*size, width), BF16) for size in lands],
            pltpu.SemaphoreType.DMA((2, 2)),
            pltpu.SemaphoreType.DMA((steps,)),
            pltpu.SemaphoreType.DMA((steps, chunks)),
            pltpu.SemaphoreType.DMA((2 * bits,)),
            pltpu.SemaphoreType.DMA((2 * bits, 1)),
            pltpu.SemaphoreType.DMA((1,)),
            pltpu.SemaphoreType.DMA((window + 3,)),
            pltpu.SemaphoreType.DMA((window + 3,)),
            pltpu.SemaphoreType.DMA((2,)),
            pltpu.SemaphoreType.REGULAR,
        ],
        compiler_params=pltpu.CompilerParams(
            collective_id=0, has_side_effects=True, vmem_limit_bytes=VMEM_BYTES
        ),
        name="reduce_gradients",
    )(a, dm, h2, dz, h1, packed, o, dproj, y, dx, sums, tables)


def swapped(block):
    return lax.ppermute(block, "section", [(0, 1), (1, 0)])


def per_device(
    patches,
    segment_ids,
    pad_counts,
    norm1_gain,
    norm1_bias,
    qkv_weight,
    query_bias,
    value_bias,
    rel_table,
    proj_weight,
    proj_bias,
    scale_attn,
    norm2_gain,
    norm2_bias,
    fc1_weight,
    fc1_bias,
    fc2_weight,
    fc2_bias,
    scale_mlp,
    cotangent,
):
    micro, length, width = patches.shape
    heads, entries = rel_table.shape[1:]
    vectors = (
        norm1_gain,
        norm1_bias,
        query_bias,
        value_bias,
        proj_bias,
        scale_attn,
        norm2_gain,
        norm2_bias,
        fc2_bias,
        scale_mlp,
        fc1_bias,
    )
    own = pack(vectors, rel_table.transpose(1, 0, 2))
    own_band = bias_band(own, heads, length)
    other = swapped(own)
    barred = lax.optimization_barrier((other, fc1_weight[0], fc2_weight[0]))
    other, *late_weights = barred
    own_weights = (qkv_weight[0], proj_weight[0], *late_weights)
    weights = [(x, swapped(x)) for x in own_weights]
    other_band = bias_band(other, heads, length)
    packs, band = (own, other), (own_band, other_band)
    saved = None
    rows = patches
    for layer in range(2):
        saved = forward(layer, pad_counts, rows, segment_ids, packs, band, weights, saved)
    kept = None
    for layer in (1, 0):
        kept = backward(layer, cotangent, packs, weights, saved, kept)
    dm, dz, dproj, packed, dx, tables, sums = kept
    h1, mixed, h2, act, y = saved[0], saved[3], saved[6], saved[10], saved[13]
    summed, small, y, dx = reduce_gradients(
        act, dm, h2, dz, h1, packed, mixed, dproj, y, dx, sums, tables
    )
    fc2_grad, fc1_grad, qkv_grad, proj_grad, outputs, in_grads, *small_grads = widen(
        summed, small, y, dx, width, heads, entries
    )
    table_grad = small_grads[VECTORS + 1].transpose(1, 0, 2)
    return (
        outputs[None],
        in_grads[None],
        small_grads[GAIN1],
        small_grads[SHIFT1],
        qkv_grad[None],
        small_grads[QBIAS],
        small_grads[VBIAS],
        table_grad,
        proj_grad[None],
        small_grads[PBIAS],
        small_grads[SCALE_A],
        small_grads[GAIN2],
        small_grads[SHIFT2],
        fc1_grad[None],
        small_grads[B1],
        fc2_grad[None],
        small_grads[B2],
        small_grads[SCALE_M],
    )


def solution(mesh):
    placed = (
        P("dp", None, None),
        P("dp", None),
        P("dp"),
        P("section", None),
        P("section", None),
        P("section", None, None),
        P("section", None),
        P("section", None),
        P("section", None, None),
        P("section", None, None),
        P("section", None),
        P("section", None),
        P("section", None),
        P("section", None),
        P("section", None, None),
        P("section", None),
        P("section", None, None),
        P("section", None),
        P("section", None),
        P("dp", None, None),
    )
    return jax.shard_map(
        per_device,
        mesh=mesh,
        in_specs=placed,
        out_specs=(
            P("section", "dp", None, None),
            P("section", "dp", None, None),
            P("section", None),
            P("section", None),
            P("section", None, None),
            P("section", None),
            P("section", None),
            P("section", None, None),
            P("section", None, None),
            P("section", None),
            P("section", None),
            P("section", None),
            P("section", None),
            P("section", None, None),
            P("section", None),
            P("section", None, None),
            P("section", None),
            P("section", None),
        ),
        check_vma=False,
    )
```

```python
import functools
import math

import jax
import jax.numpy as jnp
from jax import lax
from jax.experimental import pallas as pl
from jax.experimental.pallas import tpu as pltpu
from jax.sharding import PartitionSpec as P

MESH = pl.DeviceIdType.MESH
BF16, F32 = jnp.bfloat16, jnp.float32
VMEM_BYTES = 60 * 1024 * 1024
LANES = 128
HALF = 64
REACH = 2 * LANES
GAIN1, SHIFT1, QBIAS, VBIAS, PBIAS, SCALE_A, GAIN2, SHIFT2, B2, SCALE_M, B1 = range(11)
VECTORS = 10
STORED = 14
BOTH, ATTENTION, MLP = range(3)
STRIP = 16
GROUP = 3


def dot(left, right, left_dim, right_dim):
    return lax.dot_general(
        left, right, (((left_dim,), (right_dim,)), ((), ())), preferred_element_type=F32
    )


def nn(left, right):
    return dot(left, right, 1, 0)


def nt(left, right):
    return dot(left, right, 1, 1)


def normalize(values):
    centered = values - jnp.mean(values, -1, keepdims=True)
    inverse = lax.rsqrt(jnp.mean(centered * centered, -1, keepdims=True) + 1e-06)
    return centered * inverse, inverse


def norm_back(upper, scaled, inverse):
    return inverse * (
        upper
        - jnp.mean(upper, -1, keepdims=True)
        - scaled * jnp.mean(upper * scaled, -1, keepdims=True)
    )


def fold(values):
    return jnp.sum(values.reshape(values.shape[0] // 8, 8, values.shape[1]), 0)


def half_mask(shape, which):
    return lax.broadcasted_iota(jnp.int32, shape, 1) // HALF == which


def strips(first, last, size):
    return [slice(start, start + size) for start in range(first, last, size)]


def chunk(index, size):
    return pl.ds(pl.multiple_of(index * size, size), size)


def skew_bias(reversed_row, target):
    span, lanes = target.shape
    rows = pltpu.roll(jnp.broadcast_to(reversed_row, (8, reversed_row.shape[1])), 1, 1, stride=1, stride_axis=0)
    tiles = span // lanes
    for fine in range(lanes // 8):
        moved = rows if fine == 0 else pltpu.roll(rows, 8 * fine, 1)
        for coarse in range(tiles):
            place = 8 * (fine + lanes // 8 * coarse)
            target[place : place + 8, :] = moved[:, lanes * (tiles - coarse) : lanes * (tiles - coarse + 1)]


def gather_diagonals(source):
    span, lanes = source.shape
    tiles = span // lanes
    width = span + lanes
    blank = jnp.zeros((8, lanes), F32)
    found = None
    for fine in range(lanes // 8):
        places = [8 * (fine + lanes // 8 * coarse) for coarse in reversed(range(tiles))]
        line = jnp.concatenate([blank] + [source[place : place + 8, :] for place in places], 1)
        if fine > 0:
            line = pltpu.roll(line, width - 8 * fine, 1)
        found = line if found is None else found + line
    row = lax.broadcasted_iota(jnp.int32, found.shape, 0)
    for place in range(3):
        moved = pltpu.roll(found, width - (1 << place), 1)
        found = jnp.where((row // (1 << place)) % 2 == 1, moved, found)
    return jnp.sum(found, 0, keepdims=True)


def key_rows(query_block, blocks):
    reach = REACH // LANES
    return max(0, query_block - reach) * LANES, min(blocks, query_block + reach + 1) * LANES


def pick(mine, own, other, act):
    @pl.when(mine)
    def _():
        act(own)

    @pl.when(jnp.logical_not(mine))
    def _():
        act(other)


def pack_kernel(*refs):
    *vectors, bias_ref, table_ref, pack_ref = refs
    width = pack_ref.shape[1]
    heads, _, entries = table_ref.shape
    pack_ref[...] = jnp.zeros_like(pack_ref)
    for row, vector in enumerate(vectors):
        pack_ref[row : row + 1, :] = vector[...]
    for part in range(bias_ref.shape[1] // width):
        pack_ref[B1 + part : B1 + part + 1, :] = bias_ref[:, part * width : (part + 1) * width]
    first = pack_ref.shape[0] - heads
    tiles = entries // LANES
    lane = lax.broadcasted_iota(jnp.int32, (heads, LANES), 1)
    ending = jnp.broadcast_to(table_ref[:, 0, entries - 1 :], (heads, LANES))
    pack_ref[first:, :LANES] = jnp.where(lane == LANES - 1, ending, 0.0)
    for tile in range(tiles):
        there = (tiles - tile) * LANES
        pack_ref[first:, there : there + LANES] = reverse_lanes(table_ref[:, 0, tile * LANES : (tile + 1) * LANES])


def pack(vectors, rel_table):
    heads = rel_table.shape[0]
    return pl.pallas_call(
        pack_kernel,
        out_shape=jax.ShapeDtypeStruct((16 + heads, vectors[0].shape[1]), F32),
        in_specs=vmem_specs(len(vectors) + 1),
        out_specs=pl.BlockSpec(memory_space=pltpu.VMEM),
        name="pack_vectors",
    )(*vectors, rel_table)


def fill(target, source):
    target[...] = source[...]


def band_kernel(pack_ref, band_hbm, band, store_sem):
    heads = band.shape[0]
    tables = pack_ref.shape[0] - heads
    edge = jnp.zeros((1, LANES), F32)

    @pl.loop(0, heads // 4)
    def _(group):
        for within in range(4):
            head = 4 * group + within
            kept = pack_ref[pl.ds(tables + head, 1), :]
            skew_bias(jnp.concatenate([edge, kept, edge], 1), band.at[head])

    there = pltpu.make_async_copy(band, band_hbm, store_sem.at[0])
    there.start()
    there.wait()


def bias_band(packed, heads, length):
    shape = (heads, 2 * length - LANES, LANES)
    return pl.pallas_call(
        band_kernel,
        out_shape=jax.ShapeDtypeStruct(shape, F32),
        in_specs=vmem_specs(1),
        out_specs=pl.BlockSpec(memory_space=pl.ANY),
        scratch_shapes=[pltpu.VMEM(shape, F32), pltpu.SemaphoreType.DMA((1,))],
        compiler_params=pltpu.CompilerParams(vmem_limit_bytes=VMEM_BYTES + 2 * 1024 * 1024),
        name="bias_band",
    )(packed)


def forward_kernel(layer, phase, pads, x_hbm, seg_ref, own_pack, other_pack, own_band, other_band, *refs):
    if phase != MLP:
        (wqkv_own, wqkv_other, wp_own, wp_other), refs = refs[:4], refs[4:]
    if phase != ATTENTION:
        (w1_own, w1_other, w2_own, w2_other), refs = refs[:4], refs[4:]
    refs = refs[STORED if layer > 0 or phase == MLP else 0 :]
    stores = refs[:STORED]
    (bias, wqkv, wp, w1, w2, mask, h1, qkv, probs, mixed, proj, x1, h2, xin, wide_mixed, scales, act, slope, mlp, out_row, held, pack_ref, load_sem, store_sem, prob_sem) = refs[STORED:]
    h1_o, qkv_o, prob_o, mixed_o, proj_o, x1_o, h2_o, xin_o, wide_o, scales_o, act_o, slope_o, mlp_o, y_o = stores
    hidden = w1.shape[1]
    length, width = xin.shape
    heads = bias.shape[0]
    blocks = length // LANES
    section = lax.axis_index("section")
    mine = section == layer
    factor = HALF ** (-0.5)
    thirds = [pl.ds(part * width, width) for part in range(3)]

    def load(number):
        if number < 3:
            part = thirds[number]
            return wqkv_own.at[:, part], wqkv_other.at[:, part], wqkv.at[:, part], load_sem.at[number]
        if number == 3:
            return wp_own, wp_other, wp, load_sem.at[3]
        part = pl.ds((number % 4) * width, width)
        if number < 8:
            return w1_own.at[:, part], w1_other.at[:, part], w1.at[:, part], load_sem.at[number]
        return w2_own.at[part, :], w2_other.at[part, :], w2.at[part, :], load_sem.at[number]

    def start(number):
        own, other, target, sem = load(number)
        pick(mine, own, other, lambda source: pltpu.make_async_copy(source, target, sem).start())

    def wait(number):
        own, other, target, sem = load(number)
        pltpu.make_async_copy(target, target, sem).wait()

    def store(number, source, there):
        return pltpu.make_async_copy(source, there.at[layer], store_sem.at[number])

    def part_store(number, source, there, columns):
        return pltpu.make_async_copy(source.at[:, columns], there.at[layer, :, columns], store_sem.at[number])

    def vector(row):
        return pack_ref[row : row + 1, :]

    def attention():
        source = x_hbm.at[section] if layer == 0 else y_o.at[0]
        pltpu.make_async_copy(source, xin, load_sem.at[12]).start()
        start(0)
        pltpu.make_async_copy(xin, xin, load_sem.at[12]).wait()
        start(1)
        start(2)
        pick(mine, own_band, other_band, lambda source: pltpu.make_async_copy(source, bias, load_sem.at[13]).start())
        segment = seg_ref[pl.ds(section, 1), :].astype(F32)
        key_segment = jnp.broadcast_to(segment, (LANES, length)).T

        for rows in strips(0, length, STRIP):
            scaled, _ = normalize(xin[rows, :].astype(F32))
            h1[rows, :] = (scaled * vector(GAIN1) + vector(SHIFT1)).astype(BF16)
        for part in range(3):
            wait(part)

        alive = length - pads[section]
        for place in range(blocks):
            lanes = slice(place * LANES, (place + 1) * LANES)
            for rows in strips(0, length, 64):
                key = lax.broadcasted_iota(jnp.int32, (64, LANES), 0) + rows.start
                query = lax.broadcasted_iota(jnp.int32, (64, LANES), 1) + place * LANES
                allowed = ((key_segment[rows] == segment[:, lanes]) & (key < alive)) | (key == query)
                mask[rows, lanes] = jnp.where(allowed, 0.0, -1000000000.0)

        store(0, h1, h1_o).start()
        store(7, xin, xin_o).start()
        projections = [(part, pl.ds(high * (length // 2), length // 2)) for part in range(3) for high in range(2)]

        def project(number):
            part, rows = projections[number]
            return nn(h1[rows, :], wqkv[:, thirds[part]])

        coming = project(0)
        for number, (part, rows) in enumerate(projections):
            current = coming
            if number + 1 < len(projections):
                coming = project(number + 1)
            for strip in strips(0, length // 2, STRIP):
                piece = current[strip]
                if part == 0:
                    piece = (piece + vector(QBIAS)) * factor
                if part == 2:
                    piece = piece + vector(VBIAS)
                qkv[pl.ds(rows.start + strip.start, STRIP), thirds[part]] = piece.astype(BF16)
        store(1, qkv, qkv_o).start()
        pltpu.make_async_copy(bias, bias, load_sem.at[13]).wait()
        for number in range(3, 4 if phase == ATTENTION else 12):
            start(number)
        together = 2 * GROUP

        def prob_store(group):
            return pltpu.make_async_copy(
                probs.at[group % 2], prob_o.at[layer, pl.ds(together * group, together)], prob_sem.at[group % 2]
            )

        def attend(side, within, pair):
            columns = chunk(pair, LANES)
            queries = qkv[:, columns]
            keys = qkv[:, pl.ds(pl.multiple_of(width + pair * LANES, LANES), LANES)]
            values = qkv[:, pl.ds(pl.multiple_of(2 * width + pair * LANES, LANES), LANES)].T
            outs = []
            for which in range(2):
                own_keys = jnp.where(half_mask(keys.shape, which), keys, jnp.zeros_like(keys))
                lines = []
                for wide in range(blocks // 2):
                    scores = nt(own_keys, queries[2 * LANES * wide : 2 * LANES * (wide + 1)])
                    for part in range(2):
                        place = 2 * wide + part
                        low, high = key_rows(place, blocks)
                        lanes = slice(place * LANES, (place + 1) * LANES)
                        first = (blocks - 1 - place) * LANES
                        spare = (2 * within + which) * blocks + place
                        highest = None
                        for rows in strips(low, high, 64):
                            here = (
                                scores[rows, part * LANES : (part + 1) * LANES]
                                + bias[2 * pair + which, first + rows.start : first + rows.stop, :]
                                + mask[rows, lanes]
                            )
                            held[spare, rows, :] = here
                            top = jnp.max(here.reshape(8, 8, LANES), 0)
                            highest = top if highest is None else jnp.maximum(highest, top)
                        highest = jnp.max(highest, 0, keepdims=True)
                        sums = jnp.zeros((8, LANES), F32)
                        for rows in strips(low, high, 64):
                            expo = jnp.exp(held[spare, rows, :] - highest)
                            probs[side, 2 * within + which, rows, lanes] = expo.astype(BF16)
                            sums = sums + fold(expo)
                        lines.append(1.0 / jnp.sum(sums, 0, keepdims=True))
                        if low > 0:
                            probs[side, 2 * within + which, :low, lanes] = jnp.zeros((low, LANES), BF16)
                        if high < length:
                            probs[side, 2 * within + which, high:, lanes] = jnp.zeros((length - high, LANES), BF16)
                scale = jnp.concatenate(lines, 1)
                scales[pl.ds(2 * pair + which, 1), :] = scale
                outs.append(nn(values[which * HALF : (which + 1) * HALF], probs[side, 2 * within + which]) * scale)
            out = jnp.concatenate(outs, 0).T
            wide_mixed[:, columns] = out
            mixed[:, columns] = out.astype(BF16)

        @pl.loop(0, heads // together)
        def _(group):
            @pl.when(group >= 2)
            def _():
                prob_store(group - 2).wait()

            for within in range(GROUP):
                attend(group % 2, within, GROUP * group + within)
            prob_store(group).start()

        store(3, mixed, mixed_o).start()
        store(8, wide_mixed, wide_o).start()
        store(9, scales, scales_o).start()
        wait(3)

        results = [nn(mixed[half, :], wp[...]) for half in strips(0, length, length // 2)]
        for rows in strips(0, length, STRIP):
            there = rows.start % (length // 2)
            out = results[rows.start // (length // 2)][there : there + STRIP] + vector(PBIAS)
            proj[rows, :] = out.astype(BF16)
            resid = xin[rows, :].astype(F32) + vector(SCALE_A) * out
            x1[rows, :] = resid
            scaled, _ = normalize(resid)
            h2[rows, :] = (scaled * vector(GAIN2) + vector(SHIFT2)).astype(BF16)

        store(4, proj, proj_o).start()
        store(5, x1, x1_o).start()
        store(6, h2, h2_o).start()

        def finish():
            for group in range(max(0, heads // together - 2), heads // together):
                prob_store(group).wait()

        return finish

    def mlp_part():
        pieces = [
            (pl.ds(high * (length // 2), length // 2), pl.ds(part * width, width))
            for part in range(hidden // width)
            for high in range(2)
        ]

        def expand(number):
            rows, columns = pieces[number]
            if phase == MLP and number % 2 == 0:
                wait(4 + number // 2)
            return nn(h2[rows, :], w1[:, columns])

        if phase != MLP:
            for number in range(4, 12):
                wait(number)
        coming = expand(0)
        totals = [None, None]
        for number, (rows, columns) in enumerate(pieces):
            current = coming
            if number + 1 < len(pieces):
                coming = expand(number + 1)
            for strip in strips(0, length // 2, STRIP):
                there = pl.ds(rows.start + strip.start, STRIP)
                here = current[strip] + vector(B1 + number // 2)
                normal = 0.5 * lax.erf(here * math.sqrt(0.5)) + 0.5
                density = jnp.exp(-0.5 * here * here) * (1.0 / math.sqrt(2.0 * math.pi))
                act[there, columns] = (here * normal).astype(BF16)
                slope[there, columns] = (normal + here * density).astype(BF16)
            if phase == MLP and number % 2 == 0:
                wait(8 + number // 2)
            more = nn(act[rows, columns], w2[columns, :])
            totals[number % 2] = more if number < 2 else totals[number % 2] + more
            if number in (len(pieces) // 2 - 1, len(pieces) - 1):
                columns = pl.ds((number // 4) * 2 * width, 2 * width)
                part_store(10, act, act_o, columns).start()
                part_store(11, slope, slope_o, columns).start()

        if phase == MLP:
            pltpu.make_async_copy(x1, x1, load_sem.at[13]).wait()
        for half in range(2):
            for strip in strips(0, length // 2, STRIP):
                rows = pl.ds(half * (length // 2) + strip.start, STRIP)
                out = totals[half][strip] + vector(B2)
                mlp[rows, :] = out.astype(BF16)
                out_row[rows, :] = (x1[rows, :] + vector(SCALE_M) * out).astype(BF16)

        store(12, mlp, mlp_o).start()
        store(13, out_row, y_o).start()
    pick(mine, own_pack, other_pack, functools.partial(fill, pack_ref))
    if phase == MLP:
        pltpu.make_async_copy(h2_o.at[layer], h2, load_sem.at[12]).start()
        for number in (4, 8, 5, 9):
            start(number)
        pltpu.make_async_copy(h2, h2, load_sem.at[12]).wait()
        for number in (6, 10, 7, 11):
            start(number)
        pltpu.make_async_copy(x1_o.at[layer], x1, load_sem.at[13]).start()
        mlp_part()
    else:
        finish = attention()
        if phase == BOTH:
            mlp_part()
        finish()
    ends = {0: (h1, h1_o), 1: (qkv, qkv_o), 3: (mixed, mixed_o), 4: (proj, proj_o), 5: (x1, x1_o), 6: (h2, h2_o),
            7: (xin, xin_o), 8: (wide_mixed, wide_o), 9: (scales, scales_o),
            10: (act, act_o), 11: (slope, slope_o), 12: (mlp, mlp_o), 13: (out_row, y_o)}
    for number, (source, there) in ends.items():
        if phase == BOTH or (phase == MLP) == (number >= 10):
            store(number, source, there).wait()


def hbm_specs(count):
    return [pl.BlockSpec(memory_space=pl.ANY)] * count


def vmem_specs(count):
    return [pl.BlockSpec(memory_space=pltpu.VMEM)] * count


def stacked(stored):
    return [jax.ShapeDtypeStruct((2, *shape), kind) for shape, kind in stored]


def forward(layer, phase, pads, rows, segments, packs, band, weights, kept):
    length, width = rows.shape[1:]
    heads = band[0].shape[0]
    hidden = weights[2][0].shape[1]
    used = {BOTH: weights, ATTENTION: weights[:2], MLP: weights[2:]}[phase]
    stored = [
        ((length, width), BF16),
        ((length, 3 * width), BF16),
        ((heads, length, length), BF16),
        ((length, width), BF16),
        ((length, width), BF16),
        ((length, width), F32),
        ((length, width), BF16),
        ((length, width), BF16),
        ((length, width), F32),
        ((heads, length), F32),
        ((length, hidden), BF16),
        ((length, hidden), BF16),
        ((length, width), BF16),
        ((length, width), BF16),
    ]
    scratch = [pltpu.VMEM(band[0].shape, F32)] + [pltpu.VMEM(pair[0].shape, BF16) for pair in weights]
    scratch.append(pltpu.VMEM((length, length), F32))
    scratch += [
        pltpu.VMEM((2, 2 * GROUP, length, length) if n == 2 else shape, kind)
        for n, (shape, kind) in enumerate(stored)
    ]
    scratch += [
        pltpu.VMEM((2 * GROUP * length // LANES, length, LANES), F32),
        pltpu.VMEM(packs[0].shape, F32),
        pltpu.SemaphoreType.DMA((14,)),
        pltpu.SemaphoreType.DMA((STORED,)),
        pltpu.SemaphoreType.DMA((2,)),
    ]
    operands = [pads, rows, segments, *packs, *band, *[x for pair in used for x in pair]]
    held = STORED if layer > 0 or phase == MLP else 0
    return pl.pallas_call(
        functools.partial(forward_kernel, layer, phase),
        out_shape=stacked(stored),
        in_specs=[pl.BlockSpec(memory_space=pltpu.SMEM)] + hbm_specs(1) + vmem_specs(3) + hbm_specs(2 + 2 * len(used) + held),
        out_specs=hbm_specs(STORED),
        scratch_shapes=scratch,
        input_output_aliases={len(operands) + n: n for n in range(held)},
        compiler_params=pltpu.CompilerParams(vmem_limit_bytes=VMEM_BYTES),
        name="forward_layer",
    )(*operands, *(kept if held else ()))


def backward_kernel(layer, cotangent_hbm, own_pack, other_pack, *refs):
    weights, refs = refs[:8], refs[8:]
    (qkv_i, prob_i, mixed_i, proj_i, x1_i, slope_i, mlp_i, xin_i, scales_i) = refs[:9]
    refs = refs[9 + (7 if layer == 0 else 0) :]
    stores = refs[:7]
    (wqkv, wp, w1, w2, qkv, probs, mixed, proj, x1, slope, mlp, xin, scales, dm, dz, dproj, packed, dx_ref, dx1, dmixed, dscore, diag, sums, tables, g_ref, pack_ref, load_sem, store_sem, prob_sem) = refs[7:]
    dm_o, dz_o, dproj_o, packed_o, dx_o, tables_o, sums_o = stores
    wqkv_hbm, wp_hbm, w1_hbm, w2_hbm = zip(weights[::2], weights[1::2])
    length, width = g_ref.shape
    hidden = w1.shape[1]
    blocks = length // LANES
    pairs = width // LANES
    section = lax.axis_index("section")
    mine = section == layer
    factor = HALF ** (-0.5)
    parts = [pl.ds(part * width, width) for part in range(hidden // width)]
    loads = [(mlp_i.at[layer], mlp)]
    loads += [(tuple(x.at[part, :] for x in w2_hbm), w2.at[part, :]) for part in parts]
    loads += [(slope_i.at[layer, :, part], slope.at[:, part]) for part in parts]
    loads += [(tuple(x.at[:, part] for x in w1_hbm), w1.at[:, part]) for part in parts]
    early = len(loads)
    loads += [
        (x1_i.at[layer], x1), (proj_i.at[layer], proj), (wp_hbm, wp), (qkv_i.at[layer], qkv), (mixed_i.at[layer], mixed),
        (scales_i.at[layer], scales), (wqkv_hbm, wqkv), (xin_i.at[layer], xin),
    ]
    upstream_sem = load_sem.at[len(loads)]

    def start(number):
        source, target = loads[number]

        def go(ref):
            pltpu.make_async_copy(ref, target, load_sem.at[number]).start()

        if isinstance(source, tuple):
            pick(mine, *source, go)
        else:
            go(source)

    def load(number):
        target = loads[number][1]
        return pltpu.make_async_copy(target, target, load_sem.at[number])

    def store(number, source, there):
        return pltpu.make_async_copy(source, there.at[layer], store_sem.at[number])

    together = 2 * GROUP

    def prob_load(group):
        return pltpu.make_async_copy(
            prob_i.at[layer, pl.ds(together * group, together)], probs.at[group % 2], prob_sem.at[group % 2]
        )

    def vector(row):
        return pack_ref[row : row + 1, :]

    def put(row, partial):
        sums[row : row + 1, :] = jnp.sum(partial, 0, keepdims=True)

    nothing = jnp.zeros((8, width), F32)

    upstream_hbm = cotangent_hbm.at[section] if layer == 1 else dx_o.at[1]
    pltpu.make_async_copy(upstream_hbm, g_ref, upstream_sem).start()
    pick(mine, own_pack, other_pack, functools.partial(fill, pack_ref))
    for number in (0, 1):
        start(number)
    pltpu.make_async_copy(g_ref, g_ref, upstream_sem).wait()
    load(0).wait()
    for number in (5, 9, 2, 6, 10):
        start(number)
    scale_sum = bias_sum = nothing
    for rows in strips(0, length, STRIP):
        upstream = g_ref[rows, :].astype(F32)
        low = (upstream * vector(SCALE_M)).astype(BF16)
        dm[rows, :] = low
        scale_sum = scale_sum + fold(upstream * mlp[rows, :].astype(F32))
        bias_sum = bias_sum + fold(low.astype(F32))
    put(SCALE_M, scale_sum)
    put(B2, bias_sum)
    store(0, dm, dm_o).start()
    pieces = [pl.ds(part * width, width) for part in range(hidden // width)]

    def expand(number):
        load(1 + number).wait()
        return nt(dm[...], w2[pieces[number], :])

    coming = expand(0)
    upper_sum = None
    for number, columns in enumerate(pieces):
        if number == 0:
            for later in (3, 7, 11, 4, 8, 12):
                start(later)
        if number == 2:
            for later in range(early, len(loads)):
                start(later)
            prob_load(0).start()
        load(5 + number).wait()
        load(9 + number).wait()
        current = coming
        if number + 1 < len(pieces):
            coming = expand(number + 1)
        act_sum = nothing
        for there in strips(0, length, STRIP):
            low = (current[there] * slope[there, columns].astype(F32)).astype(BF16)
            dz[there, columns] = low
            act_sum = act_sum + fold(low.astype(F32))
        put(B1 + number, act_sum)
        more = nt(dz[:, columns], w1[:, columns])
        upper_sum = more if number == 0 else upper_sum + more
    store(1, dz, dz_o).start()
    load(early).wait()
    load(early + 1).wait()
    found = [nothing] * 4
    for rows in strips(0, length, STRIP):
        upper = upper_sum[rows]
        scaled, inverse = normalize(x1[rows, :])
        resid = g_ref[rows, :].astype(F32) + norm_back(upper * vector(GAIN2), scaled, inverse)
        dx1[rows, :] = resid
        low = (resid * vector(SCALE_A)).astype(BF16)
        dproj[rows, :] = low
        terms = (upper * scaled, upper, resid * proj[rows, :].astype(F32), low.astype(F32))
        found = [old + fold(term) for old, term in zip(found, terms)]
    for row, partial in zip((GAIN2, SHIFT2, SCALE_A, PBIAS), found):
        put(row, partial)
    store(2, dproj, dproj_o).start()
    load(early + 2).wait()
    dmixed[...] = nt(dproj[...], wp[...]).astype(BF16)
    for number in range(early + 3, early + 6):
        load(number).wait()

    def attend(side, within, pair):
        columns = chunk(pair, LANES)
        key_columns = pl.ds(pl.multiple_of(width + pair * LANES, LANES), LANES)
        value_columns = pl.ds(pl.multiple_of(2 * width + pair * LANES, LANES), LANES)
        values = qkv[:, value_columns]
        above = dmixed[:, columns]
        queries_t = qkv[:, columns].T
        keys_t = qkv[:, key_columns].T
        above_t = above.astype(F32).T
        products = (above.astype(F32) * mixed[:, columns]).T
        grads = [], [], []
        for which in range(2):
            place_in = 2 * within + which
            half = slice(which * HALF, (which + 1) * HALF)
            delta = jnp.sum(products[half], 0, keepdims=True)
            scale = scales[pl.ds(2 * pair + which, 1), :]
            own_values = jnp.where(half_mask(values.shape, which), values, jnp.zeros_like(values))
            edge = (blocks - 1) * LANES
            diag[place_in, :edge, :] = jnp.zeros((edge, LANES), F32)
            for wide in range(blocks // 2):
                prob_grad = nt(own_values, above[2 * LANES * wide : 2 * LANES * (wide + 1)])
                for part in range(2):
                    place = 2 * wide + part
                    low, high = key_rows(place, blocks)
                    lanes = slice(place * LANES, (place + 1) * LANES)
                    first_row = (blocks - 1 - place) * LANES
                    for rows in strips(low, high, 64):
                        here = (probs[side, place_in, rows, lanes].astype(F32) * scale[:, lanes]) * (
                            prob_grad[rows, part * LANES : (part + 1) * LANES] - delta[:, lanes]
                        )
                        dscore[place_in, rows, lanes] = here.astype(BF16)
                        there = slice(first_row + rows.start, first_row + rows.stop)
                        diag[place_in, there, :] = here if place == 0 else diag[place_in, there, :] + here
                    if low > 0:
                        dscore[place_in, :low, lanes] = jnp.zeros((low, LANES), BF16)
                    if high < length:
                        dscore[place_in, high:, lanes] = jnp.zeros((length - high, LANES), BF16)
                    if place == 0:
                        diag[place_in, edge + high :, :] = jnp.zeros((length - high, LANES), F32)
            line = gather_diagonals(diag.at[place_in])
            most = tables.shape[1] - LANES
            tables[pl.ds(2 * pair + which, 1), :] = jnp.concatenate(
                [line[:, REACH + 1 : REACH + 1 + most], line[:, REACH : REACH + LANES]], 1
            )
            grads[0].append(nn(keys_t[half], dscore[place_in]))
            grads[1].append(nt(queries_t[half], dscore[place_in]))
            grads[2].append(nt((above_t[half] * scale).astype(BF16), probs[side, place_in]))
        for found, where, scale in zip(grads, (columns, key_columns, value_columns), (factor, None, None)):
            low = jnp.concatenate(found, 0).astype(BF16)
            if scale is not None:
                low = (low.astype(F32) * scale).astype(BF16)
            packed[:, where] = low.T

    @pl.loop(0, pairs // GROUP)
    def _(group):
        prob_load(group).wait()

        @pl.when(group + 1 < pairs // GROUP)
        def _():
            prob_load(group + 1).start()

        for within in range(GROUP):
            attend(group % 2, within, GROUP * group + within)

    store(3, packed, packed_o).start()
    load(early + 6).wait()
    result = nt(packed[...], wqkv[...])
    load(early + 7).wait()
    found = [nothing] * 4
    for rows in strips(0, length, STRIP):
        upper = result[rows]
        scaled, inverse = normalize(xin[rows, :].astype(F32))
        dx_ref[rows, :] = (dx1[rows, :] + norm_back(upper * vector(GAIN1), scaled, inverse)).astype(BF16)
        terms = (
            upper * scaled,
            upper,
            packed[rows, :width].astype(F32),
            packed[rows, 2 * width :].astype(F32),
        )
        found = [old + fold(term) for old, term in zip(found, terms)]
    for row, partial in zip((GAIN1, SHIFT1, QBIAS, VBIAS), found):
        put(row, partial)
    store(4, dx_ref, dx_o).start()
    store(5, tables, tables_o).start()
    store(6, sums, sums_o).start()
    ends = {0: (dm, dm_o), 1: (dz, dz_o), 2: (dproj, dproj_o), 3: (packed, packed_o), 4: (dx_ref, dx_o), 5: (tables, tables_o), 6: (sums, sums_o)}
    for number, (source, there) in ends.items():
        store(number, source, there).wait()


def backward(layer, cotangent, packs, weights, saved, kept):
    length, width = cotangent.shape[1:]
    hidden = weights[2][0].shape[1]
    h1, qkv, probs, mixed, proj, x1, h2, xin, wide, scales, act, slope, mlp, y = saved
    heads = probs.shape[1]
    span = 2 * length - LANES
    summed = (16, width)
    table = (heads, 5 * LANES)
    stored = [
        ((length, width), BF16),
        ((length, hidden), BF16),
        ((length, width), BF16),
        ((length, 3 * width), BF16),
        ((length, width), BF16),
        (table, F32),
        (summed, F32),
    ]
    reads = [qkv, probs, wide, proj, x1, slope, mlp, xin, scales]
    scratch = [pltpu.VMEM(pair[0].shape, BF16) for pair in weights]
    scratch += [pltpu.VMEM((2, 2 * GROUP, length, length) if x is probs else x.shape[1:], x.dtype) for x in reads]
    scratch += [pltpu.VMEM(shape, kind) for shape, kind in stored[:5]]
    scratch += [
        pltpu.VMEM((length, width), F32),
        pltpu.VMEM((length, width), BF16),
        pltpu.VMEM((2 * GROUP, length, length), BF16),
        pltpu.VMEM((2 * GROUP, span, LANES), F32),
        pltpu.VMEM(summed, F32),
        pltpu.VMEM(table, F32),
        pltpu.VMEM((length, width), BF16),
        pltpu.VMEM(packs[0].shape, F32),
        pltpu.SemaphoreType.DMA((22,)),
        pltpu.SemaphoreType.DMA((7,)),
        pltpu.SemaphoreType.DMA((2,)),
    ]
    operands = [cotangent, *packs, *[x for pair in weights for x in pair], *reads]
    held = 7 if layer == 0 else 0
    return pl.pallas_call(
        functools.partial(backward_kernel, layer),
        out_shape=stacked(stored),
        in_specs=hbm_specs(1) + vmem_specs(2) + hbm_specs(8 + len(reads) + held),
        out_specs=hbm_specs(7),
        scratch_shapes=scratch,
        input_output_aliases={len(operands) + n: n for n in range(held)},
        compiler_params=pltpu.CompilerParams(vmem_limit_bytes=VMEM_BYTES),
        name="backward_layer",
    )(*operands, *(kept if layer == 0 else ()))


def small_lines(width):
    lines = width // LANES
    places = [(row, tile, row * lines + tile) for row in range(10) for tile in range(lines)]
    return places + [(B1, tile, B1 * lines + tile) for tile in range(4 * lines)]


def reverse_lanes(values):
    lane = lax.broadcasted_iota(jnp.int32, values.shape, 1)
    for place in range(LANES.bit_length() - 1):
        step = 1 << place
        up, down = pltpu.roll(values, step, 1), pltpu.roll(values, LANES - step, 1)
        values = jnp.where((lane // step) % 2 == 1, up, down)
    return values


def widen_kernel(sum_hbm, y_hbm, dx_hbm, small_ref, *refs):
    bigs, rows_out, vectors, table_ref = refs[:4], refs[4:6], refs[6 : 7 + VECTORS], refs[7 + VECTORS]
    narrow, wide, passing, load_sem, store_sem, pass_sem = refs[8 + VECTORS :]
    depth, width = narrow.shape[:2]
    blocks = [(0, slice(b * width, (b + 1) * width), slice(0, width)) for b in range(4)]
    for target, count in ((1, 4), (2, 3), (3, 1)):
        blocks += [(target, slice(0, width), slice(b * width, (b + 1) * width)) for b in range(count)]

    def load(block):
        rows = pl.ds(block * width, width)
        return pltpu.make_async_copy(sum_hbm.at[rows, :], narrow.at[block % depth], load_sem.at[block % depth])

    def store(block):
        target, rows, columns = blocks[block]
        there = bigs[target].at[rows, columns]
        return pltpu.make_async_copy(wide.at[block % depth], there, store_sem.at[block % depth])

    def fetch(number):
        return pltpu.make_async_copy((y_hbm, dx_hbm)[number], passing.at[number], pass_sem.at[0, number])

    def put(number):
        return pltpu.make_async_copy(passing.at[number], rows_out[number], pass_sem.at[1, number])

    for block in range(depth):
        load(block).start()
    for number in range(2):
        fetch(number).start()
    for block in range(len(blocks)):
        if block == depth:
            for number in range(2):
                fetch(number).wait()
                put(number).start()
        load(block).wait()
        if block >= depth:
            store(block - depth).wait()
        for rows in strips(0, width, 64):
            wide[block % depth, rows, :] = narrow[block % depth, rows, :].astype(F32)
        store(block).start()
        if block + depth < len(blocks):
            load(block + depth).start()
    places = small_lines(width)
    for row, tile, line in places:
        vectors[row][:, tile * LANES : (tile + 1) * LANES] = small_ref[line : line + 1, :]
    first = len(places)
    heads, _, entries = table_ref.shape
    tiles = -(-entries // LANES)
    flipped = reverse_lanes(small_ref[first : first + heads * tiles, :])
    for head in range(heads):
        for tile in range(tiles - 1):
            line = head * tiles + tile
            there = (tiles - 2 - tile) * LANES
            table_ref[head, :, there : there + LANES] = flipped[line : line + 1]
        line = first + head * tiles + tiles - 1
        table_ref[head, :, entries - 1 :] = small_ref[line : line + 1, 0:1]
    for block in range(len(blocks) - depth, len(blocks)):
        store(block).wait()
    for number in range(2):
        put(number).wait()


def widen(summed, small, y, dx, width, heads, entries):
    bigs = [(4 * width, width), (width, 4 * width), (width, 3 * width), (width, width)]
    shapes = [(1, width)] * 10 + [(1, 4 * width), (heads, 1, entries)]
    return pl.pallas_call(
        widen_kernel,
        out_shape=[jax.ShapeDtypeStruct(shape, F32) for shape in bigs]
        + [jax.ShapeDtypeStruct(y.shape, BF16)] * 2
        + [jax.ShapeDtypeStruct(shape, F32) for shape in shapes],
        in_specs=hbm_specs(3) + vmem_specs(1),
        out_specs=hbm_specs(6) + vmem_specs(VECTORS + 2),
        scratch_shapes=[
            pltpu.VMEM((3, width, width), BF16),
            pltpu.VMEM((3, width, width), F32),
            pltpu.VMEM((2, *y.shape), BF16),
            pltpu.SemaphoreType.DMA((3,)),
            pltpu.SemaphoreType.DMA((3,)),
            pltpu.SemaphoreType.DMA((2, 2)),
        ],
        compiler_params=pltpu.CompilerParams(vmem_limit_bytes=VMEM_BYTES),
        name="widen",
    )(summed, y, dx, small)


BLOCK = 256
LAG = 3


def reduce_kernel(bits, chunks, blocks, lags, window, lined, *refs):
    (a_ref, dm_ref, h2_ref, dz_ref, h1_ref, dp_ref, o_ref, dproj_ref, y_ref, dx_ref, sums_ref, tables_ref) = refs[:12]
    out_ref, small_out_ref, y_out, dx_out = refs[12:16]
    refs = refs[16:]
    (lhs, rhs, grads, total, crossing, landed, smalls, small_ref, small_landed, small_total) = refs[:10]
    small_received, received = refs[10 : 10 + bits], refs[10 + bits : -10]
    (load_sem, send_sem, recv_sem, small_send, small_recv, store_sem, cross_send, cross_recv, row_sem, credit) = refs[-10:]
    me = lax.axis_index("dp")
    section = lax.axis_index("section")
    beside = 1 - section
    rows = BLOCK * blocks
    width = grads.shape[1]
    per_side = width // BLOCK
    last = 2 * bits
    steps = 10 if lined else last
    starts = [0] + [lags[0] + lags[1] * place for place in range(steps + 1)]

    barrier = pltpu.get_barrier_semaphore()
    for place in range(bits):
        stride = 1 << place
        other = me + stride * (1 - 2 * ((me // stride) % 2))
        pl.semaphore_signal(barrier, inc=1, device_id={"dp": other}, device_id_type=MESH)
    pl.semaphore_signal(barrier, inc=1, device_id={"section": beside}, device_id_type=MESH)
    pl.semaphore_wait(barrier, bits + 1)

    def across(source, target, number):
        return pltpu.make_async_remote_copy(
            src_ref=source,
            dst_ref=target,
            send_sem=cross_send.at[number],
            recv_sem=cross_recv.at[number],
            device_id={"section": beside},
            device_id_type=MESH,
        )

    def row_copy(number):
        source, target = ((y_ref, y_out), (dx_ref, dx_out))[number]
        return pltpu.make_async_copy(source.at[section], target.at[section], row_sem.at[number])

    def row_across(number):
        source, target = ((y_ref, y_out), (dx_ref, dx_out))[number]
        return across(source.at[beside], target.at[section], window + 1 + number)

    families = (
        (a_ref, dm_ref, 4 * per_side, True),
        (h2_ref, dz_ref, 4 * per_side, False),
        (h1_ref, dp_ref, 3 * per_side, False),
        (o_ref, dproj_ref, per_side, False),
    )
    n_blocks = 12 * per_side

    def load(block):
        slot = block % 2
        first = 0
        for left, right, count, walks in families:
            @pl.when((block >= first) & (block < first + count))
            def _():
                local = block - first
                if walks:
                    left_column = local * BLOCK
                    right_column = 0
                else:
                    left_column = (local % per_side) * BLOCK
                    right_column = (local // per_side) * width
                for number, layer in enumerate((section, beside)):
                    pltpu.make_async_copy(
                        left.at[layer, :, pl.ds(pl.multiple_of(left_column, BLOCK), BLOCK)],
                        lhs.at[slot, number],
                        load_sem.at[0, slot],
                    ).start()
                    pltpu.make_async_copy(
                        right.at[layer, :, pl.ds(pl.multiple_of(right_column, BLOCK), width)],
                        rhs.at[slot, number],
                        load_sem.at[1, slot],
                    ).start()
            first += count

    def produce(block, sub, side):
        slot = block % 2
        pltpu.make_async_copy(lhs.at[slot], lhs.at[slot], load_sem.at[0, slot]).wait()
        pltpu.make_async_copy(rhs.at[slot], rhs.at[slot], load_sem.at[1, slot]).wait()

        @pl.when(block + 1 < n_blocks)
        def _():
            load(block + 1)

        crossing[side, sub * BLOCK : (sub + 1) * BLOCK, :] = dot(lhs[slot, 1], rhs[slot, 1], 0, 0).astype(BF16)
        grads[chunk(block, BLOCK), :] = dot(lhs[slot, 0], rhs[slot, 0], 0, 0).astype(BF16)

    def turn(chunk):
        place = chunk % 9
        return place % 2 + place // 5 - place // 6

    def partner(rotation, stage):
        stride = lax.shift_left(jnp.int32(1), (stage + rotation) % bits)
        mine = (me // stride) % 2
        return mine, me + stride * (1 - 2 * mine)

    def offset(base, height, rotation, stage):
        for earlier in range(stage):
            mine, _ = partner(rotation, earlier)
            base = base + mine * (height >> (earlier + 1))
        return base

    def piece(ref, start, size):
        return ref.at[pl.ds(pl.multiple_of(start, size), size)]

    def send(position, base, height, rotation, source, landing, result, slot, sems):
        send_at, recv_at = sems
        if position < bits:
            stage = position
            half = height >> (stage + 1)
            mine, other = partner(rotation, stage)
            start = offset(base, height, rotation, stage) + (1 - mine) * half
            src, dst = piece(source, start, half), landing[stage].at[slot]
        else:
            stage = last - 1 - position
            half = height >> (stage + 1)
            mine, other = partner(rotation, stage)
            start = offset(base, height, rotation, stage + 1)
            src = dst = piece(result, start, half)
        return pltpu.make_async_remote_copy(
            src_ref=src,
            dst_ref=dst,
            send_sem=send_at.at[position],
            recv_sem=recv_at.at[position, slot],
            device_id={"dp": other},
            device_id_type=MESH,
        )

    def take(position, base, height, rotation, source, landing, result, slot, sems):
        send(position - 1, base, height, rotation, source, landing, result, slot, sems).wait_recv()
        stage = position - 1
        if stage < bits:
            half = height >> (stage + 1)
            start = pl.multiple_of(offset(base, height, rotation, stage + 1), half)
            keep = pl.ds(start, half)
            value = source[keep, :].astype(jnp.float32) + landing[stage][slot].astype(jnp.float32)
            target = result if stage == bits - 1 else source
            target[keep, :] = value.astype(target.dtype)

    def step(position, *way):
        if position > 0:
            take(position, *way)
        if position < last:
            send(position, *way).start()

    main = (grads, received, total)
    main_sems = (send_sem, recv_sem)

    def cross(side):
        return across(crossing.at[side], landed.at[side], side)

    def give(part):
        side = part % window

        @pl.when(part >= window)
        def _():
            cross(side).wait_send()
            pl.semaphore_wait(credit, 1)

        for sub in range(blocks):
            block = part * blocks + sub

            @pl.when(block < n_blocks)
            def _():
                produce(block, sub, side)

        cross(side).start()

    def join(part):
        side = part % window
        cross(side).wait_recv()
        there = chunk(part, rows)
        grads[there, :] = (grads[there, :].astype(F32) + landed[side].astype(F32)).astype(BF16)

        @pl.when(part < chunks - window)
        def _():
            pl.semaphore_signal(credit, inc=1, device_id={"section": beside}, device_id_type=MESH)

    row_z = me // 4
    side_z = row_z // 2
    middle = (row_z + side_z) % 2
    inner, outer = me + 4 * (1 - 2 * side_z), me - 4 * (1 - 2 * side_z)

    def line_plan(early, part):
        place = part % 8
        first = 1 + (place // 2 if early else place % 2 * ((place + 5) // 8))
        second = 3 - first
        mine_first, mine_second = (me // first) % 2, (me // second) % 2
        peer_first = me + first * (1 - 2 * mine_first)
        peer_second = me + second * (1 - 2 * mine_second)
        base = part * rows
        before = 1 + (place + 5) // 8
        if early:
            slot = 2 * (part // 8) + place // 2
            landing = received[4:]
            quarter = rows // 4
            line = base
            whole = base + row_z * quarter
            size_first = quarter // 2
        else:
            slot = part - 2 * (part // 8) - before
            landing = received[:4]
            whole = base
            size_first = rows // 2
        size_second = size_first // 2
        keep_first = whole + mine_first * size_first
        keep_second = keep_first + mine_second * size_second
        if not early:
            line = keep_second
            quarter = size_second // 4
        everyone = None
        line_land, cross_land, first_land, second_land = [ref.at[slot] for ref in landing]
        mostly = line + quarter * (1 - side_z)
        ending = line + 3 * quarter * side_z
        near, far = line + 2 * quarter * side_z, line + 2 * quarter * (1 - side_z)
        swap_first = (everyone, everyone, peer_first, whole + (1 - mine_first) * size_first, size_first, keep_first, first_land)
        swap_second = (
            everyone, everyone, peer_second, keep_first + (1 - mine_second) * size_second, size_second, keep_second, second_land
        )
        inward = (0, 1, inner, mostly, 3 * quarter, mostly, line_land)
        between = (1, 1, inner, far, 2 * quarter, near, cross_land)
        outward = (1, 0, outer, ending, quarter, ending, line_land.at[pl.ds(0, quarter)])
        back_inward = (0, 1, inner, ending, quarter, None, None)
        back_between = (1, 1, inner, near, 2 * quarter, None, None)
        back_outward = (1, 0, outer, mostly, 3 * quarter, None, None)
        back_first = (everyone, everyone, peer_first, keep_first, size_first, None, None)
        back_second = (everyone, everyone, peer_second, keep_second, size_second, None, None)
        if early:
            return [inward, between, outward, swap_first, swap_second,
                    back_second, back_first, back_inward, back_between, back_outward]
        return [swap_first, swap_second, inward, between, outward,
                back_inward, back_between, back_outward, back_second, back_first]

    def only(role, act):
        if role is None:
            act()
        else:
            pl.when(middle == role)(act)

    def line_step(position, part):
        def run(early):
            plan = line_plan(early, part)

            def copy(number):
                sender, receiver, peer, start, size, arrives, lands = plan[number]
                source = grads if arrives is not None else total
                here = pl.ds(pl.multiple_of(start, 16), size)
                return pltpu.make_async_remote_copy(
                    src_ref=source.at[here],
                    dst_ref=total.at[here] if arrives is None else lands,
                    send_sem=send_sem.at[number],
                    recv_sem=recv_sem.at[number, part],
                    device_id={"dp": peer},
                    device_id_type=MESH,
                )

            def arrive():
                size, arrives, lands = plan[position - 1][4:]
                copy(position - 1).wait_recv()
                if arrives is not None:
                    there = pl.ds(pl.multiple_of(arrives, 16), size)
                    value = (grads[there, :].astype(F32) + lands[...].astype(F32)).astype(BF16)
                    if position == 5:
                        total[there, :] = value
                    else:
                        grads[there, :] = value

            if position > 0:
                only(plan[position - 1][1], arrive)
            if position == 5 and not early:

                def keep():
                    size = rows // 16
                    there = pl.ds(pl.multiple_of(plan[1][5] + row_z * size, 16), size)
                    total[there, :] = grads[there, :]

                only(1, keep)
            if position < 10:
                only(plan[position][0], lambda: copy(position).start())

        early = (part % 8 == 0) | (part % 8 == 2)

        @pl.when(early)
        def _():
            run(True)

        @pl.when(jnp.logical_not(early))
        def _():
            run(False)

    def line_rows(role):
        ends = ([128, 64, 48, 0, 0, 16, 0, 0, 64, 128], [192, 0, 0, 32, 16, 16, 32, 64, 0, 0])
        middles = ([128, 64, 0, 32, 16, 0, 32, 48, 64, 128], [0, 128, 64, 32, 16, 16, 32, 0, 128, 192])
        late, soon = middles if role else ends
        count = sum(part % 8 in (0, 2) for part in range(chunks))
        return [(chunks - count) * a + count * b for a, b in zip(late, soon)]

    def walk(position, part):
        if position == 0:
            join(part)
        base = part * rows
        if lined:
            line_step(position, part)
        else:
            step(position, base, rows, turn(part), *main, part, main_sems)
        if position == steps:
            there = pl.ds(pl.multiple_of(base, rows), rows)
            pltpu.make_async_copy(total.at[there], out_ref.at[there], store_sem.at[0]).start()

    def small_cross():
        return across(smalls.at[beside], small_landed, window)

    def walk_small(position):
        height = small_ref.shape[0]
        if position == 0:
            small_cross().wait_recv()
            small_ref[...] = smalls[section] + small_landed[...]
        way = (0, height, 0, small_ref, small_received, small_total, 0, (small_send, small_recv))
        step(position, *way)

    load(jnp.int32(0))
    smalls[...] = jnp.zeros_like(smalls)
    places = small_lines(width)
    for layer in range(2):
        for row, tile, line in places:
            if row == B1:
                row, tile = B1 + tile // (width // LANES), tile % (width // LANES)
            smalls[layer, line : line + 1, :] = sums_ref[layer, row : row + 1, tile * LANES : (tile + 1) * LANES]
        line = len(places)
        for head in range(tables_ref.shape[1]):
            for tile in range(tables_ref.shape[2] // LANES):
                lanes = slice(tile * LANES, (tile + 1) * LANES)
                smalls[layer, line : line + 1, :] = tables_ref[layer, head : head + 1, lanes]
                line += 1
    small_cross().start()
    for number in range(2):
        row_copy(number).start()
        row_across(number).start()

    @pl.loop(0, chunks + starts[-1])
    def _(tick):
        @pl.when(tick < chunks)
        def _():
            give(tick)

        for position in range(steps + 1):
            part = tick - starts[position + 1]

            @pl.when((part >= 0) & (part < chunks))
            def _():
                walk(position, part)

            if position <= last:

                @pl.when(part == 0)
                def _():
                    walk_small(position)

    small_out_ref[...] = small_total[...]
    for position in range(last):
        stage = position if position < bits else last - 1 - position
        size = small_received[stage]
        pltpu.make_async_copy(size, size, small_send.at[position]).wait()
        if not lined:
            size = received[stage]
            pltpu.make_async_copy(size, size, send_sem.at[position]).wait()
    if lined:
        for role in range(2):

            @pl.when(middle == role)
            def _():
                for number, amount in enumerate(line_rows(role)):
                    if amount > 0:
                        size = grads.at[pl.ds(0, amount)]
                        pltpu.make_async_copy(size, size, send_sem.at[number]).wait()
    for side in range(window):
        cross(side).wait_send()
    small_cross().wait_send()
    for number in range(2):
        row_copy(number).wait()
        row_across(number).wait()
    pltpu.make_async_copy(total, out_ref, store_sem.at[0]).wait()


def reduce_gradients(a, dm, h2, dz, h1, packed, o, dproj, y, dx, sums, tables):
    parts = lax.axis_size("dp")
    bits = parts.bit_length() - 1
    blocks = max(1, 16 * parts // BLOCK)
    layers, length, width = h1.shape
    n_blocks = 12 * width // BLOCK
    chunks = -(-n_blocks // blocks)
    rows = BLOCK * blocks
    lags, window = ((1, LAG), 4) if blocks == 1 else ((0, LAG), 1)
    lines = len(small_lines(width)) + tables.shape[1] * tables.shape[2] // LANES
    height = -(-lines // (8 * parts)) * 8 * parts
    small = (height, LANES)
    lined = parts == 16
    if lined:
        early = sum(part % 8 in (0, 2) for part in range(chunks))
        lands = [(chunks - early, size) for size in (48, 32, 128, 64)] + [(early, size) for size in (192, 128, 32, 16)]
    else:
        lands = [(chunks, rows >> (s + 1)) for s in range(bits)]
    steps = 10 if lined else 2 * bits
    return pl.pallas_call(
        functools.partial(reduce_kernel, bits, chunks, blocks, lags, window, lined),
        out_shape=(
            jax.ShapeDtypeStruct((chunks * rows, width), BF16),
            jax.ShapeDtypeStruct(small, F32),
            jax.ShapeDtypeStruct(y.shape, BF16),
            jax.ShapeDtypeStruct(dx.shape, BF16),
        ),
        in_specs=hbm_specs(10) + vmem_specs(2),
        out_specs=hbm_specs(1) + vmem_specs(1) + hbm_specs(2),
        scratch_shapes=[
            pltpu.VMEM((2, layers, length, BLOCK), BF16),
            pltpu.VMEM((2, layers, length, width), BF16),
            pltpu.VMEM((chunks * rows, width), BF16),
            pltpu.VMEM((chunks * rows, width), BF16),
            pltpu.VMEM((window, rows, width), BF16),
            pltpu.VMEM((window, rows, width), BF16),
            pltpu.VMEM((layers, *small), F32),
            pltpu.VMEM(small, F32),
            pltpu.VMEM(small, F32),
            pltpu.VMEM(small, F32),
            *[pltpu.VMEM((1, height >> (s + 1), LANES), F32) for s in range(bits)],
            *[pltpu.VMEM((*size, width), BF16) for size in lands],
            pltpu.SemaphoreType.DMA((2, 2)),
            pltpu.SemaphoreType.DMA((steps,)),
            pltpu.SemaphoreType.DMA((steps, chunks)),
            pltpu.SemaphoreType.DMA((2 * bits,)),
            pltpu.SemaphoreType.DMA((2 * bits, 1)),
            pltpu.SemaphoreType.DMA((1,)),
            pltpu.SemaphoreType.DMA((window + 3,)),
            pltpu.SemaphoreType.DMA((window + 3,)),
            pltpu.SemaphoreType.DMA((2,)),
            pltpu.SemaphoreType.REGULAR,
        ],
        compiler_params=pltpu.CompilerParams(
            collective_id=0, has_side_effects=True, vmem_limit_bytes=VMEM_BYTES
        ),
        name="reduce_gradients",
    )(a, dm, h2, dz, h1, packed, o, dproj, y, dx, sums, tables)


def swapped(block):
    return lax.ppermute(block, "section", [(0, 1), (1, 0)])


def per_device(
    patches,
    segment_ids,
    pad_counts,
    norm1_gain,
    norm1_bias,
    qkv_weight,
    query_bias,
    value_bias,
    rel_table,
    proj_weight,
    proj_bias,
    scale_attn,
    norm2_gain,
    norm2_bias,
    fc1_weight,
    fc1_bias,
    fc2_weight,
    fc2_bias,
    scale_mlp,
    cotangent,
):
    micro, length, width = patches.shape
    heads, entries = rel_table.shape[1:]
    vectors = (
        norm1_gain,
        norm1_bias,
        query_bias,
        value_bias,
        proj_bias,
        scale_attn,
        norm2_gain,
        norm2_bias,
        fc2_bias,
        scale_mlp,
        fc1_bias,
    )
    own = pack(vectors, rel_table.transpose(1, 0, 2))
    own_band = bias_band(own, heads, length)
    other = swapped(own)
    weights = [(x, swapped(x)) for x in (qkv_weight[0], proj_weight[0])]
    own_band, other, *late = lax.optimization_barrier(
        (own_band, other, weights[0][1], weights[1][1], fc1_weight[0], fc2_weight[0])
    )
    weights = [(weights[0][0], late[0]), (weights[1][0], late[1])] + [(x, swapped(x)) for x in late[2:]]
    other_band = bias_band(other, heads, length)
    packs, band = (own, other), (own_band, other_band)
    saved = None
    rows = patches
    for layer, phase in ((0, ATTENTION), (0, MLP), (1, BOTH)):
        saved = forward(layer, phase, pad_counts, rows, segment_ids, packs, band, weights, saved)
    kept = None
    for layer in (1, 0):
        kept = backward(layer, cotangent, packs, weights, saved, kept)
    dm, dz, dproj, packed, dx, tables, sums = kept
    h1, mixed, h2, act, y = saved[0], saved[3], saved[6], saved[10], saved[13]
    summed, small, y, dx = reduce_gradients(
        act, dm, h2, dz, h1, packed, mixed, dproj, y, dx, sums, tables
    )
    fc2_grad, fc1_grad, qkv_grad, proj_grad, outputs, in_grads, *small_grads = widen(
        summed, small, y, dx, width, heads, entries
    )
    table_grad = small_grads[VECTORS + 1].transpose(1, 0, 2)
    return (
        outputs[None],
        in_grads[None],
        small_grads[GAIN1],
        small_grads[SHIFT1],
        qkv_grad[None],
        small_grads[QBIAS],
        small_grads[VBIAS],
        table_grad,
        proj_grad[None],
        small_grads[PBIAS],
        small_grads[SCALE_A],
        small_grads[GAIN2],
        small_grads[SHIFT2],
        fc1_grad[None],
        small_grads[B1],
        fc2_grad[None],
        small_grads[B2],
        small_grads[SCALE_M],
    )


def solution(mesh):
    placed = (
        P("dp", None, None),
        P("dp", None),
        P("dp"),
        P("section", None),
        P("section", None),
        P("section", None, None),
        P("section", None),
        P("section", None),
        P("section", None, None),
        P("section", None, None),
        P("section", None),
        P("section", None),
        P("section", None),
        P("section", None),
        P("section", None, None),
        P("section", None),
        P("section", None, None),
        P("section", None),
        P("section", None),
        P("dp", None, None),
    )
    return jax.shard_map(
        per_device,
        mesh=mesh,
        in_specs=placed,
        out_specs=(
            P("section", "dp", None, None),
            P("section", "dp", None, None),
            P("section", None),
            P("section", None),
            P("section", None, None),
            P("section", None),
            P("section", None),
            P("section", None, None),
            P("section", None, None),
            P("section", None),
            P("section", None),
            P("section", None),
            P("section", None),
            P("section", None, None),
            P("section", None),
            P("section", None, None),
            P("section", None),
            P("section", None),
        ),
        check_vma=False,
    )
```

```python
import functools
import math

import jax
import jax.numpy as jnp
from jax import lax
from jax.experimental import pallas as pl
from jax.experimental.pallas import tpu as pltpu
from jax.sharding import PartitionSpec as P

MESH = pl.DeviceIdType.MESH
BF16, F32 = jnp.bfloat16, jnp.float32
VMEM_BYTES = 60 * 1024 * 1024
LANES = 128
HALF = 64
REACH = 2 * LANES
GAIN1, SHIFT1, QBIAS, VBIAS, PBIAS, SCALE_A, GAIN2, SHIFT2, B2, SCALE_M, B1 = range(11)
VECTORS = 10
STORED = 14
BOTH, ATTENTION, MLP = range(3)
STRIP = 16
GROUP = 3


def dot(left, right, left_dim, right_dim):
    return lax.dot_general(
        left, right, (((left_dim,), (right_dim,)), ((), ())), preferred_element_type=F32
    )


def nn(left, right):
    return dot(left, right, 1, 0)


def nt(left, right):
    return dot(left, right, 1, 1)


def normalize(values):
    centered = values - jnp.mean(values, -1, keepdims=True)
    inverse = lax.rsqrt(jnp.mean(centered * centered, -1, keepdims=True) + 1e-06)
    return centered * inverse, inverse


def norm_back(upper, scaled, inverse):
    return inverse * (
        upper
        - jnp.mean(upper, -1, keepdims=True)
        - scaled * jnp.mean(upper * scaled, -1, keepdims=True)
    )


def fold(values):
    return jnp.sum(values.reshape(values.shape[0] // 8, 8, values.shape[1]), 0)


def half_mask(shape, which):
    return lax.broadcasted_iota(jnp.int32, shape, 1) // HALF == which


def strips(first, last, size):
    return [slice(start, start + size) for start in range(first, last, size)]


def chunk(index, size):
    return pl.ds(pl.multiple_of(index * size, size), size)


def skew_bias(reversed_row, target):
    span, lanes = target.shape
    rows = pltpu.roll(jnp.broadcast_to(reversed_row, (8, reversed_row.shape[1])), 1, 1, stride=1, stride_axis=0)
    tiles = span // lanes
    for fine in range(lanes // 8):
        moved = rows if fine == 0 else pltpu.roll(rows, 8 * fine, 1)
        for coarse in range(tiles):
            place = 8 * (fine + lanes // 8 * coarse)
            target[place : place + 8, :] = moved[:, lanes * (tiles - coarse) : lanes * (tiles - coarse + 1)]


def gather_diagonals(source):
    span, lanes = source.shape
    tiles = span // lanes
    width = span + lanes
    blank = jnp.zeros((8, lanes), F32)
    found = None
    for fine in range(lanes // 8):
        places = [8 * (fine + lanes // 8 * coarse) for coarse in reversed(range(tiles))]
        line = jnp.concatenate([blank] + [source[place : place + 8, :] for place in places], 1)
        if fine > 0:
            line = pltpu.roll(line, width - 8 * fine, 1)
        found = line if found is None else found + line
    row = lax.broadcasted_iota(jnp.int32, found.shape, 0)
    for place in range(3):
        moved = pltpu.roll(found, width - (1 << place), 1)
        found = jnp.where((row // (1 << place)) % 2 == 1, moved, found)
    return jnp.sum(found, 0, keepdims=True)


def key_rows(query_block, blocks):
    reach = REACH // LANES
    return max(0, query_block - reach) * LANES, min(blocks, query_block + reach + 1) * LANES


def pick(mine, own, other, act):
    @pl.when(mine)
    def _():
        act(own)

    @pl.when(jnp.logical_not(mine))
    def _():
        act(other)


def pack_kernel(*refs):
    *vectors, bias_ref, table_ref, pack_ref = refs
    width = pack_ref.shape[1]
    heads, _, entries = table_ref.shape
    pack_ref[...] = jnp.zeros_like(pack_ref)
    for row, vector in enumerate(vectors):
        pack_ref[row : row + 1, :] = vector[...]
    for part in range(bias_ref.shape[1] // width):
        pack_ref[B1 + part : B1 + part + 1, :] = bias_ref[:, part * width : (part + 1) * width]
    first = pack_ref.shape[0] - heads
    tiles = entries // LANES
    lane = lax.broadcasted_iota(jnp.int32, (heads, LANES), 1)
    ending = jnp.broadcast_to(table_ref[:, 0, entries - 1 :], (heads, LANES))
    pack_ref[first:, :LANES] = jnp.where(lane == LANES - 1, ending, 0.0)
    for tile in range(tiles):
        there = (tiles - tile) * LANES
        pack_ref[first:, there : there + LANES] = reverse_lanes(table_ref[:, 0, tile * LANES : (tile + 1) * LANES])


def pack(vectors, rel_table):
    heads = rel_table.shape[0]
    return pl.pallas_call(
        pack_kernel,
        out_shape=jax.ShapeDtypeStruct((16 + heads, vectors[0].shape[1]), F32),
        in_specs=vmem_specs(len(vectors) + 1),
        out_specs=pl.BlockSpec(memory_space=pltpu.VMEM),
        name="pack_vectors",
    )(*vectors, rel_table)


def fill(target, source):
    target[...] = source[...]


def band_kernel(pack_ref, band_hbm, band, store_sem):
    heads = band.shape[0]
    tables = pack_ref.shape[0] - heads
    edge = jnp.zeros((1, LANES), F32)

    @pl.loop(0, heads // 4)
    def _(group):
        for within in range(4):
            head = 4 * group + within
            kept = pack_ref[pl.ds(tables + head, 1), :]
            skew_bias(jnp.concatenate([edge, kept, edge], 1), band.at[head])
        some = pl.ds(4 * group, 4)
        pltpu.make_async_copy(band.at[some], band_hbm.at[some], store_sem.at[group]).start()

    for group in range(heads // 4):
        some = pl.ds(4 * group, 4)
        pltpu.make_async_copy(band.at[some], band_hbm.at[some], store_sem.at[group]).wait()


def bias_band(packed, heads, length):
    shape = (heads, 2 * length - LANES, LANES)
    return pl.pallas_call(
        band_kernel,
        out_shape=jax.ShapeDtypeStruct(shape, F32),
        in_specs=vmem_specs(1),
        out_specs=pl.BlockSpec(memory_space=pl.ANY),
        scratch_shapes=[pltpu.VMEM(shape, F32), pltpu.SemaphoreType.DMA((heads // 4,))],
        compiler_params=pltpu.CompilerParams(vmem_limit_bytes=VMEM_BYTES + 2 * 1024 * 1024),
        name="bias_band",
    )(packed)


def forward_kernel(layer, phase, pads, x_hbm, seg_ref, own_pack, other_pack, own_band, other_band, *refs):
    if phase != MLP:
        (wqkv_own, wqkv_other, wp_own, wp_other), refs = refs[:4], refs[4:]
    if phase != ATTENTION:
        (w1_own, w1_other, w2_own, w2_other), refs = refs[:4], refs[4:]
    refs = refs[STORED if layer > 0 or phase == MLP else 0 :]
    stores = refs[:STORED]
    (bias, wqkv, wp, w1, w2, mask, h1, qkv, probs, mixed, proj, x1, h2, xin, wide_mixed, scales, act, slope, mlp, out_row, held, pack_ref, load_sem, store_sem, prob_sem) = refs[STORED:]
    h1_o, qkv_o, prob_o, mixed_o, proj_o, x1_o, h2_o, xin_o, wide_o, scales_o, act_o, slope_o, mlp_o, y_o = stores
    hidden = w1.shape[1]
    length, width = xin.shape
    heads = bias.shape[0]
    blocks = length // LANES
    section = lax.axis_index("section")
    mine = section == layer
    factor = HALF ** (-0.5)
    thirds = [pl.ds(part * width, width) for part in range(3)]

    def load(number):
        if number < 3:
            part = thirds[number]
            return wqkv_own.at[:, part], wqkv_other.at[:, part], wqkv.at[:, part], load_sem.at[number]
        if number == 3:
            return wp_own, wp_other, wp, load_sem.at[3]
        part = pl.ds((number % 4) * width, width)
        if number < 8:
            return w1_own.at[:, part], w1_other.at[:, part], w1.at[:, part], load_sem.at[number]
        return w2_own.at[part, :], w2_other.at[part, :], w2.at[part, :], load_sem.at[number]

    def start(number):
        own, other, target, sem = load(number)
        pick(mine, own, other, lambda source: pltpu.make_async_copy(source, target, sem).start())

    def wait(number):
        own, other, target, sem = load(number)
        pltpu.make_async_copy(target, target, sem).wait()

    def store(number, source, there):
        return pltpu.make_async_copy(source, there.at[layer], store_sem.at[number])

    def part_store(number, source, there, columns):
        return pltpu.make_async_copy(source.at[:, columns], there.at[layer, :, columns], store_sem.at[number])

    def vector(row):
        return pack_ref[row : row + 1, :]

    def attention():
        source = x_hbm.at[section] if layer == 0 else y_o.at[0]
        pltpu.make_async_copy(source, xin, load_sem.at[12]).start()
        start(0)
        pltpu.make_async_copy(xin, xin, load_sem.at[12]).wait()
        start(1)
        start(2)
        pick(mine, own_band, other_band, lambda source: pltpu.make_async_copy(source, bias, load_sem.at[13]).start())
        segment = seg_ref[pl.ds(section, 1), :].astype(F32)
        key_segment = jnp.broadcast_to(segment, (LANES, length)).T

        for rows in strips(0, length, STRIP):
            scaled, _ = normalize(xin[rows, :].astype(F32))
            h1[rows, :] = (scaled * vector(GAIN1) + vector(SHIFT1)).astype(BF16)
        for part in range(3):
            wait(part)

        alive = length - pads[section]
        for place in range(blocks):
            lanes = slice(place * LANES, (place + 1) * LANES)
            for rows in strips(0, length, 64):
                key = lax.broadcasted_iota(jnp.int32, (64, LANES), 0) + rows.start
                query = lax.broadcasted_iota(jnp.int32, (64, LANES), 1) + place * LANES
                allowed = ((key_segment[rows] == segment[:, lanes]) & (key < alive)) | (key == query)
                mask[rows, lanes] = jnp.where(allowed, 0.0, -1000000000.0)

        store(0, h1, h1_o).start()
        store(7, xin, xin_o).start()
        projections = [(part, pl.ds(high * (length // 2), length // 2)) for part in range(3) for high in range(2)]

        def project(number):
            part, rows = projections[number]
            return nn(h1[rows, :], wqkv[:, thirds[part]])

        coming = project(0)
        for number, (part, rows) in enumerate(projections):
            current = coming
            if number + 1 < len(projections):
                coming = project(number + 1)
            for strip in strips(0, length // 2, STRIP):
                piece = current[strip]
                if part == 0:
                    piece = (piece + vector(QBIAS)) * factor
                if part == 2:
                    piece = piece + vector(VBIAS)
                qkv[pl.ds(rows.start + strip.start, STRIP), thirds[part]] = piece.astype(BF16)
        store(1, qkv, qkv_o).start()
        pltpu.make_async_copy(bias, bias, load_sem.at[13]).wait()
        for number in range(3, 4 if phase == ATTENTION else 12):
            start(number)
        together = 2 * GROUP

        def prob_store(group):
            return pltpu.make_async_copy(
                probs.at[group % 2], prob_o.at[layer, pl.ds(together * group, together)], prob_sem.at[group % 2]
            )

        def attend(side, within, pair):
            columns = chunk(pair, LANES)
            queries = qkv[:, columns]
            keys = qkv[:, pl.ds(pl.multiple_of(width + pair * LANES, LANES), LANES)]
            values = qkv[:, pl.ds(pl.multiple_of(2 * width + pair * LANES, LANES), LANES)].T
            outs = []
            for which in range(2):
                own_keys = jnp.where(half_mask(keys.shape, which), keys, jnp.zeros_like(keys))
                lines = []
                for wide in range(blocks // 2):
                    scores = nt(own_keys, queries[2 * LANES * wide : 2 * LANES * (wide + 1)])
                    for part in range(2):
                        place = 2 * wide + part
                        low, high = key_rows(place, blocks)
                        lanes = slice(place * LANES, (place + 1) * LANES)
                        first = (blocks - 1 - place) * LANES
                        spare = (2 * within + which) * blocks + place
                        highest = None
                        for rows in strips(low, high, 64):
                            here = (
                                scores[rows, part * LANES : (part + 1) * LANES]
                                + bias[2 * pair + which, first + rows.start : first + rows.stop, :]
                                + mask[rows, lanes]
                            )
                            held[spare, rows, :] = here
                            top = jnp.max(here.reshape(8, 8, LANES), 0)
                            highest = top if highest is None else jnp.maximum(highest, top)
                        highest = jnp.max(highest, 0, keepdims=True)
                        sums = jnp.zeros((8, LANES), F32)
                        for rows in strips(low, high, 64):
                            expo = jnp.exp(held[spare, rows, :] - highest)
                            probs[side, 2 * within + which, rows, lanes] = expo.astype(BF16)
                            sums = sums + fold(expo)
                        lines.append(1.0 / jnp.sum(sums, 0, keepdims=True))
                        if low > 0:
                            probs[side, 2 * within + which, :low, lanes] = jnp.zeros((low, LANES), BF16)
                        if high < length:
                            probs[side, 2 * within + which, high:, lanes] = jnp.zeros((length - high, LANES), BF16)
                scale = jnp.concatenate(lines, 1)
                scales[pl.ds(2 * pair + which, 1), :] = scale
                outs.append(nn(values[which * HALF : (which + 1) * HALF], probs[side, 2 * within + which]) * scale)
            out = jnp.concatenate(outs, 0).T
            wide_mixed[:, columns] = out
            mixed[:, columns] = out.astype(BF16)

        @pl.loop(0, heads // together)
        def _(group):
            @pl.when(group >= 2)
            def _():
                prob_store(group - 2).wait()

            for within in range(GROUP):
                attend(group % 2, within, GROUP * group + within)
            prob_store(group).start()

        store(3, mixed, mixed_o).start()
        store(8, wide_mixed, wide_o).start()
        store(9, scales, scales_o).start()
        wait(3)

        results = [nn(mixed[half, :], wp[...]) for half in strips(0, length, length // 2)]
        for rows in strips(0, length, STRIP):
            there = rows.start % (length // 2)
            out = results[rows.start // (length // 2)][there : there + STRIP] + vector(PBIAS)
            proj[rows, :] = out.astype(BF16)
            resid = xin[rows, :].astype(F32) + vector(SCALE_A) * out
            x1[rows, :] = resid
            scaled, _ = normalize(resid)
            h2[rows, :] = (scaled * vector(GAIN2) + vector(SHIFT2)).astype(BF16)

        store(4, proj, proj_o).start()
        store(5, x1, x1_o).start()
        store(6, h2, h2_o).start()

        def finish():
            for group in range(max(0, heads // together - 2), heads // together):
                prob_store(group).wait()

        return finish

    def mlp_part():
        pieces = [
            (pl.ds(high * (length // 2), length // 2), pl.ds(part * width, width))
            for part in range(hidden // width)
            for high in range(2)
        ]

        def expand(number):
            rows, columns = pieces[number]
            if phase == MLP and number % 2 == 0:
                wait(4 + number // 2)
            return nn(h2[rows, :], w1[:, columns])

        if phase != MLP:
            for number in range(4, 12):
                wait(number)
        coming = expand(0)
        totals = [None, None]
        for number, (rows, columns) in enumerate(pieces):
            current = coming
            if number + 1 < len(pieces):
                coming = expand(number + 1)
            for strip in strips(0, length // 2, STRIP):
                there = pl.ds(rows.start + strip.start, STRIP)
                here = current[strip] + vector(B1 + number // 2)
                normal = 0.5 * lax.erf(here * math.sqrt(0.5)) + 0.5
                density = jnp.exp(-0.5 * here * here) * (1.0 / math.sqrt(2.0 * math.pi))
                act[there, columns] = (here * normal).astype(BF16)
                slope[there, columns] = (normal + here * density).astype(BF16)
            if phase == MLP and number % 2 == 0:
                wait(8 + number // 2)
            more = nn(act[rows, columns], w2[columns, :])
            totals[number % 2] = more if number < 2 else totals[number % 2] + more
            if number in (len(pieces) // 2 - 1, len(pieces) - 1):
                columns = pl.ds((number // 4) * 2 * width, 2 * width)
                part_store(10, act, act_o, columns).start()
                part_store(11, slope, slope_o, columns).start()

        if phase == MLP:
            pltpu.make_async_copy(x1, x1, load_sem.at[13]).wait()
        for half in range(2):
            for strip in strips(0, length // 2, STRIP):
                rows = pl.ds(half * (length // 2) + strip.start, STRIP)
                out = totals[half][strip] + vector(B2)
                mlp[rows, :] = out.astype(BF16)
                out_row[rows, :] = (x1[rows, :] + vector(SCALE_M) * out).astype(BF16)

        store(12, mlp, mlp_o).start()
        store(13, out_row, y_o).start()
    pick(mine, own_pack, other_pack, functools.partial(fill, pack_ref))
    if phase == MLP:
        pltpu.make_async_copy(h2_o.at[layer], h2, load_sem.at[12]).start()
        start(4)
        pltpu.make_async_copy(h2, h2, load_sem.at[12]).wait()
        for number in (8, 5, 9, 6, 10, 7, 11):
            start(number)
        pltpu.make_async_copy(x1_o.at[layer], x1, load_sem.at[13]).start()
        mlp_part()
    else:
        finish = attention()
        if phase == BOTH:
            mlp_part()
        finish()
    ends = {0: (h1, h1_o), 1: (qkv, qkv_o), 3: (mixed, mixed_o), 4: (proj, proj_o), 5: (x1, x1_o), 6: (h2, h2_o),
            7: (xin, xin_o), 8: (wide_mixed, wide_o), 9: (scales, scales_o),
            10: (act, act_o), 11: (slope, slope_o), 12: (mlp, mlp_o), 13: (out_row, y_o)}
    for number, (source, there) in ends.items():
        if phase == BOTH or (phase == MLP) == (number >= 10):
            store(number, source, there).wait()


def hbm_specs(count):
    return [pl.BlockSpec(memory_space=pl.ANY)] * count


def vmem_specs(count):
    return [pl.BlockSpec(memory_space=pltpu.VMEM)] * count


def stacked(stored):
    return [jax.ShapeDtypeStruct((2, *shape), kind) for shape, kind in stored]


def forward(layer, phase, pads, rows, segments, packs, band, weights, kept):
    length, width = rows.shape[1:]
    heads = band[0].shape[0]
    hidden = weights[2][0].shape[1]
    used = {BOTH: weights, ATTENTION: weights[:2], MLP: weights[2:]}[phase]
    stored = [
        ((length, width), BF16),
        ((length, 3 * width), BF16),
        ((heads, length, length), BF16),
        ((length, width), BF16),
        ((length, width), BF16),
        ((length, width), F32),
        ((length, width), BF16),
        ((length, width), BF16),
        ((length, width), F32),
        ((heads, length), F32),
        ((length, hidden), BF16),
        ((length, hidden), BF16),
        ((length, width), BF16),
        ((length, width), BF16),
    ]
    scratch = [pltpu.VMEM(band[0].shape, F32)] + [pltpu.VMEM(pair[0].shape, BF16) for pair in weights]
    scratch.append(pltpu.VMEM((length, length), F32))
    scratch += [
        pltpu.VMEM((2, 2 * GROUP, length, length) if n == 2 else shape, kind)
        for n, (shape, kind) in enumerate(stored)
    ]
    scratch += [
        pltpu.VMEM((2 * GROUP * length // LANES, length, LANES), F32),
        pltpu.VMEM(packs[0].shape, F32),
        pltpu.SemaphoreType.DMA((14,)),
        pltpu.SemaphoreType.DMA((STORED,)),
        pltpu.SemaphoreType.DMA((2,)),
    ]
    operands = [pads, rows, segments, *packs, *band, *[x for pair in used for x in pair]]
    held = STORED if layer > 0 or phase == MLP else 0
    return pl.pallas_call(
        functools.partial(forward_kernel, layer, phase),
        out_shape=stacked(stored),
        in_specs=[pl.BlockSpec(memory_space=pltpu.SMEM)] + hbm_specs(1) + vmem_specs(3) + hbm_specs(2 + 2 * len(used) + held),
        out_specs=hbm_specs(STORED),
        scratch_shapes=scratch,
        input_output_aliases={len(operands) + n: n for n in range(held)},
        compiler_params=pltpu.CompilerParams(vmem_limit_bytes=VMEM_BYTES),
        name="forward_layer",
    )(*operands, *(kept if held else ()))


def backward_kernel(layer, cotangent_hbm, own_pack, other_pack, *refs):
    weights, refs = refs[:8], refs[8:]
    (qkv_i, prob_i, mixed_i, proj_i, x1_i, slope_i, mlp_i, xin_i, scales_i) = refs[:9]
    refs = refs[9 + (7 if layer == 0 else 0) :]
    stores = refs[:7]
    (wqkv, wp, w1, w2, qkv, probs, mixed, proj, x1, slope, mlp, xin, scales, dm, dz, dproj, packed, dx_ref, dx1, dmixed, dscore, diag, sums, tables, g_ref, pack_ref, load_sem, store_sem, prob_sem) = refs[7:]
    dm_o, dz_o, dproj_o, packed_o, dx_o, tables_o, sums_o = stores
    wqkv_hbm, wp_hbm, w1_hbm, w2_hbm = zip(weights[::2], weights[1::2])
    length, width = g_ref.shape
    hidden = w1.shape[1]
    blocks = length // LANES
    pairs = width // LANES
    section = lax.axis_index("section")
    mine = section == layer
    factor = HALF ** (-0.5)
    parts = [pl.ds(part * width, width) for part in range(hidden // width)]
    loads = [(mlp_i.at[layer], mlp)]
    loads += [(tuple(x.at[part, :] for x in w2_hbm), w2.at[part, :]) for part in parts]
    loads += [(slope_i.at[layer, :, part], slope.at[:, part]) for part in parts]
    loads += [(tuple(x.at[:, part] for x in w1_hbm), w1.at[:, part]) for part in parts]
    early = len(loads)
    loads += [
        (x1_i.at[layer], x1), (proj_i.at[layer], proj), (wp_hbm, wp), (qkv_i.at[layer], qkv), (mixed_i.at[layer], mixed),
        (scales_i.at[layer], scales), (wqkv_hbm, wqkv), (xin_i.at[layer], xin),
    ]
    upstream_sem = load_sem.at[len(loads)]

    def start(number):
        source, target = loads[number]

        def go(ref):
            pltpu.make_async_copy(ref, target, load_sem.at[number]).start()

        if isinstance(source, tuple):
            pick(mine, *source, go)
        else:
            go(source)

    def load(number):
        target = loads[number][1]
        return pltpu.make_async_copy(target, target, load_sem.at[number])

    def store(number, source, there):
        return pltpu.make_async_copy(source, there.at[layer], store_sem.at[number])

    together = 2 * GROUP

    def prob_load(group):
        return pltpu.make_async_copy(
            prob_i.at[layer, pl.ds(together * group, together)], probs.at[group % 2], prob_sem.at[group % 2]
        )

    def vector(row):
        return pack_ref[row : row + 1, :]

    def put(row, partial):
        sums[row : row + 1, :] = jnp.sum(partial, 0, keepdims=True)

    nothing = jnp.zeros((8, width), F32)

    upstream_hbm = cotangent_hbm.at[section] if layer == 1 else dx_o.at[1]
    pltpu.make_async_copy(upstream_hbm, g_ref, upstream_sem).start()
    pick(mine, own_pack, other_pack, functools.partial(fill, pack_ref))
    for number in (0, 1):
        start(number)
    pltpu.make_async_copy(g_ref, g_ref, upstream_sem).wait()
    load(0).wait()
    for number in (5, 9, 2, 6, 10):
        start(number)
    scale_sum = bias_sum = nothing
    for rows in strips(0, length, STRIP):
        upstream = g_ref[rows, :].astype(F32)
        low = (upstream * vector(SCALE_M)).astype(BF16)
        dm[rows, :] = low
        scale_sum = scale_sum + fold(upstream * mlp[rows, :].astype(F32))
        bias_sum = bias_sum + fold(low.astype(F32))
    put(SCALE_M, scale_sum)
    put(B2, bias_sum)
    store(0, dm, dm_o).start()
    pieces = [pl.ds(part * width, width) for part in range(hidden // width)]

    def expand(number):
        load(1 + number).wait()
        return nt(dm[...], w2[pieces[number], :])

    coming = expand(0)
    upper_sum = None
    for number, columns in enumerate(pieces):
        if number == 0:
            for later in (3, 7, 11, 4, 8, 12):
                start(later)
        if number == 2:
            for later in range(early, len(loads)):
                start(later)
            prob_load(0).start()
        load(5 + number).wait()
        load(9 + number).wait()
        current = coming
        if number + 1 < len(pieces):
            coming = expand(number + 1)
        act_sum = nothing
        for there in strips(0, length, STRIP):
            low = (current[there] * slope[there, columns].astype(F32)).astype(BF16)
            dz[there, columns] = low
            act_sum = act_sum + fold(low.astype(F32))
        put(B1 + number, act_sum)
        more = nt(dz[:, columns], w1[:, columns])
        upper_sum = more if number == 0 else upper_sum + more
    store(1, dz, dz_o).start()
    load(early).wait()
    load(early + 1).wait()
    found = [nothing] * 4
    for rows in strips(0, length, STRIP):
        upper = upper_sum[rows]
        scaled, inverse = normalize(x1[rows, :])
        resid = g_ref[rows, :].astype(F32) + norm_back(upper * vector(GAIN2), scaled, inverse)
        dx1[rows, :] = resid
        low = (resid * vector(SCALE_A)).astype(BF16)
        dproj[rows, :] = low
        terms = (upper * scaled, upper, resid * proj[rows, :].astype(F32), low.astype(F32))
        found = [old + fold(term) for old, term in zip(found, terms)]
    for row, partial in zip((GAIN2, SHIFT2, SCALE_A, PBIAS), found):
        put(row, partial)
    store(2, dproj, dproj_o).start()
    load(early + 2).wait()
    dmixed[...] = nt(dproj[...], wp[...]).astype(BF16)
    for number in range(early + 3, early + 6):
        load(number).wait()

    def attend(side, within, pair):
        columns = chunk(pair, LANES)
        key_columns = pl.ds(pl.multiple_of(width + pair * LANES, LANES), LANES)
        value_columns = pl.ds(pl.multiple_of(2 * width + pair * LANES, LANES), LANES)
        values = qkv[:, value_columns]
        above = dmixed[:, columns]
        queries_t = qkv[:, columns].T
        keys_t = qkv[:, key_columns].T
        above_t = above.astype(F32).T
        products = (above.astype(F32) * mixed[:, columns]).T
        grads = [], [], []
        for which in range(2):
            place_in = 2 * within + which
            half = slice(which * HALF, (which + 1) * HALF)
            delta = jnp.sum(products[half], 0, keepdims=True)
            scale = scales[pl.ds(2 * pair + which, 1), :]
            own_values = jnp.where(half_mask(values.shape, which), values, jnp.zeros_like(values))
            edge = (blocks - 1) * LANES
            diag[place_in, :edge, :] = jnp.zeros((edge, LANES), F32)
            for wide in range(blocks // 2):
                prob_grad = nt(own_values, above[2 * LANES * wide : 2 * LANES * (wide + 1)])
                for part in range(2):
                    place = 2 * wide + part
                    low, high = key_rows(place, blocks)
                    lanes = slice(place * LANES, (place + 1) * LANES)
                    first_row = (blocks - 1 - place) * LANES
                    for rows in strips(low, high, 64):
                        here = (probs[side, place_in, rows, lanes].astype(F32) * scale[:, lanes]) * (
                            prob_grad[rows, part * LANES : (part + 1) * LANES] - delta[:, lanes]
                        )
                        dscore[place_in, rows, lanes] = here.astype(BF16)
                        there = slice(first_row + rows.start, first_row + rows.stop)
                        diag[place_in, there, :] = here if place == 0 else diag[place_in, there, :] + here
                    if low > 0:
                        dscore[place_in, :low, lanes] = jnp.zeros((low, LANES), BF16)
                    if high < length:
                        dscore[place_in, high:, lanes] = jnp.zeros((length - high, LANES), BF16)
                    if place == 0:
                        diag[place_in, edge + high :, :] = jnp.zeros((length - high, LANES), F32)
            line = gather_diagonals(diag.at[place_in])
            most = tables.shape[1] - LANES
            tables[pl.ds(2 * pair + which, 1), :] = jnp.concatenate(
                [line[:, REACH + 1 : REACH + 1 + most], line[:, REACH : REACH + LANES]], 1
            )
            grads[0].append(nn(keys_t[half], dscore[place_in]))
            grads[1].append(nt(queries_t[half], dscore[place_in]))
            grads[2].append(nt((above_t[half] * scale).astype(BF16), probs[side, place_in]))
        for found, where, scale in zip(grads, (columns, key_columns, value_columns), (factor, None, None)):
            low = jnp.concatenate(found, 0).astype(BF16)
            if scale is not None:
                low = (low.astype(F32) * scale).astype(BF16)
            packed[:, where] = low.T

    @pl.loop(0, pairs // GROUP)
    def _(group):
        prob_load(group).wait()

        @pl.when(group + 1 < pairs // GROUP)
        def _():
            prob_load(group + 1).start()

        for within in range(GROUP):
            attend(group % 2, within, GROUP * group + within)

    store(3, packed, packed_o).start()
    load(early + 6).wait()
    result = nt(packed[...], wqkv[...])
    load(early + 7).wait()
    found = [nothing] * 4
    for rows in strips(0, length, STRIP):
        upper = result[rows]
        scaled, inverse = normalize(xin[rows, :].astype(F32))
        dx_ref[rows, :] = (dx1[rows, :] + norm_back(upper * vector(GAIN1), scaled, inverse)).astype(BF16)
        terms = (
            upper * scaled,
            upper,
            packed[rows, :width].astype(F32),
            packed[rows, 2 * width :].astype(F32),
        )
        found = [old + fold(term) for old, term in zip(found, terms)]
    for row, partial in zip((GAIN1, SHIFT1, QBIAS, VBIAS), found):
        put(row, partial)
    store(4, dx_ref, dx_o).start()
    store(5, tables, tables_o).start()
    store(6, sums, sums_o).start()
    ends = {0: (dm, dm_o), 1: (dz, dz_o), 2: (dproj, dproj_o), 3: (packed, packed_o), 4: (dx_ref, dx_o), 5: (tables, tables_o), 6: (sums, sums_o)}
    for number, (source, there) in ends.items():
        store(number, source, there).wait()


def backward(layer, cotangent, packs, weights, saved, kept):
    length, width = cotangent.shape[1:]
    hidden = weights[2][0].shape[1]
    h1, qkv, probs, mixed, proj, x1, h2, xin, wide, scales, act, slope, mlp, y = saved
    heads = probs.shape[1]
    span = 2 * length - LANES
    summed = (16, width)
    table = (heads, 5 * LANES)
    stored = [
        ((length, width), BF16),
        ((length, hidden), BF16),
        ((length, width), BF16),
        ((length, 3 * width), BF16),
        ((length, width), BF16),
        (table, F32),
        (summed, F32),
    ]
    reads = [qkv, probs, wide, proj, x1, slope, mlp, xin, scales]
    scratch = [pltpu.VMEM(pair[0].shape, BF16) for pair in weights]
    scratch += [pltpu.VMEM((2, 2 * GROUP, length, length) if x is probs else x.shape[1:], x.dtype) for x in reads]
    scratch += [pltpu.VMEM(shape, kind) for shape, kind in stored[:5]]
    scratch += [
        pltpu.VMEM((length, width), F32),
        pltpu.VMEM((length, width), BF16),
        pltpu.VMEM((2 * GROUP, length, length), BF16),
        pltpu.VMEM((2 * GROUP, span, LANES), F32),
        pltpu.VMEM(summed, F32),
        pltpu.VMEM(table, F32),
        pltpu.VMEM((length, width), BF16),
        pltpu.VMEM(packs[0].shape, F32),
        pltpu.SemaphoreType.DMA((22,)),
        pltpu.SemaphoreType.DMA((7,)),
        pltpu.SemaphoreType.DMA((2,)),
    ]
    operands = [cotangent, *packs, *[x for pair in weights for x in pair], *reads]
    held = 7 if layer == 0 else 0
    return pl.pallas_call(
        functools.partial(backward_kernel, layer),
        out_shape=stacked(stored),
        in_specs=hbm_specs(1) + vmem_specs(2) + hbm_specs(8 + len(reads) + held),
        out_specs=hbm_specs(7),
        scratch_shapes=scratch,
        input_output_aliases={len(operands) + n: n for n in range(held)},
        compiler_params=pltpu.CompilerParams(vmem_limit_bytes=VMEM_BYTES),
        name="backward_layer",
    )(*operands, *(kept if layer == 0 else ()))


def small_lines(width):
    lines = width // LANES
    places = [(row, tile, row * lines + tile) for row in range(10) for tile in range(lines)]
    return places + [(B1, tile, B1 * lines + tile) for tile in range(4 * lines)]


def reverse_lanes(values):
    lane = lax.broadcasted_iota(jnp.int32, values.shape, 1)
    for place in range(LANES.bit_length() - 1):
        step = 1 << place
        up, down = pltpu.roll(values, step, 1), pltpu.roll(values, LANES - step, 1)
        values = jnp.where((lane // step) % 2 == 1, up, down)
    return values


def widen_kernel(sum_hbm, y_hbm, dx_hbm, small_ref, *refs):
    bigs, rows_out, vectors, table_ref = refs[:4], refs[4:6], refs[6 : 7 + VECTORS], refs[7 + VECTORS]
    narrow, wide, passing, load_sem, store_sem, pass_sem = refs[8 + VECTORS :]
    depth, width = narrow.shape[:2]
    blocks = [(0, slice(b * width, (b + 1) * width), slice(0, width)) for b in range(4)]
    for target, count in ((1, 4), (2, 3), (3, 1)):
        blocks += [(target, slice(0, width), slice(b * width, (b + 1) * width)) for b in range(count)]

    def load(block):
        rows = pl.ds(block * width, width)
        return pltpu.make_async_copy(sum_hbm.at[rows, :], narrow.at[block % depth], load_sem.at[block % depth])

    def store(block):
        target, rows, columns = blocks[block]
        there = bigs[target].at[rows, columns]
        return pltpu.make_async_copy(wide.at[block % depth], there, store_sem.at[block % depth])

    def fetch(number):
        return pltpu.make_async_copy((y_hbm, dx_hbm)[number], passing.at[number], pass_sem.at[0, number])

    def put(number):
        return pltpu.make_async_copy(passing.at[number], rows_out[number], pass_sem.at[1, number])

    for block in range(depth):
        load(block).start()
    for number in range(2):
        fetch(number).start()
    for block in range(len(blocks)):
        if block == depth:
            for number in range(2):
                fetch(number).wait()
                put(number).start()
        load(block).wait()
        if block >= depth:
            store(block - depth).wait()
        for rows in strips(0, width, 64):
            wide[block % depth, rows, :] = narrow[block % depth, rows, :].astype(F32)
        store(block).start()
        if block + depth < len(blocks):
            load(block + depth).start()
    places = small_lines(width)
    for row, tile, line in places:
        vectors[row][:, tile * LANES : (tile + 1) * LANES] = small_ref[line : line + 1, :]
    first = len(places)
    heads, _, entries = table_ref.shape
    tiles = -(-entries // LANES)
    flipped = reverse_lanes(small_ref[first : first + heads * tiles, :])
    for head in range(heads):
        for tile in range(tiles - 1):
            line = head * tiles + tile
            there = (tiles - 2 - tile) * LANES
            table_ref[head, :, there : there + LANES] = flipped[line : line + 1]
        line = first + head * tiles + tiles - 1
        table_ref[head, :, entries - 1 :] = small_ref[line : line + 1, 0:1]
    for block in range(len(blocks) - depth, len(blocks)):
        store(block).wait()
    for number in range(2):
        put(number).wait()


def widen(summed, small, y, dx, width, heads, entries):
    bigs = [(4 * width, width), (width, 4 * width), (width, 3 * width), (width, width)]
    shapes = [(1, width)] * 10 + [(1, 4 * width), (heads, 1, entries)]
    return pl.pallas_call(
        widen_kernel,
        out_shape=[jax.ShapeDtypeStruct(shape, F32) for shape in bigs]
        + [jax.ShapeDtypeStruct(y.shape, BF16)] * 2
        + [jax.ShapeDtypeStruct(shape, F32) for shape in shapes],
        in_specs=hbm_specs(3) + vmem_specs(1),
        out_specs=hbm_specs(6) + vmem_specs(VECTORS + 2),
        scratch_shapes=[
            pltpu.VMEM((3, width, width), BF16),
            pltpu.VMEM((3, width, width), F32),
            pltpu.VMEM((2, *y.shape), BF16),
            pltpu.SemaphoreType.DMA((3,)),
            pltpu.SemaphoreType.DMA((3,)),
            pltpu.SemaphoreType.DMA((2, 2)),
        ],
        compiler_params=pltpu.CompilerParams(vmem_limit_bytes=VMEM_BYTES),
        name="widen",
    )(summed, y, dx, small)


BLOCK = 256
LAG = 3


def reduce_kernel(bits, chunks, blocks, lags, window, lined, *refs):
    (a_ref, dm_ref, h2_ref, dz_ref, h1_ref, dp_ref, o_ref, dproj_ref, y_ref, dx_ref, sums_ref, tables_ref) = refs[:12]
    out_ref, small_out_ref, y_out, dx_out = refs[12:16]
    refs = refs[16:]
    (lhs, rhs, grads, total, crossing, landed, smalls, small_ref, small_landed, small_total) = refs[:10]
    small_received, received = refs[10 : 10 + bits], refs[10 + bits : -10]
    (load_sem, send_sem, recv_sem, small_send, small_recv, store_sem, cross_send, cross_recv, row_sem, credit) = refs[-10:]
    me = lax.axis_index("dp")
    section = lax.axis_index("section")
    beside = 1 - section
    rows = BLOCK * blocks
    width = grads.shape[1]
    per_side = width // BLOCK
    last = 2 * bits
    steps = 10 if lined else last
    starts = [0] + [lags[0] + lags[1] * place for place in range(steps + 1)]

    barrier = pltpu.get_barrier_semaphore()
    for place in range(bits):
        stride = 1 << place
        other = me + stride * (1 - 2 * ((me // stride) % 2))
        pl.semaphore_signal(barrier, inc=1, device_id={"dp": other}, device_id_type=MESH)
    pl.semaphore_signal(barrier, inc=1, device_id={"section": beside}, device_id_type=MESH)
    pl.semaphore_wait(barrier, bits + 1)

    def across(source, target, number):
        return pltpu.make_async_remote_copy(
            src_ref=source,
            dst_ref=target,
            send_sem=cross_send.at[number],
            recv_sem=cross_recv.at[number],
            device_id={"section": beside},
            device_id_type=MESH,
        )

    def row_copy(number):
        source, target = ((y_ref, y_out), (dx_ref, dx_out))[number]
        return pltpu.make_async_copy(source.at[section], target.at[section], row_sem.at[number])

    def row_across(number):
        source, target = ((y_ref, y_out), (dx_ref, dx_out))[number]
        return across(source.at[beside], target.at[section], window + 1 + number)

    families = (
        (a_ref, dm_ref, 4 * per_side, True),
        (h2_ref, dz_ref, 4 * per_side, False),
        (h1_ref, dp_ref, 3 * per_side, False),
        (o_ref, dproj_ref, per_side, False),
    )
    n_blocks = 12 * per_side

    def load(block):
        slot = block % 2
        first = 0
        for left, right, count, walks in families:
            @pl.when((block >= first) & (block < first + count))
            def _():
                local = block - first
                if walks:
                    left_column = local * BLOCK
                    right_column = 0
                else:
                    left_column = (local % per_side) * BLOCK
                    right_column = (local // per_side) * width
                for number, layer in enumerate((section, beside)):
                    pltpu.make_async_copy(
                        left.at[layer, :, pl.ds(pl.multiple_of(left_column, BLOCK), BLOCK)],
                        lhs.at[slot, number],
                        load_sem.at[0, slot],
                    ).start()
                    pltpu.make_async_copy(
                        right.at[layer, :, pl.ds(pl.multiple_of(right_column, BLOCK), width)],
                        rhs.at[slot, number],
                        load_sem.at[1, slot],
                    ).start()
            first += count

    def produce(block, sub, side):
        slot = block % 2
        pltpu.make_async_copy(lhs.at[slot], lhs.at[slot], load_sem.at[0, slot]).wait()
        pltpu.make_async_copy(rhs.at[slot], rhs.at[slot], load_sem.at[1, slot]).wait()

        @pl.when(block + 1 < n_blocks)
        def _():
            load(block + 1)

        crossing[side, sub * BLOCK : (sub + 1) * BLOCK, :] = dot(lhs[slot, 1], rhs[slot, 1], 0, 0).astype(BF16)
        grads[chunk(block, BLOCK), :] = dot(lhs[slot, 0], rhs[slot, 0], 0, 0).astype(BF16)

    def turn(chunk):
        place = chunk % 9
        return place % 2 + place // 5 - place // 6

    def partner(rotation, stage):
        stride = lax.shift_left(jnp.int32(1), (stage + rotation) % bits)
        mine = (me // stride) % 2
        return mine, me + stride * (1 - 2 * mine)

    def offset(base, height, rotation, stage):
        for earlier in range(stage):
            mine, _ = partner(rotation, earlier)
            base = base + mine * (height >> (earlier + 1))
        return base

    def piece(ref, start, size):
        return ref.at[pl.ds(pl.multiple_of(start, size), size)]

    def send(position, base, height, rotation, source, landing, result, slot, sems):
        send_at, recv_at = sems
        if position < bits:
            stage = position
            half = height >> (stage + 1)
            mine, other = partner(rotation, stage)
            start = offset(base, height, rotation, stage) + (1 - mine) * half
            src, dst = piece(source, start, half), landing[stage].at[slot]
        else:
            stage = last - 1 - position
            half = height >> (stage + 1)
            mine, other = partner(rotation, stage)
            start = offset(base, height, rotation, stage + 1)
            src = dst = piece(result, start, half)
        return pltpu.make_async_remote_copy(
            src_ref=src,
            dst_ref=dst,
            send_sem=send_at.at[position],
            recv_sem=recv_at.at[position, slot],
            device_id={"dp": other},
            device_id_type=MESH,
        )

    def take(position, base, height, rotation, source, landing, result, slot, sems):
        send(position - 1, base, height, rotation, source, landing, result, slot, sems).wait_recv()
        stage = position - 1
        if stage < bits:
            half = height >> (stage + 1)
            start = pl.multiple_of(offset(base, height, rotation, stage + 1), half)
            keep = pl.ds(start, half)
            value = source[keep, :].astype(jnp.float32) + landing[stage][slot].astype(jnp.float32)
            target = result if stage == bits - 1 else source
            target[keep, :] = value.astype(target.dtype)

    def step(position, *way):
        if position > 0:
            take(position, *way)
        if position < last:
            send(position, *way).start()

    main = (grads, received, total)
    main_sems = (send_sem, recv_sem)

    def cross(side):
        return across(crossing.at[side], landed.at[side], side)

    def give(part):
        side = part % window

        @pl.when(part >= window)
        def _():
            cross(side).wait_send()
            pl.semaphore_wait(credit, 1)

        for sub in range(blocks):
            block = part * blocks + sub

            @pl.when(block < n_blocks)
            def _():
                produce(block, sub, side)

        cross(side).start()

    def join(part):
        side = part % window
        cross(side).wait_recv()
        there = chunk(part, rows)
        grads[there, :] = (grads[there, :].astype(F32) + landed[side].astype(F32)).astype(BF16)

        @pl.when(part < chunks - window)
        def _():
            pl.semaphore_signal(credit, inc=1, device_id={"section": beside}, device_id_type=MESH)

    row_z = me // 4
    side_z = row_z // 2
    middle = (row_z + side_z) % 2
    inner, outer = me + 4 * (1 - 2 * side_z), me - 4 * (1 - 2 * side_z)

    def line_plan(early, part):
        place = part % 8
        first = 1 + (place // 2 if early else place % 2 * ((place + 5) // 8))
        second = 3 - first
        mine_first, mine_second = (me // first) % 2, (me // second) % 2
        peer_first = me + first * (1 - 2 * mine_first)
        peer_second = me + second * (1 - 2 * mine_second)
        base = part * rows
        before = 1 + (place + 5) // 8
        if early:
            slot = 2 * (part // 8) + place // 2
            landing = received[4:]
            quarter = rows // 4
            line = base
            whole = base + row_z * quarter
            size_first = quarter // 2
        else:
            slot = part - 2 * (part // 8) - before
            landing = received[:4]
            whole = base
            size_first = rows // 2
        size_second = size_first // 2
        keep_first = whole + mine_first * size_first
        keep_second = keep_first + mine_second * size_second
        if not early:
            line = keep_second
            quarter = size_second // 4
        everyone = None
        line_land, cross_land, first_land, second_land = [ref.at[slot] for ref in landing]
        mostly = line + quarter * (1 - side_z)
        ending = line + 3 * quarter * side_z
        near, far = line + 2 * quarter * side_z, line + 2 * quarter * (1 - side_z)
        swap_first = (everyone, everyone, peer_first, whole + (1 - mine_first) * size_first, size_first, keep_first, first_land)
        swap_second = (
            everyone, everyone, peer_second, keep_first + (1 - mine_second) * size_second, size_second, keep_second, second_land
        )
        inward = (0, 1, inner, mostly, 3 * quarter, mostly, line_land)
        between = (1, 1, inner, far, 2 * quarter, near, cross_land)
        outward = (1, 0, outer, ending, quarter, ending, line_land.at[pl.ds(0, quarter)])
        back_inward = (0, 1, inner, ending, quarter, None, None)
        back_between = (1, 1, inner, near, 2 * quarter, None, None)
        back_outward = (1, 0, outer, mostly, 3 * quarter, None, None)
        back_first = (everyone, everyone, peer_first, keep_first, size_first, None, None)
        back_second = (everyone, everyone, peer_second, keep_second, size_second, None, None)
        if early:
            return [inward, between, outward, swap_first, swap_second,
                    back_second, back_first, back_inward, back_between, back_outward]
        return [swap_first, swap_second, inward, between, outward,
                back_inward, back_between, back_outward, back_second, back_first]

    def only(role, act):
        if role is None:
            act()
        else:
            pl.when(middle == role)(act)

    def line_step(position, part):
        def run(early):
            plan = line_plan(early, part)

            def copy(number):
                sender, receiver, peer, start, size, arrives, lands = plan[number]
                source = grads if arrives is not None else total
                here = pl.ds(pl.multiple_of(start, 16), size)
                return pltpu.make_async_remote_copy(
                    src_ref=source.at[here],
                    dst_ref=total.at[here] if arrives is None else lands,
                    send_sem=send_sem.at[number],
                    recv_sem=recv_sem.at[number, part],
                    device_id={"dp": peer},
                    device_id_type=MESH,
                )

            def arrive():
                size, arrives, lands = plan[position - 1][4:]
                copy(position - 1).wait_recv()
                if arrives is not None:
                    there = pl.ds(pl.multiple_of(arrives, 16), size)
                    value = (grads[there, :].astype(F32) + lands[...].astype(F32)).astype(BF16)
                    if position == 5:
                        total[there, :] = value
                    else:
                        grads[there, :] = value

            if position > 0:
                only(plan[position - 1][1], arrive)
            if position == 5 and not early:

                def keep():
                    size = rows // 16
                    there = pl.ds(pl.multiple_of(plan[1][5] + row_z * size, 16), size)
                    total[there, :] = grads[there, :]

                only(1, keep)
            if position < 10:
                only(plan[position][0], lambda: copy(position).start())

        early = (part % 8 == 0) | (part % 8 == 2)

        @pl.when(early)
        def _():
            run(True)

        @pl.when(jnp.logical_not(early))
        def _():
            run(False)

    def line_rows(role):
        ends = ([128, 64, 48, 0, 0, 16, 0, 0, 64, 128], [192, 0, 0, 32, 16, 16, 32, 64, 0, 0])
        middles = ([128, 64, 0, 32, 16, 0, 32, 48, 64, 128], [0, 128, 64, 32, 16, 16, 32, 0, 128, 192])
        late, soon = middles if role else ends
        count = sum(part % 8 in (0, 2) for part in range(chunks))
        return [(chunks - count) * a + count * b for a, b in zip(late, soon)]

    def walk(position, part):
        if position == 0:
            join(part)
        base = part * rows
        if lined:
            line_step(position, part)
        else:
            step(position, base, rows, turn(part), *main, part, main_sems)
        if position == steps:
            there = pl.ds(pl.multiple_of(base, rows), rows)
            pltpu.make_async_copy(total.at[there], out_ref.at[there], store_sem.at[0]).start()

    def small_cross():
        return across(smalls.at[beside], small_landed, window)

    def walk_small(position):
        height = small_ref.shape[0]
        if position == 0:
            small_cross().wait_recv()
            small_ref[...] = smalls[section] + small_landed[...]
        way = (0, height, 0, small_ref, small_received, small_total, 0, (small_send, small_recv))
        step(position, *way)

    load(jnp.int32(0))
    def assemble():
        smalls[...] = jnp.zeros_like(smalls)
        places = small_lines(width)
        for layer in range(2):
            for row, tile, line in places:
                if row == B1:
                    row, tile = B1 + tile // (width // LANES), tile % (width // LANES)
                smalls[layer, line : line + 1, :] = sums_ref[layer, row : row + 1, tile * LANES : (tile + 1) * LANES]
            line = len(places)
            for head in range(tables_ref.shape[1]):
                for tile in range(tables_ref.shape[2] // LANES):
                    lanes = slice(tile * LANES, (tile + 1) * LANES)
                    smalls[layer, line : line + 1, :] = tables_ref[layer, head : head + 1, lanes]
                    line += 1
        small_cross().start()
        for number in range(2):
            row_copy(number).start()
            row_across(number).start()

    @pl.loop(0, chunks + starts[-1])
    def _(tick):
        @pl.when(tick < chunks)
        def _():
            give(tick)

        pl.when(tick == 0)(assemble)

        for position in range(steps + 1):
            part = tick - starts[position + 1]

            @pl.when((part >= 0) & (part < chunks))
            def _():
                walk(position, part)

            if position <= last:

                @pl.when(part == 0)
                def _():
                    walk_small(position)

    small_out_ref[...] = small_total[...]
    for position in range(last):
        stage = position if position < bits else last - 1 - position
        size = small_received[stage]
        pltpu.make_async_copy(size, size, small_send.at[position]).wait()
        if not lined:
            size = received[stage]
            pltpu.make_async_copy(size, size, send_sem.at[position]).wait()
    if lined:
        for role in range(2):

            @pl.when(middle == role)
            def _():
                for number, amount in enumerate(line_rows(role)):
                    if amount > 0:
                        size = grads.at[pl.ds(0, amount)]
                        pltpu.make_async_copy(size, size, send_sem.at[number]).wait()
    for side in range(window):
        cross(side).wait_send()
    small_cross().wait_send()
    for number in range(2):
        row_copy(number).wait()
        row_across(number).wait()
    pltpu.make_async_copy(total, out_ref, store_sem.at[0]).wait()


def reduce_gradients(a, dm, h2, dz, h1, packed, o, dproj, y, dx, sums, tables):
    parts = lax.axis_size("dp")
    bits = parts.bit_length() - 1
    blocks = max(1, 16 * parts // BLOCK)
    layers, length, width = h1.shape
    n_blocks = 12 * width // BLOCK
    chunks = -(-n_blocks // blocks)
    rows = BLOCK * blocks
    lags, window = ((1, LAG), 4) if blocks == 1 else ((0, LAG), 1)
    lines = len(small_lines(width)) + tables.shape[1] * tables.shape[2] // LANES
    height = -(-lines // (8 * parts)) * 8 * parts
    small = (height, LANES)
    lined = parts == 16
    if lined:
        early = sum(part % 8 in (0, 2) for part in range(chunks))
        lands = [(chunks - early, size) for size in (48, 32, 128, 64)] + [(early, size) for size in (192, 128, 32, 16)]
    else:
        lands = [(chunks, rows >> (s + 1)) for s in range(bits)]
    steps = 10 if lined else 2 * bits
    return pl.pallas_call(
        functools.partial(reduce_kernel, bits, chunks, blocks, lags, window, lined),
        out_shape=(
            jax.ShapeDtypeStruct((chunks * rows, width), BF16),
            jax.ShapeDtypeStruct(small, F32),
            jax.ShapeDtypeStruct(y.shape, BF16),
            jax.ShapeDtypeStruct(dx.shape, BF16),
        ),
        in_specs=hbm_specs(10) + vmem_specs(2),
        out_specs=hbm_specs(1) + vmem_specs(1) + hbm_specs(2),
        scratch_shapes=[
            pltpu.VMEM((2, layers, length, BLOCK), BF16),
            pltpu.VMEM((2, layers, length, width), BF16),
            pltpu.VMEM((chunks * rows, width), BF16),
            pltpu.VMEM((chunks * rows, width), BF16),
            pltpu.VMEM((window, rows, width), BF16),
            pltpu.VMEM((window, rows, width), BF16),
            pltpu.VMEM((layers, *small), F32),
            pltpu.VMEM(small, F32),
            pltpu.VMEM(small, F32),
            pltpu.VMEM(small, F32),
            *[pltpu.VMEM((1, height >> (s + 1), LANES), F32) for s in range(bits)],
            *[pltpu.VMEM((*size, width), BF16) for size in lands],
            pltpu.SemaphoreType.DMA((2, 2)),
            pltpu.SemaphoreType.DMA((steps,)),
            pltpu.SemaphoreType.DMA((steps, chunks)),
            pltpu.SemaphoreType.DMA((2 * bits,)),
            pltpu.SemaphoreType.DMA((2 * bits, 1)),
            pltpu.SemaphoreType.DMA((1,)),
            pltpu.SemaphoreType.DMA((window + 3,)),
            pltpu.SemaphoreType.DMA((window + 3,)),
            pltpu.SemaphoreType.DMA((2,)),
            pltpu.SemaphoreType.REGULAR,
        ],
        compiler_params=pltpu.CompilerParams(
            collective_id=0, has_side_effects=True, vmem_limit_bytes=VMEM_BYTES
        ),
        name="reduce_gradients",
    )(a, dm, h2, dz, h1, packed, o, dproj, y, dx, sums, tables)


def swapped(block):
    return lax.ppermute(block, "section", [(0, 1), (1, 0)])


def per_device(
    patches,
    segment_ids,
    pad_counts,
    norm1_gain,
    norm1_bias,
    qkv_weight,
    query_bias,
    value_bias,
    rel_table,
    proj_weight,
    proj_bias,
    scale_attn,
    norm2_gain,
    norm2_bias,
    fc1_weight,
    fc1_bias,
    fc2_weight,
    fc2_bias,
    scale_mlp,
    cotangent,
):
    micro, length, width = patches.shape
    heads, entries = rel_table.shape[1:]
    vectors = (
        norm1_gain,
        norm1_bias,
        query_bias,
        value_bias,
        proj_bias,
        scale_attn,
        norm2_gain,
        norm2_bias,
        fc2_bias,
        scale_mlp,
        fc1_bias,
    )
    own = pack(vectors, rel_table.transpose(1, 0, 2))
    own_band = bias_band(own, heads, length)
    other = swapped(own)
    weights = [(x, swapped(x)) for x in (qkv_weight[0], proj_weight[0])]
    own_band, other, *late = lax.optimization_barrier(
        (own_band, other, weights[0][1], weights[1][1], fc1_weight[0], fc2_weight[0])
    )
    weights = [(weights[0][0], late[0]), (weights[1][0], late[1])] + [(x, swapped(x)) for x in late[2:]]
    other_band = bias_band(other, heads, length)
    packs, band = (own, other), (own_band, other_band)
    saved = None
    rows = patches
    for layer, phase in ((0, ATTENTION), (0, MLP), (1, BOTH)):
        saved = forward(layer, phase, pad_counts, rows, segment_ids, packs, band, weights, saved)
    kept = None
    for layer in (1, 0):
        kept = backward(layer, cotangent, packs, weights, saved, kept)
    dm, dz, dproj, packed, dx, tables, sums = kept
    h1, mixed, h2, act, y = saved[0], saved[3], saved[6], saved[10], saved[13]
    summed, small, y, dx = reduce_gradients(
        act, dm, h2, dz, h1, packed, mixed, dproj, y, dx, sums, tables
    )
    fc2_grad, fc1_grad, qkv_grad, proj_grad, outputs, in_grads, *small_grads = widen(
        summed, small, y, dx, width, heads, entries
    )
    table_grad = small_grads[VECTORS + 1].transpose(1, 0, 2)
    return (
        outputs[None],
        in_grads[None],
        small_grads[GAIN1],
        small_grads[SHIFT1],
        qkv_grad[None],
        small_grads[QBIAS],
        small_grads[VBIAS],
        table_grad,
        proj_grad[None],
        small_grads[PBIAS],
        small_grads[SCALE_A],
        small_grads[GAIN2],
        small_grads[SHIFT2],
        fc1_grad[None],
        small_grads[B1],
        fc2_grad[None],
        small_grads[B2],
        small_grads[SCALE_M],
    )


def solution(mesh):
    placed = (
        P("dp", None, None),
        P("dp", None),
        P("dp"),
        P("section", None),
        P("section", None),
        P("section", None, None),
        P("section", None),
        P("section", None),
        P("section", None, None),
        P("section", None, None),
        P("section", None),
        P("section", None),
        P("section", None),
        P("section", None),
        P("section", None, None),
        P("section", None),
        P("section", None, None),
        P("section", None),
        P("section", None),
        P("dp", None, None),
    )
    return jax.shard_map(
        per_device,
        mesh=mesh,
        in_specs=placed,
        out_specs=(
            P("section", "dp", None, None),
            P("section", "dp", None, None),
            P("section", None),
            P("section", None),
            P("section", None, None),
            P("section", None),
            P("section", None),
            P("section", None, None),
            P("section", None, None),
            P("section", None),
            P("section", None),
            P("section", None),
            P("section", None),
            P("section", None, None),
            P("section", None),
            P("section", None, None),
            P("section", None),
            P("section", None),
        ),
        check_vma=False,
    )
```

```python
import functools
import math

import jax
import jax.numpy as jnp
from jax import lax
from jax.experimental import pallas as pl
from jax.experimental.pallas import tpu as pltpu
from jax.sharding import PartitionSpec as P

MESH = pl.DeviceIdType.MESH
BF16, F32 = jnp.bfloat16, jnp.float32
VMEM_BYTES = 60 * 1024 * 1024
LANES = 128
HALF = 64
REACH = 2 * LANES
GAIN1, SHIFT1, QBIAS, VBIAS, PBIAS, SCALE_A, GAIN2, SHIFT2, B2, SCALE_M, B1 = range(11)
VECTORS = 10
STORED = 14
BOTH, ATTENTION, MLP = range(3)
STRIP = 16
GROUP = 3


def dot(left, right, left_dim, right_dim):
    return lax.dot_general(
        left, right, (((left_dim,), (right_dim,)), ((), ())), preferred_element_type=F32
    )


def nn(left, right):
    return dot(left, right, 1, 0)


def nt(left, right):
    return dot(left, right, 1, 1)


def normalize(values):
    centered = values - jnp.mean(values, -1, keepdims=True)
    inverse = lax.rsqrt(jnp.mean(centered * centered, -1, keepdims=True) + 1e-06)
    return centered * inverse, inverse


def norm_back(upper, scaled, inverse):
    return inverse * (
        upper
        - jnp.mean(upper, -1, keepdims=True)
        - scaled * jnp.mean(upper * scaled, -1, keepdims=True)
    )


def fold(values):
    return jnp.sum(values.reshape(values.shape[0] // 8, 8, values.shape[1]), 0)


def half_mask(shape, which):
    return lax.broadcasted_iota(jnp.int32, shape, 1) // HALF == which


def strips(first, last, size):
    return [slice(start, start + size) for start in range(first, last, size)]


def chunk(index, size):
    return pl.ds(pl.multiple_of(index * size, size), size)


def skew_bias(reversed_row, target):
    span, lanes = target.shape
    rows = pltpu.roll(jnp.broadcast_to(reversed_row, (8, reversed_row.shape[1])), 1, 1, stride=1, stride_axis=0)
    tiles = span // lanes
    for fine in range(lanes // 8):
        moved = rows if fine == 0 else pltpu.roll(rows, 8 * fine, 1)
        for coarse in range(tiles):
            place = 8 * (fine + lanes // 8 * coarse)
            target[place : place + 8, :] = moved[:, lanes * (tiles - coarse) : lanes * (tiles - coarse + 1)]


def gather_diagonals(source):
    span, lanes = source.shape
    tiles = span // lanes
    width = span + lanes
    blank = jnp.zeros((8, lanes), F32)
    found = None
    for fine in range(lanes // 8):
        places = [8 * (fine + lanes // 8 * coarse) for coarse in reversed(range(tiles))]
        line = jnp.concatenate([blank] + [source[place : place + 8, :] for place in places], 1)
        if fine > 0:
            line = pltpu.roll(line, width - 8 * fine, 1)
        found = line if found is None else found + line
    row = lax.broadcasted_iota(jnp.int32, found.shape, 0)
    for place in range(3):
        moved = pltpu.roll(found, width - (1 << place), 1)
        found = jnp.where((row // (1 << place)) % 2 == 1, moved, found)
    return jnp.sum(found, 0, keepdims=True)


def key_rows(query_block, blocks):
    reach = REACH // LANES
    return max(0, query_block - reach) * LANES, min(blocks, query_block + reach + 1) * LANES


def pick(mine, own, other, act):
    @pl.when(mine)
    def _():
        act(own)

    @pl.when(jnp.logical_not(mine))
    def _():
        act(other)


def pack_kernel(*refs):
    *vectors, bias_ref, table_ref, pack_ref = refs
    width = pack_ref.shape[1]
    heads, _, entries = table_ref.shape
    pack_ref[...] = jnp.zeros_like(pack_ref)
    for row, vector in enumerate(vectors):
        pack_ref[row : row + 1, :] = vector[...]
    for part in range(bias_ref.shape[1] // width):
        pack_ref[B1 + part : B1 + part + 1, :] = bias_ref[:, part * width : (part + 1) * width]
    first = pack_ref.shape[0] - heads
    tiles = entries // LANES
    lane = lax.broadcasted_iota(jnp.int32, (heads, LANES), 1)
    ending = jnp.broadcast_to(table_ref[:, 0, entries - 1 :], (heads, LANES))
    pack_ref[first:, :LANES] = jnp.where(lane == LANES - 1, ending, 0.0)
    for tile in range(tiles):
        there = (tiles - tile) * LANES
        pack_ref[first:, there : there + LANES] = reverse_lanes(table_ref[:, 0, tile * LANES : (tile + 1) * LANES])


def pack(vectors, rel_table):
    heads = rel_table.shape[0]
    return pl.pallas_call(
        pack_kernel,
        out_shape=jax.ShapeDtypeStruct((16 + heads, vectors[0].shape[1]), F32),
        in_specs=vmem_specs(len(vectors) + 1),
        out_specs=pl.BlockSpec(memory_space=pltpu.VMEM),
        name="pack_vectors",
    )(*vectors, rel_table)


def fill(target, source):
    target[...] = source[...]


def band_kernel(pack_ref, band_hbm, band, store_sem):
    heads = band.shape[0]
    tables = pack_ref.shape[0] - heads
    edge = jnp.zeros((1, LANES), F32)

    @pl.loop(0, heads // 4)
    def _(group):
        for within in range(4):
            head = 4 * group + within
            kept = pack_ref[pl.ds(tables + head, 1), :]
            skew_bias(jnp.concatenate([edge, kept, edge], 1), band.at[head])
        some = pl.ds(4 * group, 4)
        pltpu.make_async_copy(band.at[some], band_hbm.at[some], store_sem.at[group]).start()

    for group in range(heads // 4):
        some = pl.ds(4 * group, 4)
        pltpu.make_async_copy(band.at[some], band_hbm.at[some], store_sem.at[group]).wait()


def bias_band(packed, heads, length):
    shape = (heads, 2 * length - LANES, LANES)
    return pl.pallas_call(
        band_kernel,
        out_shape=jax.ShapeDtypeStruct(shape, F32),
        in_specs=vmem_specs(1),
        out_specs=pl.BlockSpec(memory_space=pl.ANY),
        scratch_shapes=[pltpu.VMEM(shape, F32), pltpu.SemaphoreType.DMA((heads // 4,))],
        compiler_params=pltpu.CompilerParams(vmem_limit_bytes=VMEM_BYTES + 2 * 1024 * 1024),
        name="bias_band",
    )(packed)


def forward_kernel(layer, phase, pads, x_hbm, seg_ref, own_pack, other_pack, own_band, other_band, *refs):
    if phase != MLP:
        (wqkv_own, wqkv_other, wp_own, wp_other), refs = refs[:4], refs[4:]
    if phase != ATTENTION:
        (w1_own, w1_other, w2_own, w2_other), refs = refs[:4], refs[4:]
    refs = refs[STORED if layer > 0 or phase == MLP else 0 :]
    stores = refs[:STORED]
    (bias, wqkv, wp, w1, w2, mask, h1, qkv, probs, mixed, proj, x1, h2, xin, wide_mixed, scales, act, slope, mlp, out_row, held, pack_ref, load_sem, store_sem, prob_sem) = refs[STORED:]
    h1_o, qkv_o, prob_o, mixed_o, proj_o, x1_o, h2_o, xin_o, wide_o, scales_o, act_o, slope_o, mlp_o, y_o = stores
    hidden = w1.shape[1]
    length, width = xin.shape
    heads = bias.shape[0]
    blocks = length // LANES
    section = lax.axis_index("section")
    mine = section == layer
    factor = HALF ** (-0.5)
    thirds = [pl.ds(part * width, width) for part in range(3)]

    def load(number):
        if number < 3:
            part = thirds[number]
            return wqkv_own.at[:, part], wqkv_other.at[:, part], wqkv.at[:, part], load_sem.at[number]
        if number == 3:
            return wp_own, wp_other, wp, load_sem.at[3]
        part = pl.ds((number % 4) * width, width)
        if number < 8:
            return w1_own.at[:, part], w1_other.at[:, part], w1.at[:, part], load_sem.at[number]
        return w2_own.at[part, :], w2_other.at[part, :], w2.at[part, :], load_sem.at[number]

    def start(number):
        own, other, target, sem = load(number)
        pick(mine, own, other, lambda source: pltpu.make_async_copy(source, target, sem).start())

    def wait(number):
        own, other, target, sem = load(number)
        pltpu.make_async_copy(target, target, sem).wait()

    def store(number, source, there):
        return pltpu.make_async_copy(source, there.at[layer], store_sem.at[number])

    def part_store(number, source, there, columns):
        return pltpu.make_async_copy(source.at[:, columns], there.at[layer, :, columns], store_sem.at[number])

    def vector(row):
        return pack_ref[row : row + 1, :]

    def attention():
        source = x_hbm.at[section] if layer == 0 else y_o.at[0]
        pltpu.make_async_copy(source, xin, load_sem.at[12]).start()
        start(0)
        pltpu.make_async_copy(xin, xin, load_sem.at[12]).wait()
        start(1)
        start(2)
        pick(mine, own_band, other_band, lambda source: pltpu.make_async_copy(source, bias, load_sem.at[13]).start())
        segment = seg_ref[pl.ds(section, 1), :].astype(F32)
        key_segment = jnp.broadcast_to(segment, (LANES, length)).T

        for rows in strips(0, length, STRIP):
            scaled, _ = normalize(xin[rows, :].astype(F32))
            h1[rows, :] = (scaled * vector(GAIN1) + vector(SHIFT1)).astype(BF16)
        for part in range(3):
            wait(part)

        alive = length - pads[section]
        for place in range(blocks):
            lanes = slice(place * LANES, (place + 1) * LANES)
            for rows in strips(0, length, 64):
                key = lax.broadcasted_iota(jnp.int32, (64, LANES), 0) + rows.start
                query = lax.broadcasted_iota(jnp.int32, (64, LANES), 1) + place * LANES
                allowed = ((key_segment[rows] == segment[:, lanes]) & (key < alive)) | (key == query)
                mask[rows, lanes] = jnp.where(allowed, 0.0, -1000000000.0)

        store(0, h1, h1_o).start()
        store(7, xin, xin_o).start()
        projections = [(part, pl.ds(high * (length // 2), length // 2)) for part in range(3) for high in range(2)]

        def project(number):
            part, rows = projections[number]
            return nn(h1[rows, :], wqkv[:, thirds[part]])

        coming = project(0)
        for number, (part, rows) in enumerate(projections):
            current = coming
            if number + 1 < len(projections):
                coming = project(number + 1)
            for strip in strips(0, length // 2, STRIP):
                piece = current[strip]
                if part == 0:
                    piece = (piece + vector(QBIAS)) * factor
                if part == 2:
                    piece = piece + vector(VBIAS)
                qkv[pl.ds(rows.start + strip.start, STRIP), thirds[part]] = piece.astype(BF16)
        store(1, qkv, qkv_o).start()
        pltpu.make_async_copy(bias, bias, load_sem.at[13]).wait()
        for number in range(3, 4 if phase == ATTENTION else 12):
            start(number)
        together = 2 * GROUP

        def prob_store(group):
            return pltpu.make_async_copy(
                probs.at[group % 2], prob_o.at[layer, pl.ds(together * group, together)], prob_sem.at[group % 2]
            )

        def attend(side, within, pair):
            columns = chunk(pair, LANES)
            queries = qkv[:, columns]
            keys = qkv[:, pl.ds(pl.multiple_of(width + pair * LANES, LANES), LANES)]
            values = qkv[:, pl.ds(pl.multiple_of(2 * width + pair * LANES, LANES), LANES)].T
            outs = []
            for which in range(2):
                own_keys = jnp.where(half_mask(keys.shape, which), keys, jnp.zeros_like(keys))
                lines = []
                for wide in range(blocks // 2):
                    scores = nt(own_keys, queries[2 * LANES * wide : 2 * LANES * (wide + 1)])
                    for part in range(2):
                        place = 2 * wide + part
                        low, high = key_rows(place, blocks)
                        lanes = slice(place * LANES, (place + 1) * LANES)
                        first = (blocks - 1 - place) * LANES
                        spare = (2 * within + which) * blocks + place
                        highest = None
                        for rows in strips(low, high, 64):
                            here = (
                                scores[rows, part * LANES : (part + 1) * LANES]
                                + bias[2 * pair + which, first + rows.start : first + rows.stop, :]
                                + mask[rows, lanes]
                            )
                            held[spare, rows, :] = here
                            top = jnp.max(here.reshape(8, 8, LANES), 0)
                            highest = top if highest is None else jnp.maximum(highest, top)
                        highest = jnp.max(highest, 0, keepdims=True)
                        sums = jnp.zeros((8, LANES), F32)
                        for rows in strips(low, high, 64):
                            expo = jnp.exp(held[spare, rows, :] - highest)
                            probs[side, 2 * within + which, rows, lanes] = expo.astype(BF16)
                            sums = sums + fold(expo)
                        lines.append(1.0 / jnp.sum(sums, 0, keepdims=True))
                        if low > 0:
                            probs[side, 2 * within + which, :low, lanes] = jnp.zeros((low, LANES), BF16)
                        if high < length:
                            probs[side, 2 * within + which, high:, lanes] = jnp.zeros((length - high, LANES), BF16)
                scale = jnp.concatenate(lines, 1)
                scales[pl.ds(2 * pair + which, 1), :] = scale
                outs.append(nn(values[which * HALF : (which + 1) * HALF], probs[side, 2 * within + which]) * scale)
            out = jnp.concatenate(outs, 0).T
            wide_mixed[:, columns] = out
            mixed[:, columns] = out.astype(BF16)

        @pl.loop(0, heads // together)
        def _(group):
            @pl.when(group >= 2)
            def _():
                prob_store(group - 2).wait()

            for within in range(GROUP):
                attend(group % 2, within, GROUP * group + within)
            prob_store(group).start()

        store(3, mixed, mixed_o).start()
        store(8, wide_mixed, wide_o).start()
        store(9, scales, scales_o).start()
        wait(3)

        results = [nn(mixed[half, :], wp[...]) for half in strips(0, length, length // 2)]
        for rows in strips(0, length, STRIP):
            there = rows.start % (length // 2)
            out = results[rows.start // (length // 2)][there : there + STRIP] + vector(PBIAS)
            proj[rows, :] = out.astype(BF16)
            resid = xin[rows, :].astype(F32) + vector(SCALE_A) * out
            x1[rows, :] = resid
            scaled, _ = normalize(resid)
            h2[rows, :] = (scaled * vector(GAIN2) + vector(SHIFT2)).astype(BF16)

        store(4, proj, proj_o).start()
        store(5, x1, x1_o).start()
        store(6, h2, h2_o).start()

        def finish():
            for group in range(max(0, heads // together - 2), heads // together):
                prob_store(group).wait()

        return finish

    def mlp_part():
        cuts = 4
        height = length // cuts
        pieces = [
            (pl.ds(high * height, height), pl.ds(part * width, width))
            for part in range(hidden // width)
            for high in range(cuts)
        ]

        def expand(number):
            rows, columns = pieces[number]
            if phase == MLP and number % cuts == 0:
                wait(4 + number // cuts)
            return nn(h2[rows, :], w1[:, columns])

        if phase != MLP:
            for number in range(4, 12):
                wait(number)
        coming = expand(0)
        totals = [None] * cuts
        for number, (rows, columns) in enumerate(pieces):
            current = coming
            if number + 1 < len(pieces):
                coming = expand(number + 1)
            for strip in strips(0, height, STRIP):
                there = pl.ds(rows.start + strip.start, STRIP)
                here = current[strip] + vector(B1 + number // cuts)
                normal = 0.5 * lax.erf(here * math.sqrt(0.5)) + 0.5
                density = jnp.exp(-0.5 * here * here) * (1.0 / math.sqrt(2.0 * math.pi))
                act[there, columns] = (here * normal).astype(BF16)
                slope[there, columns] = (normal + here * density).astype(BF16)
            if phase == MLP and number % cuts == 0:
                wait(8 + number // cuts)
            more = nn(act[rows, columns], w2[columns, :])
            totals[number % cuts] = more if number < cuts else totals[number % cuts] + more
            if number in (len(pieces) // 2 - 1, len(pieces) - 1):
                columns = pl.ds((number // (2 * cuts)) * 2 * width, 2 * width)
                part_store(10, act, act_o, columns).start()
                part_store(11, slope, slope_o, columns).start()

        if phase == MLP:
            pltpu.make_async_copy(x1, x1, load_sem.at[13]).wait()
        for half in range(cuts):
            for strip in strips(0, height, STRIP):
                rows = pl.ds(half * height + strip.start, STRIP)
                out = totals[half][strip] + vector(B2)
                mlp[rows, :] = out.astype(BF16)
                out_row[rows, :] = (x1[rows, :] + vector(SCALE_M) * out).astype(BF16)

        store(12, mlp, mlp_o).start()
        store(13, out_row, y_o).start()
    pick(mine, own_pack, other_pack, functools.partial(fill, pack_ref))
    if phase == MLP:
        pltpu.make_async_copy(h2_o.at[layer], h2, load_sem.at[12]).start()
        start(4)
        pltpu.make_async_copy(h2, h2, load_sem.at[12]).wait()
        for number in (8, 5, 9, 6, 10, 7, 11):
            start(number)
        pltpu.make_async_copy(x1_o.at[layer], x1, load_sem.at[13]).start()
        mlp_part()
    else:
        finish = attention()
        if phase == BOTH:
            mlp_part()
        finish()
    ends = {0: (h1, h1_o), 1: (qkv, qkv_o), 3: (mixed, mixed_o), 4: (proj, proj_o), 5: (x1, x1_o), 6: (h2, h2_o),
            7: (xin, xin_o), 8: (wide_mixed, wide_o), 9: (scales, scales_o),
            10: (act, act_o), 11: (slope, slope_o), 12: (mlp, mlp_o), 13: (out_row, y_o)}
    for number, (source, there) in ends.items():
        if phase == BOTH or (phase == MLP) == (number >= 10):
            store(number, source, there).wait()


def hbm_specs(count):
    return [pl.BlockSpec(memory_space=pl.ANY)] * count


def vmem_specs(count):
    return [pl.BlockSpec(memory_space=pltpu.VMEM)] * count


def stacked(stored):
    return [jax.ShapeDtypeStruct((2, *shape), kind) for shape, kind in stored]


def forward(layer, phase, pads, rows, segments, packs, band, weights, kept):
    length, width = rows.shape[1:]
    heads = band[0].shape[0]
    hidden = weights[2][0].shape[1]
    used = {BOTH: weights, ATTENTION: weights[:2], MLP: weights[2:]}[phase]
    stored = [
        ((length, width), BF16),
        ((length, 3 * width), BF16),
        ((heads, length, length), BF16),
        ((length, width), BF16),
        ((length, width), BF16),
        ((length, width), F32),
        ((length, width), BF16),
        ((length, width), BF16),
        ((length, width), F32),
        ((heads, length), F32),
        ((length, hidden), BF16),
        ((length, hidden), BF16),
        ((length, width), BF16),
        ((length, width), BF16),
    ]
    scratch = [pltpu.VMEM(band[0].shape, F32)] + [pltpu.VMEM(pair[0].shape, BF16) for pair in weights]
    scratch.append(pltpu.VMEM((length, length), F32))
    scratch += [
        pltpu.VMEM((2, 2 * GROUP, length, length) if n == 2 else shape, kind)
        for n, (shape, kind) in enumerate(stored)
    ]
    scratch += [
        pltpu.VMEM((2 * GROUP * length // LANES, length, LANES), F32),
        pltpu.VMEM(packs[0].shape, F32),
        pltpu.SemaphoreType.DMA((14,)),
        pltpu.SemaphoreType.DMA((STORED,)),
        pltpu.SemaphoreType.DMA((2,)),
    ]
    operands = [pads, rows, segments, *packs, *band, *[x for pair in used for x in pair]]
    held = STORED if layer > 0 or phase == MLP else 0
    return pl.pallas_call(
        functools.partial(forward_kernel, layer, phase),
        out_shape=stacked(stored),
        in_specs=[pl.BlockSpec(memory_space=pltpu.SMEM)] + hbm_specs(1) + vmem_specs(3) + hbm_specs(2 + 2 * len(used) + held),
        out_specs=hbm_specs(STORED),
        scratch_shapes=scratch,
        input_output_aliases={len(operands) + n: n for n in range(held)},
        compiler_params=pltpu.CompilerParams(vmem_limit_bytes=VMEM_BYTES),
        name="forward_layer",
    )(*operands, *(kept if held else ()))


def backward_kernel(layer, cotangent_hbm, own_pack, other_pack, *refs):
    weights, refs = refs[:8], refs[8:]
    (qkv_i, prob_i, mixed_i, proj_i, x1_i, slope_i, mlp_i, xin_i, scales_i) = refs[:9]
    refs = refs[9 + (7 if layer == 0 else 0) :]
    stores = refs[:7]
    (wqkv, wp, w1, w2, qkv, probs, mixed, proj, x1, slope, mlp, xin, scales, dm, dz, dproj, packed, dx_ref, dx1, dmixed, dscore, diag, sums, tables, g_ref, pack_ref, load_sem, store_sem, prob_sem) = refs[7:]
    dm_o, dz_o, dproj_o, packed_o, dx_o, tables_o, sums_o = stores
    wqkv_hbm, wp_hbm, w1_hbm, w2_hbm = zip(weights[::2], weights[1::2])
    length, width = g_ref.shape
    hidden = w1.shape[1]
    blocks = length // LANES
    pairs = width // LANES
    section = lax.axis_index("section")
    mine = section == layer
    factor = HALF ** (-0.5)
    parts = [pl.ds(part * width, width) for part in range(hidden // width)]
    loads = [(mlp_i.at[layer], mlp)]
    loads += [(tuple(x.at[part, :] for x in w2_hbm), w2.at[part, :]) for part in parts]
    loads += [(slope_i.at[layer, :, part], slope.at[:, part]) for part in parts]
    loads += [(tuple(x.at[:, part] for x in w1_hbm), w1.at[:, part]) for part in parts]
    early = len(loads)
    loads += [
        (x1_i.at[layer], x1), (proj_i.at[layer], proj), (wp_hbm, wp), (qkv_i.at[layer], qkv), (mixed_i.at[layer], mixed),
        (scales_i.at[layer], scales), (wqkv_hbm, wqkv), (xin_i.at[layer], xin),
    ]
    upstream_sem = load_sem.at[len(loads)]

    def start(number):
        source, target = loads[number]

        def go(ref):
            pltpu.make_async_copy(ref, target, load_sem.at[number]).start()

        if isinstance(source, tuple):
            pick(mine, *source, go)
        else:
            go(source)

    def load(number):
        target = loads[number][1]
        return pltpu.make_async_copy(target, target, load_sem.at[number])

    def store(number, source, there):
        return pltpu.make_async_copy(source, there.at[layer], store_sem.at[number])

    together = 2 * GROUP

    def prob_load(group):
        return pltpu.make_async_copy(
            prob_i.at[layer, pl.ds(together * group, together)], probs.at[group % 2], prob_sem.at[group % 2]
        )

    def vector(row):
        return pack_ref[row : row + 1, :]

    def put(row, partial):
        sums[row : row + 1, :] = jnp.sum(partial, 0, keepdims=True)

    nothing = jnp.zeros((8, width), F32)

    upstream_hbm = cotangent_hbm.at[section] if layer == 1 else dx_o.at[1]
    pltpu.make_async_copy(upstream_hbm, g_ref, upstream_sem).start()
    pick(mine, own_pack, other_pack, functools.partial(fill, pack_ref))
    for number in (0, 1):
        start(number)
    pltpu.make_async_copy(g_ref, g_ref, upstream_sem).wait()
    load(0).wait()
    for number in (5, 9, 2, 6, 10):
        start(number)
    scale_sum = bias_sum = nothing
    for rows in strips(0, length, STRIP):
        upstream = g_ref[rows, :].astype(F32)
        low = (upstream * vector(SCALE_M)).astype(BF16)
        dm[rows, :] = low
        scale_sum = scale_sum + fold(upstream * mlp[rows, :].astype(F32))
        bias_sum = bias_sum + fold(low.astype(F32))
    put(SCALE_M, scale_sum)
    put(B2, bias_sum)
    store(0, dm, dm_o).start()
    pieces = [pl.ds(part * width, width) for part in range(hidden // width)]

    def expand(number):
        load(1 + number).wait()
        return nt(dm[...], w2[pieces[number], :])

    coming = expand(0)
    upper_sum = None
    for number, columns in enumerate(pieces):
        if number == 0:
            for later in (3, 7, 11, 4, 8, 12):
                start(later)
        if number == 2:
            for later in range(early, len(loads)):
                start(later)
            prob_load(0).start()
        load(5 + number).wait()
        load(9 + number).wait()
        current = coming
        if number + 1 < len(pieces):
            coming = expand(number + 1)
        act_sum = nothing
        for there in strips(0, length, STRIP):
            low = (current[there] * slope[there, columns].astype(F32)).astype(BF16)
            dz[there, columns] = low
            act_sum = act_sum + fold(low.astype(F32))
        put(B1 + number, act_sum)
        more = nt(dz[:, columns], w1[:, columns])
        upper_sum = more if number == 0 else upper_sum + more
    store(1, dz, dz_o).start()
    load(early).wait()
    load(early + 1).wait()
    found = [nothing] * 4
    for rows in strips(0, length, STRIP):
        upper = upper_sum[rows]
        scaled, inverse = normalize(x1[rows, :])
        resid = g_ref[rows, :].astype(F32) + norm_back(upper * vector(GAIN2), scaled, inverse)
        dx1[rows, :] = resid
        low = (resid * vector(SCALE_A)).astype(BF16)
        dproj[rows, :] = low
        terms = (upper * scaled, upper, resid * proj[rows, :].astype(F32), low.astype(F32))
        found = [old + fold(term) for old, term in zip(found, terms)]
    for row, partial in zip((GAIN2, SHIFT2, SCALE_A, PBIAS), found):
        put(row, partial)
    store(2, dproj, dproj_o).start()
    load(early + 2).wait()
    dmixed[...] = nt(dproj[...], wp[...]).astype(BF16)
    for number in range(early + 3, early + 6):
        load(number).wait()

    def attend(side, within, pair):
        columns = chunk(pair, LANES)
        key_columns = pl.ds(pl.multiple_of(width + pair * LANES, LANES), LANES)
        value_columns = pl.ds(pl.multiple_of(2 * width + pair * LANES, LANES), LANES)
        values = qkv[:, value_columns]
        above = dmixed[:, columns]
        queries_t = qkv[:, columns].T
        keys_t = qkv[:, key_columns].T
        above_t = above.astype(F32).T
        products = (above.astype(F32) * mixed[:, columns]).T
        grads = [], [], []
        for which in range(2):
            place_in = 2 * within + which
            half = slice(which * HALF, (which + 1) * HALF)
            delta = jnp.sum(products[half], 0, keepdims=True)
            scale = scales[pl.ds(2 * pair + which, 1), :]
            own_values = jnp.where(half_mask(values.shape, which), values, jnp.zeros_like(values))
            edge = (blocks - 1) * LANES
            diag[place_in, :edge, :] = jnp.zeros((edge, LANES), F32)
            for wide in range(blocks // 2):
                prob_grad = nt(own_values, above[2 * LANES * wide : 2 * LANES * (wide + 1)])
                for part in range(2):
                    place = 2 * wide + part
                    low, high = key_rows(place, blocks)
                    lanes = slice(place * LANES, (place + 1) * LANES)
                    first_row = (blocks - 1 - place) * LANES
                    for rows in strips(low, high, 64):
                        here = (probs[side, place_in, rows, lanes].astype(F32) * scale[:, lanes]) * (
                            prob_grad[rows, part * LANES : (part + 1) * LANES] - delta[:, lanes]
                        )
                        dscore[place_in, rows, lanes] = here.astype(BF16)
                        there = slice(first_row + rows.start, first_row + rows.stop)
                        diag[place_in, there, :] = here if place == 0 else diag[place_in, there, :] + here
                    if low > 0:
                        dscore[place_in, :low, lanes] = jnp.zeros((low, LANES), BF16)
                    if high < length:
                        dscore[place_in, high:, lanes] = jnp.zeros((length - high, LANES), BF16)
                    if place == 0:
                        diag[place_in, edge + high :, :] = jnp.zeros((length - high, LANES), F32)
            line = gather_diagonals(diag.at[place_in])
            most = tables.shape[1] - LANES
            tables[pl.ds(2 * pair + which, 1), :] = jnp.concatenate(
                [line[:, REACH + 1 : REACH + 1 + most], line[:, REACH : REACH + LANES]], 1
            )
            grads[0].append(nn(keys_t[half], dscore[place_in]))
            grads[1].append(nt(queries_t[half], dscore[place_in]))
            grads[2].append(nt((above_t[half] * scale).astype(BF16), probs[side, place_in]))
        for found, where, scale in zip(grads, (columns, key_columns, value_columns), (factor, None, None)):
            low = jnp.concatenate(found, 0).astype(BF16)
            if scale is not None:
                low = (low.astype(F32) * scale).astype(BF16)
            packed[:, where] = low.T

    @pl.loop(0, pairs // GROUP)
    def _(group):
        prob_load(group).wait()

        @pl.when(group + 1 < pairs // GROUP)
        def _():
            prob_load(group + 1).start()

        for within in range(GROUP):
            attend(group % 2, within, GROUP * group + within)

    store(3, packed, packed_o).start()
    load(early + 6).wait()
    result = nt(packed[...], wqkv[...])
    load(early + 7).wait()
    found = [nothing] * 4
    for rows in strips(0, length, STRIP):
        upper = result[rows]
        scaled, inverse = normalize(xin[rows, :].astype(F32))
        dx_ref[rows, :] = (dx1[rows, :] + norm_back(upper * vector(GAIN1), scaled, inverse)).astype(BF16)
        terms = (
            upper * scaled,
            upper,
            packed[rows, :width].astype(F32),
            packed[rows, 2 * width :].astype(F32),
        )
        found = [old + fold(term) for old, term in zip(found, terms)]
    for row, partial in zip((GAIN1, SHIFT1, QBIAS, VBIAS), found):
        put(row, partial)
    store(4, dx_ref, dx_o).start()
    store(5, tables, tables_o).start()
    store(6, sums, sums_o).start()
    ends = {0: (dm, dm_o), 1: (dz, dz_o), 2: (dproj, dproj_o), 3: (packed, packed_o), 4: (dx_ref, dx_o), 5: (tables, tables_o), 6: (sums, sums_o)}
    for number, (source, there) in ends.items():
        store(number, source, there).wait()


def backward(layer, cotangent, packs, weights, saved, kept):
    length, width = cotangent.shape[1:]
    hidden = weights[2][0].shape[1]
    h1, qkv, probs, mixed, proj, x1, h2, xin, wide, scales, act, slope, mlp, y = saved
    heads = probs.shape[1]
    span = 2 * length - LANES
    summed = (16, width)
    table = (heads, 5 * LANES)
    stored = [
        ((length, width), BF16),
        ((length, hidden), BF16),
        ((length, width), BF16),
        ((length, 3 * width), BF16),
        ((length, width), BF16),
        (table, F32),
        (summed, F32),
    ]
    reads = [qkv, probs, wide, proj, x1, slope, mlp, xin, scales]
    scratch = [pltpu.VMEM(pair[0].shape, BF16) for pair in weights]
    scratch += [pltpu.VMEM((2, 2 * GROUP, length, length) if x is probs else x.shape[1:], x.dtype) for x in reads]
    scratch += [pltpu.VMEM(shape, kind) for shape, kind in stored[:5]]
    scratch += [
        pltpu.VMEM((length, width), F32),
        pltpu.VMEM((length, width), BF16),
        pltpu.VMEM((2 * GROUP, length, length), BF16),
        pltpu.VMEM((2 * GROUP, span, LANES), F32),
        pltpu.VMEM(summed, F32),
        pltpu.VMEM(table, F32),
        pltpu.VMEM((length, width), BF16),
        pltpu.VMEM(packs[0].shape, F32),
        pltpu.SemaphoreType.DMA((22,)),
        pltpu.SemaphoreType.DMA((7,)),
        pltpu.SemaphoreType.DMA((2,)),
    ]
    operands = [cotangent, *packs, *[x for pair in weights for x in pair], *reads]
    held = 7 if layer == 0 else 0
    return pl.pallas_call(
        functools.partial(backward_kernel, layer),
        out_shape=stacked(stored),
        in_specs=hbm_specs(1) + vmem_specs(2) + hbm_specs(8 + len(reads) + held),
        out_specs=hbm_specs(7),
        scratch_shapes=scratch,
        input_output_aliases={len(operands) + n: n for n in range(held)},
        compiler_params=pltpu.CompilerParams(vmem_limit_bytes=VMEM_BYTES),
        name="backward_layer",
    )(*operands, *(kept if layer == 0 else ()))


def small_lines(width):
    lines = width // LANES
    places = [(row, tile, row * lines + tile) for row in range(10) for tile in range(lines)]
    return places + [(B1, tile, B1 * lines + tile) for tile in range(4 * lines)]


def reverse_lanes(values):
    lane = lax.broadcasted_iota(jnp.int32, values.shape, 1)
    for place in range(LANES.bit_length() - 1):
        step = 1 << place
        up, down = pltpu.roll(values, step, 1), pltpu.roll(values, LANES - step, 1)
        values = jnp.where((lane // step) % 2 == 1, up, down)
    return values


def widen_kernel(sum_hbm, y_hbm, dx_hbm, small_ref, *refs):
    bigs, rows_out, vectors, table_ref = refs[:4], refs[4:6], refs[6 : 7 + VECTORS], refs[7 + VECTORS]
    narrow, wide, passing, load_sem, store_sem, pass_sem = refs[8 + VECTORS :]
    depth, width = narrow.shape[:2]
    blocks = [(0, slice(b * width, (b + 1) * width), slice(0, width)) for b in range(4)]
    for target, count in ((1, 4), (2, 3), (3, 1)):
        blocks += [(target, slice(0, width), slice(b * width, (b + 1) * width)) for b in range(count)]

    def load(block):
        rows = pl.ds(block * width, width)
        return pltpu.make_async_copy(sum_hbm.at[rows, :], narrow.at[block % depth], load_sem.at[block % depth])

    def store(block):
        target, rows, columns = blocks[block]
        there = bigs[target].at[rows, columns]
        return pltpu.make_async_copy(wide.at[block % depth], there, store_sem.at[block % depth])

    def fetch(number):
        return pltpu.make_async_copy((y_hbm, dx_hbm)[number], passing.at[number], pass_sem.at[0, number])

    def put(number):
        return pltpu.make_async_copy(passing.at[number], rows_out[number], pass_sem.at[1, number])

    for block in range(depth):
        load(block).start()
    for number in range(2):
        fetch(number).start()
    for block in range(len(blocks)):
        if block == depth:
            for number in range(2):
                fetch(number).wait()
                put(number).start()
        load(block).wait()
        if block >= depth:
            store(block - depth).wait()
        for rows in strips(0, width, 64):
            wide[block % depth, rows, :] = narrow[block % depth, rows, :].astype(F32)
        store(block).start()
        if block + depth < len(blocks):
            load(block + depth).start()
    places = small_lines(width)
    for row, tile, line in places:
        vectors[row][:, tile * LANES : (tile + 1) * LANES] = small_ref[line : line + 1, :]
    first = len(places)
    heads, _, entries = table_ref.shape
    tiles = -(-entries // LANES)
    flipped = reverse_lanes(small_ref[first : first + heads * tiles, :])
    for head in range(heads):
        for tile in range(tiles - 1):
            line = head * tiles + tile
            there = (tiles - 2 - tile) * LANES
            table_ref[head, :, there : there + LANES] = flipped[line : line + 1]
        line = first + head * tiles + tiles - 1
        table_ref[head, :, entries - 1 :] = small_ref[line : line + 1, 0:1]
    for block in range(len(blocks) - depth, len(blocks)):
        store(block).wait()
    for number in range(2):
        put(number).wait()


def widen(summed, small, y, dx, width, heads, entries):
    bigs = [(4 * width, width), (width, 4 * width), (width, 3 * width), (width, width)]
    shapes = [(1, width)] * 10 + [(1, 4 * width), (heads, 1, entries)]
    return pl.pallas_call(
        widen_kernel,
        out_shape=[jax.ShapeDtypeStruct(shape, F32) for shape in bigs]
        + [jax.ShapeDtypeStruct(y.shape, BF16)] * 2
        + [jax.ShapeDtypeStruct(shape, F32) for shape in shapes],
        in_specs=hbm_specs(3) + vmem_specs(1),
        out_specs=hbm_specs(6) + vmem_specs(VECTORS + 2),
        scratch_shapes=[
            pltpu.VMEM((3, width, width), BF16),
            pltpu.VMEM((3, width, width), F32),
            pltpu.VMEM((2, *y.shape), BF16),
            pltpu.SemaphoreType.DMA((3,)),
            pltpu.SemaphoreType.DMA((3,)),
            pltpu.SemaphoreType.DMA((2, 2)),
        ],
        compiler_params=pltpu.CompilerParams(vmem_limit_bytes=VMEM_BYTES),
        name="widen",
    )(summed, y, dx, small)


BLOCK = 256
LAG = 3


def reduce_kernel(bits, chunks, blocks, lags, window, lined, *refs):
    (a_ref, dm_ref, h2_ref, dz_ref, h1_ref, dp_ref, o_ref, dproj_ref, y_ref, dx_ref, sums_ref, tables_ref) = refs[:12]
    out_ref, small_out_ref, y_out, dx_out = refs[12:16]
    refs = refs[16:]
    (lhs, rhs, grads, total, crossing, landed, smalls, small_ref, small_landed, small_total) = refs[:10]
    small_received, received = refs[10 : 10 + bits], refs[10 + bits : -10]
    (load_sem, send_sem, recv_sem, small_send, small_recv, store_sem, cross_send, cross_recv, row_sem, credit) = refs[-10:]
    me = lax.axis_index("dp")
    section = lax.axis_index("section")
    beside = 1 - section
    rows = BLOCK * blocks
    width = grads.shape[1]
    per_side = width // BLOCK
    last = 2 * bits
    steps = 10 if lined else last
    starts = [0] + [lags[0] + lags[1] * place for place in range(steps + 1)]

    barrier = pltpu.get_barrier_semaphore()
    for place in range(bits):
        stride = 1 << place
        other = me + stride * (1 - 2 * ((me // stride) % 2))
        pl.semaphore_signal(barrier, inc=1, device_id={"dp": other}, device_id_type=MESH)
    pl.semaphore_signal(barrier, inc=1, device_id={"section": beside}, device_id_type=MESH)
    pl.semaphore_wait(barrier, bits + 1)

    def across(source, target, number):
        return pltpu.make_async_remote_copy(
            src_ref=source,
            dst_ref=target,
            send_sem=cross_send.at[number],
            recv_sem=cross_recv.at[number],
            device_id={"section": beside},
            device_id_type=MESH,
        )

    def row_copy(number):
        source, target = ((y_ref, y_out), (dx_ref, dx_out))[number]
        return pltpu.make_async_copy(source.at[section], target.at[section], row_sem.at[number])

    def row_across(number):
        source, target = ((y_ref, y_out), (dx_ref, dx_out))[number]
        return across(source.at[beside], target.at[section], window + 1 + number)

    families = (
        (a_ref, dm_ref, 4 * per_side, True),
        (h2_ref, dz_ref, 4 * per_side, False),
        (h1_ref, dp_ref, 3 * per_side, False),
        (o_ref, dproj_ref, per_side, False),
    )
    n_blocks = 12 * per_side

    def load(block):
        slot = block % 2
        first = 0
        for left, right, count, walks in families:
            @pl.when((block >= first) & (block < first + count))
            def _():
                local = block - first
                if walks:
                    left_column = local * BLOCK
                    right_column = 0
                else:
                    left_column = (local % per_side) * BLOCK
                    right_column = (local // per_side) * width
                for number, layer in enumerate((section, beside)):
                    pltpu.make_async_copy(
                        left.at[layer, :, pl.ds(pl.multiple_of(left_column, BLOCK), BLOCK)],
                        lhs.at[slot, number],
                        load_sem.at[0, slot],
                    ).start()
                    pltpu.make_async_copy(
                        right.at[layer, :, pl.ds(pl.multiple_of(right_column, BLOCK), width)],
                        rhs.at[slot, number],
                        load_sem.at[1, slot],
                    ).start()
            first += count

    def produce(block, sub, side):
        slot = block % 2
        pltpu.make_async_copy(lhs.at[slot], lhs.at[slot], load_sem.at[0, slot]).wait()
        pltpu.make_async_copy(rhs.at[slot], rhs.at[slot], load_sem.at[1, slot]).wait()

        @pl.when(block + 1 < n_blocks)
        def _():
            load(block + 1)

        crossing[side, sub * BLOCK : (sub + 1) * BLOCK, :] = dot(lhs[slot, 1], rhs[slot, 1], 0, 0).astype(BF16)
        grads[chunk(block, BLOCK), :] = dot(lhs[slot, 0], rhs[slot, 0], 0, 0).astype(BF16)

    def turn(chunk):
        place = chunk % 9
        return place % 2 + place // 5 - place // 6

    def partner(rotation, stage):
        stride = lax.shift_left(jnp.int32(1), (stage + rotation) % bits)
        mine = (me // stride) % 2
        return mine, me + stride * (1 - 2 * mine)

    def offset(base, height, rotation, stage):
        for earlier in range(stage):
            mine, _ = partner(rotation, earlier)
            base = base + mine * (height >> (earlier + 1))
        return base

    def piece(ref, start, size):
        return ref.at[pl.ds(pl.multiple_of(start, size), size)]

    def send(position, base, height, rotation, source, landing, result, slot, sems):
        send_at, recv_at = sems
        if position < bits:
            stage = position
            half = height >> (stage + 1)
            mine, other = partner(rotation, stage)
            start = offset(base, height, rotation, stage) + (1 - mine) * half
            src, dst = piece(source, start, half), landing[stage].at[slot]
        else:
            stage = last - 1 - position
            half = height >> (stage + 1)
            mine, other = partner(rotation, stage)
            start = offset(base, height, rotation, stage + 1)
            src = dst = piece(result, start, half)
        return pltpu.make_async_remote_copy(
            src_ref=src,
            dst_ref=dst,
            send_sem=send_at.at[position],
            recv_sem=recv_at.at[position, slot],
            device_id={"dp": other},
            device_id_type=MESH,
        )

    def take(position, base, height, rotation, source, landing, result, slot, sems):
        send(position - 1, base, height, rotation, source, landing, result, slot, sems).wait_recv()
        stage = position - 1
        if stage < bits:
            half = height >> (stage + 1)
            start = pl.multiple_of(offset(base, height, rotation, stage + 1), half)
            keep = pl.ds(start, half)
            value = source[keep, :].astype(jnp.float32) + landing[stage][slot].astype(jnp.float32)
            target = result if stage == bits - 1 else source
            target[keep, :] = value.astype(target.dtype)

    def step(position, *way):
        if position > 0:
            take(position, *way)
        if position < last:
            send(position, *way).start()

    main = (grads, received, total)
    main_sems = (send_sem, recv_sem)

    def cross(side):
        return across(crossing.at[side], landed.at[side], side)

    def give(part):
        side = part % window

        @pl.when(part >= window)
        def _():
            cross(side).wait_send()
            pl.semaphore_wait(credit, 1)

        for sub in range(blocks):
            block = part * blocks + sub

            @pl.when(block < n_blocks)
            def _():
                produce(block, sub, side)

        cross(side).start()

    def join(part):
        side = part % window
        cross(side).wait_recv()
        there = chunk(part, rows)
        grads[there, :] = (grads[there, :].astype(F32) + landed[side].astype(F32)).astype(BF16)

        @pl.when(part < chunks - window)
        def _():
            pl.semaphore_signal(credit, inc=1, device_id={"section": beside}, device_id_type=MESH)

    row_z = me // 4
    side_z = row_z // 2
    middle = (row_z + side_z) % 2
    inner, outer = me + 4 * (1 - 2 * side_z), me - 4 * (1 - 2 * side_z)

    def line_plan(early, part):
        place = part % 8
        first = 1 + (place // 2 if early else place % 2 * ((place + 5) // 8))
        second = 3 - first
        mine_first, mine_second = (me // first) % 2, (me // second) % 2
        peer_first = me + first * (1 - 2 * mine_first)
        peer_second = me + second * (1 - 2 * mine_second)
        base = part * rows
        before = 1 + (place + 5) // 8
        if early:
            slot = 2 * (part // 8) + place // 2
            landing = received[4:]
            quarter = rows // 4
            line = base
            whole = base + row_z * quarter
            size_first = quarter // 2
        else:
            slot = part - 2 * (part // 8) - before
            landing = received[:4]
            whole = base
            size_first = rows // 2
        size_second = size_first // 2
        keep_first = whole + mine_first * size_first
        keep_second = keep_first + mine_second * size_second
        if not early:
            line = keep_second
            quarter = size_second // 4
        everyone = None
        line_land, cross_land, first_land, second_land = [ref.at[slot] for ref in landing]
        mostly = line + quarter * (1 - side_z)
        ending = line + 3 * quarter * side_z
        near, far = line + 2 * quarter * side_z, line + 2 * quarter * (1 - side_z)
        swap_first = (everyone, everyone, peer_first, whole + (1 - mine_first) * size_first, size_first, keep_first, first_land)
        swap_second = (
            everyone, everyone, peer_second, keep_first + (1 - mine_second) * size_second, size_second, keep_second, second_land
        )
        inward = (0, 1, inner, mostly, 3 * quarter, mostly, line_land)
        between = (1, 1, inner, far, 2 * quarter, near, cross_land)
        outward = (1, 0, outer, ending, quarter, ending, line_land.at[pl.ds(0, quarter)])
        back_inward = (0, 1, inner, ending, quarter, None, None)
        back_between = (1, 1, inner, near, 2 * quarter, None, None)
        back_outward = (1, 0, outer, mostly, 3 * quarter, None, None)
        back_first = (everyone, everyone, peer_first, keep_first, size_first, None, None)
        back_second = (everyone, everyone, peer_second, keep_second, size_second, None, None)
        if early:
            return [inward, between, outward, swap_first, swap_second,
                    back_second, back_first, back_inward, back_between, back_outward]
        return [swap_first, swap_second, inward, between, outward,
                back_inward, back_between, back_outward, back_second, back_first]

    def only(role, act):
        if role is None:
            act()
        else:
            pl.when(middle == role)(act)

    def line_step(position, part):
        def run(early):
            plan = line_plan(early, part)

            def copy(number):
                sender, receiver, peer, start, size, arrives, lands = plan[number]
                source = grads if arrives is not None else total
                here = pl.ds(pl.multiple_of(start, 16), size)
                return pltpu.make_async_remote_copy(
                    src_ref=source.at[here],
                    dst_ref=total.at[here] if arrives is None else lands,
                    send_sem=send_sem.at[number],
                    recv_sem=recv_sem.at[number, part],
                    device_id={"dp": peer},
                    device_id_type=MESH,
                )

            def arrive():
                size, arrives, lands = plan[position - 1][4:]
                copy(position - 1).wait_recv()
                if arrives is not None:
                    there = pl.ds(pl.multiple_of(arrives, 16), size)
                    value = (grads[there, :].astype(F32) + lands[...].astype(F32)).astype(BF16)
                    if position == 5:
                        total[there, :] = value
                    else:
                        grads[there, :] = value

            if position > 0:
                only(plan[position - 1][1], arrive)
            if position == 5 and not early:

                def keep():
                    size = rows // 16
                    there = pl.ds(pl.multiple_of(plan[1][5] + row_z * size, 16), size)
                    total[there, :] = grads[there, :]

                only(1, keep)
            if position < 10:
                only(plan[position][0], lambda: copy(position).start())

        early = (part % 8 == 0) | (part % 8 == 2)

        @pl.when(early)
        def _():
            run(True)

        @pl.when(jnp.logical_not(early))
        def _():
            run(False)

    def line_rows(role):
        ends = ([128, 64, 48, 0, 0, 16, 0, 0, 64, 128], [192, 0, 0, 32, 16, 16, 32, 64, 0, 0])
        middles = ([128, 64, 0, 32, 16, 0, 32, 48, 64, 128], [0, 128, 64, 32, 16, 16, 32, 0, 128, 192])
        late, soon = middles if role else ends
        count = sum(part % 8 in (0, 2) for part in range(chunks))
        return [(chunks - count) * a + count * b for a, b in zip(late, soon)]

    def walk(position, part):
        if position == 0:
            join(part)
        base = part * rows
        if lined:
            line_step(position, part)
        else:
            step(position, base, rows, turn(part), *main, part, main_sems)
        if position == steps:
            there = pl.ds(pl.multiple_of(base, rows), rows)
            pltpu.make_async_copy(total.at[there], out_ref.at[there], store_sem.at[0]).start()

    def small_cross():
        return across(smalls.at[beside], small_landed, window)

    def walk_small(position):
        height = small_ref.shape[0]
        if position == 0:
            small_cross().wait_recv()
            small_ref[...] = smalls[section] + small_landed[...]
        way = (0, height, 0, small_ref, small_received, small_total, 0, (small_send, small_recv))
        step(position, *way)

    load(jnp.int32(0))
    def assemble():
        smalls[...] = jnp.zeros_like(smalls)
        places = small_lines(width)
        for layer in range(2):
            for row, tile, line in places:
                if row == B1:
                    row, tile = B1 + tile // (width // LANES), tile % (width // LANES)
                smalls[layer, line : line + 1, :] = sums_ref[layer, row : row + 1, tile * LANES : (tile + 1) * LANES]
            line = len(places)
            for head in range(tables_ref.shape[1]):
                for tile in range(tables_ref.shape[2] // LANES):
                    lanes = slice(tile * LANES, (tile + 1) * LANES)
                    smalls[layer, line : line + 1, :] = tables_ref[layer, head : head + 1, lanes]
                    line += 1
        small_cross().start()
        for number in range(2):
            row_copy(number).start()
            row_across(number).start()

    @pl.loop(0, chunks + starts[-1])
    def _(tick):
        @pl.when(tick < chunks)
        def _():
            give(tick)

        pl.when(tick == 0)(assemble)

        for position in range(steps + 1):
            part = tick - starts[position + 1]

            @pl.when((part >= 0) & (part < chunks))
            def _():
                walk(position, part)

            if position <= last:

                @pl.when(part == 0)
                def _():
                    walk_small(position)

    small_out_ref[...] = small_total[...]
    for position in range(last):
        stage = position if position < bits else last - 1 - position
        size = small_received[stage]
        pltpu.make_async_copy(size, size, small_send.at[position]).wait()
        if not lined:
            size = received[stage]
            pltpu.make_async_copy(size, size, send_sem.at[position]).wait()
    if lined:
        for role in range(2):

            @pl.when(middle == role)
            def _():
                for number, amount in enumerate(line_rows(role)):
                    if amount > 0:
                        size = grads.at[pl.ds(0, amount)]
                        pltpu.make_async_copy(size, size, send_sem.at[number]).wait()
    for side in range(window):
        cross(side).wait_send()
    small_cross().wait_send()
    for number in range(2):
        row_copy(number).wait()
        row_across(number).wait()
    pltpu.make_async_copy(total, out_ref, store_sem.at[0]).wait()


def reduce_gradients(a, dm, h2, dz, h1, packed, o, dproj, y, dx, sums, tables):
    parts = lax.axis_size("dp")
    bits = parts.bit_length() - 1
    blocks = max(1, 16 * parts // BLOCK)
    layers, length, width = h1.shape
    n_blocks = 12 * width // BLOCK
    chunks = -(-n_blocks // blocks)
    rows = BLOCK * blocks
    lags, window = ((1, LAG), 4) if blocks == 1 else ((0, LAG), 1)
    lines = len(small_lines(width)) + tables.shape[1] * tables.shape[2] // LANES
    height = -(-lines // (8 * parts)) * 8 * parts
    small = (height, LANES)
    lined = parts == 16
    if lined:
        early = sum(part % 8 in (0, 2) for part in range(chunks))
        lands = [(chunks - early, size) for size in (48, 32, 128, 64)] + [(early, size) for size in (192, 128, 32, 16)]
    else:
        lands = [(chunks, rows >> (s + 1)) for s in range(bits)]
    steps = 10 if lined else 2 * bits
    return pl.pallas_call(
        functools.partial(reduce_kernel, bits, chunks, blocks, lags, window, lined),
        out_shape=(
            jax.ShapeDtypeStruct((chunks * rows, width), BF16),
            jax.ShapeDtypeStruct(small, F32),
            jax.ShapeDtypeStruct(y.shape, BF16),
            jax.ShapeDtypeStruct(dx.shape, BF16),
        ),
        in_specs=hbm_specs(10) + vmem_specs(2),
        out_specs=hbm_specs(1) + vmem_specs(1) + hbm_specs(2),
        scratch_shapes=[
            pltpu.VMEM((2, layers, length, BLOCK), BF16),
            pltpu.VMEM((2, layers, length, width), BF16),
            pltpu.VMEM((chunks * rows, width), BF16),
            pltpu.VMEM((chunks * rows, width), BF16),
            pltpu.VMEM((window, rows, width), BF16),
            pltpu.VMEM((window, rows, width), BF16),
            pltpu.VMEM((layers, *small), F32),
            pltpu.VMEM(small, F32),
            pltpu.VMEM(small, F32),
            pltpu.VMEM(small, F32),
            *[pltpu.VMEM((1, height >> (s + 1), LANES), F32) for s in range(bits)],
            *[pltpu.VMEM((*size, width), BF16) for size in lands],
            pltpu.SemaphoreType.DMA((2, 2)),
            pltpu.SemaphoreType.DMA((steps,)),
            pltpu.SemaphoreType.DMA((steps, chunks)),
            pltpu.SemaphoreType.DMA((2 * bits,)),
            pltpu.SemaphoreType.DMA((2 * bits, 1)),
            pltpu.SemaphoreType.DMA((1,)),
            pltpu.SemaphoreType.DMA((window + 3,)),
            pltpu.SemaphoreType.DMA((window + 3,)),
            pltpu.SemaphoreType.DMA((2,)),
            pltpu.SemaphoreType.REGULAR,
        ],
        compiler_params=pltpu.CompilerParams(
            collective_id=0, has_side_effects=True, vmem_limit_bytes=VMEM_BYTES
        ),
        name="reduce_gradients",
    )(a, dm, h2, dz, h1, packed, o, dproj, y, dx, sums, tables)


def swapped(block):
    return lax.ppermute(block, "section", [(0, 1), (1, 0)])


def per_device(
    patches,
    segment_ids,
    pad_counts,
    norm1_gain,
    norm1_bias,
    qkv_weight,
    query_bias,
    value_bias,
    rel_table,
    proj_weight,
    proj_bias,
    scale_attn,
    norm2_gain,
    norm2_bias,
    fc1_weight,
    fc1_bias,
    fc2_weight,
    fc2_bias,
    scale_mlp,
    cotangent,
):
    micro, length, width = patches.shape
    heads, entries = rel_table.shape[1:]
    vectors = (
        norm1_gain,
        norm1_bias,
        query_bias,
        value_bias,
        proj_bias,
        scale_attn,
        norm2_gain,
        norm2_bias,
        fc2_bias,
        scale_mlp,
        fc1_bias,
    )
    own = pack(vectors, rel_table.transpose(1, 0, 2))
    own_band = bias_band(own, heads, length)
    other = swapped(own)
    weights = [(x, swapped(x)) for x in (qkv_weight[0], proj_weight[0])]
    own_band, other, *late = lax.optimization_barrier(
        (own_band, other, weights[0][1], weights[1][1], fc1_weight[0], fc2_weight[0])
    )
    weights = [(weights[0][0], late[0]), (weights[1][0], late[1])] + [(x, swapped(x)) for x in late[2:]]
    other_band = bias_band(other, heads, length)
    packs, band = (own, other), (own_band, other_band)
    saved = None
    rows = patches
    for layer, phase in ((0, ATTENTION), (0, MLP), (1, BOTH)):
        saved = forward(layer, phase, pad_counts, rows, segment_ids, packs, band, weights, saved)
    kept = None
    for layer in (1, 0):
        kept = backward(layer, cotangent, packs, weights, saved, kept)
    dm, dz, dproj, packed, dx, tables, sums = kept
    h1, mixed, h2, act, y = saved[0], saved[3], saved[6], saved[10], saved[13]
    summed, small, y, dx = reduce_gradients(
        act, dm, h2, dz, h1, packed, mixed, dproj, y, dx, sums, tables
    )
    fc2_grad, fc1_grad, qkv_grad, proj_grad, outputs, in_grads, *small_grads = widen(
        summed, small, y, dx, width, heads, entries
    )
    table_grad = small_grads[VECTORS + 1].transpose(1, 0, 2)
    return (
        outputs[None],
        in_grads[None],
        small_grads[GAIN1],
        small_grads[SHIFT1],
        qkv_grad[None],
        small_grads[QBIAS],
        small_grads[VBIAS],
        table_grad,
        proj_grad[None],
        small_grads[PBIAS],
        small_grads[SCALE_A],
        small_grads[GAIN2],
        small_grads[SHIFT2],
        fc1_grad[None],
        small_grads[B1],
        fc2_grad[None],
        small_grads[B2],
        small_grads[SCALE_M],
    )


def solution(mesh):
    placed = (
        P("dp", None, None),
        P("dp", None),
        P("dp"),
        P("section", None),
        P("section", None),
        P("section", None, None),
        P("section", None),
        P("section", None),
        P("section", None, None),
        P("section", None, None),
        P("section", None),
        P("section", None),
        P("section", None),
        P("section", None),
        P("section", None, None),
        P("section", None),
        P("section", None, None),
        P("section", None),
        P("section", None),
        P("dp", None, None),
    )
    return jax.shard_map(
        per_device,
        mesh=mesh,
        in_specs=placed,
        out_specs=(
            P("section", "dp", None, None),
            P("section", "dp", None, None),
            P("section", None),
            P("section", None),
            P("section", None, None),
            P("section", None),
            P("section", None),
            P("section", None, None),
            P("section", None, None),
            P("section", None),
            P("section", None),
            P("section", None),
            P("section", None),
            P("section", None, None),
            P("section", None),
            P("section", None, None),
            P("section", None),
            P("section", None),
        ),
        check_vma=False,
    )
```
